32 devices in a mesh: dom: 16 (over z, y, core), band: 2 (over x).
Axes of the slice: x: 2, y: 2, z: 4, core: 2. Of those that a mesh axis runs over, the one named last changes fastest.
Arguments:
- orbitals: float32 [16, 16, 12, 16, 128], P('dom', 'band'), may hold values from -6 to 6
- potential: float32 [16, 12, 16, 128], P('dom'), may hold values from -12 to 4
- projectors: bfloat16 [4096, 4, 128], P('dom'), may hold values from -0.359375 to 0.359375
- entry_atom: int32 [4096], P('dom'), may hold values from 0 to 63, as said below
- entry_block: int32 [4096], P('dom'), may hold values from 0 to 191
- kb_energy: float32 [64, 4], replicated, may hold values from 1 to 10
- panel: bfloat16 [16, 16], replicated, may hold values from -1.5 to 1.5
Outputs:
- rotated: float32 [16, 16, 12, 16, 128], P('dom', 'band')
The draws below stay inside these ranges and needn't reach their ends.
Inputs may be any that keep to these rules, and one draw needn't show every extreme that they name: `entry_atom`: atom a is owned by domain a // 4; every entry of domain d belongs to an atom owned by d or by a domain that shares a face with d in the 2 x 2 x 4 arrangement of domains (no wrap-around).
All inputs are finite; a program needn't handle non-finite values.
Results may differ from the reference program's by a relative error of at most 0.00115.
The reference program's roundings to bfloat16 on the way (of `filtered`) count: a program that leaves them out, or rounds other values in their place, can miss the bound.
Values may be sent and summed in bfloat16 or wider, within the bound.
No kernel may reach another device: no remote copies, remote signals or barrier semaphores. Data moves between devices by JAX's collectives and lax.ppermute only.
A program may use at most 64 MiB of HBM per device.

```python
import math
import jax
import jax.numpy as jnp
from jax import lax

NORB = 16
NPROJ = 4
RADIUS = 6
BLK = 128
CX = 12
CY = 16
CZ = 128
ENT = 256
ATOM_DEV = 4
DOM_Z = 4
DOM_Y = 2
DOM_X = 2
NX = 24
NY = 32
NZ = 512
ATOMS = 64
NBLK = 192
N_DOM = 16


def draw_entry_atom(key, part):
    total = N_DOM * ENT
    domain = jnp.arange(total, dtype=jnp.int32) // ENT
    first = domain // (DOM_Y * DOM_Z)
    second = domain // DOM_Z % DOM_Y
    third = domain % DOM_Z
    key_dir = jax.random.fold_in(key, 11)
    key_loc = jax.random.fold_in(key, 23)
    direction = jax.random.randint(key_dir, (total,), 0, 7, dtype=jnp.int32)
    chosen = jax.random.randint(key_loc, (total,), 0, ATOM_DEV, dtype=jnp.int32)
    step_first = jnp.array([0, 1, -1, 0, 0, 0, 0], dtype=jnp.int32)[direction]
    step_second = jnp.array([0, 0, 0, 1, -1, 0, 0], dtype=jnp.int32)[direction]
    step_third = jnp.array([0, 0, 0, 0, 0, 1, -1], dtype=jnp.int32)[direction]
    new_first = first + step_first
    new_second = second + step_second
    new_third = third + step_third
    inside = (new_first >= 0) & (new_first < DOM_X) & (new_second >= 0) & (new_second < DOM_Y) & (new_third >= 0) & (new_third < DOM_Z)
    new_first = jnp.where(inside, new_first, first)
    new_second = jnp.where(inside, new_second, second)
    new_third = jnp.where(inside, new_third, third)
    owner = (new_first * DOM_Y + new_second) * DOM_Z + new_third
    return (owner * ATOM_DEV + chosen).astype(jnp.int32)


def draw_orbitals(key, part):
    shape = (N_DOM, NORB, CX, CY, CZ)
    domain = jnp.arange(N_DOM, dtype=jnp.int32)[:, None, None, None, None]
    first = domain // (DOM_Y * DOM_Z) * CX + jnp.arange(CX, dtype=jnp.int32)[None, None, :, None, None]
    second = domain // DOM_Z % DOM_Y * CY + jnp.arange(CY, dtype=jnp.int32)[None, None, None, :, None]
    third = domain % DOM_Z * CZ + jnp.arange(CZ, dtype=jnp.int32)[None, None, None, None, :]
    key_cycle = jax.random.fold_in(key, 31)
    key_phase = jax.random.fold_in(key, 37)
    key_rough = jax.random.fold_in(key, 41)
    cycles = jax.random.uniform(key_cycle, (3, NORB), jnp.float32, 0.5, 2.0)
    phases = jax.random.uniform(key_phase, (3, NORB), jnp.float32, -3.14159, 3.14159)

    def wave(coord, count, index):
        turns = coord.astype(jnp.float32) / float(count)
        angle = 6.2831853 * turns * cycles[index][None, :, None, None, None] + phases[index][None, :, None, None, None]
        return jnp.sin(angle)
    smooth = wave(first, NX, 0) + wave(second, NY, 1) + wave(third, NZ, 2)
    rough = 0.6 * jax.random.truncated_normal(key_rough, -3.0, 3.0, shape, jnp.float32)
    amplitude = 1.2
    return (amplitude * smooth + rough).astype(jnp.float32)


def touch_ends(values, stream_key, smallest, high):
    longest = values.shape.index(max(values.shape))
    spots = []
    for shift in (0, 1):
        where = [jax.random.randint(jax.random.fold_in(stream_key, axis), (), 0, length) for axis, length in enumerate(values.shape)]
        where[longest] = (where[longest] + shift) % values.shape[longest]
        spots.append(tuple(where))
    return values.at[spots[0]].set(smallest).at[spots[1]].set(high)


def block_scale(stream_key, dims, shards, least, largest):
    def one(axis_at, parts):
        draws = jax.random.uniform(jax.random.fold_in(jax.random.fold_in(stream_key, 6), axis_at), (parts,), jnp.float32, least / len(shards), largest / len(shards))
        return jnp.repeat(jnp.exp(draws), dims[axis_at] // parts).reshape((-1,) + (1,) * (len(dims) - axis_at - 1))

    level = one(*shards[0])
    for cut in shards[1:]:
        level = level * one(*cut)
    return level


def bell_draw(rng, shape, spread, limit, shards=(), kind=jnp.bfloat16):
    entries = spread * jax.random.normal(rng, shape, jnp.float32)
    if shards:
        entries = entries * block_scale(rng, shape, shards, -0.22, 0.18)
    return jnp.clip(entries, -limit, limit).astype(kind)


def setup_inputs(seed: int = 0) -> dict:
    key_of = jax.random.split(jax.random.key(seed), 8)
    orbitals = draw_orbitals(jax.random.fold_in(key_of[7], 71), 0)
    potential = jnp.clip(-12.0 + 16.0 * jax.random.uniform(key_of[1], (N_DOM, CX, CY, CZ), jnp.float32) ** block_scale(key_of[1], (N_DOM, CX, CY, CZ), ((0, 16),), -0.2, 0.2), -12.0, 4.0)
    projectors = bell_draw(key_of[2], (N_DOM * ENT, NPROJ, BLK), 0.06, 0.359375, ((0, 16),))
    entry_atom = draw_entry_atom(jax.random.fold_in(key_of[7], 71), 0)
    entry_block = touch_ends(jax.random.randint(key_of[4], (N_DOM * ENT,), 0, NBLK), jax.random.fold_in(key_of[4], 1), 0, NBLK - 1).astype(jnp.int32)
    kb_energy = jnp.clip(jnp.exp(jax.random.uniform(key_of[5], (ATOMS, NPROJ), jnp.float32, math.log(1.0), math.log(10.0))), 1.0, 10.0)
    panel = bell_draw(key_of[6], (NORB, NORB), NORB ** -0.5, 1.5)
    return {"orbitals": orbitals, "potential": potential, "projectors": projectors, "entry_atom": entry_atom, "entry_block": entry_block, "kb_energy": kb_energy, "panel": panel}


COEFFS = (-5369.0 / 1800.0, 12.0 / 7.0, -15.0 / 56.0, 10.0 / 189.0, -1.0 / 112.0, 2.0 / 1925.0, -1.0 / 16632.0)
KINETIC = -3.125
CENTER = 36.0
HALF_WIDTH = 34.0


def to_grid(blocks):
    shaped = blocks.reshape(DOM_X, DOM_Y, DOM_Z, CX, CY, CZ)
    return shaped.transpose(0, 3, 1, 4, 2, 5).reshape(NX, NY, NZ)


def to_blocks(grid_values):
    shaped = grid_values.reshape(DOM_X, CX, DOM_Y, CY, DOM_Z, CZ)
    return shaped.transpose(0, 2, 4, 1, 3, 5).reshape(N_DOM, CX, CY, CZ)


def window(padded, position, offset, extents):
    pieces = [slice(RADIUS, RADIUS + extents[0]), slice(RADIUS, RADIUS + extents[1]), slice(RADIUS, RADIUS + extents[2])]
    pieces[position] = slice(RADIUS + offset, RADIUS + offset + extents[position])
    return padded[tuple(pieces)]


def local_part(grid_values, pot_grid):
    padded = jnp.pad(grid_values, RADIUS)
    extents = grid_values.shape
    laplace = 3.0 * COEFFS[0] * grid_values
    for position in range(3):
        for offset in range(1, RADIUS + 1):
            upward = window(padded, position, offset, extents)
            downward = window(padded, position, -offset, extents)
            laplace = laplace + COEFFS[offset] * (upward + downward)
    return KINETIC * laplace + pot_grid * grid_values


def reference(orbitals, potential, projectors, entry_atom, entry_block, kb_energy, panel):
    pot_grid = to_grid(potential)
    proj_values = projectors.astype(jnp.float32)
    entry_domain = (jnp.arange(N_DOM * ENT, dtype=jnp.int32) // ENT).astype(jnp.int32)

    def nonlocal_part(grid_values):
        rows_all = to_blocks(grid_values).reshape(N_DOM, NBLK, BLK)
        picked = rows_all[entry_domain, entry_block]
        intersections = jnp.einsum('epk,ek->ep', proj_values, picked, precision=lax.Precision.HIGHEST)
        atom_table = jax.ops.segment_sum(intersections, entry_atom, num_segments=ATOMS)
        scaled = kb_energy * atom_table
        per_entry = scaled[entry_atom]
        additions = jnp.einsum('epk,ep->ek', proj_values, per_entry, precision=lax.Precision.HIGHEST)
        result = jnp.zeros((N_DOM, NBLK, BLK), jnp.float32).at[entry_domain, entry_block].add(additions)
        return to_grid(result.reshape(N_DOM, CX, CY, CZ))

    def apply_ham(grid_values):
        return local_part(grid_values, pot_grid) + nonlocal_part(grid_values)

    def filter_one(blocks):
        start_grid = to_grid(blocks)
        applied = apply_ham(start_grid)
        first_step = (applied - CENTER * start_grid) / HALF_WIDTH
        applied_again = apply_ham(first_step)
        second_step = 2.0 * (applied_again - CENTER * first_step) / HALF_WIDTH - start_grid
        return to_blocks(second_step).astype(jnp.bfloat16)

    filtered = lax.map(filter_one, jnp.transpose(orbitals, (1, 0, 2, 3, 4)))
    rotated = jnp.einsum('iabcd,ij->jabcd', filtered.astype(jnp.float32), panel.astype(jnp.float32), precision=lax.Precision.HIGHEST)
    return jnp.transpose(rotated, (1, 0, 2, 3, 4))
```

```python
import functools

import jax
import jax.numpy as jnp
from jax import lax
from jax.experimental import pallas as pl
from jax.experimental.pallas import tpu as pltpu
from jax.sharding import PartitionSpec as P

RADIUS = 6
COEFFS = (
    -5369.0 / 1800.0,
    12.0 / 7.0,
    -15.0 / 56.0,
    10.0 / 189.0,
    -1.0 / 112.0,
    2.0 / 1925.0,
    -1.0 / 16632.0,
)
KINETIC = -3.125
CENTER = 36.0
HALF_WIDTH = 34.0
WEIGHT = [KINETIC * c / HALF_WIDTH for c in COEFFS]
DIAGONAL = (3.0 * KINETIC * COEFFS[0] - CENTER) / HALF_WIDTH

F32 = jnp.float32
BF16 = jnp.bfloat16
VMEM = pl.BlockSpec(memory_space=pltpu.VMEM)
SMEM = pl.BlockSpec(memory_space=pltpu.SMEM)
NT = (((1,), (1,)), ((), ()))
TN = (((0,), (0,)), ((), ()))
NN = (((1,), (0,)), ((), ()))


def split2(x):
    high = x.astype(BF16)
    low = (x - high.astype(F32)).astype(BF16)
    return high, low


def iota(shape, dim):
    return lax.broadcasted_iota(jnp.int32, shape, dim)


def weight_at(distance, scale):
    out = jnp.zeros(distance.shape, F32)
    for k in range(1, RADIUS + 1):
        out = jnp.where(distance == k, scale * WEIGHT[k], out)
    return out


class Geometry:
    def __init__(self, orbitals, entries, nproj, atoms, dom_count):
        _, self.no, self.cx, self.cy, self.cz = orbitals
        self.rows = self.cx * self.cy
        self.flat = self.rows * self.no
        self.ent = entries
        self.nproj = nproj
        self.dom_count = dom_count
        self.owned = atoms // dom_count
        self.third = 4
        self.second = min(8, dom_count // 8)
        self.plane = self.second * self.third
        self.first = dom_count // self.plane
        self.strides = (0, self.plane, -self.plane, self.third, -self.third, 1, -1)
        self.table = self.owned * nproj * self.no
        self.slab = self.cy * self.no
        assert self.no == 8

    def faces(self, dom):
        out = []
        for dim, extent, place in (
            (0, self.first, dom // self.plane),
            (1, self.second, dom // self.third % self.second),
        ):
            if extent == 2:
                out.append((dim, 1 - place))
            elif extent > 2:
                out.extend([(dim, 0), (dim, 1)])
        return out

    def face_shapes(self):
        out = []
        for dim, _ in self.faces(0):
            out.append(RADIUS * self.slab if dim == 0 else self.cx * RADIUS * self.no)
        return out


def layer(side, length, j):
    if isinstance(side, int):
        return length - 1 - j if side else j
    return side * (length - 1 - j) + (1 - side) * j


def aligned(start, unit):
    return start if isinstance(start, int) else pl.multiple_of(start, unit)


def pack_faces(g, dom, v_ref, face_refs):
    for (dim, side), out in zip(g.faces(dom), face_refs):
        if dim == 0:
            for j in range(RADIUS):
                at = aligned(layer(side, g.cx, j) * g.slab, g.slab)
                out[j * g.slab : (j + 1) * g.slab, :] = v_ref[pl.ds(at, g.slab), :].astype(BF16)
        else:
            size = RADIUS * g.no
            for x in range(g.cx):
                pieces = []
                for j in range(RADIUS):
                    at = aligned(x * g.slab + layer(side, g.cy, j) * g.no, g.no)
                    pieces.append(v_ref[pl.ds(at, g.no), :])
                out[x * size : (x + 1) * size, :] = jnp.concatenate(pieces, axis=0).astype(BF16)


def pack_ends(g, v_ref, low_ref, high_ref):
    row, col = iota((16, g.cz), 0), iota((16, g.cz), 1)
    place = jnp.where(row < 8, row, g.cz - 1 - (row - 8))
    used = (row % 8) < RADIUS
    pick = jnp.where((place == col) & used, 1.0, 0.0).astype(BF16)
    pick = jnp.concatenate([pick, pick], axis=1)
    for x in range(g.cx):
        rows = slice(x * g.slab, (x + 1) * g.slab)
        both = jnp.concatenate(split2(v_ref[rows, :]), axis=1)
        ends = lax.dot_general(pick, both, NT, preferred_element_type=F32)
        low_ref[:, rows] = ends[:8]
        high_ref[:, rows] = ends[8:]


def fill_lut(g, dom, lut):
    for number, stride in enumerate(g.strides):
        lut[g.plane + dom + stride] = number * g.owned


def column_of(g, lut, atom):
    owner = lax.div(atom, jnp.int32(g.owned))
    return lut[owner + g.plane] + (atom - owner * g.owned)


def inner_tables(g, dom, v_ref, projf, blk, atom, lut, sums, table_ref):
    size = g.nproj * g.no
    for part in sums:
        part[...] = jnp.zeros(part.shape, F32)

    def step(i, _):
        for u, part in enumerate(sums):
            e = i * len(sums) + u
            col = column_of(g, lut, atom[e])
            v = v_ref[pl.ds(pl.multiple_of(blk[e] * g.no, g.no), g.no), :]
            for p in range(g.nproj):
                at = pl.ds(pl.multiple_of(col * size + p * g.no, g.no), g.no)
                coef = jnp.broadcast_to(projf[e, p : p + 1, :], v.shape)
                part[at, :] += v * coef
        return 0

    lax.fori_loop(0, g.ent // len(sums), step, 0)
    total = sums[0][...]
    for part in sums[1:]:
        total = total + part[...]
    both = jnp.concatenate(split2(total), axis=1)
    ones = jnp.ones((8, both.shape[1]), BF16)
    summed = lax.dot_general(ones, both, NT, preferred_element_type=F32)
    table_ref[...] = jnp.zeros(table_ref.shape, F32)
    for number, stride in enumerate(g.strides):
        target = jnp.clip(dom + stride, 0, g.dom_count - 1)
        table_ref[pl.ds(target, 1), :] += summed[0:1, number * g.table : (number + 1) * g.table]


def first_kernel(g, orb, proj, blk, atom, *refs):
    nf = len(g.face_shapes())
    v_ref, projf, table, low, high = refs[:5]
    face_refs = refs[5 : 5 + nf]
    lut = refs[5 + nf]
    sums = refs[6 + nf :]
    dom = lax.axis_index("dom")
    for r in range(g.rows):
        v_ref[r * g.no : (r + 1) * g.no, :] = orb[pl.ds(r, g.no, stride=g.rows), :]
    projf[...] = proj[...].astype(F32)
    pack_faces(g, dom, v_ref, face_refs)
    pack_ends(g, v_ref, low, high)
    fill_lut(g, dom, lut)
    inner_tables(g, dom, v_ref, projf, blk, atom, lut, sums, table)


def inside_kernel(g, scale, subtract, v_ref, pot, *refs):
    prev, out = refs if subtract else (None, refs[0])
    row, col = iota((g.cz, g.cz), 0), iota((g.cz, g.cz), 1)
    high, low = split2(weight_at(jnp.abs(row - col), scale))
    band = jnp.concatenate([high, low], axis=1)
    band = jnp.concatenate([band, band], axis=0)

    def cell(x, y):
        at = (x * g.cy + y) * g.no
        return v_ref[at : at + g.no, :]

    for x in range(g.cx):
        both = jnp.concatenate(split2(v_ref[x * g.slab : (x + 1) * g.slab, :]), axis=1)
        along = lax.dot_general(both, band, NN, preferred_element_type=F32)
        for y in range(g.cy):
            at = (x * g.cy + y) * g.no
            rows = slice(y * g.no, (y + 1) * g.no)
            here = cell(x, y)
            diag = jnp.broadcast_to(pot[x * g.cy + y : x * g.cy + y + 1, :], here.shape)
            total = along[rows, : g.cz] + along[rows, g.cz :]
            total = total + (scale * DIAGONAL + (scale / HALF_WIDTH) * diag) * here
            if subtract:
                total = total - prev[at : at + g.no, :]
            for k in range(1, RADIUS + 1):
                near = []
                for a, b in ((x - k, y), (x + k, y), (x, y - k), (x, y + k)):
                    if 0 <= a < g.cx and 0 <= b < g.cy:
                        near.append(cell(a, b))
                if near:
                    total = total + (scale * WEIGHT[k]) * sum(near[1:], near[0])
            out[at : at + g.no, :] = total


def add_halos(g, dom, scale, acc, low, high, face_refs, out):
    row, col = iota((16, g.cz), 0), iota((16, g.cz), 1)
    inward = jnp.where(row < 8, col, g.cz - 1 - col)
    coef = jnp.where(row % 8 < RADIUS, weight_at(inward + row % 8 + 1, scale), 0.0)
    c_high, c_low = split2(coef)
    coefs = jnp.concatenate([c_high, c_high, c_low, c_low], axis=0)
    for x in range(g.cx):
        rows = slice(x * g.slab, (x + 1) * g.slab)
        h_high, h_low = split2(jnp.concatenate([low[:, rows], high[:, rows]], axis=0))
        halo = jnp.concatenate([h_high, h_low, h_high, h_low], axis=0)
        out[rows, :] = acc[rows, :] + lax.dot_general(halo, coefs, TN, preferred_element_type=F32)
    for (dim, side), face in zip(g.faces(dom), face_refs):
        if dim == 0:
            for y in range(0, g.cy, 2):
                unit = 2 * g.no
                starts = [j * g.slab + y * g.no for j in range(RADIUS)]
                part = [face[at : at + unit, :].astype(F32) for at in starts]
                for i in range(RADIUS):
                    at = aligned(layer(side, g.cx, i) * g.slab + y * g.no, unit)
                    total = out[pl.ds(at, unit), :]
                    for j in range(RADIUS - i):
                        total = total + (scale * WEIGHT[i + j + 1]) * part[j]
                    out[pl.ds(at, unit), :] = total
        else:
            size = RADIUS * g.no
            for x in range(g.cx):
                part = face[x * size : (x + 1) * size, :].astype(F32)
                for i in range(RADIUS):
                    at = aligned(x * g.slab + layer(side, g.cy, i) * g.no, g.no)
                    total = out[pl.ds(at, g.no), :]
                    for j in range(RADIUS - i):
                        total = total + (scale * WEIGHT[i + j + 1]) * part[j * g.no : (j + 1) * g.no]
                    out[pl.ds(at, g.no), :] = total


def add_nonlocal(g, dom, scale, table, energy, projf, blk, atom, lut, spread, out):
    size = g.nproj * g.no
    lanes = g.table
    rows = []
    for stride in g.strides:
        at = jnp.clip(dom + stride, 0, g.dom_count - 1)
        rows.append(table[pl.ds(at, 1), :] * energy[pl.ds(at, 1), :])
    rows.append(jnp.zeros((1, lanes), F32))
    scaled = (scale / HALF_WIDTH) * jnp.concatenate(rows, axis=0)
    high = scaled.astype(BF16)
    rest = scaled - high.astype(F32)
    mid = rest.astype(BF16)
    low = (rest - mid.astype(F32)).astype(BF16)
    parts = jnp.concatenate([high, mid, low], axis=0)
    wide = len(g.strides) * g.cz
    row, col = iota((24, wide), 0), iota((24, wide), 1)
    ones = jnp.where(row % 8 == col // g.cz, 1.0, 0.0).astype(BF16)
    out_all = lax.dot_general(parts, ones, TN, preferred_element_type=F32)
    for number in range(len(g.strides)):
        spread[number * lanes : (number + 1) * lanes, :] = out_all[:, number * g.cz : (number + 1) * g.cz]
    unroll = 4

    def step(i, _):
        additions = []
        for u in range(unroll):
            e = i * unroll + u
            col = column_of(g, lut, atom[e])
            total = None
            for p in range(g.nproj):
                at = pl.ds(pl.multiple_of(col * size + p * g.no, g.no), g.no)
                coef = jnp.broadcast_to(projf[e, p : p + 1, :], (g.no, g.cz))
                term = spread[at, :] * coef
                total = term if total is None else total + term
            additions.append((pl.ds(pl.multiple_of(blk[e] * g.no, g.no), g.no), total))
        for at, total in additions:
            out[at, :] += total
        return 0

    lax.fori_loop(0, g.ent // unroll, step, 0)


def middle_kernel(g, acc, low, high, total, energy, projf, blk, atom, *refs):
    nf = len(g.face_shapes())
    face_in = refs[:nf]
    u_ref, table, low_out, high_out = refs[nf : nf + 4]
    face_out = refs[nf + 4 : 2 * nf + 4]
    lut, spread = refs[2 * nf + 4 : 2 * nf + 6]
    sums = refs[2 * nf + 6 :]
    dom = lax.axis_index("dom")
    fill_lut(g, dom, lut)
    add_halos(g, dom, 1.0, acc, low, high, face_in, u_ref)
    add_nonlocal(g, dom, 1.0, total, energy, projf, blk, atom, lut, spread, u_ref)
    pack_faces(g, dom, u_ref, face_out)
    pack_ends(g, u_ref, low_out, high_out)
    inner_tables(g, dom, u_ref, projf, blk, atom, lut, sums, table)


def last_kernel(g, acc, low, high, total, energy, projf, blk, atom, *refs):
    nf = len(g.face_shapes())
    face_in = refs[:nf]
    filtered, lut, spread, work = refs[nf:]
    dom = lax.axis_index("dom")
    fill_lut(g, dom, lut)
    add_halos(g, dom, 2.0, acc, low, high, face_in, work)
    add_nonlocal(g, dom, 2.0, total, energy, projf, blk, atom, lut, spread, work)
    filtered[...] = work[...].astype(BF16)


def rotate_kernel(g, own, other, panel, out):
    band = lax.axis_index("band")
    group = 16
    span = group * g.no
    norb = panel.shape[0]
    row, col = iota((span, norb), 0), iota((span, norb), 1)
    pick_out = jnp.where(col == band * g.no + row // group, 1.0, 0.0).astype(BF16)
    picked = lax.dot_general(pick_out, panel[...], NT, preferred_element_type=F32).astype(BF16)
    row, col = iota((norb, 2 * span), 0), iota((norb, 2 * span), 1)
    source = jnp.where(col < span, band, 1 - band) * g.no + col % g.no
    pick_in = jnp.where(row == source, 1.0, 0.0).astype(BF16)
    spread = lax.dot_general(picked, pick_in, NN, preferred_element_type=F32)
    row, col = iota((span, 2 * span), 0), iota((span, 2 * span), 1)
    same = row % group == (col % span) // g.no
    weights = jnp.where(same, spread, 0.0).astype(BF16)
    for n in range(g.rows // group):
        rows = slice(n * span, (n + 1) * span)
        both = jnp.concatenate([own[rows, :], other[rows, :]], axis=0)
        result = lax.dot_general(weights, both, NN, preferred_element_type=F32)
        for j in range(g.no):
            at = j * g.rows + n * group
            out[at : at + group, :] = result[j * group : (j + 1) * group, :]


def call(kernel, name, out_shape, scratch, flops, args, specs):
    size = sum(a.size * a.dtype.itemsize for a in args)
    outs = out_shape if isinstance(out_shape, (tuple, list)) else [out_shape]
    size += sum(o.size * o.dtype.itemsize for o in outs)
    return pl.pallas_call(
        kernel,
        name=name,
        out_shape=out_shape,
        in_specs=specs,
        out_specs=jax.tree.map(lambda _: VMEM, out_shape),
        scratch_shapes=scratch,
        compiler_params=pltpu.CompilerParams(vmem_limit_bytes=48 * 1024 * 1024),
        cost_estimate=pl.CostEstimate(flops=flops, bytes_accessed=size, transcendentals=0),
    )(*args)


def exchange(g, faces, low, high):
    n = g.dom_count

    def pairs(stride, extent, step, up):
        out = []
        for i in range(n):
            place = i // stride % extent
            to = place + step
            if 0 <= to < extent:
                out.append((i, i + step * stride))
        return out

    def swap(stride):
        return [(i, i + stride if i // stride % 2 == 0 else i - stride) for i in range(n)]

    got = []
    at = 0
    for extent, stride in ((g.first, g.plane), (g.second, g.third)):
        if extent == 2:
            got.append(lax.ppermute(faces[at], "dom", swap(stride)))
            at += 1
        elif extent > 2:
            down, up = faces[at], faces[at + 1]
            got.append(lax.ppermute(up, "dom", pairs(stride, extent, 1, True)))
            got.append(lax.ppermute(down, "dom", pairs(stride, extent, -1, False)))
            at += 2
    from_low = lax.ppermute(high, "dom", pairs(1, g.third, 1, True))
    from_high = lax.ppermute(low, "dom", pairs(1, g.third, -1, False))
    return got, from_low, from_high


def shards(orbitals, potential, projectors, entry_atom, entry_block, kb_energy, panel):
    g = Geometry(
        orbitals.shape, projectors.shape[0], projectors.shape[1], kb_energy.shape[0], lax.axis_size("dom")
    )
    orb = orbitals.reshape(g.flat, g.cz)
    pot = potential.reshape(g.rows, g.cz)
    field = jax.ShapeDtypeStruct((g.flat, g.cz), F32)
    faces = [jax.ShapeDtypeStruct((n, g.cz), BF16) for n in g.face_shapes()]
    ends = jax.ShapeDtypeStruct((8, g.flat), F32)
    table = jax.ShapeDtypeStruct((g.dom_count, g.table), F32)
    projf = jax.ShapeDtypeStruct(projectors.shape, F32)
    lut = pltpu.SMEM((g.dom_count + 2 * g.plane,), jnp.int32)
    sums = [pltpu.VMEM((len(g.strides) * g.table, g.cz), F32) for _ in range(4)]
    spread = pltpu.VMEM((len(g.strides) * g.table, g.cz), F32)
    nf = len(faces)

    v, proj, part, low, high, *sent = call(
        functools.partial(first_kernel, g),
        "first_faces",
        [field, projf, table, ends, ends, *faces],
        [lut, *sums],
        10_000_000,
        [orb, projectors, entry_block, entry_atom],
        [VMEM, VMEM, SMEM, SMEM],
    )
    got, low, high = exchange(g, sent, low, high)
    total = lax.psum(part, "dom")
    energy = jnp.repeat(kb_energy.reshape(g.dom_count, g.owned * g.nproj), g.no, axis=1)
    acc = call(
        functools.partial(inside_kernel, g, 1.0, False),
        "inside_first",
        field,
        [],
        200_000_000,
        [v, pot],
        [VMEM, VMEM],
    )
    u, part, low, high, *sent = call(
        functools.partial(middle_kernel, g),
        "middle",
        [field, table, ends, ends, *faces],
        [lut, spread, *sums],
        10_000_000,
        [acc, low, high, total, energy, proj, entry_block, entry_atom, *got],
        [VMEM] * 6 + [SMEM] * 2 + [VMEM] * nf,
    )
    got, low, high = exchange(g, sent, low, high)
    total = lax.psum(part, "dom")
    acc = call(
        functools.partial(inside_kernel, g, 2.0, True),
        "inside_second",
        field,
        [],
        200_000_000,
        [u, pot, v],
        [VMEM, VMEM, VMEM],
    )
    filtered = call(
        functools.partial(last_kernel, g),
        "filtered",
        jax.ShapeDtypeStruct((g.flat, g.cz), BF16),
        [lut, spread, pltpu.VMEM((g.flat, g.cz), F32)],
        10_000_000,
        [acc, low, high, total, energy, proj, entry_block, entry_atom, *got],
        [VMEM] * 6 + [SMEM] * 2 + [VMEM] * nf,
    )
    other = lax.ppermute(filtered, "band", [(0, 1), (1, 0)])
    rotated = call(
        functools.partial(rotate_kernel, g),
        "rotate",
        field,
        [],
        200_000_000,
        [filtered, other, panel],
        [VMEM] * 3,
    )
    return rotated.reshape(orbitals.shape)


def solution(mesh):
    in_specs = (
        P("dom", "band", None, None, None),
        P("dom", None, None, None),
        P("dom", None, None),
        P("dom"),
        P("dom"),
        P(),
        P(),
    )
    out_specs = P("dom", "band", None, None, None)
    return jax.shard_map(shards, mesh=mesh, in_specs=in_specs, out_specs=out_specs, check_vma=False)
```

```python
import functools

import jax
import jax.numpy as jnp
from jax import lax
from jax.experimental import pallas as pl
from jax.experimental.pallas import tpu as pltpu
from jax.sharding import PartitionSpec as P

RADIUS = 6
COEFFS = (
    -5369.0 / 1800.0,
    12.0 / 7.0,
    -15.0 / 56.0,
    10.0 / 189.0,
    -1.0 / 112.0,
    2.0 / 1925.0,
    -1.0 / 16632.0,
)
KINETIC = -3.125
CENTER = 36.0
HALF_WIDTH = 34.0
WEIGHT = [KINETIC * c / HALF_WIDTH for c in COEFFS]
DIAGONAL = (3.0 * KINETIC * COEFFS[0] - CENTER) / HALF_WIDTH

F32 = jnp.float32
BF16 = jnp.bfloat16
VMEM = pl.BlockSpec(memory_space=pltpu.VMEM)
HBM = pl.BlockSpec(memory_space=pltpu.HBM)
NT = (((1,), (1,)), ((), ()))
TN = (((0,), (0,)), ((), ()))
NN = (((1,), (0,)), ((), ()))


def split2(x):
    high = x.astype(BF16)
    low = (x - high.astype(F32)).astype(BF16)
    return high, low


def iota(shape, dim):
    return lax.broadcasted_iota(jnp.int32, shape, dim)


def weight_at(distance, scale):
    out = jnp.zeros(distance.shape, F32)
    for k in range(1, RADIUS + 1):
        out = jnp.where(distance == k, scale * WEIGHT[k], out)
    return out


class Geometry:
    def __init__(self, orbitals, entries, nproj, atoms, dom_count):
        _, self.no, self.cx, self.cy, self.cz = orbitals
        self.rows = self.cx * self.cy
        self.flat = self.rows * self.no
        self.ent = entries
        self.nproj = nproj
        self.dom_count = dom_count
        self.owned = atoms // dom_count
        self.third = 4
        self.second = min(8, dom_count // 8)
        self.plane = self.second * self.third
        self.first = dom_count // self.plane
        self.strides = (0, self.plane, -self.plane, self.third, -self.third, 1, -1)
        self.table = self.owned * nproj * self.no
        self.slab = self.cy * self.no
        assert self.no == 8

    def faces(self, dom, dim):
        if dim == 0:
            extent, place = self.first, dom // self.plane
        else:
            extent, place = self.second, dom // self.third % self.second
        if extent == 2:
            return [(1 - place, None)]
        if extent > 2:
            return [(0, place > 0), (1, place < extent - 1)]
        return []

    def face_rows(self, dim):
        rows = RADIUS * self.slab if dim == 0 else self.cx * RADIUS * self.no
        return [rows] * len(self.faces(0, dim))


def layer(side, length, j):
    if isinstance(side, int):
        return length - 1 - j if side else j
    return side * (length - 1 - j) + (1 - side) * j


def aligned(start, unit):
    return start if isinstance(start, int) else pl.multiple_of(start, unit)


def pack_faces(g, dom, v_ref, x_refs, y_refs):
    for (side, _), out in zip(g.faces(dom, 0), x_refs):
        for j in range(RADIUS):
            at = aligned(layer(side, g.cx, j) * g.slab, g.slab)
            out[j * g.slab : (j + 1) * g.slab, :] = v_ref[pl.ds(at, g.slab), :].astype(BF16)
    size = RADIUS * g.no
    for (side, _), out in zip(g.faces(dom, 1), y_refs):
        for x in range(g.cx):
            pieces = []
            for j in range(RADIUS):
                at = aligned(x * g.slab + layer(side, g.cy, j) * g.no, g.no)
                pieces.append(v_ref[pl.ds(at, g.no), :])
            out[x * size : (x + 1) * size, :] = jnp.concatenate(pieces, axis=0).astype(BF16)


def pack_ends(g, v_ref, low_ref, high_ref):
    row, col = iota((16, g.cz), 0), iota((16, g.cz), 1)
    place = jnp.where(row < 8, row, g.cz - 1 - (row - 8))
    used = (row % 8) < RADIUS
    pick = jnp.where((place == col) & used, 1.0, 0.0).astype(BF16)
    pick = jnp.concatenate([pick, pick], axis=1)
    for x in range(g.cx):
        rows = slice(x * g.slab, (x + 1) * g.slab)
        both = jnp.concatenate(split2(v_ref[rows, :]), axis=1)
        ends = lax.dot_general(pick, both, NT, preferred_element_type=F32)
        low_ref[:, rows] = ends[:8]
        high_ref[:, rows] = ends[8:]


def fill_lut(g, dom, lut):
    for number, stride in enumerate(g.strides):
        lut[g.plane + dom + stride] = number * g.owned


def column_of(g, lut, atom):
    owner = lax.div(atom, jnp.int32(g.owned))
    return lut[owner + g.plane] + (atom - owner * g.owned)


def inner_tables(g, v_ref, projf, blk, atom, lut, sums, table_ref):
    size = g.nproj * g.no

    def step(i, _):
        for u, part in enumerate(sums):
            e = i * len(sums) + u
            col = column_of(g, lut, atom[e])
            v = v_ref[pl.ds(pl.multiple_of(blk[e] * g.no, g.no), g.no), :]
            for p in range(g.nproj):
                at = pl.ds(pl.multiple_of(col * size + p * g.no, g.no), g.no)
                coef = jnp.broadcast_to(projf[e, p : p + 1, :], v.shape)
                part[at, :] += v * coef
        return 0

    lax.fori_loop(0, g.ent // len(sums), step, 0)
    total = sums[0][...]
    for part in sums[1:]:
        total = total + part[...]
    both = jnp.concatenate(split2(total), axis=1)
    ones = jnp.ones((8, both.shape[1]), BF16)
    summed = lax.dot_general(ones, both, NT, preferred_element_type=F32)
    table_ref[...] = jnp.zeros(table_ref.shape, F32)
    for number in range(len(g.strides)):
        table_ref[number : number + 1, :] = summed[0:1, number * g.table : (number + 1) * g.table]


def clear(sums):
    for part in sums:
        part[...] = jnp.zeros(part.shape, F32)


def first_kernel(g, orb_hbm, proj_hbm, blk_hbm, atom_hbm, *refs):
    nx, ny = len(g.face_rows(0)), len(g.face_rows(1))
    v_ref, projf, table, low, high = refs[:5]
    x_refs = refs[5 : 5 + nx]
    y_refs = refs[5 + nx : 5 + nx + ny]
    orb, proj, blk, atom, lut, sem = refs[5 + nx + ny : 11 + nx + ny]
    sums = refs[11 + nx + ny :]
    copies = []
    for number, (src, dst) in enumerate(
        ((orb_hbm, orb), (proj_hbm, proj), (blk_hbm, blk), (atom_hbm, atom))
    ):
        copies.append(pltpu.make_async_copy(src, dst, sem.at[number]))
        copies[-1].start()
    dom = lax.axis_index("dom")
    fill_lut(g, dom, lut)
    clear(sums)
    copies[0].wait()
    for r in range(g.rows):
        v_ref[r * g.no : (r + 1) * g.no, :] = orb[pl.ds(r, g.no, stride=g.rows), :]
    pack_faces(g, dom, v_ref, x_refs, y_refs)
    pack_ends(g, v_ref, low, high)
    copies[1].wait()
    projf[...] = proj[...].astype(F32)
    copies[2].wait()
    copies[3].wait()
    inner_tables(g, v_ref, projf, blk, atom, lut, sums, table)


def inside_kernel(g, scale, subtract, v_ref, pot, *refs):
    prev, out = refs if subtract else (None, refs[0])
    row, col = iota((g.cz, g.cz), 0), iota((g.cz, g.cz), 1)
    high, low = split2(weight_at(jnp.abs(row - col), scale))
    band = jnp.concatenate([high, low], axis=1)
    band = jnp.concatenate([band, band], axis=0)

    def cell(x, y):
        at = (x * g.cy + y) * g.no
        return v_ref[at : at + g.no, :]

    for x in range(g.cx):
        both = jnp.concatenate(split2(v_ref[x * g.slab : (x + 1) * g.slab, :]), axis=1)
        along = lax.dot_general(both, band, NN, preferred_element_type=F32)
        for y in range(g.cy):
            at = (x * g.cy + y) * g.no
            rows = slice(y * g.no, (y + 1) * g.no)
            here = cell(x, y)
            diag = jnp.broadcast_to(pot[x * g.cy + y : x * g.cy + y + 1, :], here.shape)
            total = along[rows, : g.cz] + along[rows, g.cz :]
            total = total + (scale * DIAGONAL + (scale / HALF_WIDTH) * diag) * here
            if subtract:
                total = total - prev[at : at + g.no, :]
            for k in range(1, RADIUS + 1):
                near = []
                for a, b in ((x - k, y), (x + k, y), (x, y - k), (x, y + k)):
                    if 0 <= a < g.cx and 0 <= b < g.cy:
                        near.append(cell(a, b))
                if near:
                    total = total + (scale * WEIGHT[k]) * sum(near[1:], near[0])
            out[at : at + g.no, :] = total


def flag(present):
    return 1.0 if present is None else jnp.where(present, 1.0, 0.0)


def add_ends(g, dom, scale, acc, low, high, out):
    place = dom % g.third
    row, col = iota((16, g.cz), 0), iota((16, g.cz), 1)
    inward = jnp.where(row < 8, col, g.cz - 1 - col)
    present = jnp.where(row < 8, place, g.third - 1 - place) > 0
    coef = jnp.where((row % 8 < RADIUS) & present, weight_at(inward + row % 8 + 1, scale), 0.0)
    c_high, c_low = split2(coef)
    coefs = jnp.concatenate([c_high, c_high, c_low, c_low], axis=0)
    for x in range(g.cx):
        rows = slice(x * g.slab, (x + 1) * g.slab)
        h_high, h_low = split2(jnp.concatenate([low[:, rows], high[:, rows]], axis=0))
        halo = jnp.concatenate([h_high, h_low, h_high, h_low], axis=0)
        out[rows, :] = acc[rows, :] + lax.dot_general(halo, coefs, TN, preferred_element_type=F32)


def add_x_faces(g, dom, scale, face_refs, out):
    unit = 2 * g.no
    for (side, present), face in zip(g.faces(dom, 0), face_refs):
        for y in range(0, g.cy, 2):
            starts = [j * g.slab + y * g.no for j in range(RADIUS)]
            part = [flag(present) * face[at : at + unit, :].astype(F32) for at in starts]
            for i in range(RADIUS):
                at = aligned(layer(side, g.cx, i) * g.slab + y * g.no, unit)
                total = out[pl.ds(at, unit), :]
                for j in range(RADIUS - i):
                    total = total + (scale * WEIGHT[i + j + 1]) * part[j]
                out[pl.ds(at, unit), :] = total


def add_y_faces(g, dom, scale, face_refs, out):
    size = RADIUS * g.no
    for (side, present), face in zip(g.faces(dom, 1), face_refs):
        for x in range(g.cx):
            part = flag(present) * face[x * size : (x + 1) * size, :].astype(F32)
            for i in range(RADIUS):
                at = aligned(x * g.slab + layer(side, g.cy, i) * g.no, g.no)
                total = out[pl.ds(at, g.no), :]
                for j in range(RADIUS - i):
                    total = total + (scale * WEIGHT[i + j + 1]) * part[j * g.no : (j + 1) * g.no]
                out[pl.ds(at, g.no), :] = total


def scaled_rows(g, dom, tables, energy):
    rows = []
    for stride in g.strides:
        owner = jnp.clip(dom + stride, 0, g.dom_count - 1)
        total = None
        for number, back in enumerate(g.strides):
            source = owner - back
            inside = (source >= 0) & (source < g.dom_count)
            row = tables[pl.ds(jnp.where(inside, source * 8 + number, 7), 1), :]
            total = row if total is None else total + row
        rows.append(total * energy[pl.ds(owner, 1), :])
    return rows


def add_nonlocal(g, scale, rows, projf, blk, atom, lut, spread, out):
    size = g.nproj * g.no
    lanes = g.table
    rows.append(jnp.zeros((1, lanes), F32))
    scaled = (scale / HALF_WIDTH) * jnp.concatenate(rows, axis=0)
    high = scaled.astype(BF16)
    rest = scaled - high.astype(F32)
    mid = rest.astype(BF16)
    low = (rest - mid.astype(F32)).astype(BF16)
    parts = jnp.concatenate([high, mid, low], axis=0)
    wide = len(g.strides) * g.cz
    row, col = iota((24, wide), 0), iota((24, wide), 1)
    ones = jnp.where(row % 8 == col // g.cz, 1.0, 0.0).astype(BF16)
    out_all = lax.dot_general(parts, ones, TN, preferred_element_type=F32)
    for number in range(len(g.strides)):
        spread[number * lanes : (number + 1) * lanes, :] = out_all[:, number * g.cz : (number + 1) * g.cz]
    unroll = 4

    def step(i, _):
        additions = []
        for u in range(unroll):
            e = i * unroll + u
            col = column_of(g, lut, atom[e])
            total = None
            for p in range(g.nproj):
                at = pl.ds(pl.multiple_of(col * size + p * g.no, g.no), g.no)
                coef = jnp.broadcast_to(projf[e, p : p + 1, :], (g.no, g.cz))
                term = spread[at, :] * coef
                total = term if total is None else total + term
            additions.append((pl.ds(pl.multiple_of(blk[e] * g.no, g.no), g.no), total))
        for at, total in additions:
            out[at, :] += total
        return 0

    lax.fori_loop(0, g.ent // unroll, step, 0)


def sides_kernel(g, scale, acc, low, high, tables, energy, projf, blk_hbm, atom_hbm, *refs):
    ny = len(g.face_rows(1))
    y_refs = refs[:ny]
    out, blk, atom, lut, spread, sem = refs[ny:]
    copies = [
        pltpu.make_async_copy(blk_hbm, blk, sem.at[0]),
        pltpu.make_async_copy(atom_hbm, atom, sem.at[1]),
    ]
    for copy in copies:
        copy.start()
    dom = lax.axis_index("dom")
    fill_lut(g, dom, lut)
    add_ends(g, dom, scale, acc, low, high, out)
    add_y_faces(g, dom, scale, y_refs, out)
    rows = scaled_rows(g, dom, tables, energy)
    for copy in copies:
        copy.wait()
    add_nonlocal(g, scale, rows, projf, blk, atom, lut, spread, out)


def middle_kernel(g, acc, projf, blk_hbm, atom_hbm, *refs):
    nx, ny = len(g.face_rows(0)), len(g.face_rows(1))
    x_in = refs[:nx]
    u_ref, table, low_out, high_out = refs[nx : nx + 4]
    x_out = refs[nx + 4 : 2 * nx + 4]
    y_out = refs[2 * nx + 4 : 2 * nx + 4 + ny]
    blk, atom, lut, sem = refs[2 * nx + 4 + ny : 2 * nx + 8 + ny]
    sums = refs[2 * nx + 8 + ny :]
    copies = [
        pltpu.make_async_copy(blk_hbm, blk, sem.at[0]),
        pltpu.make_async_copy(atom_hbm, atom, sem.at[1]),
    ]
    for copy in copies:
        copy.start()
    dom = lax.axis_index("dom")
    fill_lut(g, dom, lut)
    clear(sums)
    u_ref[...] = acc[...]
    add_x_faces(g, dom, 1.0, x_in, u_ref)
    pack_faces(g, dom, u_ref, x_out, y_out)
    pack_ends(g, u_ref, low_out, high_out)
    for copy in copies:
        copy.wait()
    inner_tables(g, u_ref, projf, blk, atom, lut, sums, table)


def last_kernel(g, acc, *refs):
    x_in = refs[: len(g.face_rows(0))]
    filtered, work = refs[len(g.face_rows(0)) :]
    dom = lax.axis_index("dom")
    work[...] = acc[...]
    add_x_faces(g, dom, 2.0, x_in, work)
    filtered[...] = work[...].astype(BF16)


def rotate_kernel(g, own, other, panel, out):
    band = lax.axis_index("band")
    group = 16
    span = group * g.no
    norb = panel.shape[0]
    row, col = iota((span, norb), 0), iota((span, norb), 1)
    pick_out = jnp.where(col == band * g.no + row // group, 1.0, 0.0).astype(BF16)
    picked = lax.dot_general(pick_out, panel[...], NT, preferred_element_type=F32).astype(BF16)
    row, col = iota((norb, 2 * span), 0), iota((norb, 2 * span), 1)
    source = jnp.where(col < span, band, 1 - band) * g.no + col % g.no
    pick_in = jnp.where(row == source, 1.0, 0.0).astype(BF16)
    spread = lax.dot_general(picked, pick_in, NN, preferred_element_type=F32)
    row, col = iota((span, 2 * span), 0), iota((span, 2 * span), 1)
    same = row % group == (col % span) // g.no
    weights = jnp.where(same, spread, 0.0).astype(BF16)
    for n in range(g.rows // group):
        rows = slice(n * span, (n + 1) * span)
        both = jnp.concatenate([own[rows, :], other[rows, :]], axis=0)
        result = lax.dot_general(weights, both, NN, preferred_element_type=F32)
        for j in range(g.no):
            at = j * g.rows + n * group
            out[at : at + group, :] = result[j * group : (j + 1) * group, :]


def call(kernel, name, out_shape, scratch, flops, args, specs):
    size = sum(a.size * a.dtype.itemsize for a in args)
    outs = out_shape if isinstance(out_shape, (tuple, list)) else [out_shape]
    size += sum(o.size * o.dtype.itemsize for o in outs)
    return pl.pallas_call(
        kernel,
        name=name,
        out_shape=out_shape,
        in_specs=specs,
        out_specs=jax.tree.map(lambda _: VMEM, out_shape),
        scratch_shapes=scratch,
        compiler_params=pltpu.CompilerParams(vmem_limit_bytes=48 * 1024 * 1024),
        cost_estimate=pl.CostEstimate(flops=flops, bytes_accessed=size, transcendentals=0),
    )(*args)


def shift(g, array, stride, extent, step):
    pairs = []
    for i in range(g.dom_count):
        place = i // stride % extent
        pairs.append((i, i + ((place + step) % extent - place) * stride))
    return lax.ppermute(array, "dom", pairs)


def swap_faces(g, faces, stride, extent):
    if extent == 2:
        return [shift(g, faces[0], stride, extent, 1)]
    if extent > 2:
        return [shift(g, faces[1], stride, extent, 1), shift(g, faces[0], stride, extent, -1)]
    return []


def shards(orbitals, potential, projectors, entry_atom, entry_block, kb_energy, panel):
    g = Geometry(
        orbitals.shape, projectors.shape[0], projectors.shape[1], kb_energy.shape[0], lax.axis_size("dom")
    )
    orb = orbitals.reshape(g.flat, g.cz)
    pot = potential.reshape(g.rows, g.cz)
    field = jax.ShapeDtypeStruct((g.flat, g.cz), F32)
    x_faces = [jax.ShapeDtypeStruct((n, g.cz), BF16) for n in g.face_rows(0)]
    y_faces = [jax.ShapeDtypeStruct((n, g.cz), BF16) for n in g.face_rows(1)]
    nx, ny = len(x_faces), len(y_faces)
    ends = jax.ShapeDtypeStruct((8, g.flat), F32)
    table = jax.ShapeDtypeStruct((8, g.table), F32)
    projf = jax.ShapeDtypeStruct(projectors.shape, F32)
    lut = pltpu.SMEM((g.dom_count + 2 * g.plane,), jnp.int32)
    entries = [pltpu.SMEM((g.ent,), jnp.int32)] * 2
    sums = [pltpu.VMEM((len(g.strides) * g.table, g.cz), F32) for _ in range(4)]
    spread = pltpu.VMEM((len(g.strides) * g.table, g.cz), F32)

    def exchange(sent, low, high, part):
        tables = lax.all_gather(part, "dom", tiled=True)
        low, high = shift(g, high, 1, g.third, 1), shift(g, low, 1, g.third, -1)
        from_y = swap_faces(g, sent[nx:], g.third, g.second)
        from_x = swap_faces(g, sent[:nx], g.plane, g.first)
        return tables, low, high, from_x, from_y

    def sides(scale, name, acc, low, high, tables, from_y):
        return call(
            functools.partial(sides_kernel, g, scale),
            name,
            field,
            [*entries, lut, spread, pltpu.SemaphoreType.DMA((2,))],
            10_000_000,
            [acc, low, high, tables, energy, proj, entry_block, entry_atom, *from_y],
            [VMEM] * 6 + [HBM] * 2 + [VMEM] * ny,
        )

    v, proj, part, low, high, *sent = call(
        functools.partial(first_kernel, g),
        "first_faces",
        [field, projf, table, ends, ends, *x_faces, *y_faces],
        [
            pltpu.VMEM(orb.shape, F32),
            pltpu.VMEM(projectors.shape, BF16),
            *entries,
            lut,
            pltpu.SemaphoreType.DMA((4,)),
            *sums,
        ],
        10_000_000,
        [orb, projectors, entry_block, entry_atom],
        [HBM] * 4,
    )
    tables, low, high, from_x, from_y = exchange(sent, low, high, part)
    energy = jnp.repeat(kb_energy.reshape(g.dom_count, g.owned * g.nproj), g.no, axis=1)
    acc = call(
        functools.partial(inside_kernel, g, 1.0, False),
        "inside_first",
        field,
        [],
        200_000_000,
        [v, pot],
        [VMEM, VMEM],
    )
    acc = sides(1.0, "sides_first", acc, low, high, tables, from_y)
    u, part, low, high, *sent = call(
        functools.partial(middle_kernel, g),
        "middle",
        [field, table, ends, ends, *x_faces, *y_faces],
        [*entries, lut, pltpu.SemaphoreType.DMA((2,)), *sums],
        10_000_000,
        [acc, proj, entry_block, entry_atom, *from_x],
        [VMEM] * 2 + [HBM] * 2 + [VMEM] * nx,
    )
    tables, low, high, from_x, from_y = exchange(sent, low, high, part)
    acc = call(
        functools.partial(inside_kernel, g, 2.0, True),
        "inside_second",
        field,
        [],
        200_000_000,
        [u, pot, v],
        [VMEM, VMEM, VMEM],
    )
    acc = sides(2.0, "sides_second", acc, low, high, tables, from_y)
    filtered = call(
        functools.partial(last_kernel, g),
        "filtered",
        jax.ShapeDtypeStruct((g.flat, g.cz), BF16),
        [pltpu.VMEM((g.flat, g.cz), F32)],
        10_000_000,
        [acc, *from_x],
        [VMEM] * (1 + nx),
    )
    other = lax.ppermute(filtered, "band", [(0, 1), (1, 0)])
    rotated = call(
        functools.partial(rotate_kernel, g),
        "rotate",
        field,
        [],
        200_000_000,
        [filtered, other, panel],
        [VMEM] * 3,
    )
    return rotated.reshape(orbitals.shape)


def solution(mesh):
    in_specs = (
        P("dom", "band", None, None, None),
        P("dom", None, None, None),
        P("dom", None, None),
        P("dom"),
        P("dom"),
        P(),
        P(),
    )
    out_specs = P("dom", "band", None, None, None)
    return jax.shard_map(shards, mesh=mesh, in_specs=in_specs, out_specs=out_specs, check_vma=False)
```

```python
import functools

import jax
import jax.numpy as jnp
from jax import lax
from jax.experimental import pallas as pl
from jax.experimental.pallas import tpu as pltpu
from jax.sharding import PartitionSpec as P

RADIUS = 6
EARLY = 3
COEFFS = (
    -5369.0 / 1800.0,
    12.0 / 7.0,
    -15.0 / 56.0,
    10.0 / 189.0,
    -1.0 / 112.0,
    2.0 / 1925.0,
    -1.0 / 16632.0,
)
KINETIC = -3.125
CENTER = 36.0
HALF_WIDTH = 34.0
WEIGHT = [KINETIC * c / HALF_WIDTH for c in COEFFS]
DIAGONAL = (3.0 * KINETIC * COEFFS[0] - CENTER) / HALF_WIDTH

F32 = jnp.float32
BF16 = jnp.bfloat16
VMEM = pl.BlockSpec(memory_space=pltpu.VMEM)
HBM = pl.BlockSpec(memory_space=pltpu.HBM)
NT = (((1,), (1,)), ((), ()))
TN = (((0,), (0,)), ((), ()))
NN = (((1,), (0,)), ((), ()))


def split2(x):
    high = x.astype(BF16)
    low = (x - high.astype(F32)).astype(BF16)
    return high, low


def iota(shape, dim):
    return lax.broadcasted_iota(jnp.int32, shape, dim)


def weight_at(distance, scale):
    out = jnp.zeros(distance.shape, F32)
    for k in range(1, RADIUS + 1):
        out = jnp.where(distance == k, scale * WEIGHT[k], out)
    return out


class Geometry:
    def __init__(self, orbitals, entries, nproj, atoms, dom_count):
        _, self.no, self.cx, self.cy, self.cz = orbitals
        self.rows = self.cx * self.cy
        self.flat = self.rows * self.no
        self.ent = entries
        self.nproj = nproj
        self.dom_count = dom_count
        self.owned = atoms // dom_count
        self.third = 4
        self.second = min(8, dom_count // 8)
        self.plane = self.second * self.third
        self.first = dom_count // self.plane
        self.table = self.owned * nproj * self.no
        self.slab = self.cy * self.no
        assert self.no == 8

    def faces(self, dom, dim):
        if dim == 0:
            extent, place = self.first, dom // self.plane
        else:
            extent, place = self.second, dom // self.third % self.second
        if extent == 2:
            return [(1 - place, None)]
        if extent > 2:
            return [(0, place > 0), (1, place < extent - 1)]
        return []

    def face_rows(self, dim, layers=RADIUS):
        rows = layers * self.slab if dim == 0 else self.cx * layers * self.no
        return [rows] * len(self.faces(0, dim))

    def links(self):
        out = []
        for extent, stride in ((self.first, self.plane), (self.second, self.third), (self.third, 1)):
            if extent == 2:
                out.append((stride, 2, 0))
            elif extent > 2:
                out.extend([(stride, extent, 1), (stride, extent, -1)])
        return out


def layer(side, length, j):
    if isinstance(side, int):
        return length - 1 - j if side else j
    return side * (length - 1 - j) + (1 - side) * j


def aligned(start, unit):
    return start if isinstance(start, int) else pl.multiple_of(start, unit)


def pack_x(g, dom, v_ref, first, last, refs):
    for (side, _), out in zip(g.faces(dom, 0), refs):
        for j in range(first, last):
            at = aligned(layer(side, g.cx, j) * g.slab, g.slab)
            to = (j - first) * g.slab
            out[to : to + g.slab, :] = v_ref[pl.ds(at, g.slab), :].astype(BF16)


def pack_y(g, dom, v_ref, refs):
    size = RADIUS * g.no
    for (side, _), out in zip(g.faces(dom, 1), refs):
        for x in range(g.cx):
            pieces = []
            for j in range(RADIUS):
                at = aligned(x * g.slab + layer(side, g.cy, j) * g.no, g.no)
                pieces.append(v_ref[pl.ds(at, g.no), :])
            out[x * size : (x + 1) * size, :] = jnp.concatenate(pieces, axis=0).astype(BF16)


def pack_ends(g, v_ref, low_ref, high_ref):
    row, col = iota((16, g.cz), 0), iota((16, g.cz), 1)
    place = jnp.where(row < 8, row, g.cz - 1 - (row - 8))
    used = (row % 8) < RADIUS
    pick = jnp.where((place == col) & used, 1.0, 0.0).astype(BF16)
    pick = jnp.concatenate([pick, pick], axis=1)
    for x in range(g.cx):
        rows = slice(x * g.slab, (x + 1) * g.slab)
        both = jnp.concatenate(split2(v_ref[rows, :]), axis=1)
        ends = lax.dot_general(pick, both, NT, preferred_element_type=F32)
        low_ref[:, rows] = ends[:8]
        high_ref[:, rows] = ends[8:]


def fill_lut(g, dom, lut):
    lut[g.plane + dom] = 0
    for number, (stride, _, step) in enumerate(g.links()):
        if step == 0:
            step = 1 - 2 * (dom // stride % 2)
        lut[g.plane + dom + step * stride] = (number + 1) * g.owned


def column_of(g, lut, atom):
    owner = lax.div(atom, jnp.int32(g.owned))
    return lut[owner + g.plane] + (atom - owner * g.owned)


def inner_tables(g, v_ref, projf, blk, atom, lut, sums):
    size = g.nproj * g.no

    def step(i, _):
        for u, part in enumerate(sums):
            e = i * len(sums) + u
            col = column_of(g, lut, atom[e])
            v = v_ref[pl.ds(pl.multiple_of(blk[e] * g.no, g.no), g.no), :]
            for p in range(g.nproj):
                at = pl.ds(pl.multiple_of(col * size + p * g.no, g.no), g.no)
                coef = jnp.broadcast_to(projf[e, p : p + 1, :], v.shape)
                part[at, :] += v * coef
        return 0

    lax.fori_loop(0, g.ent // len(sums), step, 0)
    total = sums[0][...]
    for part in sums[1:]:
        total = total + part[...]
    both = jnp.concatenate(split2(total), axis=1)
    ones = jnp.ones((8, both.shape[1]), BF16)
    summed = lax.dot_general(ones, both, NT, preferred_element_type=F32)
    return [summed[0:1, n * g.table : (n + 1) * g.table] for n in range(len(g.links()) + 1)]


def clear(sums):
    for part in sums:
        part[...] = jnp.zeros(part.shape, F32)


def first_kernel(g, orb_hbm, proj_hbm, pot_hbm, v_ref, projf, pot, *refs):
    nx = len(g.face_rows(0))
    orb, proj, sem = refs[nx:]
    copies = [
        pltpu.make_async_copy(orb_hbm, orb, sem.at[0]),
        pltpu.make_async_copy(proj_hbm, proj, sem.at[1]),
        pltpu.make_async_copy(pot_hbm, pot, sem.at[2]),
    ]
    for copy in copies:
        copy.start()
    dom = lax.axis_index("dom")
    copies[0].wait()
    for r in range(g.rows):
        v_ref[r * g.no : (r + 1) * g.no, :] = orb[pl.ds(r, g.no, stride=g.rows), :]
    pack_x(g, dom, v_ref, 0, EARLY, refs[:nx])
    copies[1].wait()
    projf[...] = proj[...].astype(F32)
    copies[2].wait()


def entry_copies(blk_hbm, atom_hbm, blk, atom, sem):
    return [
        pltpu.make_async_copy(blk_hbm, blk, sem.at[0]),
        pltpu.make_async_copy(atom_hbm, atom, sem.at[1]),
    ]


def tables_kernel(g, v_ref, projf, blk_hbm, atom_hbm, *refs):
    nlinks = len(g.links())
    rows_out = refs[: nlinks - 1]
    low, high = refs[nlinks - 1 : nlinks + 1]
    blk, atom, lut, sem = refs[nlinks + 1 : nlinks + 5]
    sums = refs[nlinks + 5 :]
    copies = entry_copies(blk_hbm, atom_hbm, blk, atom, sem)
    for copy in copies:
        copy.start()
    dom = lax.axis_index("dom")
    fill_lut(g, dom, lut)
    clear(sums)
    pack_ends(g, v_ref, low, high)
    for copy in copies:
        copy.wait()
    rows = inner_tables(g, v_ref, projf, blk, atom, lut, sums)
    for out, row in zip(rows_out, rows):
        out[...] = row
    high[RADIUS : RADIUS + 1, : g.table] = rows[-2]
    low[RADIUS : RADIUS + 1, : g.table] = rows[-1]


def rest_kernel(g, v_ref, after, *refs):
    nx = len(g.face_rows(0))
    dom = lax.axis_index("dom")
    pack_x(g, dom, v_ref, EARLY, RADIUS, refs[:nx])
    pack_y(g, dom, v_ref, refs[nx:])


def scale_kernel(g, energy, low, high, *refs):
    rows, out = refs[:-1], refs[-1]
    total = low[RADIUS : RADIUS + 1, : g.table] + high[RADIUS : RADIUS + 1, : g.table]
    for row in rows:
        total = total + row[...]
    out[...] = total * energy[pl.ds(lax.axis_index("dom"), 1), :]


def inside_kernel(g, scale, subtract, v_ref, pot, *refs):
    prev, out = refs if subtract else (None, refs[0])
    row, col = iota((g.cz, g.cz), 0), iota((g.cz, g.cz), 1)
    high, low = split2(weight_at(jnp.abs(row - col), scale))
    band = jnp.concatenate([high, low], axis=1)
    band = jnp.concatenate([band, band], axis=0)

    def cell(x, y):
        at = (x * g.cy + y) * g.no
        return v_ref[at : at + g.no, :]

    for x in range(g.cx):
        both = jnp.concatenate(split2(v_ref[x * g.slab : (x + 1) * g.slab, :]), axis=1)
        along = lax.dot_general(both, band, NN, preferred_element_type=F32)
        for y in range(g.cy):
            at = (x * g.cy + y) * g.no
            rows = slice(y * g.no, (y + 1) * g.no)
            here = cell(x, y)
            diag = jnp.broadcast_to(pot[x * g.cy + y : x * g.cy + y + 1, :], here.shape)
            total = along[rows, : g.cz] + along[rows, g.cz :]
            total = total + (scale * DIAGONAL + (scale / HALF_WIDTH) * diag) * here
            if subtract:
                total = total - prev[at : at + g.no, :]
            for k in range(1, RADIUS + 1):
                near = []
                for a, b in ((x - k, y), (x + k, y), (x, y - k), (x, y + k)):
                    if 0 <= a < g.cx and 0 <= b < g.cy:
                        near.append(cell(a, b))
                if near:
                    total = total + (scale * WEIGHT[k]) * sum(near[1:], near[0])
            out[at : at + g.no, :] = total


def flag(present):
    return 1.0 if present is None else jnp.where(present, 1.0, 0.0)


def add_ends(g, dom, scale, acc, low, high, out):
    place = dom % g.third
    row, col = iota((16, g.cz), 0), iota((16, g.cz), 1)
    inward = jnp.where(row < 8, col, g.cz - 1 - col)
    present = jnp.where(row < 8, place, g.third - 1 - place) > 0
    coef = jnp.where((row % 8 < RADIUS) & present, weight_at(inward + row % 8 + 1, scale), 0.0)
    c_high, c_low = split2(coef)
    coefs = jnp.concatenate([c_high, c_high, c_low, c_low], axis=0)
    for x in range(g.cx):
        rows = slice(x * g.slab, (x + 1) * g.slab)
        h_high, h_low = split2(jnp.concatenate([low[:, rows], high[:, rows]], axis=0))
        halo = jnp.concatenate([h_high, h_low, h_high, h_low], axis=0)
        out[rows, :] = acc[rows, :] + lax.dot_general(halo, coefs, TN, preferred_element_type=F32)


def add_x_faces(g, dom, scale, early_refs, late_refs, out):
    unit = 2 * g.no
    for (side, present), early, late in zip(g.faces(dom, 0), early_refs, late_refs):
        for y in range(0, g.cy, 2):
            part = []
            for j in range(RADIUS):
                face, at = (early, j) if j < EARLY else (late, j - EARLY)
                at = at * g.slab + y * g.no
                part.append(flag(present) * face[at : at + unit, :].astype(F32))
            for i in range(RADIUS):
                at = aligned(layer(side, g.cx, i) * g.slab + y * g.no, unit)
                total = out[pl.ds(at, unit), :]
                for j in range(RADIUS - i):
                    total = total + (scale * WEIGHT[i + j + 1]) * part[j]
                out[pl.ds(at, unit), :] = total


def add_y_faces(g, dom, scale, face_refs, out):
    size = RADIUS * g.no
    for (side, present), face in zip(g.faces(dom, 1), face_refs):
        for x in range(g.cx):
            part = flag(present) * face[x * size : (x + 1) * size, :].astype(F32)
            for i in range(RADIUS):
                at = aligned(x * g.slab + layer(side, g.cy, i) * g.no, g.no)
                total = out[pl.ds(at, g.no), :]
                for j in range(RADIUS - i):
                    total = total + (scale * WEIGHT[i + j + 1]) * part[j * g.no : (j + 1) * g.no]
                out[pl.ds(at, g.no), :] = total


def add_nonlocal(g, scale, rows, projf, blk, atom, lut, spread, out):
    size = g.nproj * g.no
    lanes = g.table
    count = len(rows)
    rows = rows + [jnp.zeros((8 - count, lanes), F32)]
    scaled = (scale / HALF_WIDTH) * jnp.concatenate(rows, axis=0)
    high = scaled.astype(BF16)
    rest = scaled - high.astype(F32)
    mid = rest.astype(BF16)
    low = (rest - mid.astype(F32)).astype(BF16)
    parts = jnp.concatenate([high, mid, low], axis=0)
    wide = count * g.cz
    row, col = iota((24, wide), 0), iota((24, wide), 1)
    ones = jnp.where(row % 8 == col // g.cz, 1.0, 0.0).astype(BF16)
    out_all = lax.dot_general(parts, ones, TN, preferred_element_type=F32)
    for number in range(count):
        spread[number * lanes : (number + 1) * lanes, :] = out_all[:, number * g.cz : (number + 1) * g.cz]
    unroll = 4

    def step(i, _):
        additions = []
        for u in range(unroll):
            e = i * unroll + u
            col = column_of(g, lut, atom[e])
            total = None
            for p in range(g.nproj):
                at = pl.ds(pl.multiple_of(col * size + p * g.no, g.no), g.no)
                coef = jnp.broadcast_to(projf[e, p : p + 1, :], (g.no, g.cz))
                term = spread[at, :] * coef
                total = term if total is None else total + term
            additions.append((pl.ds(pl.multiple_of(blk[e] * g.no, g.no), g.no), total))
        for at, total in additions:
            out[at, :] += total
        return 0

    lax.fori_loop(0, g.ent // unroll, step, 0)


def sides_kernel(g, scale, acc, low, high, *refs):
    y_refs, out = refs[:-1], refs[-1]
    dom = lax.axis_index("dom")
    add_ends(g, dom, scale, acc, low, high, out)
    add_y_faces(g, dom, scale, y_refs, out)


def finish(g, scale, acc, projf, blk_hbm, atom_hbm, inputs, out, scratch):
    nx = len(g.face_rows(0))
    early, late, rows = inputs[:nx], inputs[nx : 2 * nx], inputs[2 * nx :]
    blk, atom, lut, sem, spread = scratch
    copies = entry_copies(blk_hbm, atom_hbm, blk, atom, sem)
    for copy in copies:
        copy.start()
    dom = lax.axis_index("dom")
    fill_lut(g, dom, lut)
    out[...] = acc[...]
    add_x_faces(g, dom, scale, early, late, out)
    for copy in copies:
        copy.wait()
    add_nonlocal(g, scale, [row[...] for row in rows], projf, blk, atom, lut, spread, out)
    return dom


def middle_kernel(g, acc, projf, blk_hbm, atom_hbm, *refs):
    nx = len(g.face_rows(0))
    nin = 2 * nx + len(g.links()) + 1
    u_ref = refs[nin]
    x_out = refs[nin + 1 : nin + 1 + nx]
    dom = finish(g, 1.0, acc, projf, blk_hbm, atom_hbm, refs[:nin], u_ref, refs[nin + 1 + nx :])
    pack_x(g, dom, u_ref, 0, EARLY, x_out)


def last_kernel(g, acc, projf, blk_hbm, atom_hbm, *refs):
    nin = 2 * len(g.face_rows(0)) + len(g.links()) + 1
    filtered, work = refs[nin : nin + 2]
    finish(g, 2.0, acc, projf, blk_hbm, atom_hbm, refs[:nin], work, refs[nin + 2 :])
    filtered[...] = work[...].astype(BF16)


def rotate_kernel(g, own, other, panel, out):
    band = lax.axis_index("band")
    group = 16
    span = group * g.no
    norb = panel.shape[0]
    row, col = iota((span, norb), 0), iota((span, norb), 1)
    pick_out = jnp.where(col == band * g.no + row // group, 1.0, 0.0).astype(BF16)
    picked = lax.dot_general(pick_out, panel[...], NT, preferred_element_type=F32).astype(BF16)
    row, col = iota((norb, 2 * span), 0), iota((norb, 2 * span), 1)
    source = jnp.where(col < span, band, 1 - band) * g.no + col % g.no
    pick_in = jnp.where(row == source, 1.0, 0.0).astype(BF16)
    spread = lax.dot_general(picked, pick_in, NN, preferred_element_type=F32)
    row, col = iota((span, 2 * span), 0), iota((span, 2 * span), 1)
    same = row % group == (col % span) // g.no
    weights = jnp.where(same, spread, 0.0).astype(BF16)
    for n in range(g.rows // group):
        rows = slice(n * span, (n + 1) * span)
        both = jnp.concatenate([own[rows, :], other[rows, :]], axis=0)
        result = lax.dot_general(weights, both, NN, preferred_element_type=F32)
        for j in range(g.no):
            at = j * g.rows + n * group
            out[at : at + group, :] = result[j * group : (j + 1) * group, :]


def call(kernel, name, out_shape, scratch, flops, args, specs):
    size = sum(a.size * a.dtype.itemsize for a in args)
    outs = out_shape if isinstance(out_shape, (tuple, list)) else [out_shape]
    size += sum(o.size * o.dtype.itemsize for o in outs)
    return pl.pallas_call(
        kernel,
        name=name,
        out_shape=out_shape,
        in_specs=specs,
        out_specs=jax.tree.map(lambda _: VMEM, out_shape),
        scratch_shapes=scratch,
        compiler_params=pltpu.CompilerParams(vmem_limit_bytes=48 * 1024 * 1024),
        cost_estimate=pl.CostEstimate(flops=flops, bytes_accessed=size, transcendentals=0),
    )(*args)


def shift(g, array, stride, extent, step):
    pairs = []
    for i in range(g.dom_count):
        place = i // stride % extent
        pairs.append((i, i + ((place + step) % extent - place) * stride))
    return lax.ppermute(array, "dom", pairs)


def swap_faces(g, faces, stride, extent):
    if extent == 2:
        return [shift(g, faces[0], stride, extent, 1)]
    if extent > 2:
        return [shift(g, faces[1], stride, extent, 1), shift(g, faces[0], stride, extent, -1)]
    return []


def shards(orbitals, potential, projectors, entry_atom, entry_block, kb_energy, panel):
    g = Geometry(
        orbitals.shape, projectors.shape[0], projectors.shape[1], kb_energy.shape[0], lax.axis_size("dom")
    )

    def in_hbm(array):
        return pltpu.with_memory_space_constraint(array, pltpu.HBM)

    orb = in_hbm(orbitals.reshape(g.flat, g.cz))
    pot = in_hbm(potential.reshape(g.rows, g.cz))
    proj = in_hbm(projectors)
    blk, atom = in_hbm(entry_block), in_hbm(entry_atom)
    field = jax.ShapeDtypeStruct((g.flat, g.cz), F32)
    x_early = [jax.ShapeDtypeStruct((n, g.cz), BF16) for n in g.face_rows(0, EARLY)]
    x_late = [jax.ShapeDtypeStruct((n, g.cz), BF16) for n in g.face_rows(0, RADIUS - EARLY)]
    y_faces = [jax.ShapeDtypeStruct((n, g.cz), BF16) for n in g.face_rows(1)]
    nx, ny = len(x_early), len(y_faces)
    links = g.links()
    ends = jax.ShapeDtypeStruct((8, g.flat), F32)
    row = jax.ShapeDtypeStruct((1, g.table), F32)
    slots = (len(links) + 1) * g.table
    entries = [
        pltpu.SMEM((g.ent,), jnp.int32),
        pltpu.SMEM((g.ent,), jnp.int32),
        pltpu.SMEM((g.dom_count + 2 * g.plane,), jnp.int32),
        pltpu.SemaphoreType.DMA((2,)),
    ]
    sums = [pltpu.VMEM((slots, g.cz), F32) for _ in range(4)]
    spread = pltpu.VMEM((slots, g.cz), F32)
    energy = jnp.repeat(kb_energy.reshape(g.dom_count, g.owned * g.nproj), g.no, axis=1)

    def swap_x(faces):
        return swap_faces(g, faces, g.plane, g.first)

    def neighbours(which, values, early):
        x1 = swap_x(early)
        *rows, low, high = call(
            functools.partial(tables_kernel, g),
            "tables_" + which,
            [row] * (len(links) - 1) + [ends, ends],
            [*entries, *sums],
            10_000_000,
            [values, projf, blk, atom],
            [VMEM] * 2 + [HBM] * 2,
        )
        low, high = shift(g, high, 1, g.third, 1), shift(g, low, 1, g.third, -1)
        for n, (stride, extent, step) in enumerate(links[:-2]):
            rows[n + 1] = shift(g, rows[n + 1], stride, extent, step or 1)
        later = call(
            functools.partial(rest_kernel, g),
            "rest_" + which,
            [*x_late, *y_faces],
            [],
            1_000_000,
            [values, low],
            [VMEM] * 2,
        )
        x2 = swap_x(later[:nx])
        from_y = swap_faces(g, later[nx:], g.third, g.second)
        scaled = call(
            functools.partial(scale_kernel, g),
            "scale_" + which,
            row,
            [],
            1_000_000,
            [energy, low, high, *rows],
            [VMEM] * (3 + len(rows)),
        )
        rows = [scaled]
        for stride, extent, step in links:
            rows.append(shift(g, scaled, stride, extent, -step or 1))
        return low, high, from_y, [*x1, *x2, *rows]

    def sides(scale, which, acc, low, high, from_y):
        return call(
            functools.partial(sides_kernel, g, scale),
            "sides_" + which,
            field,
            [],
            10_000_000,
            [acc, low, high, *from_y],
            [VMEM] * (3 + ny),
        )

    v, projf, pot, *early = call(
        functools.partial(first_kernel, g),
        "early_first",
        [field, jax.ShapeDtypeStruct(proj.shape, F32), jax.ShapeDtypeStruct(pot.shape, F32), *x_early],
        [pltpu.VMEM(orb.shape, F32), pltpu.VMEM(proj.shape, BF16), pltpu.SemaphoreType.DMA((3,))],
        10_000_000,
        [orb, proj, pot],
        [HBM] * 3,
    )
    low, high, from_y, others = neighbours("first", v, early)
    acc = call(
        functools.partial(inside_kernel, g, 1.0, False),
        "inside_first",
        field,
        [],
        200_000_000,
        [v, pot],
        [VMEM, VMEM],
    )
    acc = sides(1.0, "first", acc, low, high, from_y)
    u, *early = call(
        functools.partial(middle_kernel, g),
        "middle",
        [field, *x_early],
        [*entries, spread],
        10_000_000,
        [acc, projf, blk, atom, *others],
        [VMEM] * 2 + [HBM] * 2 + [VMEM] * len(others),
    )
    low, high, from_y, others = neighbours("second", u, early)
    acc = call(
        functools.partial(inside_kernel, g, 2.0, True),
        "inside_second",
        field,
        [],
        200_000_000,
        [u, pot, v],
        [VMEM, VMEM, VMEM],
    )
    acc = sides(2.0, "second", acc, low, high, from_y)
    filtered = call(
        functools.partial(last_kernel, g),
        "filtered",
        jax.ShapeDtypeStruct((g.flat, g.cz), BF16),
        [pltpu.VMEM((g.flat, g.cz), F32), *entries, spread],
        10_000_000,
        [acc, projf, blk, atom, *others],
        [VMEM] * 2 + [HBM] * 2 + [VMEM] * len(others),
    )
    other = lax.ppermute(filtered, "band", [(0, 1), (1, 0)])
    rotated = call(
        functools.partial(rotate_kernel, g),
        "rotate",
        field,
        [],
        200_000_000,
        [filtered, other, panel],
        [VMEM] * 3,
    )
    return rotated.reshape(orbitals.shape)


def solution(mesh):
    in_specs = (
        P("dom", "band", None, None, None),
        P("dom", None, None, None),
        P("dom", None, None),
        P("dom"),
        P("dom"),
        P(),
        P(),
    )
    out_specs = P("dom", "band", None, None, None)
    return jax.shard_map(shards, mesh=mesh, in_specs=in_specs, out_specs=out_specs, check_vma=False)
```

```python
import functools

import jax
import jax.numpy as jnp
from jax import lax
from jax.experimental import pallas as pl
from jax.experimental.pallas import tpu as pltpu
from jax.sharding import PartitionSpec as P

RADIUS = 6
COEFFS = (
    -5369.0 / 1800.0,
    12.0 / 7.0,
    -15.0 / 56.0,
    10.0 / 189.0,
    -1.0 / 112.0,
    2.0 / 1925.0,
    -1.0 / 16632.0,
)
KINETIC = -3.125
CENTER = 36.0
HALF_WIDTH = 34.0
WEIGHT = [KINETIC * c / HALF_WIDTH for c in COEFFS]
DIAGONAL = (3.0 * KINETIC * COEFFS[0] - CENTER) / HALF_WIDTH

F32 = jnp.float32
BF16 = jnp.bfloat16
VMEM = pl.BlockSpec(memory_space=pltpu.VMEM)
HBM = pl.BlockSpec(memory_space=pltpu.HBM)
NT = (((1,), (1,)), ((), ()))
TN = (((0,), (0,)), ((), ()))
NN = (((1,), (0,)), ((), ()))


def split2(x):
    high = x.astype(BF16)
    low = (x - high.astype(F32)).astype(BF16)
    return high, low


def iota(shape, dim):
    return lax.broadcasted_iota(jnp.int32, shape, dim)


def weight_at(distance, scale):
    out = jnp.zeros(distance.shape, F32)
    for k in range(1, RADIUS + 1):
        out = jnp.where(distance == k, scale * WEIGHT[k], out)
    return out


class Geometry:
    def __init__(self, orbitals, entries, nproj, atoms, dom_count):
        _, self.no, self.cx, self.cy, self.cz = orbitals
        self.rows = self.cx * self.cy
        self.flat = self.rows * self.no
        self.ent = entries
        self.nproj = nproj
        self.dom_count = dom_count
        self.owned = atoms // dom_count
        self.third = 4
        self.second = min(8, dom_count // 8)
        self.plane = self.second * self.third
        self.first = dom_count // self.plane
        self.table = self.owned * nproj * self.no
        self.slab = self.cy * self.no
        self.fold = self.flat // self.table
        self.butterfly = self.first == 2 and self.second == 2 and dom_count <= 2 * self.fold
        assert self.no == 8

    def faces(self, dom, dim):
        if dim == 0:
            extent, place = self.first, dom // self.plane
        else:
            extent, place = self.second, dom // self.third % self.second
        if extent == 2:
            return [(1 - place, None)]
        if extent > 2:
            return [(0, place > 0), (1, place < extent - 1)]
        return []

    def face_rows(self, dim):
        rows = RADIUS * self.slab if dim == 0 else self.cx * RADIUS * self.no
        return [rows] * len(self.faces(0, dim))

    def steps(self, dom):
        out = [0]
        for extent, stride in ((self.first, self.plane), (self.second, self.third), (self.third, 1)):
            if extent == 2:
                out.append((1 - 2 * (dom // stride % 2)) * stride)
            elif extent > 2:
                out.extend([stride, -stride])
        return out

    def slots(self):
        return len(self.steps(0))


def layer(side, length, j):
    if isinstance(side, int):
        return length - 1 - j if side else j
    return side * (length - 1 - j) + (1 - side) * j


def aligned(start, unit):
    return start if isinstance(start, int) else pl.multiple_of(start, unit)


def pack_faces(g, dom, v_ref, x_refs, y_refs):
    for (side, _), out in zip(g.faces(dom, 0), x_refs):
        for j in range(RADIUS):
            at = aligned(layer(side, g.cx, j) * g.slab, g.slab)
            out[j * g.slab : (j + 1) * g.slab, :] = v_ref[pl.ds(at, g.slab), :].astype(BF16)
    size = RADIUS * g.no
    for (side, _), out in zip(g.faces(dom, 1), y_refs):
        for x in range(g.cx):
            pieces = []
            for j in range(RADIUS):
                at = aligned(x * g.slab + layer(side, g.cy, j) * g.no, g.no)
                pieces.append(v_ref[pl.ds(at, g.no), :])
            out[x * size : (x + 1) * size, :] = jnp.concatenate(pieces, axis=0).astype(BF16)


def end_columns(g, dom):
    row, col = iota((16, g.cz), 0), iota((16, g.cz), 1)
    odd = dom % 2
    side = jnp.where(row < 8, 1 - odd, odd)
    return jnp.where(side == 1, g.cz - 1 - col, col), row


def pack_ends(g, dom, v_ref, first_ref, second_ref):
    inward, row = end_columns(g, dom)
    pick = jnp.where((inward == row % 8) & (row % 8 < RADIUS), 1.0, 0.0).astype(BF16)
    pick = jnp.concatenate([pick, pick], axis=1)
    for x in range(g.cx):
        rows = slice(x * g.slab, (x + 1) * g.slab)
        both = jnp.concatenate(split2(v_ref[rows, :]), axis=1)
        ends = lax.dot_general(pick, both, NT, preferred_element_type=F32)
        first_ref[:, rows] = ends[:8]
        second_ref[:, rows] = ends[8:]


def put_table(g, message, table):
    for n in range(g.dom_count):
        at = RADIUS + n // g.fold
        lanes = n % g.fold * g.table
        message[at : at + 1, lanes : lanes + g.table] = table[n : n + 1, :]


def get_table(g, message):
    rows = []
    for n in range(g.dom_count):
        at = RADIUS + n // g.fold
        lanes = n % g.fold * g.table
        rows.append(message[at : at + 1, lanes : lanes + g.table])
    return jnp.concatenate(rows, axis=0)


def fill_lut(g, dom, lut):
    for number, step in enumerate(g.steps(dom)):
        lut[g.plane + dom + step] = number * g.owned


def column_of(g, lut, atom):
    owner = lax.div(atom, jnp.int32(g.owned))
    return lut[owner + g.plane] + (atom - owner * g.owned)


def inner_tables(g, dom, v_ref, projf, blk, atom, lut, sums, table):
    size = g.nproj * g.no

    def step(i, _):
        for u, part in enumerate(sums):
            e = i * len(sums) + u
            col = column_of(g, lut, atom[e])
            v = v_ref[pl.ds(pl.multiple_of(blk[e] * g.no, g.no), g.no), :]
            for p in range(g.nproj):
                at = pl.ds(pl.multiple_of(col * size + p * g.no, g.no), g.no)
                coef = jnp.broadcast_to(projf[e, p : p + 1, :], v.shape)
                part[at, :] += v * coef
        return 0

    lax.fori_loop(0, g.ent // len(sums), step, 0)
    total = sums[0][...]
    for part in sums[1:]:
        total = total + part[...]
    both = jnp.concatenate(split2(total), axis=1)
    ones = jnp.ones((8, both.shape[1]), BF16)
    summed = lax.dot_general(ones, both, NT, preferred_element_type=F32)
    table[...] = jnp.zeros(table.shape, F32)
    for number, step in enumerate(g.steps(dom)):
        owner = jnp.clip(dom + step, 0, g.dom_count - 1)
        table[pl.ds(owner, 1), :] += summed[0:1, number * g.table : (number + 1) * g.table]


def clear(sums):
    for part in sums:
        part[...] = jnp.zeros(part.shape, F32)


def first_kernel(g, orb_hbm, proj_hbm, pot_hbm, v_ref, projf, pot, *refs):
    nx, ny = len(g.face_rows(0)), len(g.face_rows(1))
    orb, proj, sem = refs[nx + ny :]
    copies = [
        pltpu.make_async_copy(orb_hbm, orb, sem.at[0]),
        pltpu.make_async_copy(proj_hbm, proj, sem.at[1]),
        pltpu.make_async_copy(pot_hbm, pot, sem.at[2]),
    ]
    for copy in copies:
        copy.start()
    dom = lax.axis_index("dom")
    copies[0].wait()
    for r in range(g.rows):
        v_ref[r * g.no : (r + 1) * g.no, :] = orb[pl.ds(r, g.no, stride=g.rows), :]
    pack_faces(g, dom, v_ref, refs[:nx], refs[nx : nx + ny])
    copies[1].wait()
    projf[...] = proj[...].astype(F32)
    copies[2].wait()


def entry_copies(blk_hbm, atom_hbm, blk, atom, sem):
    return [
        pltpu.make_async_copy(blk_hbm, blk, sem.at[0]),
        pltpu.make_async_copy(atom_hbm, atom, sem.at[1]),
    ]


def tables_kernel(g, v_ref, projf, blk_hbm, atom_hbm, table, first, second, blk, atom, lut, sem, *sums):
    copies = entry_copies(blk_hbm, atom_hbm, blk, atom, sem)
    for copy in copies:
        copy.start()
    dom = lax.axis_index("dom")
    fill_lut(g, dom, lut)
    clear(sums)
    pack_ends(g, dom, v_ref, first, second)
    for copy in copies:
        copy.wait()
    inner_tables(g, dom, v_ref, projf, blk, atom, lut, sums, table)
    if g.butterfly:
        put_table(g, first, table)


def join_kernel(g, table, first_in, second, table_out, second_out):
    table_out[...] = table[...] + get_table(g, first_in)
    second_out[...] = second[...]
    put_table(g, second_out, table_out)


def unpack_kernel(g, table, second_in, *refs):
    table_out = refs[-1]
    table_out[...] = table[...] + get_table(g, second_in)


def inside_kernel(g, scale, subtract, v_ref, pot, *refs):
    prev, out = refs if subtract else (None, refs[0])
    row, col = iota((g.cz, g.cz), 0), iota((g.cz, g.cz), 1)
    high, low = split2(weight_at(jnp.abs(row - col), scale))
    band = jnp.concatenate([high, low], axis=1)
    band = jnp.concatenate([band, band], axis=0)

    def cell(x, y):
        at = (x * g.cy + y) * g.no
        return v_ref[at : at + g.no, :]

    for x in range(g.cx):
        both = jnp.concatenate(split2(v_ref[x * g.slab : (x + 1) * g.slab, :]), axis=1)
        along = lax.dot_general(both, band, NN, preferred_element_type=F32)
        for y in range(g.cy):
            at = (x * g.cy + y) * g.no
            rows = slice(y * g.no, (y + 1) * g.no)
            here = cell(x, y)
            diag = jnp.broadcast_to(pot[x * g.cy + y : x * g.cy + y + 1, :], here.shape)
            total = along[rows, : g.cz] + along[rows, g.cz :]
            total = total + (scale * DIAGONAL + (scale / HALF_WIDTH) * diag) * here
            if subtract:
                total = total - prev[at : at + g.no, :]
            for k in range(1, RADIUS + 1):
                near = []
                for a, b in ((x - k, y), (x + k, y), (x, y - k), (x, y + k)):
                    if 0 <= a < g.cx and 0 <= b < g.cy:
                        near.append(cell(a, b))
                if near:
                    total = total + (scale * WEIGHT[k]) * sum(near[1:], near[0])
            out[at : at + g.no, :] = total


def flag(present):
    return 1.0 if present is None else jnp.where(present, 1.0, 0.0)


def add_ends(g, dom, scale, acc, low, high, out):
    inward, row = end_columns(g, dom)
    middle = (dom % g.third > 0) & (dom % g.third < g.third - 1)
    present = (row % 8 < RADIUS) & ((row < 8) | middle)
    coef = jnp.where(present, weight_at(inward + row % 8 + 1, scale), 0.0)
    c_high, c_low = split2(coef)
    coefs = jnp.concatenate([c_high, c_high, c_low, c_low], axis=0)
    for x in range(g.cx):
        rows = slice(x * g.slab, (x + 1) * g.slab)
        h_high, h_low = split2(jnp.concatenate([low[:, rows], high[:, rows]], axis=0))
        halo = jnp.concatenate([h_high, h_low, h_high, h_low], axis=0)
        out[rows, :] = acc[rows, :] + lax.dot_general(halo, coefs, TN, preferred_element_type=F32)


def add_x_faces(g, dom, scale, face_refs, out):
    unit = 2 * g.no
    for (side, present), face in zip(g.faces(dom, 0), face_refs):
        for y in range(0, g.cy, 2):
            starts = [j * g.slab + y * g.no for j in range(RADIUS)]
            part = [flag(present) * face[at : at + unit, :].astype(F32) for at in starts]
            for i in range(RADIUS):
                at = aligned(layer(side, g.cx, i) * g.slab + y * g.no, unit)
                total = out[pl.ds(at, unit), :]
                for j in range(RADIUS - i):
                    total = total + (scale * WEIGHT[i + j + 1]) * part[j]
                out[pl.ds(at, unit), :] = total


def add_y_faces(g, dom, scale, face_refs, out):
    size = RADIUS * g.no
    for (side, present), face in zip(g.faces(dom, 1), face_refs):
        for x in range(g.cx):
            part = flag(present) * face[x * size : (x + 1) * size, :].astype(F32)
            for i in range(RADIUS):
                at = aligned(x * g.slab + layer(side, g.cy, i) * g.no, g.no)
                total = out[pl.ds(at, g.no), :]
                for j in range(RADIUS - i):
                    total = total + (scale * WEIGHT[i + j + 1]) * part[j * g.no : (j + 1) * g.no]
                out[pl.ds(at, g.no), :] = total


def add_nonlocal(g, dom, scale, tables, energy, projf, blk, atom, lut, spread, out):
    size = g.nproj * g.no
    lanes = g.table
    count = g.slots()
    rows = []
    for step in g.steps(dom):
        owner = pl.ds(jnp.clip(dom + step, 0, g.dom_count - 1), 1)
        total = tables[0][owner, :]
        for table in tables[1:]:
            total = total + table[owner, :]
        rows.append(total * energy[owner, :])
    rows.append(jnp.zeros((8 - count, lanes), F32))
    scaled = (scale / HALF_WIDTH) * jnp.concatenate(rows, axis=0)
    high = scaled.astype(BF16)
    rest = scaled - high.astype(F32)
    mid = rest.astype(BF16)
    low = (rest - mid.astype(F32)).astype(BF16)
    parts = jnp.concatenate([high, mid, low], axis=0)
    wide = count * g.cz
    row, col = iota((24, wide), 0), iota((24, wide), 1)
    ones = jnp.where(row % 8 == col // g.cz, 1.0, 0.0).astype(BF16)
    out_all = lax.dot_general(parts, ones, TN, preferred_element_type=F32)
    for number in range(count):
        spread[number * lanes : (number + 1) * lanes, :] = out_all[:, number * g.cz : (number + 1) * g.cz]
    unroll = 4

    def step(i, _):
        additions = []
        for u in range(unroll):
            e = i * unroll + u
            col = column_of(g, lut, atom[e])
            total = None
            for p in range(g.nproj):
                at = pl.ds(pl.multiple_of(col * size + p * g.no, g.no), g.no)
                coef = jnp.broadcast_to(projf[e, p : p + 1, :], (g.no, g.cz))
                term = spread[at, :] * coef
                total = term if total is None else total + term
            additions.append((pl.ds(pl.multiple_of(blk[e] * g.no, g.no), g.no), total))
        for at, total in additions:
            out[at, :] += total
        return 0

    lax.fori_loop(0, g.ent // unroll, step, 0)


def sides_kernel(g, scale, acc, low, high, *refs):
    nx = len(g.face_rows(0))
    out = refs[-1]
    dom = lax.axis_index("dom")
    add_ends(g, dom, scale, acc, low, high, out)
    add_x_faces(g, dom, scale, refs[:nx], out)
    add_y_faces(g, dom, scale, refs[nx:-1], out)


def finish(g, scale, acc, projf, energy, blk_hbm, atom_hbm, tables, out, scratch):
    blk, atom, lut, sem, spread = scratch
    copies = entry_copies(blk_hbm, atom_hbm, blk, atom, sem)
    for copy in copies:
        copy.start()
    dom = lax.axis_index("dom")
    fill_lut(g, dom, lut)
    out[...] = acc[...]
    for copy in copies:
        copy.wait()
    add_nonlocal(g, dom, scale, tables, energy, projf, blk, atom, lut, spread, out)
    return dom


def middle_kernel(g, nt, acc, projf, energy, blk_hbm, atom_hbm, *refs):
    nx, ny = len(g.face_rows(0)), len(g.face_rows(1))
    tables, u_ref = refs[:nt], refs[nt]
    faces = refs[nt + 1 : nt + 1 + nx + ny]
    scratch = refs[nt + 1 + nx + ny :]
    dom = finish(g, 1.0, acc, projf, energy, blk_hbm, atom_hbm, tables, u_ref, scratch)
    pack_faces(g, dom, u_ref, faces[:nx], faces[nx:])


def last_kernel(g, nt, acc, projf, energy, blk_hbm, atom_hbm, *refs):
    tables, filtered, work = refs[:nt], refs[nt], refs[nt + 1]
    finish(g, 2.0, acc, projf, energy, blk_hbm, atom_hbm, tables, work, refs[nt + 2 :])
    filtered[...] = work[...].astype(BF16)


def rotate_kernel(g, own, other, panel, out):
    band = lax.axis_index("band")
    group = 16
    span = group * g.no
    norb = panel.shape[0]
    row, col = iota((span, norb), 0), iota((span, norb), 1)
    pick_out = jnp.where(col == band * g.no + row // group, 1.0, 0.0).astype(BF16)
    picked = lax.dot_general(pick_out, panel[...], NT, preferred_element_type=F32).astype(BF16)
    row, col = iota((norb, 2 * span), 0), iota((norb, 2 * span), 1)
    source = jnp.where(col < span, band, 1 - band) * g.no + col % g.no
    pick_in = jnp.where(row == source, 1.0, 0.0).astype(BF16)
    spread = lax.dot_general(picked, pick_in, NN, preferred_element_type=F32)
    row, col = iota((span, 2 * span), 0), iota((span, 2 * span), 1)
    same = row % group == (col % span) // g.no
    weights = jnp.where(same, spread, 0.0).astype(BF16)
    for n in range(g.rows // group):
        rows = slice(n * span, (n + 1) * span)
        both = jnp.concatenate([own[rows, :], other[rows, :]], axis=0)
        result = lax.dot_general(weights, both, NN, preferred_element_type=F32)
        for j in range(g.no):
            at = j * g.rows + n * group
            out[at : at + group, :] = result[j * group : (j + 1) * group, :]


def call(kernel, name, out_shape, scratch, args, specs):
    return pl.pallas_call(
        kernel,
        name=name,
        out_shape=out_shape,
        in_specs=specs,
        out_specs=jax.tree.map(lambda _: VMEM, out_shape),
        scratch_shapes=scratch,
        compiler_params=pltpu.CompilerParams(vmem_limit_bytes=48 * 1024 * 1024),
        cost_estimate=pl.CostEstimate(flops=1000, bytes_accessed=1000, transcendentals=0),
    )(*args)


def shift(g, array, stride, extent, step):
    pairs = []
    for i in range(g.dom_count):
        place = i // stride % extent
        pairs.append((i, i + ((place + step) % extent - place) * stride))
    return lax.ppermute(array, "dom", pairs)


def swap_faces(g, faces, stride, extent):
    if extent == 2:
        return [shift(g, faces[0], stride, extent, 1)]
    if extent > 2:
        return [shift(g, faces[1], stride, extent, 1), shift(g, faces[0], stride, extent, -1)]
    return []


def shards(orbitals, potential, projectors, entry_atom, entry_block, kb_energy, panel):
    g = Geometry(
        orbitals.shape, projectors.shape[0], projectors.shape[1], kb_energy.shape[0], lax.axis_size("dom")
    )

    def in_hbm(array):
        return pltpu.with_memory_space_constraint(array, pltpu.HBM)

    orb = in_hbm(orbitals.reshape(g.flat, g.cz))
    pot = in_hbm(potential.reshape(g.rows, g.cz))
    proj = in_hbm(projectors)
    blk, atom = in_hbm(entry_block), in_hbm(entry_atom)
    field = jax.ShapeDtypeStruct((g.flat, g.cz), F32)
    faces = [jax.ShapeDtypeStruct((n, g.cz), BF16) for n in g.face_rows(0) + g.face_rows(1)]
    nx = len(g.face_rows(0))
    ends = jax.ShapeDtypeStruct((8, g.flat), F32)
    table = jax.ShapeDtypeStruct((g.dom_count, g.table), F32)
    entries = [
        pltpu.SMEM((g.ent,), jnp.int32),
        pltpu.SMEM((g.ent,), jnp.int32),
        pltpu.SMEM((g.dom_count + 2 * g.plane,), jnp.int32),
        pltpu.SemaphoreType.DMA((2,)),
    ]
    slots = g.slots() * g.table
    sums = [pltpu.VMEM((slots, g.cz), F32) for _ in range(4)]
    spread = pltpu.VMEM((slots, g.cz), F32)
    energy = jnp.repeat(kb_energy.reshape(g.dom_count, g.owned * g.nproj), g.no, axis=1)
    indices = range(g.dom_count)
    first_pairs = [(i, i ^ 1) for i in indices]
    second_pairs = [(i, i - i % g.third + g.third - 1 - i % g.third) for i in indices]

    def neighbours(which, values, sent):
        from_x = swap_faces(g, sent[:nx], g.plane, g.first)
        from_y = swap_faces(g, sent[nx:], g.third, g.second)
        part, first, second = call(
            functools.partial(tables_kernel, g),
            "tables_" + which,
            [table, ends, ends],
            [*entries, *sums],
            [values, projf, blk, atom],
            [VMEM] * 2 + [HBM] * 2,
        )
        first = lax.ppermute(first, "dom", first_pairs)
        if g.butterfly:
            part, second = call(
                functools.partial(join_kernel, g),
                "join_" + which,
                [table, ends],
                [],
                [part, first, second],
                [VMEM] * 3,
            )
        second = lax.ppermute(second, "dom", second_pairs)
        if g.butterfly:
            part = call(
                functools.partial(unpack_kernel, g),
                "unpack_" + which,
                table,
                [],
                [part, second, *from_x, *from_y],
                [VMEM] * (2 + len(sent)),
            )
            part = part + shift(g, part, g.third, 2, 1)
            tables = [part, shift(g, part, g.plane, 2, 1)]
        else:
            tables = [lax.psum(part, "dom")]
        return tables, [first, second, *from_x, *from_y]

    def sides(scale, which, acc, received):
        return call(
            functools.partial(sides_kernel, g, scale),
            "sides_" + which,
            field,
            [],
            [acc, *received],
            [VMEM] * (1 + len(received)),
        )

    v, projf, pot, *sent = call(
        functools.partial(first_kernel, g),
        "faces_first",
        [field, jax.ShapeDtypeStruct(proj.shape, F32), jax.ShapeDtypeStruct(pot.shape, F32), *faces],
        [pltpu.VMEM(orb.shape, F32), pltpu.VMEM(proj.shape, BF16), pltpu.SemaphoreType.DMA((3,))],
        [orb, proj, pot],
        [HBM] * 3,
    )
    tables, received = neighbours("first", v, sent)
    acc = call(
        functools.partial(inside_kernel, g, 1.0, False), "inside_first", field, [], [v, pot], [VMEM] * 2
    )
    acc = sides(1.0, "first", acc, received)
    nt = len(tables)
    u, *sent = call(
        functools.partial(middle_kernel, g, nt),
        "middle",
        [field, *faces],
        [*entries, spread],
        [acc, projf, energy, blk, atom, *tables],
        [VMEM] * 3 + [HBM] * 2 + [VMEM] * nt,
    )
    tables, received = neighbours("second", u, sent)
    acc = call(
        functools.partial(inside_kernel, g, 2.0, True), "inside_second", field, [], [u, pot, v], [VMEM] * 3
    )
    acc = sides(2.0, "second", acc, received)
    filtered = call(
        functools.partial(last_kernel, g, nt),
        "filtered",
        jax.ShapeDtypeStruct((g.flat, g.cz), BF16),
        [pltpu.VMEM((g.flat, g.cz), F32), *entries, spread],
        [acc, projf, energy, blk, atom, *tables],
        [VMEM] * 3 + [HBM] * 2 + [VMEM] * nt,
    )
    other = lax.ppermute(filtered, "band", [(0, 1), (1, 0)])
    rotated = call(
        functools.partial(rotate_kernel, g), "rotate", field, [], [filtered, other, panel], [VMEM] * 3
    )
    return rotated.reshape(orbitals.shape)


def solution(mesh):
    in_specs = (
        P("dom", "band", None, None, None),
        P("dom", None, None, None),
        P("dom", None, None),
        P("dom"),
        P("dom"),
        P(),
        P(),
    )
    out_specs = P("dom", "band", None, None, None)
    return jax.shard_map(shards, mesh=mesh, in_specs=in_specs, out_specs=out_specs, check_vma=False)
```

```python
import functools

import jax
import jax.numpy as jnp
from jax import lax
from jax.experimental import pallas as pl
from jax.experimental.pallas import tpu as pltpu
from jax.sharding import PartitionSpec as P

RADIUS = 6
COEFFS = (
    -5369.0 / 1800.0,
    12.0 / 7.0,
    -15.0 / 56.0,
    10.0 / 189.0,
    -1.0 / 112.0,
    2.0 / 1925.0,
    -1.0 / 16632.0,
)
KINETIC = -3.125
CENTER = 36.0
HALF_WIDTH = 34.0
WEIGHT = [KINETIC * c / HALF_WIDTH for c in COEFFS]
DIAGONAL = (3.0 * KINETIC * COEFFS[0] - CENTER) / HALF_WIDTH

F32 = jnp.float32
BF16 = jnp.bfloat16
VMEM = pl.BlockSpec(memory_space=pltpu.VMEM)
HBM = pl.BlockSpec(memory_space=pltpu.HBM)
NT = (((1,), (1,)), ((), ()))
TN = (((0,), (0,)), ((), ()))
NN = (((1,), (0,)), ((), ()))


def split2(x):
    high = x.astype(BF16)
    low = (x - high.astype(F32)).astype(BF16)
    return high, low


def iota(shape, dim):
    return lax.broadcasted_iota(jnp.int32, shape, dim)


def weight_at(distance, scale):
    out = jnp.zeros(distance.shape, F32)
    for k in range(1, RADIUS + 1):
        out = jnp.where(distance == k, scale * WEIGHT[k], out)
    return out


class Geometry:
    def __init__(self, orbitals, entries, nproj, atoms, dom_count):
        _, self.no, self.cx, self.cy, self.cz = orbitals
        self.rows = self.cx * self.cy
        self.flat = self.rows * self.no
        self.ent = entries
        self.nproj = nproj
        self.dom_count = dom_count
        self.owned = atoms // dom_count
        self.third = 4
        self.second = min(8, dom_count // 8)
        self.plane = self.second * self.third
        self.first = dom_count // self.plane
        self.table = self.owned * nproj * self.no
        self.slab = self.cy * self.no
        self.fold = self.flat // self.table
        self.butterfly = self.first == 2 and self.second == 2 and dom_count <= 2 * self.fold
        assert self.no == 8

    def faces(self, dom, dim):
        if dim == 0:
            extent, place = self.first, dom // self.plane
        else:
            extent, place = self.second, dom // self.third % self.second
        if extent == 2:
            return [(1 - place, None)]
        if extent > 2:
            return [(0, place > 0), (1, place < extent - 1)]
        return []

    def face_rows(self, dim):
        rows = RADIUS * self.slab if dim == 0 else self.cx * RADIUS * self.no
        return [rows] * len(self.faces(0, dim))

    def steps(self, dom):
        out = [0]
        for extent, stride in ((self.first, self.plane), (self.second, self.third), (self.third, 1)):
            if extent == 2:
                out.append((1 - 2 * (dom // stride % 2)) * stride)
            elif extent > 2:
                out.extend([stride, -stride])
        return out

    def slots(self):
        return len(self.steps(0))


def layer(side, length, j):
    if isinstance(side, int):
        return length - 1 - j if side else j
    return side * (length - 1 - j) + (1 - side) * j


def aligned(start, unit):
    return start if isinstance(start, int) else pl.multiple_of(start, unit)


def pack_faces(g, dom, v_ref, x_refs, y_refs):
    for (side, _), out in zip(g.faces(dom, 0), x_refs):
        for j in range(RADIUS):
            at = aligned(layer(side, g.cx, j) * g.slab, g.slab)
            out[j * g.slab : (j + 1) * g.slab, :] = v_ref[pl.ds(at, g.slab), :].astype(BF16)
    size = RADIUS * g.no
    for (side, _), out in zip(g.faces(dom, 1), y_refs):
        for x in range(g.cx):
            pieces = []
            for j in range(RADIUS):
                at = aligned(x * g.slab + layer(side, g.cy, j) * g.no, g.no)
                pieces.append(v_ref[pl.ds(at, g.no), :])
            out[x * size : (x + 1) * size, :] = jnp.concatenate(pieces, axis=0).astype(BF16)


def end_columns(g, dom):
    row, col = iota((16, g.cz), 0), iota((16, g.cz), 1)
    odd = dom % 2
    side = jnp.where(row < 8, 1 - odd, odd)
    return jnp.where(side == 1, g.cz - 1 - col, col), row


def pack_ends(g, dom, v_ref, first_ref, second_ref):
    inward, row = end_columns(g, dom)
    pick = jnp.where((inward == row % 8) & (row % 8 < RADIUS), 1.0, 0.0).astype(BF16)
    pick = jnp.concatenate([pick, pick], axis=1)
    for x in range(g.cx):
        rows = slice(x * g.slab, (x + 1) * g.slab)
        both = jnp.concatenate(split2(v_ref[rows, :]), axis=1)
        ends = lax.dot_general(pick, both, NT, preferred_element_type=F32)
        first_ref[:, rows] = ends[:8]
        second_ref[:, rows] = ends[8:]


def put_table(g, message, table):
    for n in range(g.dom_count):
        at = RADIUS + n // g.fold
        lanes = n % g.fold * g.table
        message[at : at + 1, lanes : lanes + g.table] = table[n : n + 1, :]


def get_table(g, message):
    rows = []
    for n in range(g.dom_count):
        at = RADIUS + n // g.fold
        lanes = n % g.fold * g.table
        rows.append(message[at : at + 1, lanes : lanes + g.table])
    return jnp.concatenate(rows, axis=0)


def fill_lut(g, dom, lut):
    for number, step in enumerate(g.steps(dom)):
        lut[g.plane + dom + step] = number * g.owned


def column_of(g, lut, atom):
    if g.owned & (g.owned - 1):
        owner = lax.div(atom, jnp.int32(g.owned))
        return lut[owner + g.plane] + (atom - owner * g.owned)
    owner = lax.shift_right_logical(atom, jnp.int32(g.owned.bit_length() - 1))
    return lut[owner + g.plane] + (atom & (g.owned - 1))


def inner_tables(g, dom, v_ref, projf, blk, atom, lut, sums, table):
    size = g.nproj * g.no

    def step(i, _):
        for u, part in enumerate(sums):
            e = i * len(sums) + u
            col = column_of(g, lut, atom[e])
            v = v_ref[pl.ds(pl.multiple_of(blk[e] * g.no, g.no), g.no), :]
            for p in range(g.nproj):
                at = pl.ds(pl.multiple_of(col * size + p * g.no, g.no), g.no)
                coef = jnp.broadcast_to(projf[e, p : p + 1, :], v.shape)
                part[at, :] += v * coef
        return 0

    lax.fori_loop(0, g.ent // len(sums), step, 0)
    total = sums[0][...]
    for part in sums[1:]:
        total = total + part[...]
    both = jnp.concatenate(split2(total), axis=1)
    ones = jnp.ones((8, both.shape[1]), BF16)
    summed = lax.dot_general(ones, both, NT, preferred_element_type=F32)
    table[...] = jnp.zeros(table.shape, F32)
    for number, step in enumerate(g.steps(dom)):
        owner = jnp.clip(dom + step, 0, g.dom_count - 1)
        table[pl.ds(owner, 1), :] += summed[0:1, number * g.table : (number + 1) * g.table]


def clear(sums):
    for part in sums:
        part[...] = jnp.zeros(part.shape, F32)


def entry_copies(blk_hbm, atom_hbm, blk, atom, sem):
    copies = [
        pltpu.make_async_copy(blk_hbm, blk, sem.at[0]),
        pltpu.make_async_copy(atom_hbm, atom, sem.at[1]),
    ]
    for copy in copies:
        copy.start()
    return copies


def first_kernel(g, orb_hbm, proj_hbm, pot_hbm, blk_hbm, atom_hbm, v_ref, projf, pot, table, *scratch):
    orb, proj, sem, blk, atom, lut, entry_sem = scratch[:7]
    sums = scratch[7:]
    copies = [
        pltpu.make_async_copy(orb_hbm, orb, sem.at[0]),
        pltpu.make_async_copy(proj_hbm, proj, sem.at[1]),
        pltpu.make_async_copy(pot_hbm, pot, sem.at[2]),
    ]
    for copy in copies:
        copy.start()
    copies += entry_copies(blk_hbm, atom_hbm, blk, atom, entry_sem)
    dom = lax.axis_index("dom")
    fill_lut(g, dom, lut)
    clear(sums)
    copies[1].wait()
    projf[...] = proj[...].astype(F32)
    copies[0].wait()
    for r in range(g.rows):
        v_ref[r * g.no : (r + 1) * g.no, :] = orb[pl.ds(r, g.no, stride=g.rows), :]
    for copy in copies[2:]:
        copy.wait()
    inner_tables(g, dom, v_ref, projf, blk, atom, lut, sums, table)


def pack_kernel(g, v_ref, *refs):
    nx, ny = len(g.face_rows(0)), len(g.face_rows(1))
    dom = lax.axis_index("dom")
    if g.butterfly:
        part, from_x, from_y, from_xy = refs[:4]
        group = refs[-1]
        group[...] = (part[...] + from_x[...]) + (from_y[...] + from_xy[...])
        refs = refs[4:-1]
    first, second = refs[:2]
    pack_faces(g, dom, v_ref, refs[2 : 2 + nx], refs[2 + nx :])
    pack_ends(g, dom, v_ref, first, second)
    if g.butterfly:
        put_table(g, first, group)
        put_table(g, second, group)


def inside_kernel(g, scale, subtract, v_ref, pot, *refs):
    prev, out = refs if subtract else (None, refs[0])
    row, col = iota((g.cz, g.cz), 0), iota((g.cz, g.cz), 1)
    high, low = split2(weight_at(jnp.abs(row - col), scale))
    band = jnp.concatenate([high, low], axis=1)
    band = jnp.concatenate([band, band], axis=0)

    def cell(x, y):
        at = (x * g.cy + y) * g.no
        return v_ref[at : at + g.no, :]

    for x in range(g.cx):
        both = jnp.concatenate(split2(v_ref[x * g.slab : (x + 1) * g.slab, :]), axis=1)
        along = lax.dot_general(both, band, NN, preferred_element_type=F32)
        for y in range(g.cy):
            at = (x * g.cy + y) * g.no
            rows = slice(y * g.no, (y + 1) * g.no)
            here = cell(x, y)
            diag = jnp.broadcast_to(pot[x * g.cy + y : x * g.cy + y + 1, :], here.shape)
            total = along[rows, : g.cz] + along[rows, g.cz :]
            total = total + (scale * DIAGONAL + (scale / HALF_WIDTH) * diag) * here
            if subtract:
                total = total - prev[at : at + g.no, :]
            for k in range(1, RADIUS + 1):
                near = []
                for a, b in ((x - k, y), (x + k, y), (x, y - k), (x, y + k)):
                    if 0 <= a < g.cx and 0 <= b < g.cy:
                        near.append(cell(a, b))
                if near:
                    total = total + (scale * WEIGHT[k]) * sum(near[1:], near[0])
            out[at : at + g.no, :] = total


def flag(present):
    return 1.0 if present is None else jnp.where(present, 1.0, 0.0)


def add_ends(g, dom, scale, acc, low, high, out):
    inward, row = end_columns(g, dom)
    middle = (dom % g.third > 0) & (dom % g.third < g.third - 1)
    present = (row % 8 < RADIUS) & ((row < 8) | middle)
    coef = jnp.where(present, weight_at(inward + row % 8 + 1, scale), 0.0)
    c_high, c_low = split2(coef)
    coefs = jnp.concatenate([c_high, c_high, c_low, c_low], axis=0)
    for x in range(g.cx):
        rows = slice(x * g.slab, (x + 1) * g.slab)
        h_high, h_low = split2(jnp.concatenate([low[:, rows], high[:, rows]], axis=0))
        halo = jnp.concatenate([h_high, h_low, h_high, h_low], axis=0)
        out[rows, :] = acc[rows, :] + lax.dot_general(halo, coefs, TN, preferred_element_type=F32)


def add_x_faces(g, dom, scale, face_refs, out):
    unit = 2 * g.no
    for (side, present), face in zip(g.faces(dom, 0), face_refs):
        for y in range(0, g.cy, 2):
            starts = [j * g.slab + y * g.no for j in range(RADIUS)]
            part = [flag(present) * face[at : at + unit, :].astype(F32) for at in starts]
            for i in range(RADIUS):
                at = aligned(layer(side, g.cx, i) * g.slab + y * g.no, unit)
                total = out[pl.ds(at, unit), :]
                for j in range(RADIUS - i):
                    total = total + (scale * WEIGHT[i + j + 1]) * part[j]
                out[pl.ds(at, unit), :] = total


def add_y_faces(g, dom, scale, face_refs, out):
    size = RADIUS * g.no
    for (side, present), face in zip(g.faces(dom, 1), face_refs):
        for x in range(g.cx):
            part = flag(present) * face[x * size : (x + 1) * size, :].astype(F32)
            for i in range(RADIUS):
                at = aligned(x * g.slab + layer(side, g.cy, i) * g.no, g.no)
                total = out[pl.ds(at, g.no), :]
                for j in range(RADIUS - i):
                    total = total + (scale * WEIGHT[i + j + 1]) * part[j * g.no : (j + 1) * g.no]
                out[pl.ds(at, g.no), :] = total


def add_nonlocal(g, dom, scale, table, energy, projf, blk, atom, lut, spread, out):
    size = g.nproj * g.no
    lanes = g.table
    count = g.slots()
    rows = []
    for step in g.steps(dom):
        owner = pl.ds(jnp.clip(dom + step, 0, g.dom_count - 1), 1)
        rows.append(table[owner, :] * energy[owner, :])
    rows.append(jnp.zeros((8 - count, lanes), F32))
    scaled = (scale / HALF_WIDTH) * jnp.concatenate(rows, axis=0)
    high = scaled.astype(BF16)
    rest = scaled - high.astype(F32)
    mid = rest.astype(BF16)
    low = (rest - mid.astype(F32)).astype(BF16)
    parts = jnp.concatenate([high, mid, low], axis=0)
    wide = count * g.cz
    row, col = iota((24, wide), 0), iota((24, wide), 1)
    ones = jnp.where(row % 8 == col // g.cz, 1.0, 0.0).astype(BF16)
    out_all = lax.dot_general(parts, ones, TN, preferred_element_type=F32)
    for number in range(count):
        spread[number * lanes : (number + 1) * lanes, :] = out_all[:, number * g.cz : (number + 1) * g.cz]
    unroll = 4

    def step(i, _):
        additions = []
        for u in range(unroll):
            e = i * unroll + u
            col = column_of(g, lut, atom[e])
            total = None
            for p in range(g.nproj):
                at = pl.ds(pl.multiple_of(col * size + p * g.no, g.no), g.no)
                coef = jnp.broadcast_to(projf[e, p : p + 1, :], (g.no, g.cz))
                term = spread[at, :] * coef
                total = term if total is None else total + term
            additions.append((pl.ds(pl.multiple_of(blk[e] * g.no, g.no), g.no), total))
        for at, total in additions:
            out[at, :] += total
        return 0

    lax.fori_loop(0, g.ent // unroll, step, 0)


def nonlocal_kernel(g, scale, acc, projf, energy, blk_hbm, atom_hbm, first, second, *refs):
    out, table, blk, atom, lut, sem, spread = refs[-7:]
    copies = entry_copies(blk_hbm, atom_hbm, blk, atom, sem)
    dom = lax.axis_index("dom")
    fill_lut(g, dom, lut)
    if g.butterfly:
        group, opposite = refs[:2]
        table[...] = (group[...] + get_table(g, first)) + (get_table(g, second) + opposite[...])
    else:
        table[...] = refs[0][...]
    add_ends(g, dom, scale, acc, first, second, out)
    for copy in copies:
        copy.wait()
    add_nonlocal(g, dom, scale, table, energy, projf, blk, atom, lut, spread, out)


def middle_kernel(g, acc, projf, blk_hbm, atom_hbm, *refs):
    nx, ny = len(g.face_rows(0)), len(g.face_rows(1))
    faces = refs[: nx + ny]
    u_ref, table, blk, atom, lut, sem = refs[nx + ny : nx + ny + 6]
    sums = refs[nx + ny + 6 :]
    copies = entry_copies(blk_hbm, atom_hbm, blk, atom, sem)
    dom = lax.axis_index("dom")
    fill_lut(g, dom, lut)
    clear(sums)
    u_ref[...] = acc[...]
    add_x_faces(g, dom, 1.0, faces[:nx], u_ref)
    add_y_faces(g, dom, 1.0, faces[nx:], u_ref)
    for copy in copies:
        copy.wait()
    inner_tables(g, dom, u_ref, projf, blk, atom, lut, sums, table)


def last_kernel(g, acc, *refs):
    nx = len(g.face_rows(0))
    filtered, work = refs[-2:]
    dom = lax.axis_index("dom")
    work[...] = acc[...]
    add_x_faces(g, dom, 2.0, refs[:nx], work)
    add_y_faces(g, dom, 2.0, refs[nx:-2], work)
    filtered[...] = work[...].astype(BF16)


def rotate_kernel(g, own, other, panel, out):
    band = lax.axis_index("band")
    group = 16
    span = group * g.no
    norb = panel.shape[0]
    row, col = iota((span, norb), 0), iota((span, norb), 1)
    pick_out = jnp.where(col == band * g.no + row // group, 1.0, 0.0).astype(BF16)
    picked = lax.dot_general(pick_out, panel[...], NT, preferred_element_type=F32).astype(BF16)
    row, col = iota((norb, 2 * span), 0), iota((norb, 2 * span), 1)
    source = jnp.where(col < span, band, 1 - band) * g.no + col % g.no
    pick_in = jnp.where(row == source, 1.0, 0.0).astype(BF16)
    spread = lax.dot_general(picked, pick_in, NN, preferred_element_type=F32)
    row, col = iota((span, 2 * span), 0), iota((span, 2 * span), 1)
    same = row % group == (col % span) // g.no
    weights = jnp.where(same, spread, 0.0).astype(BF16)
    for n in range(g.rows // group):
        rows = slice(n * span, (n + 1) * span)
        both = jnp.concatenate([own[rows, :], other[rows, :]], axis=0)
        result = lax.dot_general(weights, both, NN, preferred_element_type=F32)
        for j in range(g.no):
            at = j * g.rows + n * group
            out[at : at + group, :] = result[j * group : (j + 1) * group, :]


def call(kernel, name, out_shape, scratch, args, specs):
    return pl.pallas_call(
        kernel,
        name=name,
        out_shape=out_shape,
        in_specs=specs,
        out_specs=jax.tree.map(lambda _: VMEM, out_shape),
        scratch_shapes=scratch,
        compiler_params=pltpu.CompilerParams(vmem_limit_bytes=48 * 1024 * 1024),
        cost_estimate=pl.CostEstimate(flops=1000, bytes_accessed=1000, transcendentals=0),
    )(*args)


def shift(g, array, stride, extent, step):
    pairs = []
    for i in range(g.dom_count):
        place = i // stride % extent
        pairs.append((i, i + ((place + step) % extent - place) * stride))
    return lax.ppermute(array, "dom", pairs)


def swap_faces(g, faces, stride, extent):
    if extent == 2:
        return [shift(g, faces[0], stride, extent, 1)]
    if extent > 2:
        return [shift(g, faces[1], stride, extent, 1), shift(g, faces[0], stride, extent, -1)]
    return []


def shards(orbitals, potential, projectors, entry_atom, entry_block, kb_energy, panel):
    g = Geometry(
        orbitals.shape, projectors.shape[0], projectors.shape[1], kb_energy.shape[0], lax.axis_size("dom")
    )

    def in_hbm(array):
        return pltpu.with_memory_space_constraint(array, pltpu.HBM)

    orb = in_hbm(orbitals.reshape(g.flat, g.cz))
    pot = in_hbm(potential.reshape(g.rows, g.cz))
    proj = in_hbm(projectors)
    blk, atom = in_hbm(entry_block), in_hbm(entry_atom)
    field = jax.ShapeDtypeStruct((g.flat, g.cz), F32)
    faces = [jax.ShapeDtypeStruct((n, g.cz), BF16) for n in g.face_rows(0) + g.face_rows(1)]
    nx = len(g.face_rows(0))
    ends = jax.ShapeDtypeStruct((8, g.flat), F32)
    table = jax.ShapeDtypeStruct((g.dom_count, g.table), F32)
    entries = [
        pltpu.SMEM((g.ent,), jnp.int32),
        pltpu.SMEM((g.ent,), jnp.int32),
        pltpu.SMEM((g.dom_count + 2 * g.plane,), jnp.int32),
        pltpu.SemaphoreType.DMA((2,)),
    ]
    slots = g.slots() * g.table
    sums = [pltpu.VMEM((slots, g.cz), F32) for _ in range(4)]
    spread = pltpu.VMEM((slots, g.cz), F32)
    energy = jnp.repeat(kb_energy.reshape(g.dom_count, g.owned * g.nproj), g.no, axis=1)
    indices = range(g.dom_count)

    def swap(array, *strides):
        pairs = [(i, i + sum(s * (1 - 2 * (i // s % 2)) for s in strides)) for i in indices]
        return lax.ppermute(array, "dom", pairs)

    def reverse(array):
        pairs = [(i, i - i % g.third + g.third - 1 - i % g.third) for i in indices]
        return lax.ppermute(array, "dom", pairs)

    def local_and_ends(scale, which, values, prev, part):
        inputs = [values]
        outputs = [ends, ends, *faces]
        if g.butterfly:
            inputs += [part, swap(part, g.plane), swap(part, g.third), swap(part, g.plane, g.third)]
            outputs.append(table)
        acc = call(
            functools.partial(inside_kernel, g, scale, len(prev) > 0),
            "inside_" + which,
            field,
            [],
            [values, pot, *prev],
            [VMEM] * (2 + len(prev)),
        )
        first, second, *sent = call(
            functools.partial(pack_kernel, g), "pack_" + which, outputs, [], inputs, [VMEM] * len(inputs)
        )
        from_x = swap_faces(g, sent[:nx], g.plane, g.first)
        from_y = swap_faces(g, sent[nx : len(faces)], g.third, g.second)
        first, second = swap(first, 1), reverse(second)
        tables = [sent[-1], swap(sent[-1], 2)] if g.butterfly else [lax.psum(part, "dom")]
        acc = call(
            functools.partial(nonlocal_kernel, g, scale),
            "nonlocal_" + which,
            field,
            [pltpu.VMEM(table.shape, F32), *entries, spread],
            [acc, projf, energy, blk, atom, first, second, *tables],
            [VMEM] * 3 + [HBM] * 2 + [VMEM] * (2 + len(tables)),
        )
        return acc, from_x + from_y

    v, projf, pot, part = call(
        functools.partial(first_kernel, g),
        "tables_first",
        [field, jax.ShapeDtypeStruct(proj.shape, F32), jax.ShapeDtypeStruct(pot.shape, F32), table],
        [
            pltpu.VMEM(orb.shape, F32),
            pltpu.VMEM(proj.shape, BF16),
            pltpu.SemaphoreType.DMA((3,)),
            *entries,
            *sums,
        ],
        [orb, proj, pot, blk, atom],
        [HBM] * 5,
    )
    acc, received = local_and_ends(1.0, "first", v, [], part)
    u, part = call(
        functools.partial(middle_kernel, g),
        "tables_second",
        [field, table],
        [*entries, *sums],
        [acc, projf, blk, atom, *received],
        [VMEM] * 2 + [HBM] * 2 + [VMEM] * len(received),
    )
    acc, received = local_and_ends(2.0, "second", u, [v], part)
    filtered = call(
        functools.partial(last_kernel, g),
        "filtered",
        jax.ShapeDtypeStruct((g.flat, g.cz), BF16),
        [pltpu.VMEM((g.flat, g.cz), F32)],
        [acc, *received],
        [VMEM] * (1 + len(received)),
    )
    other = lax.ppermute(filtered, "band", [(0, 1), (1, 0)])
    rotated = call(
        functools.partial(rotate_kernel, g), "rotate", field, [], [filtered, other, panel], [VMEM] * 3
    )
    return rotated.reshape(orbitals.shape)


def solution(mesh):
    in_specs = (
        P("dom", "band", None, None, None),
        P("dom", None, None, None),
        P("dom", None, None),
        P("dom"),
        P("dom"),
        P(),
        P(),
    )
    out_specs = P("dom", "band", None, None, None)
    return jax.shard_map(shards, mesh=mesh, in_specs=in_specs, out_specs=out_specs, check_vma=False)
```

```python
import functools

import jax
import jax.numpy as jnp
from jax import lax
from jax.experimental import pallas as pl
from jax.experimental.pallas import tpu as pltpu
from jax.sharding import PartitionSpec as P

RADIUS = 6
COEFFS = (
    -5369.0 / 1800.0,
    12.0 / 7.0,
    -15.0 / 56.0,
    10.0 / 189.0,
    -1.0 / 112.0,
    2.0 / 1925.0,
    -1.0 / 16632.0,
)
KINETIC = -3.125
CENTER = 36.0
HALF_WIDTH = 34.0
WEIGHT = [KINETIC * c / HALF_WIDTH for c in COEFFS]
DIAGONAL = (3.0 * KINETIC * COEFFS[0] - CENTER) / HALF_WIDTH

F32 = jnp.float32
BF16 = jnp.bfloat16
VMEM = pl.BlockSpec(memory_space=pltpu.VMEM)
HBM = pl.BlockSpec(memory_space=pltpu.HBM)
NT = (((1,), (1,)), ((), ()))
TN = (((0,), (0,)), ((), ()))
NN = (((1,), (0,)), ((), ()))


def split2(x):
    high = x.astype(BF16)
    low = (x - high.astype(F32)).astype(BF16)
    return high, low


def iota(shape, dim):
    return lax.broadcasted_iota(jnp.int32, shape, dim)


def weight_at(distance, scale):
    out = jnp.zeros(distance.shape, F32)
    for k in range(1, RADIUS + 1):
        out = jnp.where(distance == k, scale * WEIGHT[k], out)
    return out


class Geometry:
    def __init__(self, orbitals, entries, nproj, atoms, dom_count):
        _, self.no, self.cx, self.cy, self.cz = orbitals
        self.rows = self.cx * self.cy
        self.flat = self.rows * self.no
        self.ent = entries
        self.nproj = nproj
        self.dom_count = dom_count
        self.owned = atoms // dom_count
        self.third = 4
        self.second = min(8, dom_count // 8)
        self.plane = self.second * self.third
        self.first = dom_count // self.plane
        self.table = self.owned * nproj * self.no
        self.slab = self.cy * self.no
        self.fold = self.flat // self.table
        self.butterfly = self.first == 2 and self.second == 2 and dom_count <= 2 * self.fold
        assert self.no == 8

    def faces(self, dom, dim):
        if dim == 0:
            extent, place = self.first, dom // self.plane
        else:
            extent, place = self.second, dom // self.third % self.second
        if extent == 2:
            return [(1 - place, None)]
        if extent > 2:
            return [(0, place > 0), (1, place < extent - 1)]
        return []

    def face_rows(self, dim):
        rows = RADIUS * self.slab if dim == 0 else self.cx * RADIUS * self.no
        return [rows] * len(self.faces(0, dim))

    def steps(self, dom):
        out = [0]
        for extent, stride in ((self.first, self.plane), (self.second, self.third), (self.third, 1)):
            if extent == 2:
                out.append((1 - 2 * (dom // stride % 2)) * stride)
            elif extent > 2:
                out.extend([stride, -stride])
        return out

    def slots(self):
        return len(self.steps(0))


def layer(side, length, j):
    if isinstance(side, int):
        return length - 1 - j if side else j
    return side * (length - 1 - j) + (1 - side) * j


def aligned(start, unit):
    return start if isinstance(start, int) else pl.multiple_of(start, unit)


def pack_faces(g, dom, v_ref, x_refs, y_refs):
    for (side, _), out in zip(g.faces(dom, 0), x_refs):
        for j in range(RADIUS):
            at = aligned(layer(side, g.cx, j) * g.slab, g.slab)
            out[j * g.slab : (j + 1) * g.slab, :] = v_ref[pl.ds(at, g.slab), :].astype(BF16)
    size = RADIUS * g.no
    for (side, _), out in zip(g.faces(dom, 1), y_refs):
        for x in range(g.cx):
            pieces = []
            for j in range(RADIUS):
                at = aligned(x * g.slab + layer(side, g.cy, j) * g.no, g.no)
                pieces.append(v_ref[pl.ds(at, g.no), :])
            out[x * size : (x + 1) * size, :] = jnp.concatenate(pieces, axis=0).astype(BF16)


def end_columns(g, dom):
    row, col = iota((16, g.cz), 0), iota((16, g.cz), 1)
    odd = dom % 2
    side = jnp.where(row < 8, 1 - odd, odd)
    return jnp.where(side == 1, g.cz - 1 - col, col), row


def pack_ends(g, dom, v_ref, first_ref, second_ref):
    inward, row = end_columns(g, dom)
    pick = jnp.where((inward == row % 8) & (row % 8 < RADIUS), 1.0, 0.0).astype(BF16)
    pick = jnp.concatenate([pick, pick], axis=1)
    for x in range(g.cx):
        rows = slice(x * g.slab, (x + 1) * g.slab)
        both = jnp.concatenate(split2(v_ref[rows, :]), axis=1)
        ends = lax.dot_general(pick, both, NT, preferred_element_type=F32)
        first_ref[:, rows] = ends[:8]
        second_ref[:, rows] = ends[8:]


def put_table(g, message, table):
    for n in range(g.dom_count):
        at = RADIUS + n // g.fold
        lanes = n % g.fold * g.table
        message[at : at + 1, lanes : lanes + g.table] = table[n : n + 1, :]


def get_table(g, message):
    rows = []
    for n in range(g.dom_count):
        at = RADIUS + n // g.fold
        lanes = n % g.fold * g.table
        rows.append(message[at : at + 1, lanes : lanes + g.table])
    return jnp.concatenate(rows, axis=0)


def fill_lut(g, dom, lut):
    for number, step in enumerate(g.steps(dom)):
        lut[g.plane + dom + step] = number * g.owned


def column_of(g, lut, atom):
    if g.owned & (g.owned - 1):
        owner = lax.div(atom, jnp.int32(g.owned))
        return lut[owner + g.plane] + (atom - owner * g.owned)
    owner = lax.shift_right_logical(atom, jnp.int32(g.owned.bit_length() - 1))
    return lut[owner + g.plane] + (atom & (g.owned - 1))


def inner_tables(g, dom, v_ref, projf, blk, atom, lut, sums, table):
    size = g.nproj * g.no

    unroll = 16

    def step(i, _):
        for u in range(unroll):
            part = sums[u % len(sums)]
            e = i * unroll + u
            col = column_of(g, lut, atom[e])
            v = v_ref[pl.ds(pl.multiple_of(blk[e] * g.no, g.no), g.no), :]
            for p in range(g.nproj):
                at = pl.ds(pl.multiple_of(col * size + p * g.no, g.no), g.no)
                coef = jnp.broadcast_to(projf[e, p : p + 1, :], v.shape)
                part[at, :] += v * coef
        return 0

    lax.fori_loop(0, g.ent // unroll, step, 0)
    total = sums[0][...]
    for part in sums[1:]:
        total = total + part[...]
    both = jnp.concatenate(split2(total), axis=1)
    ones = jnp.ones((8, both.shape[1]), BF16)
    summed = lax.dot_general(ones, both, NT, preferred_element_type=F32)
    table[...] = jnp.zeros(table.shape, F32)
    for number, step in enumerate(g.steps(dom)):
        owner = jnp.clip(dom + step, 0, g.dom_count - 1)
        table[pl.ds(owner, 1), :] += summed[0:1, number * g.table : (number + 1) * g.table]


def clear(sums):
    for part in sums:
        part[...] = jnp.zeros(part.shape, F32)


def entry_copies(blk_hbm, atom_hbm, blk, atom, sem):
    copies = [
        pltpu.make_async_copy(blk_hbm, blk, sem.at[0]),
        pltpu.make_async_copy(atom_hbm, atom, sem.at[1]),
    ]
    for copy in copies:
        copy.start()
    return copies


def first_kernel(g, orb_hbm, proj_hbm, pot_hbm, blk_hbm, atom_hbm, v_ref, projf, pot, table, *scratch):
    orb, proj, sem, blk, atom, lut, entry_sem = scratch[:7]
    sums = scratch[7:]
    copies = [
        pltpu.make_async_copy(orb_hbm, orb, sem.at[0]),
        pltpu.make_async_copy(proj_hbm, proj, sem.at[1]),
        pltpu.make_async_copy(pot_hbm, pot, sem.at[2]),
    ]
    for copy in copies:
        copy.start()
    copies += entry_copies(blk_hbm, atom_hbm, blk, atom, entry_sem)
    dom = lax.axis_index("dom")
    fill_lut(g, dom, lut)
    clear(sums)
    copies[1].wait()
    projf[...] = proj[...].astype(F32)
    copies[0].wait()
    for r in range(g.rows):
        v_ref[r * g.no : (r + 1) * g.no, :] = orb[pl.ds(r, g.no, stride=g.rows), :]
    for copy in copies[2:]:
        copy.wait()
    inner_tables(g, dom, v_ref, projf, blk, atom, lut, sums, table)


def pack_kernel(g, v_ref, after, *refs):
    nx, ny = len(g.face_rows(0)), len(g.face_rows(1))
    dom = lax.axis_index("dom")
    if g.butterfly:
        tables, group = refs[0], refs[-1]
        group[...] = (tables[0] + tables[1]) + (tables[2] + tables[3])
        refs = refs[1:-1]
    first, second = refs[:2]
    pack_faces(g, dom, v_ref, refs[2 : 2 + nx], refs[2 + nx :])
    pack_ends(g, dom, v_ref, first, second)
    if g.butterfly:
        put_table(g, first, group)
        put_table(g, second, group)


def inside_kernel(g, scale, subtract, v_ref, pot, *refs):
    prev, out = refs if subtract else (None, refs[0])
    row, col = iota((g.cz, g.cz), 0), iota((g.cz, g.cz), 1)
    high, low = split2(weight_at(jnp.abs(row - col), scale))
    band = jnp.concatenate([high, low], axis=1)
    band = jnp.concatenate([band, band], axis=0)

    def cell(x, y):
        at = (x * g.cy + y) * g.no
        return v_ref[at : at + g.no, :]

    for x in range(g.cx):
        both = jnp.concatenate(split2(v_ref[x * g.slab : (x + 1) * g.slab, :]), axis=1)
        along = lax.dot_general(both, band, NN, preferred_element_type=F32)
        for y in range(g.cy):
            at = (x * g.cy + y) * g.no
            rows = slice(y * g.no, (y + 1) * g.no)
            here = cell(x, y)
            diag = jnp.broadcast_to(pot[x * g.cy + y : x * g.cy + y + 1, :], here.shape)
            total = along[rows, : g.cz] + along[rows, g.cz :]
            total = total + (scale * DIAGONAL + (scale / HALF_WIDTH) * diag) * here
            if subtract:
                total = total - prev[at : at + g.no, :]
            for k in range(1, RADIUS + 1):
                near = []
                for a, b in ((x - k, y), (x + k, y), (x, y - k), (x, y + k)):
                    if 0 <= a < g.cx and 0 <= b < g.cy:
                        near.append(cell(a, b))
                if near:
                    total = total + (scale * WEIGHT[k]) * sum(near[1:], near[0])
            out[at : at + g.no, :] = total


def flag(present):
    return 1.0 if present is None else jnp.where(present, 1.0, 0.0)


def add_ends(g, dom, scale, acc, low, high, out):
    inward, row = end_columns(g, dom)
    middle = (dom % g.third > 0) & (dom % g.third < g.third - 1)
    present = (row % 8 < RADIUS) & ((row < 8) | middle)
    coef = jnp.where(present, weight_at(inward + row % 8 + 1, scale), 0.0)
    c_high, c_low = split2(coef)
    coefs = jnp.concatenate([c_high, c_high, c_low, c_low], axis=0)
    for x in range(g.cx):
        rows = slice(x * g.slab, (x + 1) * g.slab)
        h_high, h_low = split2(jnp.concatenate([low[:, rows], high[:, rows]], axis=0))
        halo = jnp.concatenate([h_high, h_low, h_high, h_low], axis=0)
        out[rows, :] = acc[rows, :] + lax.dot_general(halo, coefs, TN, preferred_element_type=F32)


def add_x_faces(g, dom, scale, face_refs, out):
    unit = 2 * g.no
    for (side, present), face in zip(g.faces(dom, 0), face_refs):
        for y in range(0, g.cy, 2):
            starts = [j * g.slab + y * g.no for j in range(RADIUS)]
            part = [flag(present) * face[at : at + unit, :].astype(F32) for at in starts]
            for i in range(RADIUS):
                at = aligned(layer(side, g.cx, i) * g.slab + y * g.no, unit)
                total = out[pl.ds(at, unit), :]
                for j in range(RADIUS - i):
                    total = total + (scale * WEIGHT[i + j + 1]) * part[j]
                out[pl.ds(at, unit), :] = total


def add_y_faces(g, dom, scale, face_refs, out):
    size = RADIUS * g.no
    for (side, present), face in zip(g.faces(dom, 1), face_refs):
        for x in range(g.cx):
            part = flag(present) * face[x * size : (x + 1) * size, :].astype(F32)
            for i in range(RADIUS):
                at = aligned(x * g.slab + layer(side, g.cy, i) * g.no, g.no)
                total = out[pl.ds(at, g.no), :]
                for j in range(RADIUS - i):
                    total = total + (scale * WEIGHT[i + j + 1]) * part[j * g.no : (j + 1) * g.no]
                out[pl.ds(at, g.no), :] = total


def add_nonlocal(g, dom, scale, table, energy, projf, blk, atom, lut, spread, out):
    size = g.nproj * g.no
    lanes = g.table
    count = g.slots()
    rows = []
    for step in g.steps(dom):
        owner = pl.ds(jnp.clip(dom + step, 0, g.dom_count - 1), 1)
        rows.append(table[owner, :] * energy[owner, :])
    rows.append(jnp.zeros((8 - count, lanes), F32))
    scaled = (scale / HALF_WIDTH) * jnp.concatenate(rows, axis=0)
    high = scaled.astype(BF16)
    rest = scaled - high.astype(F32)
    mid = rest.astype(BF16)
    low = (rest - mid.astype(F32)).astype(BF16)
    parts = jnp.concatenate([high, mid, low], axis=0)
    wide = count * g.cz
    row, col = iota((24, wide), 0), iota((24, wide), 1)
    ones = jnp.where(row % 8 == col // g.cz, 1.0, 0.0).astype(BF16)
    out_all = lax.dot_general(parts, ones, TN, preferred_element_type=F32)
    for number in range(count):
        spread[number * lanes : (number + 1) * lanes, :] = out_all[:, number * g.cz : (number + 1) * g.cz]
    unroll = 16

    def step(i, _):
        additions = []
        for u in range(unroll):
            e = i * unroll + u
            col = column_of(g, lut, atom[e])
            total = None
            for p in range(g.nproj):
                at = pl.ds(pl.multiple_of(col * size + p * g.no, g.no), g.no)
                coef = jnp.broadcast_to(projf[e, p : p + 1, :], (g.no, g.cz))
                term = spread[at, :] * coef
                total = term if total is None else total + term
            additions.append((pl.ds(pl.multiple_of(blk[e] * g.no, g.no), g.no), total))
        for at, total in additions:
            out[at, :] += total
        return 0

    lax.fori_loop(0, g.ent // unroll, step, 0)


def nonlocal_kernel(g, scale, acc, projf, energy, blk_hbm, atom_hbm, first, second, *refs):
    out, table, blk, atom, lut, sem, spread = refs[-7:]
    copies = entry_copies(blk_hbm, atom_hbm, blk, atom, sem)
    dom = lax.axis_index("dom")
    fill_lut(g, dom, lut)
    if g.butterfly:
        group, opposite = refs[:2]
        table[...] = (group[...] + get_table(g, first)) + (get_table(g, second) + opposite[...])
    else:
        table[...] = refs[0][...]
    add_ends(g, dom, scale, acc, first, second, out)
    for copy in copies:
        copy.wait()
    add_nonlocal(g, dom, scale, table, energy, projf, blk, atom, lut, spread, out)


def middle_kernel(g, acc, projf, blk_hbm, atom_hbm, *refs):
    nx, ny = len(g.face_rows(0)), len(g.face_rows(1))
    faces = refs[: nx + ny]
    u_ref, table, blk, atom, lut, sem = refs[nx + ny : nx + ny + 6]
    sums = refs[nx + ny + 6 :]
    copies = entry_copies(blk_hbm, atom_hbm, blk, atom, sem)
    dom = lax.axis_index("dom")
    fill_lut(g, dom, lut)
    clear(sums)
    u_ref[...] = acc[...]
    add_x_faces(g, dom, 1.0, faces[:nx], u_ref)
    add_y_faces(g, dom, 1.0, faces[nx:], u_ref)
    for copy in copies:
        copy.wait()
    inner_tables(g, dom, u_ref, projf, blk, atom, lut, sums, table)


def halves(g, dom):
    if g.first != 2 or g.cx != 2 * RADIUS:
        return [(0, g.cx)]
    side = 1 - dom // g.plane
    return [((1 - side) * RADIUS, RADIUS), (side * RADIUS, RADIUS)]


def last_kernel(g, number, acc, *refs):
    nx = len(g.face_rows(0))
    filtered, work = refs[-2:]
    refs = refs[:-2]
    dom = lax.axis_index("dom")
    parts = halves(g, dom)
    start, count = parts[number]
    work[...] = acc[...]
    if number == len(parts) - 1:
        add_x_faces(g, dom, 2.0, refs[:nx], work)
        refs = refs[nx:]
    add_y_faces(g, dom, 2.0, refs, work)
    at = aligned(start * g.slab, g.slab)
    filtered[...] = work[pl.ds(at, count * g.slab), :].astype(BF16)


def rotate_kernel(g, number, own, other, panel, *refs):
    out_hbm, out, sem = refs[-3:]
    start, count = halves(g, lax.axis_index("dom"))[number]
    band = lax.axis_index("band")
    group = 16
    span = group * g.no
    norb = panel.shape[0]
    row, col = iota((span, norb), 0), iota((span, norb), 1)
    pick_out = jnp.where(col == band * g.no + row // group, 1.0, 0.0).astype(BF16)
    picked = lax.dot_general(pick_out, panel[...], NT, preferred_element_type=F32).astype(BF16)
    row, col = iota((norb, 2 * span), 0), iota((norb, 2 * span), 1)
    source = jnp.where(col < span, band, 1 - band) * g.no + col % g.no
    pick_in = jnp.where(row == source, 1.0, 0.0).astype(BF16)
    spread = lax.dot_general(picked, pick_in, NN, preferred_element_type=F32)
    row, col = iota((span, 2 * span), 0), iota((span, 2 * span), 1)
    same = row % group == (col % span) // g.no
    weights = jnp.where(same, spread, 0.0).astype(BF16)
    size = count * g.cy
    for n in range(size // group):
        rows = slice(n * span, (n + 1) * span)
        both = jnp.concatenate([own[rows, :], other[rows, :]], axis=0)
        result = lax.dot_general(weights, both, NN, preferred_element_type=F32)
        for j in range(g.no):
            out[j, n * group : (n + 1) * group, :] = result[j * group : (j + 1) * group, :]
    copies = []
    for j in range(g.no):
        at = aligned(j * g.rows + start * g.cy, group)
        copies.append(pltpu.make_async_copy(out.at[j], out_hbm.at[pl.ds(at, size), :], sem.at[j]))
        copies[-1].start()
    for copy in copies:
        copy.wait()


def call(kernel, name, out_shape, scratch, args, specs, **options):
    return pl.pallas_call(
        kernel,
        name=name,
        out_shape=out_shape,
        in_specs=specs,
        out_specs=options.pop("out_specs", jax.tree.map(lambda _: VMEM, out_shape)),
        scratch_shapes=scratch,
        compiler_params=pltpu.CompilerParams(vmem_limit_bytes=48 * 1024 * 1024),
        cost_estimate=pl.CostEstimate(flops=1000, bytes_accessed=1000, transcendentals=0),
        **options,
    )(*args)


def shift(g, array, stride, extent, step):
    pairs = []
    for i in range(g.dom_count):
        place = i // stride % extent
        pairs.append((i, i + ((place + step) % extent - place) * stride))
    return lax.ppermute(array, "dom", pairs)


def swap_faces(g, faces, stride, extent):
    if extent == 2:
        return [shift(g, faces[0], stride, extent, 1)]
    if extent > 2:
        return [shift(g, faces[1], stride, extent, 1), shift(g, faces[0], stride, extent, -1)]
    return []


def shards(orbitals, potential, projectors, entry_atom, entry_block, kb_energy, panel):
    g = Geometry(
        orbitals.shape, projectors.shape[0], projectors.shape[1], kb_energy.shape[0], lax.axis_size("dom")
    )

    def in_hbm(array):
        return pltpu.with_memory_space_constraint(array, pltpu.HBM)

    orb = in_hbm(orbitals.reshape(g.flat, g.cz))
    pot = in_hbm(potential.reshape(g.rows, g.cz))
    proj = in_hbm(projectors)
    blk, atom = in_hbm(entry_block), in_hbm(entry_atom)
    field = jax.ShapeDtypeStruct((g.flat, g.cz), F32)
    faces = [jax.ShapeDtypeStruct((n, g.cz), BF16) for n in g.face_rows(0) + g.face_rows(1)]
    nx = len(g.face_rows(0))
    ends = jax.ShapeDtypeStruct((8, g.flat), F32)
    table = jax.ShapeDtypeStruct((g.dom_count, g.table), F32)
    entries = [
        pltpu.SMEM((g.ent,), jnp.int32),
        pltpu.SMEM((g.ent,), jnp.int32),
        pltpu.SMEM((g.dom_count + 2 * g.plane,), jnp.int32),
        pltpu.SemaphoreType.DMA((2,)),
    ]
    slots = g.slots() * g.table
    sums = [pltpu.VMEM((slots, g.cz), F32) for _ in range(4)]
    spread = pltpu.VMEM((slots, g.cz), F32)
    energy = jnp.repeat(kb_energy.reshape(g.dom_count, g.owned * g.nproj), g.no, axis=1)
    indices = range(g.dom_count)

    def swap(array, *strides):
        pairs = [(i, i + sum(s * (1 - 2 * (i // s % 2)) for s in strides)) for i in indices]
        return lax.ppermute(array, "dom", pairs)

    def reverse(array):
        pairs = [(i, i - i % g.third + g.third - 1 - i % g.third) for i in indices]
        return lax.ppermute(array, "dom", pairs)

    def local_and_ends(scale, which, values, prev, part):
        inputs = [values, energy]
        outputs = [ends, ends, *faces]
        if g.butterfly:
            groups = [[i + j * g.third for j in range(4)] for i in range(g.third)]
            inputs.append(lax.all_gather(part, "dom", axis_index_groups=groups))
            outputs.append(table)
        acc = call(
            functools.partial(inside_kernel, g, scale, len(prev) > 0),
            "inside_" + which,
            field,
            [],
            [values, pot, *prev],
            [VMEM] * (2 + len(prev)),
        )
        first, second, *sent = call(
            functools.partial(pack_kernel, g), "pack_" + which, outputs, [], inputs, [VMEM] * len(inputs)
        )
        from_x = swap_faces(g, sent[:nx], g.plane, g.first)
        from_y = swap_faces(g, sent[nx : len(faces)], g.third, g.second)
        first, second = swap(first, 1), reverse(second)
        tables = [sent[-1], swap(sent[-1], 2)] if g.butterfly else [lax.psum(part, "dom")]
        acc = call(
            functools.partial(nonlocal_kernel, g, scale),
            "nonlocal_" + which,
            field,
            [pltpu.VMEM(table.shape, F32), *entries, spread],
            [acc, projf, energy, blk, atom, first, second, *tables],
            [VMEM] * 3 + [HBM] * 2 + [VMEM] * (2 + len(tables)),
        )
        return acc, from_x + from_y

    v, projf, pot, part = call(
        functools.partial(first_kernel, g),
        "tables_first",
        [field, jax.ShapeDtypeStruct(proj.shape, F32), jax.ShapeDtypeStruct(pot.shape, F32), table],
        [
            pltpu.VMEM(orb.shape, F32),
            pltpu.VMEM(proj.shape, BF16),
            pltpu.SemaphoreType.DMA((3,)),
            *entries,
            *sums,
        ],
        [orb, proj, pot, blk, atom],
        [HBM] * 5,
    )
    acc, received = local_and_ends(1.0, "first", v, [], part)
    u, part = call(
        functools.partial(middle_kernel, g),
        "tables_second",
        [field, table],
        [*entries, *sums],
        [acc, projf, blk, atom, *received],
        [VMEM] * 2 + [HBM] * 2 + [VMEM] * len(received),
    )
    acc, received = local_and_ends(2.0, "second", u, [v], part)
    rotated = None
    pieces = []
    parts = halves(g, 0)
    for number, (_, count) in enumerate(parts):
        inputs = [acc, *received[nx:]] if number < len(parts) - 1 else [acc, *received]
        filtered = call(
            functools.partial(last_kernel, g, number),
            "filtered_%d" % number,
            jax.ShapeDtypeStruct((count * g.slab, g.cz), BF16),
            [pltpu.VMEM((g.flat, g.cz), F32)],
            inputs,
            [VMEM] * len(inputs),
        )
        pieces.append((filtered, lax.ppermute(filtered, "band", [(0, 1), (1, 0)]), count))
    for number, (filtered, other, count) in enumerate(pieces):
        inputs = [filtered, other, panel] + ([] if rotated is None else [rotated])
        rotated = call(
            functools.partial(rotate_kernel, g, number),
            "rotate_%d" % number,
            field,
            [pltpu.VMEM((g.no, count * g.cy, g.cz), F32), pltpu.SemaphoreType.DMA((g.no,))],
            inputs,
            [VMEM] * 3 + [HBM] * (len(inputs) - 3),
            out_specs=HBM,
            input_output_aliases={} if rotated is None else {3: 0},
        )
    return rotated.reshape(orbitals.shape)


def solution(mesh):
    in_specs = (
        P("dom", "band", None, None, None),
        P("dom", None, None, None),
        P("dom", None, None),
        P("dom"),
        P("dom"),
        P(),
        P(),
    )
    out_specs = P("dom", "band", None, None, None)
    return jax.shard_map(shards, mesh=mesh, in_specs=in_specs, out_specs=out_specs, check_vma=False)
```

```python
import functools

import jax
import jax.numpy as jnp
from jax import lax
from jax.experimental import pallas as pl
from jax.experimental.pallas import tpu as pltpu
from jax.sharding import PartitionSpec as P

RADIUS = 6
COEFFS = (
    -5369.0 / 1800.0,
    12.0 / 7.0,
    -15.0 / 56.0,
    10.0 / 189.0,
    -1.0 / 112.0,
    2.0 / 1925.0,
    -1.0 / 16632.0,
)
KINETIC = -3.125
CENTER = 36.0
HALF_WIDTH = 34.0
WEIGHT = [KINETIC * c / HALF_WIDTH for c in COEFFS]
DIAGONAL = (3.0 * KINETIC * COEFFS[0] - CENTER) / HALF_WIDTH

F32 = jnp.float32
BF16 = jnp.bfloat16
VMEM = pl.BlockSpec(memory_space=pltpu.VMEM)
HBM = pl.BlockSpec(memory_space=pltpu.HBM)
NT = (((1,), (1,)), ((), ()))
TN = (((0,), (0,)), ((), ()))
NN = (((1,), (0,)), ((), ()))


def split2(x):
    high = x.astype(BF16)
    low = (x - high.astype(F32)).astype(BF16)
    return high, low


def iota(shape, dim):
    return lax.broadcasted_iota(jnp.int32, shape, dim)


def weight_at(distance, scale):
    out = jnp.zeros(distance.shape, F32)
    for k in range(1, RADIUS + 1):
        out = jnp.where(distance == k, scale * WEIGHT[k], out)
    return out


class Geometry:
    def __init__(self, orbitals, entries, nproj, atoms, dom_count):
        _, self.no, self.cx, self.cy, self.cz = orbitals
        self.rows = self.cx * self.cy
        self.flat = self.rows * self.no
        self.ent = entries
        self.nproj = nproj
        self.dom_count = dom_count
        self.owned = atoms // dom_count
        self.third = 4
        self.second = min(8, dom_count // 8)
        self.plane = self.second * self.third
        self.first = dom_count // self.plane
        self.table = self.owned * nproj * self.no
        self.slab = self.cy * self.no
        self.fold = self.flat // self.table
        self.butterfly = self.first == 2 and self.second == 2 and dom_count <= 2 * self.fold
        assert self.no == 8

    def faces(self, dom, dim):
        if dim == 0:
            extent, place = self.first, dom // self.plane
        else:
            extent, place = self.second, dom // self.third % self.second
        if extent == 2:
            return [(1 - place, None)]
        if extent > 2:
            return [(0, place > 0), (1, place < extent - 1)]
        return []

    def face_rows(self, dim):
        rows = RADIUS * self.slab if dim == 0 else self.cx * RADIUS * self.no
        return [rows] * len(self.faces(0, dim))

    def steps(self, dom):
        out = [0]
        for extent, stride in ((self.first, self.plane), (self.second, self.third), (self.third, 1)):
            if extent == 2:
                out.append((1 - 2 * (dom // stride % 2)) * stride)
            elif extent > 2:
                out.extend([stride, -stride])
        return out

    def slots(self):
        return len(self.steps(0))


def layer(side, length, j):
    if isinstance(side, int):
        return length - 1 - j if side else j
    return side * (length - 1 - j) + (1 - side) * j


def aligned(start, unit):
    return start if isinstance(start, int) else pl.multiple_of(start, unit)


def pack_x(g, dom, v_ref, refs):
    for (side, _), out in zip(g.faces(dom, 0), refs):
        for j in range(RADIUS):
            at = aligned(layer(side, g.cx, j) * g.slab, g.slab)
            out[j * g.slab : (j + 1) * g.slab, :] = v_ref[pl.ds(at, g.slab), :].astype(BF16)


def pack_y(g, dom, v_ref, refs):
    size = RADIUS * g.no
    for (side, _), out in zip(g.faces(dom, 1), refs):
        for x in range(g.cx):
            pieces = []
            for j in range(RADIUS):
                at = aligned(x * g.slab + layer(side, g.cy, j) * g.no, g.no)
                pieces.append(v_ref[pl.ds(at, g.no), :])
            out[x * size : (x + 1) * size, :] = jnp.concatenate(pieces, axis=0).astype(BF16)


def end_columns(g, dom):
    row, col = iota((16, g.cz), 0), iota((16, g.cz), 1)
    odd = dom % 2
    side = jnp.where(row < 8, 1 - odd, odd)
    return jnp.where(side == 1, g.cz - 1 - col, col), row


def pack_ends(g, dom, v_ref, first_ref, second_ref):
    inward, row = end_columns(g, dom)
    pick = jnp.where((inward == row % 8) & (row % 8 < RADIUS), 1.0, 0.0).astype(BF16)
    pick = jnp.concatenate([pick, pick], axis=1)
    for x in range(g.cx):
        rows = slice(x * g.slab, (x + 1) * g.slab)
        both = jnp.concatenate(split2(v_ref[rows, :]), axis=1)
        ends = lax.dot_general(pick, both, NT, preferred_element_type=F32)
        first_ref[:, rows] = ends[:8]
        second_ref[:, rows] = ends[8:]


def put_table(g, message, table):
    for n in range(g.dom_count):
        at = RADIUS + n // g.fold
        lanes = n % g.fold * g.table
        message[at : at + 1, lanes : lanes + g.table] = table[n : n + 1, :]


def get_table(g, message):
    rows = []
    for n in range(g.dom_count):
        at = RADIUS + n // g.fold
        lanes = n % g.fold * g.table
        rows.append(message[at : at + 1, lanes : lanes + g.table])
    return jnp.concatenate(rows, axis=0)


def fill_lut(g, dom, lut):
    for number, step in enumerate(g.steps(dom)):
        lut[g.plane + dom + step] = number * g.owned


def column_of(g, lut, atom):
    if g.owned & (g.owned - 1):
        owner = lax.div(atom, jnp.int32(g.owned))
        return lut[owner + g.plane] + (atom - owner * g.owned)
    owner = lax.shift_right_logical(atom, jnp.int32(g.owned.bit_length() - 1))
    return lut[owner + g.plane] + (atom & (g.owned - 1))


def inner_tables(g, dom, v_ref, projf, blk, atom, lut, sums, table):
    size = g.nproj * g.no

    unroll = 16

    def step(i, _):
        for u in range(unroll):
            part = sums[u % len(sums)]
            e = i * unroll + u
            col = column_of(g, lut, atom[e])
            v = v_ref[pl.ds(pl.multiple_of(blk[e] * g.no, g.no), g.no), :]
            for p in range(g.nproj):
                at = pl.ds(pl.multiple_of(col * size + p * g.no, g.no), g.no)
                coef = jnp.broadcast_to(projf[e, p : p + 1, :], v.shape)
                part[at, :] += v * coef
        return 0

    lax.fori_loop(0, g.ent // unroll, step, 0)
    total = sums[0][...]
    for part in sums[1:]:
        total = total + part[...]
    both = jnp.concatenate(split2(total), axis=1)
    ones = jnp.ones((8, both.shape[1]), BF16)
    summed = lax.dot_general(ones, both, NT, preferred_element_type=F32)
    table[...] = jnp.zeros(table.shape, F32)
    for number, step in enumerate(g.steps(dom)):
        owner = jnp.clip(dom + step, 0, g.dom_count - 1)
        table[pl.ds(owner, 1), :] += summed[0:1, number * g.table : (number + 1) * g.table]


def clear(sums):
    for part in sums:
        part[...] = jnp.zeros(part.shape, F32)


def entry_copies(blk_hbm, atom_hbm, blk, atom, sem):
    copies = [
        pltpu.make_async_copy(blk_hbm, blk, sem.at[0]),
        pltpu.make_async_copy(atom_hbm, atom, sem.at[1]),
    ]
    for copy in copies:
        copy.start()
    return copies


def first_kernel(g, orb_hbm, proj_hbm, pot_hbm, blk_hbm, atom_hbm, v_ref, projf, pot, table, *scratch):
    orb, proj, sem, blk, atom, lut, entry_sem = scratch[:7]
    sums = scratch[7:]
    copies = [
        pltpu.make_async_copy(orb_hbm, orb, sem.at[0]),
        pltpu.make_async_copy(proj_hbm, proj, sem.at[1]),
        pltpu.make_async_copy(pot_hbm, pot, sem.at[2]),
    ]
    for copy in copies:
        copy.start()
    copies += entry_copies(blk_hbm, atom_hbm, blk, atom, entry_sem)
    dom = lax.axis_index("dom")
    fill_lut(g, dom, lut)
    clear(sums)
    copies[1].wait()
    projf[...] = proj[...].astype(F32)
    copies[0].wait()
    for r in range(g.rows):
        v_ref[r * g.no : (r + 1) * g.no, :] = orb[pl.ds(r, g.no, stride=g.rows), :]
    for copy in copies[2:]:
        copy.wait()
    inner_tables(g, dom, v_ref, projf, blk, atom, lut, sums, table)


def pack_kernel(g, v_ref, energy, inside, *refs):
    nx = len(g.face_rows(0))
    dom = lax.axis_index("dom")
    if g.butterfly:
        part, from_x, from_y, from_xy = refs[:4]
        group = refs[-1]
        group[...] = (part[...] + from_x[...]) + (from_y[...] + from_xy[...])
        refs = refs[4:-1]
    first, second = refs[:2]
    pack_x(g, dom, v_ref, refs[2 : 2 + nx])
    pack_y(g, dom, v_ref, refs[2 + nx :])
    pack_ends(g, dom, v_ref, first, second)
    if g.butterfly:
        put_table(g, first, group)
        put_table(g, second, group)


def inside_kernel(g, scale, subtract, v_ref, pot, *refs):
    prev, out = refs if subtract else (None, refs[0])
    row, col = iota((g.cz, g.cz), 0), iota((g.cz, g.cz), 1)
    high, low = split2(weight_at(jnp.abs(row - col), scale))
    band = jnp.concatenate([high, low], axis=1)
    band = jnp.concatenate([band, band], axis=0)

    def cell(x, y):
        at = (x * g.cy + y) * g.no
        return v_ref[at : at + g.no, :]

    for x in range(g.cx):
        both = jnp.concatenate(split2(v_ref[x * g.slab : (x + 1) * g.slab, :]), axis=1)
        along = lax.dot_general(both, band, NN, preferred_element_type=F32)
        for y in range(g.cy):
            at = (x * g.cy + y) * g.no
            rows = slice(y * g.no, (y + 1) * g.no)
            here = cell(x, y)
            diag = jnp.broadcast_to(pot[x * g.cy + y : x * g.cy + y + 1, :], here.shape)
            total = along[rows, : g.cz] + along[rows, g.cz :]
            total = total + (scale * DIAGONAL + (scale / HALF_WIDTH) * diag) * here
            if subtract:
                total = total - prev[at : at + g.no, :]
            for k in range(1, RADIUS + 1):
                near = []
                for a, b in ((x - k, y), (x + k, y), (x, y - k), (x, y + k)):
                    if 0 <= a < g.cx and 0 <= b < g.cy:
                        near.append(cell(a, b))
                if near:
                    total = total + (scale * WEIGHT[k]) * sum(near[1:], near[0])
            out[at : at + g.no, :] = total


def flag(present):
    return 1.0 if present is None else jnp.where(present, 1.0, 0.0)


def add_ends(g, dom, scale, acc, low, high, out):
    inward, row = end_columns(g, dom)
    middle = (dom % g.third > 0) & (dom % g.third < g.third - 1)
    present = (row % 8 < RADIUS) & ((row < 8) | middle)
    coef = jnp.where(present, weight_at(inward + row % 8 + 1, scale), 0.0)
    c_high, c_low = split2(coef)
    coefs = jnp.concatenate([c_high, c_high, c_low, c_low], axis=0)
    for x in range(g.cx):
        rows = slice(x * g.slab, (x + 1) * g.slab)
        h_high, h_low = split2(jnp.concatenate([low[:, rows], high[:, rows]], axis=0))
        halo = jnp.concatenate([h_high, h_low, h_high, h_low], axis=0)
        out[rows, :] = acc[rows, :] + lax.dot_general(halo, coefs, TN, preferred_element_type=F32)


def add_x_faces(g, dom, scale, face_refs, out):
    unit = 2 * g.no
    for (side, present), face in zip(g.faces(dom, 0), face_refs):
        for y in range(0, g.cy, 2):
            starts = [j * g.slab + y * g.no for j in range(RADIUS)]
            part = [flag(present) * face[at : at + unit, :].astype(F32) for at in starts]
            for i in range(RADIUS):
                at = aligned(layer(side, g.cx, i) * g.slab + y * g.no, unit)
                total = out[pl.ds(at, unit), :]
                for j in range(RADIUS - i):
                    total = total + (scale * WEIGHT[i + j + 1]) * part[j]
                out[pl.ds(at, unit), :] = total


def add_y_faces(g, dom, scale, face_refs, out):
    size = RADIUS * g.no
    for (side, present), face in zip(g.faces(dom, 1), face_refs):
        for x in range(g.cx):
            part = flag(present) * face[x * size : (x + 1) * size, :].astype(F32)
            for i in range(RADIUS):
                at = aligned(x * g.slab + layer(side, g.cy, i) * g.no, g.no)
                total = out[pl.ds(at, g.no), :]
                for j in range(RADIUS - i):
                    total = total + (scale * WEIGHT[i + j + 1]) * part[j * g.no : (j + 1) * g.no]
                out[pl.ds(at, g.no), :] = total


def add_nonlocal(g, dom, scale, table, energy, projf, blk, atom, lut, spread, out):
    size = g.nproj * g.no
    lanes = g.table
    count = g.slots()
    rows = []
    for step in g.steps(dom):
        owner = pl.ds(jnp.clip(dom + step, 0, g.dom_count - 1), 1)
        rows.append(table[owner, :] * energy[owner, :])
    rows.append(jnp.zeros((8 - count, lanes), F32))
    scaled = (scale / HALF_WIDTH) * jnp.concatenate(rows, axis=0)
    high = scaled.astype(BF16)
    rest = scaled - high.astype(F32)
    mid = rest.astype(BF16)
    low = (rest - mid.astype(F32)).astype(BF16)
    parts = jnp.concatenate([high, mid, low], axis=0)
    wide = count * g.cz
    row, col = iota((24, wide), 0), iota((24, wide), 1)
    ones = jnp.where(row % 8 == col // g.cz, 1.0, 0.0).astype(BF16)
    out_all = lax.dot_general(parts, ones, TN, preferred_element_type=F32)
    for number in range(count):
        spread[number * lanes : (number + 1) * lanes, :] = out_all[:, number * g.cz : (number + 1) * g.cz]
    unroll = 16

    def step(i, _):
        additions = []
        for u in range(unroll):
            e = i * unroll + u
            col = column_of(g, lut, atom[e])
            total = None
            for p in range(g.nproj):
                at = pl.ds(pl.multiple_of(col * size + p * g.no, g.no), g.no)
                coef = jnp.broadcast_to(projf[e, p : p + 1, :], (g.no, g.cz))
                term = spread[at, :] * coef
                total = term if total is None else total + term
            additions.append((pl.ds(pl.multiple_of(blk[e] * g.no, g.no), g.no), total))
        for at, total in additions:
            out[at, :] += total
        return 0

    lax.fori_loop(0, g.ent // unroll, step, 0)


def nonlocal_kernel(g, scale, acc, projf, energy, blk_hbm, atom_hbm, first, second, *refs):
    out, table, blk, atom, lut, sem, spread = refs[-7:]
    copies = entry_copies(blk_hbm, atom_hbm, blk, atom, sem)
    dom = lax.axis_index("dom")
    fill_lut(g, dom, lut)
    if g.butterfly:
        group, opposite = refs[:2]
        table[...] = (group[...] + get_table(g, first)) + (get_table(g, second) + opposite[...])
    else:
        table[...] = refs[0][...]
    add_ends(g, dom, scale, acc, first, second, out)
    for copy in copies:
        copy.wait()
    add_nonlocal(g, dom, scale, table, energy, projf, blk, atom, lut, spread, out)


def middle_kernel(g, acc, projf, blk_hbm, atom_hbm, *refs):
    nx, ny = len(g.face_rows(0)), len(g.face_rows(1))
    faces = refs[: nx + ny]
    u_ref, table, blk, atom, lut, sem = refs[nx + ny : nx + ny + 6]
    sums = refs[nx + ny + 6 :]
    copies = entry_copies(blk_hbm, atom_hbm, blk, atom, sem)
    dom = lax.axis_index("dom")
    fill_lut(g, dom, lut)
    clear(sums)
    u_ref[...] = acc[...]
    add_x_faces(g, dom, 1.0, faces[:nx], u_ref)
    add_y_faces(g, dom, 1.0, faces[nx:], u_ref)
    for copy in copies:
        copy.wait()
    inner_tables(g, dom, u_ref, projf, blk, atom, lut, sums, table)


def halves(g, dom):
    if g.first != 2 or g.cx != 2 * RADIUS:
        return [(0, g.cx)]
    side = 1 - dom // g.plane
    return [((1 - side) * RADIUS, RADIUS), (side * RADIUS, RADIUS)]


def last_kernel(g, number, acc, *refs):
    nx = len(g.face_rows(0))
    filtered, work = refs[-2:]
    refs = refs[:-2]
    dom = lax.axis_index("dom")
    parts = halves(g, dom)
    start, count = parts[number]
    work[...] = acc[...]
    if number == len(parts) - 1:
        add_x_faces(g, dom, 2.0, refs[:nx], work)
        refs = refs[nx:]
    add_y_faces(g, dom, 2.0, refs, work)
    at = aligned(start * g.slab, g.slab)
    filtered[...] = work[pl.ds(at, count * g.slab), :].astype(BF16)


def panel_kernel(g, panel, weights):
    band = lax.axis_index("band")
    group = 16
    span = group * g.no
    norb = panel.shape[0]
    row, col = iota((span, norb), 0), iota((span, norb), 1)
    pick_out = jnp.where(col == band * g.no + row // group, 1.0, 0.0).astype(BF16)
    picked = lax.dot_general(pick_out, panel[...], NT, preferred_element_type=F32).astype(BF16)
    row, col = iota((norb, 2 * span), 0), iota((norb, 2 * span), 1)
    source = jnp.where(col < span, band, 1 - band) * g.no + col % g.no
    pick_in = jnp.where(row == source, 1.0, 0.0).astype(BF16)
    spread = lax.dot_general(picked, pick_in, NN, preferred_element_type=F32)
    row, col = iota((span, 2 * span), 0), iota((span, 2 * span), 1)
    same = row % group == (col % span) // g.no
    weights[...] = jnp.where(same, spread, 0.0).astype(BF16)


def rotate_kernel(g, number, own, other, weights, *refs):
    out_hbm, out, sem = refs[-3:]
    start, count = halves(g, lax.axis_index("dom"))[number]
    group = 16
    span = group * g.no
    copies = []
    size = count * g.cy
    for n in range(size // group):
        rows = slice(n * span, (n + 1) * span)
        both = jnp.concatenate([own[rows, :], other[rows, :]], axis=0)
        result = lax.dot_general(weights[...], both, NN, preferred_element_type=F32)
        for j in range(g.no):
            out[j, n * group : (n + 1) * group, :] = result[j * group : (j + 1) * group, :]
        to = pl.ds(aligned(start * g.cy + n * group, group), group)
        source = out.at[:, pl.ds(n * group, group), :]
        copies.append(pltpu.make_async_copy(source, out_hbm.at[:, to, :], sem.at[n]))
        copies[-1].start()
    for copy in copies:
        copy.wait()


def call(kernel, name, out_shape, scratch, args, specs, **options):
    return pl.pallas_call(
        kernel,
        name=name,
        out_shape=out_shape,
        in_specs=specs,
        out_specs=options.pop("out_specs", jax.tree.map(lambda _: VMEM, out_shape)),
        scratch_shapes=scratch,
        compiler_params=pltpu.CompilerParams(vmem_limit_bytes=48 * 1024 * 1024),
        cost_estimate=pl.CostEstimate(flops=1000, bytes_accessed=1000, transcendentals=0),
        **options,
    )(*args)


def shift(g, array, stride, extent, step):
    pairs = []
    for i in range(g.dom_count):
        place = i // stride % extent
        pairs.append((i, i + ((place + step) % extent - place) * stride))
    return lax.ppermute(array, "dom", pairs)


def swap_faces(g, faces, stride, extent):
    if extent == 2:
        return [shift(g, faces[0], stride, extent, 1)]
    if extent > 2:
        return [shift(g, faces[1], stride, extent, 1), shift(g, faces[0], stride, extent, -1)]
    return []


def shards(orbitals, potential, projectors, entry_atom, entry_block, kb_energy, panel):
    g = Geometry(
        orbitals.shape, projectors.shape[0], projectors.shape[1], kb_energy.shape[0], lax.axis_size("dom")
    )

    def in_hbm(array):
        return pltpu.with_memory_space_constraint(array, pltpu.HBM)

    orb = in_hbm(orbitals.reshape(g.flat, g.cz))
    pot = in_hbm(potential.reshape(g.rows, g.cz))
    proj = in_hbm(projectors)
    blk, atom = in_hbm(entry_block), in_hbm(entry_atom)
    field = jax.ShapeDtypeStruct((g.flat, g.cz), F32)
    x_faces = [jax.ShapeDtypeStruct((n, g.cz), BF16) for n in g.face_rows(0)]
    y_faces = [jax.ShapeDtypeStruct((n, g.cz), BF16) for n in g.face_rows(1)]
    nx = len(x_faces)
    ends = jax.ShapeDtypeStruct((8, g.flat), F32)
    table = jax.ShapeDtypeStruct((g.dom_count, g.table), F32)
    entries = [
        pltpu.SMEM((g.ent,), jnp.int32),
        pltpu.SMEM((g.ent,), jnp.int32),
        pltpu.SMEM((g.dom_count + 2 * g.plane,), jnp.int32),
        pltpu.SemaphoreType.DMA((2,)),
    ]
    slots = g.slots() * g.table
    sums = [pltpu.VMEM((slots, g.cz), F32) for _ in range(4)]
    spread = pltpu.VMEM((slots, g.cz), F32)
    energy = jnp.repeat(kb_energy.reshape(g.dom_count, g.owned * g.nproj), g.no, axis=1)
    indices = range(g.dom_count)

    def swap(array, *strides):
        pairs = [(i, i + sum(s * (1 - 2 * (i // s % 2)) for s in strides)) for i in indices]
        return lax.ppermute(array, "dom", pairs)

    def reverse(array):
        pairs = [(i, i - i % g.third + g.third - 1 - i % g.third) for i in indices]
        return lax.ppermute(array, "dom", pairs)

    def local_and_ends(scale, which, values, prev, part):
        acc = call(
            functools.partial(inside_kernel, g, scale, len(prev) > 0),
            "inside_" + which,
            field,
            [],
            [values, pot, *prev],
            [VMEM] * (2 + len(prev)),
        )
        inputs = [values, energy, acc]
        outputs = [ends, ends, *x_faces, *y_faces]
        if g.butterfly:
            inputs += [part, swap(part, g.plane), swap(part, g.third), swap(part, g.plane, g.third)]
            outputs.append(table)
        first, second, *sent = call(
            functools.partial(pack_kernel, g), "pack_" + which, outputs, [], inputs, [VMEM] * len(inputs)
        )
        from_x = swap_faces(g, sent[:nx], g.plane, g.first)
        from_y = swap_faces(g, sent[nx : nx + len(y_faces)], g.third, g.second)
        first, second = swap(first, 1), reverse(second)
        tables = [sent[-1], swap(sent[-1], 2)] if g.butterfly else [lax.psum(part, "dom")]
        acc = call(
            functools.partial(nonlocal_kernel, g, scale),
            "nonlocal_" + which,
            field,
            [pltpu.VMEM(table.shape, F32), *entries, spread],
            [acc, projf, energy, blk, atom, first, second, *tables],
            [VMEM] * 3 + [HBM] * 2 + [VMEM] * (2 + len(tables)),
        )
        return acc, from_x + from_y

    v, projf, pot, part = call(
        functools.partial(first_kernel, g),
        "tables_first",
        [field, jax.ShapeDtypeStruct(proj.shape, F32), jax.ShapeDtypeStruct(pot.shape, F32), table],
        [
            pltpu.VMEM(orb.shape, F32),
            pltpu.VMEM(proj.shape, BF16),
            pltpu.SemaphoreType.DMA((3,)),
            *entries,
            *sums,
        ],
        [orb, proj, pot, blk, atom],
        [HBM] * 5,
    )
    acc, received = local_and_ends(1.0, "first", v, [], part)
    u, part = call(
        functools.partial(middle_kernel, g),
        "tables_second",
        [field, table],
        [*entries, *sums],
        [acc, projf, blk, atom, *received],
        [VMEM] * 2 + [HBM] * 2 + [VMEM] * len(received),
    )
    acc, received = local_and_ends(2.0, "second", u, [v], part)
    weights = call(
        functools.partial(panel_kernel, g),
        "panel",
        jax.ShapeDtypeStruct((16 * g.no, 32 * g.no), BF16),
        [],
        [panel],
        [VMEM],
    )
    rotated = None
    pieces = []
    parts = halves(g, 0)
    for number, (_, count) in enumerate(parts):
        inputs = [acc, *received[nx:]] if number < len(parts) - 1 else [acc, *received]
        filtered = call(
            functools.partial(last_kernel, g, number),
            "filtered_%d" % number,
            jax.ShapeDtypeStruct((count * g.slab, g.cz), BF16),
            [pltpu.VMEM((g.flat, g.cz), F32)],
            inputs,
            [VMEM] * len(inputs),
        )
        pieces.append((filtered, lax.ppermute(filtered, "band", [(0, 1), (1, 0)]), count))
    for number, (filtered, other, count) in enumerate(pieces):
        inputs = [filtered, other, weights] + ([] if rotated is None else [rotated])
        rotated = call(
            functools.partial(rotate_kernel, g, number),
            "rotate_%d" % number,
            jax.ShapeDtypeStruct((g.no, g.rows, g.cz), F32),
            [pltpu.VMEM((g.no, count * g.cy, g.cz), F32), pltpu.SemaphoreType.DMA((count * g.cy // 16,))],
            inputs,
            [VMEM] * 3 + [HBM] * (len(inputs) - 3),
            out_specs=HBM,
            input_output_aliases={} if rotated is None else {3: 0},
        )
    return rotated.reshape(orbitals.shape)


def solution(mesh):
    in_specs = (
        P("dom", "band", None, None, None),
        P("dom", None, None, None),
        P("dom", None, None),
        P("dom"),
        P("dom"),
        P(),
        P(),
    )
    out_specs = P("dom", "band", None, None, None)
    return jax.shard_map(shards, mesh=mesh, in_specs=in_specs, out_specs=out_specs, check_vma=False)
```

```python
import functools

import jax
import jax.numpy as jnp
from jax import lax
from jax.experimental import pallas as pl
from jax.experimental.pallas import tpu as pltpu
from jax.sharding import PartitionSpec as P

RADIUS = 6
COEFFS = (
    -5369.0 / 1800.0,
    12.0 / 7.0,
    -15.0 / 56.0,
    10.0 / 189.0,
    -1.0 / 112.0,
    2.0 / 1925.0,
    -1.0 / 16632.0,
)
KINETIC = -3.125
CENTER = 36.0
HALF_WIDTH = 34.0
WEIGHT = [KINETIC * c / HALF_WIDTH for c in COEFFS]
DIAGONAL = (3.0 * KINETIC * COEFFS[0] - CENTER) / HALF_WIDTH

F32 = jnp.float32
BF16 = jnp.bfloat16
VMEM = pl.BlockSpec(memory_space=pltpu.VMEM)
HBM = pl.BlockSpec(memory_space=pltpu.HBM)
NT = (((1,), (1,)), ((), ()))
TN = (((0,), (0,)), ((), ()))
NN = (((1,), (0,)), ((), ()))


def split2(x):
    high = x.astype(BF16)
    low = (x - high.astype(F32)).astype(BF16)
    return high, low


def iota(shape, dim):
    return lax.broadcasted_iota(jnp.int32, shape, dim)


def weight_at(distance, scale):
    out = jnp.zeros(distance.shape, F32)
    for k in range(1, RADIUS + 1):
        out = jnp.where(distance == k, scale * WEIGHT[k], out)
    return out


class Geometry:
    def __init__(self, orbitals, entries, nproj, atoms, dom_count):
        _, self.no, self.cx, self.cy, self.cz = orbitals
        self.rows = self.cx * self.cy
        self.flat = self.rows * self.no
        self.ent = entries
        self.nproj = nproj
        self.dom_count = dom_count
        self.owned = atoms // dom_count
        self.third = 4
        self.second = min(8, dom_count // 8)
        self.plane = self.second * self.third
        self.first = dom_count // self.plane
        self.table = self.owned * nproj * self.no
        self.slab = self.cy * self.no
        self.fold = self.flat // self.table
        self.butterfly = self.first == 2 and self.second == 2 and dom_count <= 2 * self.fold
        assert self.no == 8

    def faces(self, dom, dim):
        if dim == 0:
            extent, place = self.first, dom // self.plane
        else:
            extent, place = self.second, dom // self.third % self.second
        if extent == 2:
            return [(1 - place, None)]
        if extent > 2:
            return [(0, place > 0), (1, place < extent - 1)]
        return []

    def face_rows(self, dim):
        rows = RADIUS * self.slab if dim == 0 else self.cx * RADIUS * self.no
        return [rows] * len(self.faces(0, dim))

    def steps(self, dom):
        out = [0]
        for extent, stride in ((self.first, self.plane), (self.second, self.third), (self.third, 1)):
            if extent == 2:
                out.append((1 - 2 * (dom // stride % 2)) * stride)
            elif extent > 2:
                out.extend([stride, -stride])
        return out

    def slots(self):
        return len(self.steps(0))


def layer(side, length, j):
    if isinstance(side, int):
        return length - 1 - j if side else j
    return side * (length - 1 - j) + (1 - side) * j


def aligned(start, unit):
    return start if isinstance(start, int) else pl.multiple_of(start, unit)


def pack_x(g, dom, v_ref, refs):
    for (side, _), out in zip(g.faces(dom, 0), refs):
        for j in range(RADIUS):
            at = aligned(layer(side, g.cx, j) * g.slab, g.slab)
            out[j * g.slab : (j + 1) * g.slab, :] = v_ref[pl.ds(at, g.slab), :].astype(BF16)


def pack_y(g, dom, v_ref, refs):
    size = RADIUS * g.no
    for (side, _), out in zip(g.faces(dom, 1), refs):
        for x in range(g.cx):
            pieces = []
            for j in range(RADIUS):
                at = aligned(x * g.slab + layer(side, g.cy, j) * g.no, g.no)
                pieces.append(v_ref[pl.ds(at, g.no), :])
            out[x * size : (x + 1) * size, :] = jnp.concatenate(pieces, axis=0).astype(BF16)


def end_columns(g, dom):
    row, col = iota((16, g.cz), 0), iota((16, g.cz), 1)
    odd = dom % 2
    side = jnp.where(row < 8, 1 - odd, odd)
    return jnp.where(side == 1, g.cz - 1 - col, col), row


def pack_ends(g, dom, v_ref, first_ref, second_ref):
    inward, row = end_columns(g, dom)
    pick = jnp.where((inward == row % 8) & (row % 8 < RADIUS), 1.0, 0.0).astype(BF16)
    pick = jnp.concatenate([pick, pick], axis=1)
    for x in range(g.cx):
        rows = slice(x * g.slab, (x + 1) * g.slab)
        both = jnp.concatenate(split2(v_ref[rows, :]), axis=1)
        ends = lax.dot_general(pick, both, NT, preferred_element_type=F32)
        first_ref[:, rows] = ends[:8]
        second_ref[:, rows] = ends[8:]


def put_table(g, message, table):
    for n in range(g.dom_count):
        at = RADIUS + n // g.fold
        lanes = n % g.fold * g.table
        message[at : at + 1, lanes : lanes + g.table] = table[n : n + 1, :]


def get_table(g, message):
    rows = []
    for n in range(g.dom_count):
        at = RADIUS + n // g.fold
        lanes = n % g.fold * g.table
        rows.append(message[at : at + 1, lanes : lanes + g.table])
    return jnp.concatenate(rows, axis=0)


def fill_lut(g, dom, lut):
    for number, step in enumerate(g.steps(dom)):
        lut[g.plane + dom + step] = number * g.owned


def column_of(g, lut, atom):
    if g.owned & (g.owned - 1):
        owner = lax.div(atom, jnp.int32(g.owned))
        return lut[owner + g.plane] + (atom - owner * g.owned)
    owner = lax.shift_right_logical(atom, jnp.int32(g.owned.bit_length() - 1))
    return lut[owner + g.plane] + (atom & (g.owned - 1))


def inner_tables(g, dom, v_ref, projf, blk, atom, lut, sums, table):
    size = g.nproj * g.no

    unroll = 16

    def step(i, _):
        for u in range(unroll):
            part = sums[u % len(sums)]
            e = i * unroll + u
            col = column_of(g, lut, atom[e])
            v = v_ref[pl.ds(pl.multiple_of(blk[e] * g.no, g.no), g.no), :]
            for p in range(g.nproj):
                at = pl.ds(pl.multiple_of(col * size + p * g.no, g.no), g.no)
                coef = jnp.broadcast_to(projf[e, p : p + 1, :], v.shape)
                part[at, :] += v * coef
        return 0

    lax.fori_loop(0, g.ent // unroll, step, 0)
    total = sums[0][...]
    for part in sums[1:]:
        total = total + part[...]
    both = jnp.concatenate(split2(total), axis=1)
    ones = jnp.ones((8, both.shape[1]), BF16)
    summed = lax.dot_general(ones, both, NT, preferred_element_type=F32)
    table[...] = jnp.zeros(table.shape, F32)
    for number, step in enumerate(g.steps(dom)):
        owner = jnp.clip(dom + step, 0, g.dom_count - 1)
        table[pl.ds(owner, 1), :] += summed[0:1, number * g.table : (number + 1) * g.table]


def clear(sums):
    for part in sums:
        part[...] = jnp.zeros(part.shape, F32)


def entry_copies(blk_hbm, atom_hbm, blk, atom, sem):
    copies = [
        pltpu.make_async_copy(blk_hbm, blk, sem.at[0]),
        pltpu.make_async_copy(atom_hbm, atom, sem.at[1]),
    ]
    for copy in copies:
        copy.start()
    return copies


def first_kernel(g, orb_hbm, proj_hbm, pot_hbm, blk_hbm, atom_hbm, v_ref, projf, pot, table, *scratch):
    orb, proj, sem, blk, atom, lut, entry_sem = scratch[:7]
    sums = scratch[7:]
    copies = [
        pltpu.make_async_copy(orb_hbm, orb, sem.at[0]),
        pltpu.make_async_copy(proj_hbm, proj, sem.at[1]),
        pltpu.make_async_copy(pot_hbm, pot, sem.at[2]),
    ]
    for copy in copies:
        copy.start()
    copies += entry_copies(blk_hbm, atom_hbm, blk, atom, entry_sem)
    dom = lax.axis_index("dom")
    fill_lut(g, dom, lut)
    clear(sums)
    copies[1].wait()
    projf[...] = proj[...].astype(F32)
    copies[0].wait()
    for r in range(g.rows):
        v_ref[r * g.no : (r + 1) * g.no, :] = orb[pl.ds(r, g.no, stride=g.rows), :]
    for copy in copies[2:]:
        copy.wait()
    inner_tables(g, dom, v_ref, projf, blk, atom, lut, sums, table)


def pack_kernel(g, v_ref, energy, *refs):
    dom = lax.axis_index("dom")
    if g.butterfly:
        part, from_x, from_y, from_xy = refs[:4]
        group = refs[-1]
        group[...] = (part[...] + from_x[...]) + (from_y[...] + from_xy[...])
        refs = refs[4:-1]
    first, second = refs[:2]
    pack_y(g, dom, v_ref, refs[2:])
    pack_ends(g, dom, v_ref, first, second)
    if g.butterfly:
        put_table(g, first, group)
        put_table(g, second, group)


def pack_x_kernel(g, nafter, v_ref, *refs):
    pack_x(g, lax.axis_index("dom"), v_ref, refs[nafter:])


def inside_kernel(g, scale, subtract, v_ref, pot, *refs):
    prev, out = refs if subtract else (None, refs[0])
    row, col = iota((g.cz, g.cz), 0), iota((g.cz, g.cz), 1)
    high, low = split2(weight_at(jnp.abs(row - col), scale))
    band = jnp.concatenate([high, low], axis=1)
    band = jnp.concatenate([band, band], axis=0)

    def cell(x, y):
        at = (x * g.cy + y) * g.no
        return v_ref[at : at + g.no, :]

    for x in range(g.cx):
        both = jnp.concatenate(split2(v_ref[x * g.slab : (x + 1) * g.slab, :]), axis=1)
        along = lax.dot_general(both, band, NN, preferred_element_type=F32)
        for y in range(g.cy):
            at = (x * g.cy + y) * g.no
            rows = slice(y * g.no, (y + 1) * g.no)
            here = cell(x, y)
            diag = jnp.broadcast_to(pot[x * g.cy + y : x * g.cy + y + 1, :], here.shape)
            total = along[rows, : g.cz] + along[rows, g.cz :]
            total = total + (scale * DIAGONAL + (scale / HALF_WIDTH) * diag) * here
            if subtract:
                total = total - prev[at : at + g.no, :]
            for k in range(1, RADIUS + 1):
                near = []
                for a, b in ((x - k, y), (x + k, y), (x, y - k), (x, y + k)):
                    if 0 <= a < g.cx and 0 <= b < g.cy:
                        near.append(cell(a, b))
                if near:
                    total = total + (scale * WEIGHT[k]) * sum(near[1:], near[0])
            out[at : at + g.no, :] = total


def flag(present):
    return 1.0 if present is None else jnp.where(present, 1.0, 0.0)


def add_ends(g, dom, scale, acc, low, high, out):
    inward, row = end_columns(g, dom)
    middle = (dom % g.third > 0) & (dom % g.third < g.third - 1)
    present = (row % 8 < RADIUS) & ((row < 8) | middle)
    coef = jnp.where(present, weight_at(inward + row % 8 + 1, scale), 0.0)
    c_high, c_low = split2(coef)
    coefs = jnp.concatenate([c_high, c_high, c_low, c_low], axis=0)
    for x in range(g.cx):
        rows = slice(x * g.slab, (x + 1) * g.slab)
        h_high, h_low = split2(jnp.concatenate([low[:, rows], high[:, rows]], axis=0))
        halo = jnp.concatenate([h_high, h_low, h_high, h_low], axis=0)
        out[rows, :] = acc[rows, :] + lax.dot_general(halo, coefs, TN, preferred_element_type=F32)


def add_x_faces(g, dom, scale, face_refs, out):
    unit = 2 * g.no
    for (side, present), face in zip(g.faces(dom, 0), face_refs):
        for y in range(0, g.cy, 2):
            starts = [j * g.slab + y * g.no for j in range(RADIUS)]
            part = [flag(present) * face[at : at + unit, :].astype(F32) for at in starts]
            for i in range(RADIUS):
                at = aligned(layer(side, g.cx, i) * g.slab + y * g.no, unit)
                total = out[pl.ds(at, unit), :]
                for j in range(RADIUS - i):
                    total = total + (scale * WEIGHT[i + j + 1]) * part[j]
                out[pl.ds(at, unit), :] = total


def add_y_faces(g, dom, scale, face_refs, out):
    size = RADIUS * g.no
    for (side, present), face in zip(g.faces(dom, 1), face_refs):
        for x in range(g.cx):
            part = flag(present) * face[x * size : (x + 1) * size, :].astype(F32)
            for i in range(RADIUS):
                at = aligned(x * g.slab + layer(side, g.cy, i) * g.no, g.no)
                total = out[pl.ds(at, g.no), :]
                for j in range(RADIUS - i):
                    total = total + (scale * WEIGHT[i + j + 1]) * part[j * g.no : (j + 1) * g.no]
                out[pl.ds(at, g.no), :] = total


def add_nonlocal(g, dom, table, energy, projf, blk, atom, lut, spread, out):
    size = g.nproj * g.no
    lanes = g.table
    count = g.slots()
    rows = []
    for step in g.steps(dom):
        owner = pl.ds(jnp.clip(dom + step, 0, g.dom_count - 1), 1)
        rows.append(table[owner, :] * energy[owner, :])
    rows.append(jnp.zeros((8 - count, lanes), F32))
    scaled = jnp.concatenate(rows, axis=0)
    high = scaled.astype(BF16)
    rest = scaled - high.astype(F32)
    mid = rest.astype(BF16)
    low = (rest - mid.astype(F32)).astype(BF16)
    parts = jnp.concatenate([high, mid, low], axis=0)
    wide = count * g.cz
    row, col = iota((24, wide), 0), iota((24, wide), 1)
    ones = jnp.where(row % 8 == col // g.cz, 1.0, 0.0).astype(BF16)
    out_all = lax.dot_general(parts, ones, TN, preferred_element_type=F32)
    for number in range(count):
        spread[number * lanes : (number + 1) * lanes, :] = out_all[:, number * g.cz : (number + 1) * g.cz]
    unroll = 16

    def step(i, _):
        additions = []
        for u in range(unroll):
            e = i * unroll + u
            col = column_of(g, lut, atom[e])
            total = None
            for p in range(g.nproj):
                at = pl.ds(pl.multiple_of(col * size + p * g.no, g.no), g.no)
                coef = jnp.broadcast_to(projf[e, p : p + 1, :], (g.no, g.cz))
                term = spread[at, :] * coef
                total = term if total is None else total + term
            additions.append((pl.ds(pl.multiple_of(blk[e] * g.no, g.no), g.no), total))
        for at, total in additions:
            out[at, :] += total
        return 0

    lax.fori_loop(0, g.ent // unroll, step, 0)


def nonlocal_kernel(g, scale, acc, projf, energy, blk_hbm, atom_hbm, first, second, *refs):
    out, table, blk, atom, lut, sem, spread = refs[-7:]
    copies = entry_copies(blk_hbm, atom_hbm, blk, atom, sem)
    dom = lax.axis_index("dom")
    fill_lut(g, dom, lut)
    if g.butterfly:
        group, opposite = refs[:2]
        table[...] = (group[...] + get_table(g, first)) + (get_table(g, second) + opposite[...])
    else:
        table[...] = refs[0][...]
    add_ends(g, dom, scale, acc, first, second, out)
    for copy in copies:
        copy.wait()
    add_nonlocal(g, dom, table, energy, projf, blk, atom, lut, spread, out)


def middle_kernel(g, acc, projf, blk_hbm, atom_hbm, *refs):
    nx, ny = len(g.face_rows(0)), len(g.face_rows(1))
    faces = refs[: nx + ny]
    u_ref, table, blk, atom, lut, sem = refs[nx + ny : nx + ny + 6]
    sums = refs[nx + ny + 6 :]
    copies = entry_copies(blk_hbm, atom_hbm, blk, atom, sem)
    dom = lax.axis_index("dom")
    fill_lut(g, dom, lut)
    clear(sums)
    u_ref[...] = acc[...]
    add_x_faces(g, dom, 1.0, faces[:nx], u_ref)
    add_y_faces(g, dom, 1.0, faces[nx:], u_ref)
    for copy in copies:
        copy.wait()
    inner_tables(g, dom, u_ref, projf, blk, atom, lut, sums, table)


def halves(g, dom):
    if g.first != 2 or g.cx != 2 * RADIUS:
        return [(0, g.cx)]
    side = 1 - dom // g.plane
    return [((1 - side) * RADIUS, RADIUS), (side * RADIUS, RADIUS)]


def last_kernel(g, number, acc, *refs):
    nx = len(g.face_rows(0))
    filtered, work = refs[-2:]
    refs = refs[:-2]
    dom = lax.axis_index("dom")
    parts = halves(g, dom)
    start, count = parts[number]
    work[...] = acc[...]
    if number == len(parts) - 1:
        add_x_faces(g, dom, 2.0, refs[:nx], work)
        refs = refs[nx:]
    add_y_faces(g, dom, 2.0, refs, work)
    at = aligned(start * g.slab, g.slab)
    filtered[...] = work[pl.ds(at, count * g.slab), :].astype(BF16)


def panel_kernel(g, panel, weights):
    band = lax.axis_index("band")
    group = 16
    span = group * g.no
    norb = panel.shape[0]
    row, col = iota((span, norb), 0), iota((span, norb), 1)
    pick_out = jnp.where(col == band * g.no + row // group, 1.0, 0.0).astype(BF16)
    picked = lax.dot_general(pick_out, panel[...], NT, preferred_element_type=F32).astype(BF16)
    row, col = iota((norb, 2 * span), 0), iota((norb, 2 * span), 1)
    source = jnp.where(col < span, band, 1 - band) * g.no + col % g.no
    pick_in = jnp.where(row == source, 1.0, 0.0).astype(BF16)
    spread = lax.dot_general(picked, pick_in, NN, preferred_element_type=F32)
    row, col = iota((span, 2 * span), 0), iota((span, 2 * span), 1)
    same = row % group == (col % span) // g.no
    weights[...] = jnp.where(same, spread, 0.0).astype(BF16)


def rotate_kernel(g, number, own, other, weights, *refs):
    out_hbm, out, sem = refs[-3:]
    start, count = halves(g, lax.axis_index("dom"))[number]
    group = 16
    span = group * g.no
    copies = []
    size = count * g.cy
    for n in range(size // group):
        rows = slice(n * span, (n + 1) * span)
        both = jnp.concatenate([own[rows, :], other[rows, :]], axis=0)
        result = lax.dot_general(weights[...], both, NN, preferred_element_type=F32)
        for j in range(g.no):
            out[j, n * group : (n + 1) * group, :] = result[j * group : (j + 1) * group, :]
        to = pl.ds(aligned(start * g.cy + n * group, group), group)
        source = out.at[:, pl.ds(n * group, group), :]
        copies.append(pltpu.make_async_copy(source, out_hbm.at[:, to, :], sem.at[n]))
        copies[-1].start()
    for copy in copies:
        copy.wait()


def call(kernel, name, out_shape, scratch, args, specs, **options):
    return pl.pallas_call(
        kernel,
        name=name,
        out_shape=out_shape,
        in_specs=specs,
        out_specs=options.pop("out_specs", jax.tree.map(lambda _: VMEM, out_shape)),
        scratch_shapes=scratch,
        compiler_params=pltpu.CompilerParams(vmem_limit_bytes=48 * 1024 * 1024),
        cost_estimate=pl.CostEstimate(flops=1000, bytes_accessed=1000, transcendentals=0),
        **options,
    )(*args)


def shift(g, array, stride, extent, step):
    pairs = []
    for i in range(g.dom_count):
        place = i // stride % extent
        pairs.append((i, i + ((place + step) % extent - place) * stride))
    return lax.ppermute(array, "dom", pairs)


def swap_faces(g, faces, stride, extent):
    if extent == 2:
        return [shift(g, faces[0], stride, extent, 1)]
    if extent > 2:
        return [shift(g, faces[1], stride, extent, 1), shift(g, faces[0], stride, extent, -1)]
    return []


def shards(orbitals, potential, projectors, entry_atom, entry_block, kb_energy, panel):
    g = Geometry(
        orbitals.shape, projectors.shape[0], projectors.shape[1], kb_energy.shape[0], lax.axis_size("dom")
    )

    def in_hbm(array):
        return pltpu.with_memory_space_constraint(array, pltpu.HBM)

    orb = in_hbm(orbitals.reshape(g.flat, g.cz))
    pot = in_hbm(potential.reshape(g.rows, g.cz))
    proj = in_hbm(projectors)
    blk, atom = in_hbm(entry_block), in_hbm(entry_atom)
    field = jax.ShapeDtypeStruct((g.flat, g.cz), F32)
    x_faces = [jax.ShapeDtypeStruct((n, g.cz), BF16) for n in g.face_rows(0)]
    y_faces = [jax.ShapeDtypeStruct((n, g.cz), BF16) for n in g.face_rows(1)]
    nx = len(x_faces)
    ends = jax.ShapeDtypeStruct((8, g.flat), F32)
    table = jax.ShapeDtypeStruct((g.dom_count, g.table), F32)
    entries = [
        pltpu.SMEM((g.ent,), jnp.int32),
        pltpu.SMEM((g.ent,), jnp.int32),
        pltpu.SMEM((g.dom_count + 2 * g.plane,), jnp.int32),
        pltpu.SemaphoreType.DMA((2,)),
    ]
    slots = g.slots() * g.table
    sums = [pltpu.VMEM((slots, g.cz), F32) for _ in range(4)]
    spread = pltpu.VMEM((slots, g.cz), F32)
    indices = range(g.dom_count)

    def swap(array, *strides):
        pairs = [(i, i + sum(s * (1 - 2 * (i // s % 2)) for s in strides)) for i in indices]
        return lax.ppermute(array, "dom", pairs)

    def reverse(array):
        pairs = [(i, i - i % g.third + g.third - 1 - i % g.third) for i in indices]
        return lax.ppermute(array, "dom", pairs)

    def local_and_ends(scale, which, values, prev, part):
        energy = (scale / HALF_WIDTH) * kb_energy
        energy = jnp.repeat(energy.reshape(g.dom_count, g.owned * g.nproj), g.no, axis=1)
        acc = call(
            functools.partial(inside_kernel, g, scale, len(prev) > 0),
            "inside_" + which,
            field,
            [],
            [values, pot, *prev],
            [VMEM] * (2 + len(prev)),
        )
        inputs = [values, energy]
        outputs = [ends, ends, *y_faces]
        after = [acc]
        if g.butterfly:
            inputs += [part, swap(part, g.plane), swap(part, g.third), swap(part, g.plane, g.third)]
            outputs.append(table)
            after.append(inputs[-2])
        sent_x = call(
            functools.partial(pack_x_kernel, g, len(after)),
            "pack_x_" + which,
            x_faces,
            [],
            [values, *after],
            [VMEM] * (1 + len(after)),
        )
        from_x = swap_faces(g, sent_x, g.plane, g.first)
        first, second, *sent = call(
            functools.partial(pack_kernel, g), "pack_" + which, outputs, [], inputs, [VMEM] * len(inputs)
        )
        from_y = swap_faces(g, sent[: len(y_faces)], g.third, g.second)
        first, second = swap(first, 1), reverse(second)
        tables = [sent[-1], swap(sent[-1], 2)] if g.butterfly else [lax.psum(part, "dom")]
        acc = call(
            functools.partial(nonlocal_kernel, g, scale),
            "nonlocal_" + which,
            field,
            [pltpu.VMEM(table.shape, F32), *entries, spread],
            [acc, projf, energy, blk, atom, first, second, *tables],
            [VMEM] * 3 + [HBM] * 2 + [VMEM] * (2 + len(tables)),
        )
        return acc, from_x + from_y

    v, projf, pot, part = call(
        functools.partial(first_kernel, g),
        "tables_first",
        [field, jax.ShapeDtypeStruct(proj.shape, F32), jax.ShapeDtypeStruct(pot.shape, F32), table],
        [
            pltpu.VMEM(orb.shape, F32),
            pltpu.VMEM(proj.shape, BF16),
            pltpu.SemaphoreType.DMA((3,)),
            *entries,
            *sums,
        ],
        [orb, proj, pot, blk, atom],
        [HBM] * 5,
    )
    acc, received = local_and_ends(1.0, "first", v, [], part)
    u, part = call(
        functools.partial(middle_kernel, g),
        "tables_second",
        [field, table],
        [*entries, *sums],
        [acc, projf, blk, atom, *received],
        [VMEM] * 2 + [HBM] * 2 + [VMEM] * len(received),
    )
    acc, received = local_and_ends(2.0, "second", u, [v], part)
    weights = call(
        functools.partial(panel_kernel, g),
        "panel",
        jax.ShapeDtypeStruct((16 * g.no, 32 * g.no), BF16),
        [],
        [panel],
        [VMEM],
    )
    rotated = None
    pieces = []
    parts = halves(g, 0)
    for number, (_, count) in enumerate(parts):
        inputs = [acc, *received[nx:]] if number < len(parts) - 1 else [acc, *received]
        filtered = call(
            functools.partial(last_kernel, g, number),
            "filtered_%d" % number,
            jax.ShapeDtypeStruct((count * g.slab, g.cz), BF16),
            [pltpu.VMEM((g.flat, g.cz), F32)],
            inputs,
            [VMEM] * len(inputs),
        )
        pieces.append((filtered, lax.ppermute(filtered, "band", [(0, 1), (1, 0)]), count))
    for number, (filtered, other, count) in enumerate(pieces):
        inputs = [filtered, other, weights] + ([] if rotated is None else [rotated])
        rotated = call(
            functools.partial(rotate_kernel, g, number),
            "rotate_%d" % number,
            jax.ShapeDtypeStruct((g.no, g.rows, g.cz), F32),
            [pltpu.VMEM((g.no, count * g.cy, g.cz), F32), pltpu.SemaphoreType.DMA((count * g.cy // 16,))],
            inputs,
            [VMEM] * 3 + [HBM] * (len(inputs) - 3),
            out_specs=HBM,
            input_output_aliases={} if rotated is None else {3: 0},
        )
    return rotated.reshape(orbitals.shape)


def solution(mesh):
    in_specs = (
        P("dom", "band", None, None, None),
        P("dom", None, None, None),
        P("dom", None, None),
        P("dom"),
        P("dom"),
        P(),
        P(),
    )
    out_specs = P("dom", "band", None, None, None)
    return jax.shard_map(shards, mesh=mesh, in_specs=in_specs, out_specs=out_specs, check_vma=False)
```

```python
import functools

import jax
import jax.numpy as jnp
from jax import lax
from jax.experimental import pallas as pl
from jax.experimental.pallas import tpu as pltpu
from jax.sharding import PartitionSpec as P

RADIUS = 6
COEFFS = (
    -5369.0 / 1800.0,
    12.0 / 7.0,
    -15.0 / 56.0,
    10.0 / 189.0,
    -1.0 / 112.0,
    2.0 / 1925.0,
    -1.0 / 16632.0,
)
KINETIC = -3.125
CENTER = 36.0
HALF_WIDTH = 34.0
WEIGHT = [KINETIC * c / HALF_WIDTH for c in COEFFS]
DIAGONAL = (3.0 * KINETIC * COEFFS[0] - CENTER) / HALF_WIDTH

F32 = jnp.float32
BF16 = jnp.bfloat16
VMEM = pl.BlockSpec(memory_space=pltpu.VMEM)
HBM = pl.BlockSpec(memory_space=pltpu.HBM)
NT = (((1,), (1,)), ((), ()))
TN = (((0,), (0,)), ((), ()))
NN = (((1,), (0,)), ((), ()))


def split2(x):
    high = x.astype(BF16)
    low = (x - high.astype(F32)).astype(BF16)
    return high, low


def iota(shape, dim):
    return lax.broadcasted_iota(jnp.int32, shape, dim)


def weight_at(distance, scale):
    out = jnp.zeros(distance.shape, F32)
    for k in range(1, RADIUS + 1):
        out = jnp.where(distance == k, scale * WEIGHT[k], out)
    return out


class Geometry:
    def __init__(self, orbitals, entries, nproj, atoms, dom_count):
        _, self.no, self.cx, self.cy, self.cz = orbitals
        self.rows = self.cx * self.cy
        self.flat = self.rows * self.no
        self.ent = entries
        self.nproj = nproj
        self.dom_count = dom_count
        self.owned = atoms // dom_count
        self.third = 4
        self.second = min(8, dom_count // 8)
        self.plane = self.second * self.third
        self.first = dom_count // self.plane
        self.table = self.owned * nproj * self.no
        self.slab = self.cy * self.no
        self.fold = self.flat // self.table
        self.butterfly = self.first == 2 and self.second == 2 and dom_count <= 2 * self.fold
        assert self.no == 8

    def faces(self, dom, dim):
        if dim == 0:
            extent, place = self.first, dom // self.plane
        else:
            extent, place = self.second, dom // self.third % self.second
        if extent == 2:
            return [(1 - place, None)]
        if extent > 2:
            return [(0, place > 0), (1, place < extent - 1)]
        return []

    def face_rows(self, dim):
        rows = RADIUS * self.slab if dim == 0 else self.cx * RADIUS * self.no
        return [rows] * len(self.faces(0, dim))

    def steps(self, dom):
        out = [0]
        for extent, stride in ((self.first, self.plane), (self.second, self.third), (self.third, 1)):
            if extent == 2:
                out.append((1 - 2 * (dom // stride % 2)) * stride)
            elif extent > 2:
                out.extend([stride, -stride])
        return out

    def slots(self):
        return len(self.steps(0))


def layer(side, length, j):
    if isinstance(side, int):
        return length - 1 - j if side else j
    return side * (length - 1 - j) + (1 - side) * j


def aligned(start, unit):
    return start if isinstance(start, int) else pl.multiple_of(start, unit)


def pack_x(g, dom, v_ref, refs):
    for (side, _), out in zip(g.faces(dom, 0), refs):
        for j in range(RADIUS):
            at = aligned(layer(side, g.cx, j) * g.slab, g.slab)
            out[j * g.slab : (j + 1) * g.slab, :] = v_ref[pl.ds(at, g.slab), :].astype(BF16)


def pack_y(g, dom, v_ref, refs):
    size = RADIUS * g.no
    for (side, _), out in zip(g.faces(dom, 1), refs):
        for x in range(g.cx):
            pieces = []
            for j in range(RADIUS):
                at = aligned(x * g.slab + layer(side, g.cy, j) * g.no, g.no)
                pieces.append(v_ref[pl.ds(at, g.no), :])
            out[x * size : (x + 1) * size, :] = jnp.concatenate(pieces, axis=0).astype(BF16)


def end_columns(g, dom):
    row, col = iota((16, g.cz), 0), iota((16, g.cz), 1)
    odd = dom % 2
    side = jnp.where(row < 8, 1 - odd, odd)
    return jnp.where(side == 1, g.cz - 1 - col, col), row


def pack_ends(g, dom, v_ref, first_ref, second_ref):
    inward, row = end_columns(g, dom)
    pick = jnp.where((inward == row % 8) & (row % 8 < RADIUS), 1.0, 0.0).astype(BF16)
    pick = jnp.concatenate([pick, pick], axis=1)
    for x in range(g.cx):
        rows = slice(x * g.slab, (x + 1) * g.slab)
        both = jnp.concatenate(split2(v_ref[rows, :]), axis=1)
        ends = lax.dot_general(pick, both, NT, preferred_element_type=F32)
        first_ref[:, rows] = ends[:8]
        second_ref[:, rows] = ends[8:]


def put_table(g, message, table):
    for n in range(g.dom_count):
        at = RADIUS + n // g.fold
        lanes = n % g.fold * g.table
        message[at : at + 1, lanes : lanes + g.table] = table[n : n + 1, :]


def get_table(g, message):
    rows = []
    for n in range(g.dom_count):
        at = RADIUS + n // g.fold
        lanes = n % g.fold * g.table
        rows.append(message[at : at + 1, lanes : lanes + g.table])
    return jnp.concatenate(rows, axis=0)


def fill_lut(g, dom, lut):
    for number, step in enumerate(g.steps(dom)):
        lut[g.plane + dom + step] = number * g.owned


def column_of(g, lut, atom):
    if g.owned & (g.owned - 1):
        owner = lax.div(atom, jnp.int32(g.owned))
        return lut[owner + g.plane] + (atom - owner * g.owned)
    owner = lax.shift_right_logical(atom, jnp.int32(g.owned.bit_length() - 1))
    return lut[owner + g.plane] + (atom & (g.owned - 1))


def inner_tables(g, dom, v_ref, projf, blk, atom, lut, sums, table):
    size = g.nproj * g.no

    unroll = 16

    def step(i, _):
        for u in range(unroll):
            part = sums[u % len(sums)]
            e = i * unroll + u
            col = column_of(g, lut, atom[e])
            v = v_ref[pl.ds(pl.multiple_of(blk[e] * g.no, g.no), g.no), :]
            for p in range(g.nproj):
                at = pl.ds(pl.multiple_of(col * size + p * g.no, g.no), g.no)
                coef = jnp.broadcast_to(projf[e, p : p + 1, :], v.shape)
                part[at, :] += v * coef
        return 0

    lax.fori_loop(0, g.ent // unroll, step, 0)
    total = sums[0][...]
    for part in sums[1:]:
        total = total + part[...]
    both = jnp.concatenate(split2(total), axis=1)
    ones = jnp.ones((8, both.shape[1]), BF16)
    summed = lax.dot_general(ones, both, NT, preferred_element_type=F32)
    table[...] = jnp.zeros(table.shape, F32)
    for number, step in enumerate(g.steps(dom)):
        owner = jnp.clip(dom + step, 0, g.dom_count - 1)
        table[pl.ds(owner, 1), :] += summed[0:1, number * g.table : (number + 1) * g.table]


def clear(sums):
    for part in sums:
        part[...] = jnp.zeros(part.shape, F32)


def entry_copies(blk_hbm, atom_hbm, blk, atom, sem):
    copies = [
        pltpu.make_async_copy(blk_hbm, blk, sem.at[0]),
        pltpu.make_async_copy(atom_hbm, atom, sem.at[1]),
    ]
    for copy in copies:
        copy.start()
    return copies


def first_kernel(g, orb_hbm, proj_hbm, pot_hbm, blk_hbm, atom_hbm, v_ref, projf, pot, table, *scratch):
    orb, proj, sem, blk, atom, lut, entry_sem = scratch[:7]
    sums = scratch[7:]
    copies = [
        pltpu.make_async_copy(orb_hbm, orb, sem.at[0]),
        pltpu.make_async_copy(proj_hbm, proj, sem.at[1]),
        pltpu.make_async_copy(pot_hbm, pot, sem.at[2]),
    ]
    for copy in copies:
        copy.start()
    copies += entry_copies(blk_hbm, atom_hbm, blk, atom, entry_sem)
    dom = lax.axis_index("dom")
    fill_lut(g, dom, lut)
    clear(sums)
    copies[1].wait()
    projf[...] = proj[...].astype(F32)
    copies[0].wait()
    for r in range(g.rows):
        v_ref[r * g.no : (r + 1) * g.no, :] = orb[pl.ds(r, g.no, stride=g.rows), :]
    for copy in copies[2:]:
        copy.wait()
    inner_tables(g, dom, v_ref, projf, blk, atom, lut, sums, table)


def pack_kernel(g, v_ref, *refs):
    dom = lax.axis_index("dom")
    if g.butterfly:
        part, from_x, from_y, from_xy = refs[:4]
        group = refs[-1]
        group[...] = (part[...] + from_x[...]) + (from_y[...] + from_xy[...])
        refs = refs[:-1]
    first, second = refs[-2:]
    pack_ends(g, dom, v_ref, first, second)
    if g.butterfly:
        put_table(g, first, group)
        put_table(g, second, group)


def pack_x_kernel(g, nafter, v_ref, *refs):
    pack_x(g, lax.axis_index("dom"), v_ref, refs[nafter:])


def pack_y_kernel(g, nafter, v_ref, *refs):
    pack_y(g, lax.axis_index("dom"), v_ref, refs[nafter:])


def inside_kernel(g, scale, subtract, v_ref, pot, *refs):
    prev, out = refs if subtract else (None, refs[0])
    row, col = iota((g.cz, g.cz), 0), iota((g.cz, g.cz), 1)
    high, low = split2(weight_at(jnp.abs(row - col), scale))
    band = jnp.concatenate([high, low], axis=1)
    band = jnp.concatenate([band, band], axis=0)

    def cell(x, y):
        at = (x * g.cy + y) * g.no
        return v_ref[at : at + g.no, :]

    for x in range(g.cx):
        both = jnp.concatenate(split2(v_ref[x * g.slab : (x + 1) * g.slab, :]), axis=1)
        along = lax.dot_general(both, band, NN, preferred_element_type=F32)
        for y in range(g.cy):
            at = (x * g.cy + y) * g.no
            rows = slice(y * g.no, (y + 1) * g.no)
            here = cell(x, y)
            diag = jnp.broadcast_to(pot[x * g.cy + y : x * g.cy + y + 1, :], here.shape)
            total = along[rows, : g.cz] + along[rows, g.cz :]
            total = total + (scale * DIAGONAL + (scale / HALF_WIDTH) * diag) * here
            if subtract:
                total = total - prev[at : at + g.no, :]
            for k in range(1, RADIUS + 1):
                near = []
                for a, b in ((x - k, y), (x + k, y), (x, y - k), (x, y + k)):
                    if 0 <= a < g.cx and 0 <= b < g.cy:
                        near.append(cell(a, b))
                if near:
                    total = total + (scale * WEIGHT[k]) * sum(near[1:], near[0])
            out[at : at + g.no, :] = total


def flag(present):
    return 1.0 if present is None else jnp.where(present, 1.0, 0.0)


def add_ends(g, dom, scale, acc, low, high, out):
    inward, row = end_columns(g, dom)
    middle = (dom % g.third > 0) & (dom % g.third < g.third - 1)
    present = (row % 8 < RADIUS) & ((row < 8) | middle)
    coef = jnp.where(present, weight_at(inward + row % 8 + 1, scale), 0.0)
    c_high, c_low = split2(coef)
    coefs = jnp.concatenate([c_high, c_high, c_low, c_low], axis=0)
    for x in range(g.cx):
        rows = slice(x * g.slab, (x + 1) * g.slab)
        h_high, h_low = split2(jnp.concatenate([low[:, rows], high[:, rows]], axis=0))
        halo = jnp.concatenate([h_high, h_low, h_high, h_low], axis=0)
        out[rows, :] = acc[rows, :] + lax.dot_general(halo, coefs, TN, preferred_element_type=F32)


def add_x_faces(g, dom, scale, face_refs, out):
    unit = 2 * g.no
    for (side, present), face in zip(g.faces(dom, 0), face_refs):
        for y in range(0, g.cy, 2):
            starts = [j * g.slab + y * g.no for j in range(RADIUS)]
            part = [flag(present) * face[at : at + unit, :].astype(F32) for at in starts]
            for i in range(RADIUS):
                at = aligned(layer(side, g.cx, i) * g.slab + y * g.no, unit)
                total = out[pl.ds(at, unit), :]
                for j in range(RADIUS - i):
                    total = total + (scale * WEIGHT[i + j + 1]) * part[j]
                out[pl.ds(at, unit), :] = total


def add_y_faces(g, dom, scale, face_refs, out):
    size = RADIUS * g.no
    for (side, present), face in zip(g.faces(dom, 1), face_refs):
        for x in range(g.cx):
            part = flag(present) * face[x * size : (x + 1) * size, :].astype(F32)
            for i in range(RADIUS):
                at = aligned(x * g.slab + layer(side, g.cy, i) * g.no, g.no)
                total = out[pl.ds(at, g.no), :]
                for j in range(RADIUS - i):
                    total = total + (scale * WEIGHT[i + j + 1]) * part[j * g.no : (j + 1) * g.no]
                out[pl.ds(at, g.no), :] = total


def add_nonlocal(g, dom, table, energy, projf, blk, atom, lut, spread, out):
    size = g.nproj * g.no
    lanes = g.table
    count = g.slots()
    rows = []
    for step in g.steps(dom):
        owner = pl.ds(jnp.clip(dom + step, 0, g.dom_count - 1), 1)
        rows.append(table[owner, :] * energy[owner, :])
    rows.append(jnp.zeros((8 - count, lanes), F32))
    scaled = jnp.concatenate(rows, axis=0)
    high = scaled.astype(BF16)
    rest = scaled - high.astype(F32)
    mid = rest.astype(BF16)
    low = (rest - mid.astype(F32)).astype(BF16)
    parts = jnp.concatenate([high, mid, low], axis=0)
    wide = count * g.cz
    row, col = iota((24, wide), 0), iota((24, wide), 1)
    ones = jnp.where(row % 8 == col // g.cz, 1.0, 0.0).astype(BF16)
    out_all = lax.dot_general(parts, ones, TN, preferred_element_type=F32)
    for number in range(count):
        spread[number * lanes : (number + 1) * lanes, :] = out_all[:, number * g.cz : (number + 1) * g.cz]
    unroll = 16

    def step(i, _):
        additions = []
        for u in range(unroll):
            e = i * unroll + u
            col = column_of(g, lut, atom[e])
            total = None
            for p in range(g.nproj):
                at = pl.ds(pl.multiple_of(col * size + p * g.no, g.no), g.no)
                coef = jnp.broadcast_to(projf[e, p : p + 1, :], (g.no, g.cz))
                term = spread[at, :] * coef
                total = term if total is None else total + term
            additions.append((pl.ds(pl.multiple_of(blk[e] * g.no, g.no), g.no), total))
        for at, total in additions:
            out[at, :] += total
        return 0

    lax.fori_loop(0, g.ent // unroll, step, 0)


def nonlocal_kernel(g, scale, acc, projf, energy, blk_hbm, atom_hbm, first, second, *refs):
    out, table, blk, atom, lut, sem, spread = refs[-7:]
    copies = entry_copies(blk_hbm, atom_hbm, blk, atom, sem)
    dom = lax.axis_index("dom")
    fill_lut(g, dom, lut)
    if g.butterfly:
        group, opposite = refs[:2]
        table[...] = (group[...] + get_table(g, first)) + (get_table(g, second) + opposite[...])
    else:
        table[...] = refs[0][...]
    add_ends(g, dom, scale, acc, first, second, out)
    for copy in copies:
        copy.wait()
    add_nonlocal(g, dom, table, energy, projf, blk, atom, lut, spread, out)


def middle_kernel(g, acc, projf, blk_hbm, atom_hbm, *refs):
    nx, ny = len(g.face_rows(0)), len(g.face_rows(1))
    faces = refs[: nx + ny]
    u_ref, table, blk, atom, lut, sem = refs[nx + ny : nx + ny + 6]
    sums = refs[nx + ny + 6 :]
    copies = entry_copies(blk_hbm, atom_hbm, blk, atom, sem)
    dom = lax.axis_index("dom")
    fill_lut(g, dom, lut)
    clear(sums)
    u_ref[...] = acc[...]
    add_x_faces(g, dom, 1.0, faces[:nx], u_ref)
    add_y_faces(g, dom, 1.0, faces[nx:], u_ref)
    for copy in copies:
        copy.wait()
    inner_tables(g, dom, u_ref, projf, blk, atom, lut, sums, table)


def halves(g, dom):
    if g.first != 2 or g.cx != 2 * RADIUS:
        return [(0, g.cx)]
    side = 1 - dom // g.plane
    return [((1 - side) * RADIUS, RADIUS), (side * RADIUS, RADIUS)]


def last_kernel(g, number, acc, *refs):
    nx = len(g.face_rows(0))
    filtered, work = refs[-2:]
    refs = refs[:-2]
    dom = lax.axis_index("dom")
    parts = halves(g, dom)
    start, count = parts[number]
    work[...] = acc[...]
    if number == len(parts) - 1:
        add_x_faces(g, dom, 2.0, refs[:nx], work)
        refs = refs[nx:]
    add_y_faces(g, dom, 2.0, refs, work)
    at = aligned(start * g.slab, g.slab)
    filtered[...] = work[pl.ds(at, count * g.slab), :].astype(BF16)


def panel_kernel(g, panel, weights):
    band = lax.axis_index("band")
    group = 16
    span = group * g.no
    norb = panel.shape[0]
    row, col = iota((span, norb), 0), iota((span, norb), 1)
    pick_out = jnp.where(col == band * g.no + row // group, 1.0, 0.0).astype(BF16)
    picked = lax.dot_general(pick_out, panel[...], NT, preferred_element_type=F32).astype(BF16)
    row, col = iota((norb, 2 * span), 0), iota((norb, 2 * span), 1)
    source = jnp.where(col < span, band, 1 - band) * g.no + col % g.no
    pick_in = jnp.where(row == source, 1.0, 0.0).astype(BF16)
    spread = lax.dot_general(picked, pick_in, NN, preferred_element_type=F32)
    row, col = iota((span, 2 * span), 0), iota((span, 2 * span), 1)
    same = row % group == (col % span) // g.no
    weights[...] = jnp.where(same, spread, 0.0).astype(BF16)


def rotate_kernel(g, number, own, other, weights, *refs):
    out_hbm, out, sem = refs[-3:]
    start, count = halves(g, lax.axis_index("dom"))[number]
    group = 16
    span = group * g.no
    copies = []
    size = count * g.cy
    for n in range(size // group):
        rows = slice(n * span, (n + 1) * span)
        both = jnp.concatenate([own[rows, :], other[rows, :]], axis=0)
        result = lax.dot_general(weights[...], both, NN, preferred_element_type=F32)
        for j in range(g.no):
            out[j, n * group : (n + 1) * group, :] = result[j * group : (j + 1) * group, :]
        to = pl.ds(aligned(start * g.cy + n * group, group), group)
        source = out.at[:, pl.ds(n * group, group), :]
        copies.append(pltpu.make_async_copy(source, out_hbm.at[:, to, :], sem.at[n]))
        copies[-1].start()
    for copy in copies:
        copy.wait()


def call(kernel, name, out_shape, scratch, args, specs, **options):
    return pl.pallas_call(
        kernel,
        name=name,
        out_shape=out_shape,
        in_specs=specs,
        out_specs=options.pop("out_specs", jax.tree.map(lambda _: VMEM, out_shape)),
        scratch_shapes=scratch,
        compiler_params=pltpu.CompilerParams(vmem_limit_bytes=48 * 1024 * 1024),
        cost_estimate=pl.CostEstimate(flops=1000, bytes_accessed=1000, transcendentals=0),
        **options,
    )(*args)


def shift(g, array, stride, extent, step):
    pairs = []
    for i in range(g.dom_count):
        place = i // stride % extent
        pairs.append((i, i + ((place + step) % extent - place) * stride))
    return lax.ppermute(array, "dom", pairs)


def swap_faces(g, faces, stride, extent):
    if extent == 2:
        return [shift(g, faces[0], stride, extent, 1)]
    if extent > 2:
        return [shift(g, faces[1], stride, extent, 1), shift(g, faces[0], stride, extent, -1)]
    return []


def shards(orbitals, potential, projectors, entry_atom, entry_block, kb_energy, panel):
    g = Geometry(
        orbitals.shape, projectors.shape[0], projectors.shape[1], kb_energy.shape[0], lax.axis_size("dom")
    )

    def in_hbm(array):
        return pltpu.with_memory_space_constraint(array, pltpu.HBM)

    orb = in_hbm(orbitals.reshape(g.flat, g.cz))
    pot = in_hbm(potential.reshape(g.rows, g.cz))
    proj = in_hbm(projectors)
    blk, atom = in_hbm(entry_block), in_hbm(entry_atom)
    field = jax.ShapeDtypeStruct((g.flat, g.cz), F32)
    x_faces = [jax.ShapeDtypeStruct((n, g.cz), BF16) for n in g.face_rows(0)]
    y_faces = [jax.ShapeDtypeStruct((n, g.cz), BF16) for n in g.face_rows(1)]
    nx = len(x_faces)
    ends = jax.ShapeDtypeStruct((8, g.flat), F32)
    table = jax.ShapeDtypeStruct((g.dom_count, g.table), F32)
    entries = [
        pltpu.SMEM((g.ent,), jnp.int32),
        pltpu.SMEM((g.ent,), jnp.int32),
        pltpu.SMEM((g.dom_count + 2 * g.plane,), jnp.int32),
        pltpu.SemaphoreType.DMA((2,)),
    ]
    slots = g.slots() * g.table
    sums = [pltpu.VMEM((slots, g.cz), F32) for _ in range(4)]
    spread = pltpu.VMEM((slots, g.cz), F32)
    indices = range(g.dom_count)

    def swap(array, *strides):
        pairs = [(i, i + sum(s * (1 - 2 * (i // s % 2)) for s in strides)) for i in indices]
        return lax.ppermute(array, "dom", pairs)

    def reverse(array):
        pairs = [(i, i - i % g.third + g.third - 1 - i % g.third) for i in indices]
        return lax.ppermute(array, "dom", pairs)

    def local_and_ends(scale, which, values, prev, part):
        energy = (scale / HALF_WIDTH) * kb_energy
        energy = jnp.repeat(energy.reshape(g.dom_count, g.owned * g.nproj), g.no, axis=1)
        acc = call(
            functools.partial(inside_kernel, g, scale, len(prev) > 0),
            "inside_" + which,
            field,
            [],
            [values, pot, *prev],
            [VMEM] * (2 + len(prev)),
        )

        def layers(dim, shapes, after):
            kernel = (pack_x_kernel, pack_y_kernel)[dim]
            return call(
                functools.partial(kernel, g, len(after)),
                "pack_%s_%s" % ("xy"[dim], which),
                shapes,
                [],
                [values, *after],
                [VMEM] * (1 + len(after)),
            )

        inputs = [values]
        outputs = [ends, ends]
        if g.butterfly:
            inputs += [part, swap(part, g.plane), swap(part, g.third), swap(part, g.plane, g.third)]
            outputs.append(table)
        if not prev:
            sent_x = layers(0, x_faces, inputs[-2:-1])
            inputs += [energy]
        first, second, *sent = call(
            functools.partial(pack_kernel, g), "pack_" + which, outputs, [], inputs, [VMEM] * len(inputs)
        )
        sent_first = first
        first, second = swap(first, 1), reverse(second)
        from_y = swap_faces(g, layers(1, y_faces, [first if prev else sent_first]), g.third, g.second)
        if prev:
            sent_x = layers(0, x_faces, [first])
        from_x = swap_faces(g, sent_x, g.plane, g.first)
        tables = [sent[-1], swap(sent[-1], 2)] if g.butterfly else [lax.psum(part, "dom")]
        acc = call(
            functools.partial(nonlocal_kernel, g, scale),
            "nonlocal_" + which,
            field,
            [pltpu.VMEM(table.shape, F32), *entries, spread],
            [acc, projf, energy, blk, atom, first, second, *tables],
            [VMEM] * 3 + [HBM] * 2 + [VMEM] * (2 + len(tables)),
        )
        return acc, from_x + from_y

    v, projf, pot, part = call(
        functools.partial(first_kernel, g),
        "tables_first",
        [field, jax.ShapeDtypeStruct(proj.shape, F32), jax.ShapeDtypeStruct(pot.shape, F32), table],
        [
            pltpu.VMEM(orb.shape, F32),
            pltpu.VMEM(proj.shape, BF16),
            pltpu.SemaphoreType.DMA((3,)),
            *entries,
            *sums,
        ],
        [orb, proj, pot, blk, atom],
        [HBM] * 5,
    )
    acc, received = local_and_ends(1.0, "first", v, [], part)
    u, part = call(
        functools.partial(middle_kernel, g),
        "tables_second",
        [field, table],
        [*entries, *sums],
        [acc, projf, blk, atom, *received],
        [VMEM] * 2 + [HBM] * 2 + [VMEM] * len(received),
    )
    acc, received = local_and_ends(2.0, "second", u, [v], part)
    weights = call(
        functools.partial(panel_kernel, g),
        "panel",
        jax.ShapeDtypeStruct((16 * g.no, 32 * g.no), BF16),
        [],
        [panel],
        [VMEM],
    )
    rotated = None
    pieces = []
    parts = halves(g, 0)
    for number, (_, count) in enumerate(parts):
        inputs = [acc, *received[nx:]] if number < len(parts) - 1 else [acc, *received]
        filtered = call(
            functools.partial(last_kernel, g, number),
            "filtered_%d" % number,
            jax.ShapeDtypeStruct((count * g.slab, g.cz), BF16),
            [pltpu.VMEM((g.flat, g.cz), F32)],
            inputs,
            [VMEM] * len(inputs),
        )
        pieces.append((filtered, lax.ppermute(filtered, "band", [(0, 1), (1, 0)]), count))
    for number, (filtered, other, count) in enumerate(pieces):
        inputs = [filtered, other, weights] + ([] if rotated is None else [rotated])
        rotated = call(
            functools.partial(rotate_kernel, g, number),
            "rotate_%d" % number,
            jax.ShapeDtypeStruct((g.no, g.rows, g.cz), F32),
            [pltpu.VMEM((g.no, count * g.cy, g.cz), F32), pltpu.SemaphoreType.DMA((count * g.cy // 16,))],
            inputs,
            [VMEM] * 3 + [HBM] * (len(inputs) - 3),
            out_specs=HBM,
            input_output_aliases={} if rotated is None else {3: 0},
        )
    return rotated.reshape(orbitals.shape)


def solution(mesh):
    in_specs = (
        P("dom", "band", None, None, None),
        P("dom", None, None, None),
        P("dom", None, None),
        P("dom"),
        P("dom"),
        P(),
        P(),
    )
    out_specs = P("dom", "band", None, None, None)
    return jax.shard_map(shards, mesh=mesh, in_specs=in_specs, out_specs=out_specs, check_vma=False)
```

```python
import functools

import jax
import jax.numpy as jnp
from jax import lax
from jax.experimental import pallas as pl
from jax.experimental.pallas import tpu as pltpu
from jax.sharding import PartitionSpec as P

RADIUS = 6
COEFFS = (
    -5369.0 / 1800.0,
    12.0 / 7.0,
    -15.0 / 56.0,
    10.0 / 189.0,
    -1.0 / 112.0,
    2.0 / 1925.0,
    -1.0 / 16632.0,
)
KINETIC = -3.125
CENTER = 36.0
HALF_WIDTH = 34.0
WEIGHT = [KINETIC * c / HALF_WIDTH for c in COEFFS]
DIAGONAL = (3.0 * KINETIC * COEFFS[0] - CENTER) / HALF_WIDTH

F32 = jnp.float32
BF16 = jnp.bfloat16
VMEM = pl.BlockSpec(memory_space=pltpu.VMEM)
HBM = pl.BlockSpec(memory_space=pltpu.HBM)
NT = (((1,), (1,)), ((), ()))
TN = (((0,), (0,)), ((), ()))
NN = (((1,), (0,)), ((), ()))


def split2(x):
    high = x.astype(BF16)
    low = (x - high.astype(F32)).astype(BF16)
    return high, low


def iota(shape, dim):
    return lax.broadcasted_iota(jnp.int32, shape, dim)


def weight_at(distance, scale):
    out = jnp.zeros(distance.shape, F32)
    for k in range(1, RADIUS + 1):
        out = jnp.where(distance == k, scale * WEIGHT[k], out)
    return out


class Geometry:
    def __init__(self, orbitals, entries, nproj, atoms, dom_count):
        _, self.no, self.cx, self.cy, self.cz = orbitals
        self.rows = self.cx * self.cy
        self.flat = self.rows * self.no
        self.ent = entries
        self.nproj = nproj
        self.dom_count = dom_count
        self.owned = atoms // dom_count
        self.third = 4
        self.second = min(8, dom_count // 8)
        self.plane = self.second * self.third
        self.first = dom_count // self.plane
        self.table = self.owned * nproj * self.no
        self.slab = self.cy * self.no
        self.fold = self.flat // self.table
        self.butterfly = self.first == 2 and self.second == 2 and dom_count <= 2 * self.fold
        assert self.no == 8

    def faces(self, dom, dim):
        if dim == 0:
            extent, place = self.first, dom // self.plane
        else:
            extent, place = self.second, dom // self.third % self.second
        if extent == 2:
            return [(1 - place, None)]
        if extent > 2:
            return [(0, place > 0), (1, place < extent - 1)]
        return []

    def face_rows(self, dim):
        rows = RADIUS * self.slab if dim == 0 else self.cx * RADIUS * self.no
        return [rows] * len(self.faces(0, dim))

    def steps(self, dom):
        out = [0]
        for extent, stride in ((self.first, self.plane), (self.second, self.third), (self.third, 1)):
            if extent == 2:
                out.append((1 - 2 * (dom // stride % 2)) * stride)
            elif extent > 2:
                out.extend([stride, -stride])
        return out

    def slots(self):
        return len(self.steps(0))


def layer(side, length, j):
    if isinstance(side, int):
        return length - 1 - j if side else j
    return side * (length - 1 - j) + (1 - side) * j


def aligned(start, unit):
    return start if isinstance(start, int) else pl.multiple_of(start, unit)


def pack_x(g, dom, v_ref, refs):
    for (side, _), out in zip(g.faces(dom, 0), refs):
        for j in range(RADIUS):
            at = aligned(layer(side, g.cx, j) * g.slab, g.slab)
            out[j * g.slab : (j + 1) * g.slab, :] = v_ref[pl.ds(at, g.slab), :].astype(BF16)


def pack_y(g, dom, v_ref, refs):
    size = RADIUS * g.no
    for (side, _), out in zip(g.faces(dom, 1), refs):
        for x in range(g.cx):
            pieces = []
            for j in range(RADIUS):
                at = aligned(x * g.slab + layer(side, g.cy, j) * g.no, g.no)
                pieces.append(v_ref[pl.ds(at, g.no), :])
            out[x * size : (x + 1) * size, :] = jnp.concatenate(pieces, axis=0).astype(BF16)


def end_columns(g, dom):
    row, col = iota((16, g.cz), 0), iota((16, g.cz), 1)
    odd = dom % 2
    side = jnp.where(row < 8, 1 - odd, odd)
    return jnp.where(side == 1, g.cz - 1 - col, col), row


def pack_ends(g, dom, v_ref, first_ref, second_ref):
    inward, row = end_columns(g, dom)
    pick = jnp.where((inward == row % 8) & (row % 8 < RADIUS), 1.0, 0.0).astype(BF16)
    pick = jnp.concatenate([pick, pick], axis=1)
    for x in range(g.cx):
        rows = slice(x * g.slab, (x + 1) * g.slab)
        both = jnp.concatenate(split2(v_ref[rows, :]), axis=1)
        ends = lax.dot_general(pick, both, NT, preferred_element_type=F32)
        first_ref[:, rows] = ends[:8]
        second_ref[:, rows] = ends[8:]


def put_table(g, message, table):
    for n in range(g.dom_count):
        at = RADIUS + n // g.fold
        lanes = n % g.fold * g.table
        message[at : at + 1, lanes : lanes + g.table] = table[n : n + 1, :]


def get_table(g, message):
    rows = []
    for n in range(g.dom_count):
        at = RADIUS + n // g.fold
        lanes = n % g.fold * g.table
        rows.append(message[at : at + 1, lanes : lanes + g.table])
    return jnp.concatenate(rows, axis=0)


def fill_lut(g, dom, lut):
    for number, step in enumerate(g.steps(dom)):
        lut[g.plane + dom + step] = number * g.owned


def column_of(g, lut, atom):
    if g.owned & (g.owned - 1):
        owner = lax.div(atom, jnp.int32(g.owned))
        return lut[owner + g.plane] + (atom - owner * g.owned)
    owner = lax.shift_right_logical(atom, jnp.int32(g.owned.bit_length() - 1))
    return lut[owner + g.plane] + (atom & (g.owned - 1))


def inner_tables(g, dom, v_ref, projf, blk, atom, lut, sums, table):
    size = g.nproj * g.no

    unroll = 16

    def step(i, _):
        for u in range(unroll):
            part = sums[u % len(sums)]
            e = i * unroll + u
            col = column_of(g, lut, atom[e])
            v = v_ref[pl.ds(pl.multiple_of(blk[e] * g.no, g.no), g.no), :]
            for p in range(g.nproj):
                at = pl.ds(pl.multiple_of(col * size + p * g.no, g.no), g.no)
                coef = jnp.broadcast_to(projf[e, p : p + 1, :], v.shape)
                part[at, :] += v * coef
        return 0

    lax.fori_loop(0, g.ent // unroll, step, 0)
    total = sums[0][...]
    for part in sums[1:]:
        total = total + part[...]
    both = jnp.concatenate(split2(total), axis=1)
    ones = jnp.ones((8, both.shape[1]), BF16)
    summed = lax.dot_general(ones, both, NT, preferred_element_type=F32)
    table[...] = jnp.zeros(table.shape, F32)
    for number, step in enumerate(g.steps(dom)):
        owner = jnp.clip(dom + step, 0, g.dom_count - 1)
        table[pl.ds(owner, 1), :] += summed[0:1, number * g.table : (number + 1) * g.table]


def clear(sums):
    for part in sums:
        part[...] = jnp.zeros(part.shape, F32)


def entry_copies(blk_hbm, atom_hbm, blk, atom, sem):
    copies = [
        pltpu.make_async_copy(blk_hbm, blk, sem.at[0]),
        pltpu.make_async_copy(atom_hbm, atom, sem.at[1]),
    ]
    for copy in copies:
        copy.start()
    return copies


def first_kernel(g, orb_hbm, proj_hbm, pot_hbm, blk_hbm, atom_hbm, v_ref, projf, pot, table, *scratch):
    orb, proj, sem, blk, atom, lut, entry_sem = scratch[:7]
    sums = scratch[7:]
    copies = [
        pltpu.make_async_copy(orb_hbm, orb, sem.at[0]),
        pltpu.make_async_copy(proj_hbm, proj, sem.at[1]),
        pltpu.make_async_copy(pot_hbm, pot, sem.at[2]),
    ]
    for copy in copies:
        copy.start()
    copies += entry_copies(blk_hbm, atom_hbm, blk, atom, entry_sem)
    dom = lax.axis_index("dom")
    fill_lut(g, dom, lut)
    clear(sums)
    copies[1].wait()
    projf[...] = proj[...].astype(F32)
    copies[0].wait()
    for r in range(g.rows):
        v_ref[r * g.no : (r + 1) * g.no, :] = orb[pl.ds(r, g.no, stride=g.rows), :]
    for copy in copies[2:]:
        copy.wait()
    inner_tables(g, dom, v_ref, projf, blk, atom, lut, sums, table)


def add_kernel(g, a, b, *refs):
    refs[-1][...] = a[...] + b[...]


def pack_kernel(g, v_ref, *refs):
    dom = lax.axis_index("dom")
    ny = len(g.face_rows(1))
    if g.butterfly:
        a, b = refs[:2]
        group = refs[-1]
        group[...] = a[...] + b[...]
        refs = refs[:-1]
    inner, outer = refs[len(refs) - ny - 2 : len(refs) - ny]
    pack_y(g, dom, v_ref, refs[len(refs) - ny :])
    pack_ends(g, dom, v_ref, inner, outer)
    if g.butterfly:
        put_table(g, outer, group)


def join_kernel(g, table, outer_in, inner, table_out, inner_out):
    table_out[...] = table[...] + get_table(g, outer_in)
    inner_out[...] = inner[...]
    put_table(g, inner_out, table_out)


def pack_x_kernel(g, nafter, v_ref, *refs):
    pack_x(g, lax.axis_index("dom"), v_ref, refs[nafter:])


def inside_kernel(g, scale, subtract, v_ref, pot, *refs):
    prev, out = refs if subtract else (None, refs[0])
    row, col = iota((g.cz, g.cz), 0), iota((g.cz, g.cz), 1)
    high, low = split2(weight_at(jnp.abs(row - col), scale))
    band = jnp.concatenate([high, low], axis=1)
    band = jnp.concatenate([band, band], axis=0)

    def cell(x, y):
        at = (x * g.cy + y) * g.no
        return v_ref[at : at + g.no, :]

    for x in range(g.cx):
        both = jnp.concatenate(split2(v_ref[x * g.slab : (x + 1) * g.slab, :]), axis=1)
        along = lax.dot_general(both, band, NN, preferred_element_type=F32)
        for y in range(g.cy):
            at = (x * g.cy + y) * g.no
            rows = slice(y * g.no, (y + 1) * g.no)
            here = cell(x, y)
            diag = jnp.broadcast_to(pot[x * g.cy + y : x * g.cy + y + 1, :], here.shape)
            total = along[rows, : g.cz] + along[rows, g.cz :]
            total = total + (scale * DIAGONAL + (scale / HALF_WIDTH) * diag) * here
            if subtract:
                total = total - prev[at : at + g.no, :]
            for k in range(1, RADIUS + 1):
                near = []
                for a, b in ((x - k, y), (x + k, y), (x, y - k), (x, y + k)):
                    if 0 <= a < g.cx and 0 <= b < g.cy:
                        near.append(cell(a, b))
                if near:
                    total = total + (scale * WEIGHT[k]) * sum(near[1:], near[0])
            out[at : at + g.no, :] = total


def flag(present):
    return 1.0 if present is None else jnp.where(present, 1.0, 0.0)


def add_ends(g, dom, scale, acc, low, high, out):
    inward, row = end_columns(g, dom)
    middle = (dom % g.third > 0) & (dom % g.third < g.third - 1)
    present = (row % 8 < RADIUS) & ((row < 8) | middle)
    coef = jnp.where(present, weight_at(inward + row % 8 + 1, scale), 0.0)
    c_high, c_low = split2(coef)
    coefs = jnp.concatenate([c_high, c_high, c_low, c_low], axis=0)
    for x in range(g.cx):
        rows = slice(x * g.slab, (x + 1) * g.slab)
        h_high, h_low = split2(jnp.concatenate([low[:, rows], high[:, rows]], axis=0))
        halo = jnp.concatenate([h_high, h_low, h_high, h_low], axis=0)
        out[rows, :] = acc[rows, :] + lax.dot_general(halo, coefs, TN, preferred_element_type=F32)


def add_x_faces(g, dom, scale, face_refs, out):
    unit = 2 * g.no
    for (side, present), face in zip(g.faces(dom, 0), face_refs):
        for y in range(0, g.cy, 2):
            starts = [j * g.slab + y * g.no for j in range(RADIUS)]
            part = [flag(present) * face[at : at + unit, :].astype(F32) for at in starts]
            for i in range(RADIUS):
                at = aligned(layer(side, g.cx, i) * g.slab + y * g.no, unit)
                total = out[pl.ds(at, unit), :]
                for j in range(RADIUS - i):
                    total = total + (scale * WEIGHT[i + j + 1]) * part[j]
                out[pl.ds(at, unit), :] = total


def add_y_faces(g, dom, scale, face_refs, out):
    size = RADIUS * g.no
    for (side, present), face in zip(g.faces(dom, 1), face_refs):
        for x in range(g.cx):
            part = flag(present) * face[x * size : (x + 1) * size, :].astype(F32)
            for i in range(RADIUS):
                at = aligned(x * g.slab + layer(side, g.cy, i) * g.no, g.no)
                total = out[pl.ds(at, g.no), :]
                for j in range(RADIUS - i):
                    total = total + (scale * WEIGHT[i + j + 1]) * part[j * g.no : (j + 1) * g.no]
                out[pl.ds(at, g.no), :] = total


def add_nonlocal(g, dom, table, energy, projf, blk, atom, lut, spread, out):
    size = g.nproj * g.no
    lanes = g.table
    count = g.slots()
    rows = []
    for step in g.steps(dom):
        owner = pl.ds(jnp.clip(dom + step, 0, g.dom_count - 1), 1)
        rows.append(table[owner, :] * energy[owner, :])
    rows.append(jnp.zeros((8 - count, lanes), F32))
    scaled = jnp.concatenate(rows, axis=0)
    high = scaled.astype(BF16)
    rest = scaled - high.astype(F32)
    mid = rest.astype(BF16)
    low = (rest - mid.astype(F32)).astype(BF16)
    parts = jnp.concatenate([high, mid, low], axis=0)
    wide = count * g.cz
    row, col = iota((24, wide), 0), iota((24, wide), 1)
    ones = jnp.where(row % 8 == col // g.cz, 1.0, 0.0).astype(BF16)
    out_all = lax.dot_general(parts, ones, TN, preferred_element_type=F32)
    for number in range(count):
        spread[number * lanes : (number + 1) * lanes, :] = out_all[:, number * g.cz : (number + 1) * g.cz]
    unroll = 16

    def step(i, _):
        additions = []
        for u in range(unroll):
            e = i * unroll + u
            col = column_of(g, lut, atom[e])
            total = None
            for p in range(g.nproj):
                at = pl.ds(pl.multiple_of(col * size + p * g.no, g.no), g.no)
                coef = jnp.broadcast_to(projf[e, p : p + 1, :], (g.no, g.cz))
                term = spread[at, :] * coef
                total = term if total is None else total + term
            additions.append((pl.ds(pl.multiple_of(blk[e] * g.no, g.no), g.no), total))
        for at, total in additions:
            out[at, :] += total
        return 0

    lax.fori_loop(0, g.ent // unroll, step, 0)


def nonlocal_kernel(g, scale, acc, projf, energy, blk_hbm, atom_hbm, first, second, *refs):
    out, table, blk, atom, lut, sem, spread = refs[-7:]
    copies = entry_copies(blk_hbm, atom_hbm, blk, atom, sem)
    dom = lax.axis_index("dom")
    fill_lut(g, dom, lut)
    table[...] = refs[0][...]
    if g.butterfly:
        table[...] += get_table(g, first)
    add_ends(g, dom, scale, acc, first, second, out)
    for copy in copies:
        copy.wait()
    add_nonlocal(g, dom, table, energy, projf, blk, atom, lut, spread, out)


def middle_kernel(g, acc, projf, blk_hbm, atom_hbm, *refs):
    nx, ny = len(g.face_rows(0)), len(g.face_rows(1))
    faces = refs[: nx + ny]
    u_ref, table, blk, atom, lut, sem = refs[nx + ny : nx + ny + 6]
    sums = refs[nx + ny + 6 :]
    copies = entry_copies(blk_hbm, atom_hbm, blk, atom, sem)
    dom = lax.axis_index("dom")
    fill_lut(g, dom, lut)
    clear(sums)
    u_ref[...] = acc[...]
    add_x_faces(g, dom, 1.0, faces[:nx], u_ref)
    add_y_faces(g, dom, 1.0, faces[nx:], u_ref)
    for copy in copies:
        copy.wait()
    inner_tables(g, dom, u_ref, projf, blk, atom, lut, sums, table)


def halves(g, dom):
    if g.first != 2 or g.cx != 2 * RADIUS:
        return [(0, g.cx)]
    side = 1 - dom // g.plane
    return [((1 - side) * RADIUS, RADIUS), (side * RADIUS, RADIUS)]


def last_kernel(g, number, acc, *refs):
    nx = len(g.face_rows(0))
    filtered, work = refs[-2:]
    refs = refs[:-2]
    dom = lax.axis_index("dom")
    parts = halves(g, dom)
    start, count = parts[number]
    work[...] = acc[...]
    if number == len(parts) - 1:
        add_x_faces(g, dom, 2.0, refs[:nx], work)
        refs = refs[nx:]
    add_y_faces(g, dom, 2.0, refs, work)
    at = aligned(start * g.slab, g.slab)
    filtered[...] = work[pl.ds(at, count * g.slab), :].astype(BF16)


def panel_kernel(g, panel, weights):
    band = lax.axis_index("band")
    group = 16
    span = group * g.no
    norb = panel.shape[0]
    row, col = iota((span, norb), 0), iota((span, norb), 1)
    pick_out = jnp.where(col == band * g.no + row // group, 1.0, 0.0).astype(BF16)
    picked = lax.dot_general(pick_out, panel[...], NT, preferred_element_type=F32).astype(BF16)
    row, col = iota((norb, 2 * span), 0), iota((norb, 2 * span), 1)
    source = jnp.where(col < span, band, 1 - band) * g.no + col % g.no
    pick_in = jnp.where(row == source, 1.0, 0.0).astype(BF16)
    spread = lax.dot_general(picked, pick_in, NN, preferred_element_type=F32)
    row, col = iota((span, 2 * span), 0), iota((span, 2 * span), 1)
    same = row % group == (col % span) // g.no
    weights[...] = jnp.where(same, spread, 0.0).astype(BF16)


def rotate_kernel(g, number, own, other, weights, *refs):
    out_hbm, out, sem = refs[-3:]
    start, count = halves(g, lax.axis_index("dom"))[number]
    group = 16
    span = group * g.no
    copies = []
    size = count * g.cy
    for n in range(size // group):
        rows = slice(n * span, (n + 1) * span)
        both = jnp.concatenate([own[rows, :], other[rows, :]], axis=0)
        result = lax.dot_general(weights[...], both, NN, preferred_element_type=F32)
        for j in range(g.no):
            out[j, n * group : (n + 1) * group, :] = result[j * group : (j + 1) * group, :]
        to = pl.ds(aligned(start * g.cy + n * group, group), group)
        source = out.at[:, pl.ds(n * group, group), :]
        copies.append(pltpu.make_async_copy(source, out_hbm.at[:, to, :], sem.at[n]))
        copies[-1].start()
    for copy in copies:
        copy.wait()


def call(kernel, name, out_shape, scratch, args, specs, **options):
    return pl.pallas_call(
        kernel,
        name=name,
        out_shape=out_shape,
        in_specs=specs,
        out_specs=options.pop("out_specs", jax.tree.map(lambda _: VMEM, out_shape)),
        scratch_shapes=scratch,
        compiler_params=pltpu.CompilerParams(vmem_limit_bytes=48 * 1024 * 1024),
        cost_estimate=pl.CostEstimate(flops=1000, bytes_accessed=1000, transcendentals=0),
        **options,
    )(*args)


def shift(g, array, stride, extent, step):
    pairs = []
    for i in range(g.dom_count):
        place = i // stride % extent
        pairs.append((i, i + ((place + step) % extent - place) * stride))
    return lax.ppermute(array, "dom", pairs)


def swap_faces(g, faces, stride, extent):
    if extent == 2:
        return [shift(g, faces[0], stride, extent, 1)]
    if extent > 2:
        return [shift(g, faces[1], stride, extent, 1), shift(g, faces[0], stride, extent, -1)]
    return []


def shards(orbitals, potential, projectors, entry_atom, entry_block, kb_energy, panel):
    g = Geometry(
        orbitals.shape, projectors.shape[0], projectors.shape[1], kb_energy.shape[0], lax.axis_size("dom")
    )

    def in_hbm(array):
        return pltpu.with_memory_space_constraint(array, pltpu.HBM)

    orb = in_hbm(orbitals.reshape(g.flat, g.cz))
    pot = in_hbm(potential.reshape(g.rows, g.cz))
    proj = in_hbm(projectors)
    blk, atom = in_hbm(entry_block), in_hbm(entry_atom)
    field = jax.ShapeDtypeStruct((g.flat, g.cz), F32)
    x_faces = [jax.ShapeDtypeStruct((n, g.cz), BF16) for n in g.face_rows(0)]
    y_faces = [jax.ShapeDtypeStruct((n, g.cz), BF16) for n in g.face_rows(1)]
    nx = len(x_faces)
    ends = jax.ShapeDtypeStruct((8, g.flat), F32)
    table = jax.ShapeDtypeStruct((g.dom_count, g.table), F32)
    entries = [
        pltpu.SMEM((g.ent,), jnp.int32),
        pltpu.SMEM((g.ent,), jnp.int32),
        pltpu.SMEM((g.dom_count + 2 * g.plane,), jnp.int32),
        pltpu.SemaphoreType.DMA((2,)),
    ]
    slots = g.slots() * g.table
    sums = [pltpu.VMEM((slots, g.cz), F32) for _ in range(4)]
    spread = pltpu.VMEM((slots, g.cz), F32)
    indices = range(g.dom_count)

    def swap(array, *strides):
        pairs = [(i, i + sum(s * (1 - 2 * (i // s % 2)) for s in strides)) for i in indices]
        return lax.ppermute(array, "dom", pairs)

    def reverse(array):
        pairs = [(i, i - i % g.third + g.third - 1 - i % g.third) for i in indices]
        return lax.ppermute(array, "dom", pairs)

    def local_and_ends(scale, which, values, prev, part):
        energy = (scale / HALF_WIDTH) * kb_energy
        energy = jnp.repeat(energy.reshape(g.dom_count, g.owned * g.nproj), g.no, axis=1)
        acc = call(
            functools.partial(inside_kernel, g, scale, len(prev) > 0),
            "inside_" + which,
            field,
            [],
            [values, pot, *prev],
            [VMEM] * (2 + len(prev)),
        )
        inputs = [values]
        outputs = [ends, ends, *y_faces]
        after = [acc]
        if g.butterfly:
            part = call(
                functools.partial(add_kernel, g),
                "pair_" + which,
                table,
                [],
                [part, swap(part, g.third), acc],
                [VMEM] * 3,
            )
            inputs += [part, swap(part, g.plane)]
            outputs.append(table)
            after = [part]
        sent_x = call(
            functools.partial(pack_x_kernel, g, len(after)),
            "pack_x_" + which,
            x_faces,
            [],
            [values, *after],
            [VMEM] * (1 + len(after)),
        )
        from_x = swap_faces(g, sent_x, g.plane, g.first)
        inputs.append(energy)
        inner, outer, *sent = call(
            functools.partial(pack_kernel, g), "pack_" + which, outputs, [], inputs, [VMEM] * len(inputs)
        )
        outer = reverse(outer)
        from_y = swap_faces(g, sent[: len(y_faces)], g.third, g.second)
        if g.butterfly:
            part, inner = call(
                functools.partial(join_kernel, g),
                "join_" + which,
                [table, ends],
                [],
                [sent[-1], outer, inner],
                [VMEM] * 3,
            )
        inner = swap(inner, 1)
        tables = [part] if g.butterfly else [lax.psum(part, "dom")]
        acc = call(
            functools.partial(nonlocal_kernel, g, scale),
            "nonlocal_" + which,
            field,
            [pltpu.VMEM(table.shape, F32), *entries, spread],
            [acc, projf, energy, blk, atom, inner, outer, *tables],
            [VMEM] * 3 + [HBM] * 2 + [VMEM] * (2 + len(tables)),
        )
        return acc, from_x + from_y

    v, projf, pot, part = call(
        functools.partial(first_kernel, g),
        "tables_first",
        [field, jax.ShapeDtypeStruct(proj.shape, F32), jax.ShapeDtypeStruct(pot.shape, F32), table],
        [
            pltpu.VMEM(orb.shape, F32),
            pltpu.VMEM(proj.shape, BF16),
            pltpu.SemaphoreType.DMA((3,)),
            *entries,
            *sums,
        ],
        [orb, proj, pot, blk, atom],
        [HBM] * 5,
    )
    acc, received = local_and_ends(1.0, "first", v, [], part)
    u, part = call(
        functools.partial(middle_kernel, g),
        "tables_second",
        [field, table],
        [*entries, *sums],
        [acc, projf, blk, atom, *received],
        [VMEM] * 2 + [HBM] * 2 + [VMEM] * len(received),
    )
    acc, received = local_and_ends(2.0, "second", u, [v], part)
    weights = call(
        functools.partial(panel_kernel, g),
        "panel",
        jax.ShapeDtypeStruct((16 * g.no, 32 * g.no), BF16),
        [],
        [panel],
        [VMEM],
    )
    rotated = None
    pieces = []
    parts = halves(g, 0)
    for number, (_, count) in enumerate(parts):
        inputs = [acc, *received[nx:]] if number < len(parts) - 1 else [acc, *received]
        filtered = call(
            functools.partial(last_kernel, g, number),
            "filtered_%d" % number,
            jax.ShapeDtypeStruct((count * g.slab, g.cz), BF16),
            [pltpu.VMEM((g.flat, g.cz), F32)],
            inputs,
            [VMEM] * len(inputs),
        )
        pieces.append((filtered, lax.ppermute(filtered, "band", [(0, 1), (1, 0)]), count))
    for number, (filtered, other, count) in enumerate(pieces):
        inputs = [filtered, other, weights] + ([] if rotated is None else [rotated])
        rotated = call(
            functools.partial(rotate_kernel, g, number),
            "rotate_%d" % number,
            jax.ShapeDtypeStruct((g.no, g.rows, g.cz), F32),
            [pltpu.VMEM((g.no, count * g.cy, g.cz), F32), pltpu.SemaphoreType.DMA((count * g.cy // 16,))],
            inputs,
            [VMEM] * 3 + [HBM] * (len(inputs) - 3),
            out_specs=HBM,
            input_output_aliases={} if rotated is None else {3: 0},
        )
    return rotated.reshape(orbitals.shape)


def solution(mesh):
    in_specs = (
        P("dom", "band", None, None, None),
        P("dom", None, None, None),
        P("dom", None, None),
        P("dom"),
        P("dom"),
        P(),
        P(),
    )
    out_specs = P("dom", "band", None, None, None)
    return jax.shard_map(shards, mesh=mesh, in_specs=in_specs, out_specs=out_specs, check_vma=False)
```

```python
import functools

import jax
import jax.numpy as jnp
from jax import lax
from jax.experimental import pallas as pl
from jax.experimental.pallas import tpu as pltpu
from jax.sharding import PartitionSpec as P

RADIUS = 6
COEFFS = (
    -5369.0 / 1800.0,
    12.0 / 7.0,
    -15.0 / 56.0,
    10.0 / 189.0,
    -1.0 / 112.0,
    2.0 / 1925.0,
    -1.0 / 16632.0,
)
KINETIC = -3.125
CENTER = 36.0
HALF_WIDTH = 34.0
WEIGHT = [KINETIC * c / HALF_WIDTH for c in COEFFS]
DIAGONAL = (3.0 * KINETIC * COEFFS[0] - CENTER) / HALF_WIDTH

F32 = jnp.float32
BF16 = jnp.bfloat16
VMEM = pl.BlockSpec(memory_space=pltpu.VMEM)
HBM = pl.BlockSpec(memory_space=pltpu.HBM)
NT = (((1,), (1,)), ((), ()))
TN = (((0,), (0,)), ((), ()))
NN = (((1,), (0,)), ((), ()))


def split2(x):
    high = x.astype(BF16)
    low = (x - high.astype(F32)).astype(BF16)
    return high, low


def iota(shape, dim):
    return lax.broadcasted_iota(jnp.int32, shape, dim)


def weight_at(distance, scale):
    out = jnp.zeros(distance.shape, F32)
    for k in range(1, RADIUS + 1):
        out = jnp.where(distance == k, scale * WEIGHT[k], out)
    return out


class Geometry:
    def __init__(self, orbitals, entries, nproj, atoms, dom_count):
        _, self.no, self.cx, self.cy, self.cz = orbitals
        self.rows = self.cx * self.cy
        self.flat = self.rows * self.no
        self.ent = entries
        self.nproj = nproj
        self.dom_count = dom_count
        self.owned = atoms // dom_count
        self.third = 4
        self.second = min(8, dom_count // 8)
        self.plane = self.second * self.third
        self.first = dom_count // self.plane
        self.table = self.owned * nproj * self.no
        self.slab = self.cy * self.no
        self.fold = self.flat // self.table
        self.butterfly = self.first == 2 and self.second == 2 and dom_count <= 2 * self.fold
        assert self.no == 8

    def faces(self, dom, dim):
        if dim == 0:
            extent, place = self.first, dom // self.plane
        else:
            extent, place = self.second, dom // self.third % self.second
        if extent == 2:
            return [(1 - place, None)]
        if extent > 2:
            return [(0, place > 0), (1, place < extent - 1)]
        return []

    def face_rows(self, dim):
        rows = RADIUS * self.slab if dim == 0 else self.cx * RADIUS * self.no
        return [rows] * len(self.faces(0, dim))

    def steps(self, dom):
        out = [0]
        for extent, stride in ((self.first, self.plane), (self.second, self.third), (self.third, 1)):
            if extent == 2:
                out.append((1 - 2 * (dom // stride % 2)) * stride)
            elif extent > 2:
                out.extend([stride, -stride])
        return out

    def slots(self):
        return len(self.steps(0))


def layer(side, length, j):
    if isinstance(side, int):
        return length - 1 - j if side else j
    return side * (length - 1 - j) + (1 - side) * j


def aligned(start, unit):
    return start if isinstance(start, int) else pl.multiple_of(start, unit)


def pack_x(g, dom, v_ref, refs):
    for (side, _), out in zip(g.faces(dom, 0), refs):
        for j in range(RADIUS):
            at = aligned(layer(side, g.cx, j) * g.slab, g.slab)
            out[j * g.slab : (j + 1) * g.slab, :] = v_ref[pl.ds(at, g.slab), :].astype(BF16)


def pack_y(g, dom, v_ref, refs):
    size = RADIUS * g.no
    for (side, _), out in zip(g.faces(dom, 1), refs):
        for x in range(g.cx):
            pieces = []
            for j in range(RADIUS):
                at = aligned(x * g.slab + layer(side, g.cy, j) * g.no, g.no)
                pieces.append(v_ref[pl.ds(at, g.no), :])
            out[x * size : (x + 1) * size, :] = jnp.concatenate(pieces, axis=0).astype(BF16)


def end_columns(g, dom):
    row, col = iota((16, g.cz), 0), iota((16, g.cz), 1)
    odd = dom % 2
    side = jnp.where(row < 8, 1 - odd, odd)
    return jnp.where(side == 1, g.cz - 1 - col, col), row


def pack_ends(g, dom, v_ref, first_ref, second_ref):
    inward, row = end_columns(g, dom)
    pick = jnp.where((inward == row % 8) & (row % 8 < RADIUS), 1.0, 0.0).astype(BF16)
    pick = jnp.concatenate([pick, pick], axis=1)
    for x in range(g.cx):
        rows = slice(x * g.slab, (x + 1) * g.slab)
        both = jnp.concatenate(split2(v_ref[rows, :]), axis=1)
        ends = lax.dot_general(pick, both, NT, preferred_element_type=F32)
        first_ref[:, rows] = ends[:8]
        second_ref[:, rows] = ends[8:]


def put_table(g, message, table):
    for n in range(g.dom_count):
        at = RADIUS + n // g.fold
        lanes = n % g.fold * g.table
        message[at : at + 1, lanes : lanes + g.table] = table[n : n + 1, :]


def get_table(g, message):
    rows = []
    for n in range(g.dom_count):
        at = RADIUS + n // g.fold
        lanes = n % g.fold * g.table
        rows.append(message[at : at + 1, lanes : lanes + g.table])
    return jnp.concatenate(rows, axis=0)


def fill_lut(g, dom, lut):
    for number, step in enumerate(g.steps(dom)):
        lut[g.plane + dom + step] = number * g.owned


def column_of(g, lut, atom):
    if g.owned & (g.owned - 1):
        owner = lax.div(atom, jnp.int32(g.owned))
        return lut[owner + g.plane] + (atom - owner * g.owned)
    owner = lax.shift_right_logical(atom, jnp.int32(g.owned.bit_length() - 1))
    return lut[owner + g.plane] + (atom & (g.owned - 1))


def inner_tables(g, dom, v_ref, projf, blk, atom, lut, sums, table):
    size = g.nproj * g.no

    unroll = 16

    def step(i, _):
        for u in range(unroll):
            part = sums[u % len(sums)]
            e = i * unroll + u
            col = column_of(g, lut, atom[e])
            v = v_ref[pl.ds(pl.multiple_of(blk[e] * g.no, g.no), g.no), :]
            for p in range(g.nproj):
                at = pl.ds(pl.multiple_of(col * size + p * g.no, g.no), g.no)
                coef = jnp.broadcast_to(projf[e, p : p + 1, :], v.shape)
                part[at, :] += v * coef
        return 0

    lax.fori_loop(0, g.ent // unroll, step, 0)
    total = sums[0][...]
    for part in sums[1:]:
        total = total + part[...]
    both = jnp.concatenate(split2(total), axis=1)
    ones = jnp.ones((8, both.shape[1]), BF16)
    summed = lax.dot_general(ones, both, NT, preferred_element_type=F32)
    table[...] = jnp.zeros(table.shape, F32)
    for number, step in enumerate(g.steps(dom)):
        owner = jnp.clip(dom + step, 0, g.dom_count - 1)
        table[pl.ds(owner, 1), :] += summed[0:1, number * g.table : (number + 1) * g.table]


def clear(sums):
    for part in sums:
        part[...] = jnp.zeros(part.shape, F32)


def entry_copies(blk_hbm, atom_hbm, blk, atom, sem):
    copies = [
        pltpu.make_async_copy(blk_hbm, blk, sem.at[0]),
        pltpu.make_async_copy(atom_hbm, atom, sem.at[1]),
    ]
    for copy in copies:
        copy.start()
    return copies


def first_kernel(g, orb_hbm, proj_hbm, pot_hbm, blk_hbm, atom_hbm, v_ref, projf, pot, table, *scratch):
    orb, proj, sem, blk, atom, lut, entry_sem = scratch[:7]
    sums = scratch[7:]
    copies = [
        pltpu.make_async_copy(orb_hbm, orb, sem.at[0]),
        pltpu.make_async_copy(proj_hbm, proj, sem.at[1]),
        pltpu.make_async_copy(pot_hbm, pot, sem.at[2]),
    ]
    for copy in copies:
        copy.start()
    copies += entry_copies(blk_hbm, atom_hbm, blk, atom, entry_sem)
    dom = lax.axis_index("dom")
    fill_lut(g, dom, lut)
    clear(sums)
    copies[1].wait()
    projf[...] = proj[...].astype(F32)
    copies[0].wait()
    for r in range(g.rows):
        v_ref[r * g.no : (r + 1) * g.no, :] = orb[pl.ds(r, g.no, stride=g.rows), :]
    for copy in copies[2:]:
        copy.wait()
    inner_tables(g, dom, v_ref, projf, blk, atom, lut, sums, table)


def pack_kernel(g, v_ref, *refs):
    dom = lax.axis_index("dom")
    if g.butterfly:
        part, from_x, from_y, from_xy = refs[:4]
        group = refs[-1]
        group[...] = (part[...] + from_x[...]) + (from_y[...] + from_xy[...])
        refs = refs[:-1]
    first, second = refs[-2:]
    pack_ends(g, dom, v_ref, first, second)
    if g.butterfly:
        put_table(g, first, group)
        put_table(g, second, group)


def pack_faces_kernel(g, nafter, v_ref, *refs):
    nx = len(g.face_rows(0))
    dom = lax.axis_index("dom")
    refs = refs[nafter:]
    pack_x(g, dom, v_ref, refs[:nx])
    pack_y(g, dom, v_ref, refs[nx:])


def inside_kernel(g, scale, subtract, v_ref, pot, *refs):
    prev, out = refs if subtract else (None, refs[0])
    row, col = iota((g.cz, g.cz), 0), iota((g.cz, g.cz), 1)
    high, low = split2(weight_at(jnp.abs(row - col), scale))
    band = jnp.concatenate([high, low], axis=1)
    band = jnp.concatenate([band, band], axis=0)

    def cell(x, y):
        at = (x * g.cy + y) * g.no
        return v_ref[at : at + g.no, :]

    for x in range(g.cx):
        both = jnp.concatenate(split2(v_ref[x * g.slab : (x + 1) * g.slab, :]), axis=1)
        along = lax.dot_general(both, band, NN, preferred_element_type=F32)
        for y in range(g.cy):
            at = (x * g.cy + y) * g.no
            rows = slice(y * g.no, (y + 1) * g.no)
            here = cell(x, y)
            diag = jnp.broadcast_to(pot[x * g.cy + y : x * g.cy + y + 1, :], here.shape)
            total = along[rows, : g.cz] + along[rows, g.cz :]
            total = total + (scale * DIAGONAL + (scale / HALF_WIDTH) * diag) * here
            if subtract:
                total = total - prev[at : at + g.no, :]
            for k in range(1, RADIUS + 1):
                near = []
                for a, b in ((x - k, y), (x + k, y), (x, y - k), (x, y + k)):
                    if 0 <= a < g.cx and 0 <= b < g.cy:
                        near.append(cell(a, b))
                if near:
                    total = total + (scale * WEIGHT[k]) * sum(near[1:], near[0])
            out[at : at + g.no, :] = total


def flag(present):
    return 1.0 if present is None else jnp.where(present, 1.0, 0.0)


def add_ends(g, dom, scale, acc, low, high, out):
    inward, row = end_columns(g, dom)
    middle = (dom % g.third > 0) & (dom % g.third < g.third - 1)
    present = (row % 8 < RADIUS) & ((row < 8) | middle)
    coef = jnp.where(present, weight_at(inward + row % 8 + 1, scale), 0.0)
    c_high, c_low = split2(coef)
    coefs = jnp.concatenate([c_high, c_high, c_low, c_low], axis=0)
    for x in range(g.cx):
        rows = slice(x * g.slab, (x + 1) * g.slab)
        h_high, h_low = split2(jnp.concatenate([low[:, rows], high[:, rows]], axis=0))
        halo = jnp.concatenate([h_high, h_low, h_high, h_low], axis=0)
        out[rows, :] = acc[rows, :] + lax.dot_general(halo, coefs, TN, preferred_element_type=F32)


def add_x_faces(g, dom, scale, face_refs, out, count):
    unit = 2 * g.no
    for (side, present), face in zip(g.faces(dom, 0), face_refs):
        for y in range(0, g.cy, 2):
            starts = [j * g.slab + y * g.no for j in range(RADIUS)]
            part = [flag(present) * face[at : at + unit, :].astype(F32) for at in starts]
            for i in range(RADIUS):
                at = aligned(layer(side, count, i) * g.slab + y * g.no, unit)
                total = out[pl.ds(at, unit), :]
                for j in range(RADIUS - i):
                    total = total + (scale * WEIGHT[i + j + 1]) * part[j]
                out[pl.ds(at, unit), :] = total


def add_y_faces(g, dom, scale, face_refs, out, start, count):
    size = RADIUS * g.no
    for (side, present), face in zip(g.faces(dom, 1), face_refs):
        for x in range(count):
            part = face[pl.ds(aligned((start + x) * size, 16), size), :]
            part = flag(present) * part.astype(F32)
            for i in range(RADIUS):
                at = aligned(x * g.slab + layer(side, g.cy, i) * g.no, g.no)
                total = out[pl.ds(at, g.no), :]
                for j in range(RADIUS - i):
                    total = total + (scale * WEIGHT[i + j + 1]) * part[j * g.no : (j + 1) * g.no]
                out[pl.ds(at, g.no), :] = total


def add_nonlocal(g, dom, table, energy, projf, blk, atom, lut, spread, out):
    size = g.nproj * g.no
    lanes = g.table
    count = g.slots()
    rows = []
    for step in g.steps(dom):
        owner = pl.ds(jnp.clip(dom + step, 0, g.dom_count - 1), 1)
        rows.append(table[owner, :] * energy[owner, :])
    rows.append(jnp.zeros((8 - count, lanes), F32))
    scaled = jnp.concatenate(rows, axis=0)
    high = scaled.astype(BF16)
    rest = scaled - high.astype(F32)
    mid = rest.astype(BF16)
    low = (rest - mid.astype(F32)).astype(BF16)
    parts = jnp.concatenate([high, mid, low], axis=0)
    wide = count * g.cz
    row, col = iota((24, wide), 0), iota((24, wide), 1)
    ones = jnp.where(row % 8 == col // g.cz, 1.0, 0.0).astype(BF16)
    out_all = lax.dot_general(parts, ones, TN, preferred_element_type=F32)
    for number in range(count):
        spread[number * lanes : (number + 1) * lanes, :] = out_all[:, number * g.cz : (number + 1) * g.cz]
    unroll = 16

    def step(i, _):
        additions = []
        for u in range(unroll):
            e = i * unroll + u
            col = column_of(g, lut, atom[e])
            total = None
            for p in range(g.nproj):
                at = pl.ds(pl.multiple_of(col * size + p * g.no, g.no), g.no)
                coef = jnp.broadcast_to(projf[e, p : p + 1, :], (g.no, g.cz))
                term = spread[at, :] * coef
                total = term if total is None else total + term
            additions.append((pl.ds(pl.multiple_of(blk[e] * g.no, g.no), g.no), total))
        for at, total in additions:
            out[at, :] += total
        return 0

    lax.fori_loop(0, g.ent // unroll, step, 0)


def nonlocal_kernel(g, scale, acc, projf, energy, blk_hbm, atom_hbm, first, second, *refs):
    out, table, blk, atom, lut, sem, spread = refs[-7:]
    copies = entry_copies(blk_hbm, atom_hbm, blk, atom, sem)
    dom = lax.axis_index("dom")
    fill_lut(g, dom, lut)
    if g.butterfly:
        group, opposite = refs[:2]
        table[...] = (group[...] + get_table(g, first)) + (get_table(g, second) + opposite[...])
    else:
        table[...] = refs[0][...]
    add_ends(g, dom, scale, acc, first, second, out)
    for copy in copies:
        copy.wait()
    add_nonlocal(g, dom, table, energy, projf, blk, atom, lut, spread, out)


def middle_kernel(g, acc, projf, blk_hbm, atom_hbm, *refs):
    nx, ny = len(g.face_rows(0)), len(g.face_rows(1))
    faces = refs[: nx + ny]
    u_ref, table, blk, atom, lut, sem = refs[nx + ny : nx + ny + 6]
    sums = refs[nx + ny + 6 :]
    copies = entry_copies(blk_hbm, atom_hbm, blk, atom, sem)
    dom = lax.axis_index("dom")
    fill_lut(g, dom, lut)
    clear(sums)
    u_ref[...] = acc[...]
    add_x_faces(g, dom, 1.0, faces[:nx], u_ref, g.cx)
    add_y_faces(g, dom, 1.0, faces[nx:], u_ref, 0, g.cx)
    for copy in copies:
        copy.wait()
    inner_tables(g, dom, u_ref, projf, blk, atom, lut, sums, table)


def halves(g, dom):
    if g.first != 2 or g.cx != 2 * RADIUS:
        return [(0, g.cx)]
    side = 1 - dom // g.plane
    return [((1 - side) * RADIUS, RADIUS), (side * RADIUS, RADIUS)]


def last_kernel(g, number, acc, *refs):
    nx = len(g.face_rows(0))
    filtered, work = refs[-2:]
    refs = refs[:-2]
    dom = lax.axis_index("dom")
    parts = halves(g, dom)
    start, count = parts[number]
    work[...] = acc[pl.ds(aligned(start * g.slab, g.slab), count * g.slab), :]
    if number == len(parts) - 1:
        add_x_faces(g, dom, 2.0, refs[:nx], work, count)
        refs = refs[nx:]
    add_y_faces(g, dom, 2.0, refs, work, start, count)
    filtered[...] = work[...].astype(BF16)


def panel_kernel(g, panel, weights):
    band = lax.axis_index("band")
    group = 16
    span = group * g.no
    norb = panel.shape[0]
    row, col = iota((span, norb), 0), iota((span, norb), 1)
    pick_out = jnp.where(col == band * g.no + row // group, 1.0, 0.0).astype(BF16)
    picked = lax.dot_general(pick_out, panel[...], NT, preferred_element_type=F32).astype(BF16)
    row, col = iota((norb, 2 * span), 0), iota((norb, 2 * span), 1)
    source = jnp.where(col < span, band, 1 - band) * g.no + col % g.no
    pick_in = jnp.where(row == source, 1.0, 0.0).astype(BF16)
    spread = lax.dot_general(picked, pick_in, NN, preferred_element_type=F32)
    row, col = iota((span, 2 * span), 0), iota((span, 2 * span), 1)
    same = row % group == (col % span) // g.no
    weights[...] = jnp.where(same, spread, 0.0).astype(BF16)


def rotate_kernel(g, number, own, other, weights, *refs):
    out_hbm, out, sem = refs[-3:]
    start, count = halves(g, lax.axis_index("dom"))[number]
    group = 16
    span = group * g.no
    copies = []
    size = count * g.cy
    for n in range(size // group):
        rows = slice(n * span, (n + 1) * span)
        both = jnp.concatenate([own[rows, :], other[rows, :]], axis=0)
        result = lax.dot_general(weights[...], both, NN, preferred_element_type=F32)
        for j in range(g.no):
            out[j, n * group : (n + 1) * group, :] = result[j * group : (j + 1) * group, :]
        to = pl.ds(aligned(start * g.cy + n * group, group), group)
        source = out.at[:, pl.ds(n * group, group), :]
        copies.append(pltpu.make_async_copy(source, out_hbm.at[:, to, :], sem.at[n]))
        copies[-1].start()
    for copy in copies:
        copy.wait()


def call(kernel, name, out_shape, scratch, args, specs, **options):
    return pl.pallas_call(
        kernel,
        name=name,
        out_shape=out_shape,
        in_specs=specs,
        out_specs=options.pop("out_specs", jax.tree.map(lambda _: VMEM, out_shape)),
        scratch_shapes=scratch,
        compiler_params=pltpu.CompilerParams(vmem_limit_bytes=48 * 1024 * 1024),
        cost_estimate=pl.CostEstimate(flops=1000, bytes_accessed=1000, transcendentals=0),
        **options,
    )(*args)


def shift(g, array, stride, extent, step):
    pairs = []
    for i in range(g.dom_count):
        place = i // stride % extent
        pairs.append((i, i + ((place + step) % extent - place) * stride))
    return lax.ppermute(array, "dom", pairs)


def swap_faces(g, faces, stride, extent):
    if extent == 2:
        return [shift(g, faces[0], stride, extent, 1)]
    if extent > 2:
        return [shift(g, faces[1], stride, extent, 1), shift(g, faces[0], stride, extent, -1)]
    return []


def shards(orbitals, potential, projectors, entry_atom, entry_block, kb_energy, panel):
    g = Geometry(
        orbitals.shape, projectors.shape[0], projectors.shape[1], kb_energy.shape[0], lax.axis_size("dom")
    )

    def in_hbm(array):
        return pltpu.with_memory_space_constraint(array, pltpu.HBM)

    orb = in_hbm(orbitals.reshape(g.flat, g.cz))
    pot = in_hbm(potential.reshape(g.rows, g.cz))
    proj = in_hbm(projectors)
    blk, atom = in_hbm(entry_block), in_hbm(entry_atom)
    field = jax.ShapeDtypeStruct((g.flat, g.cz), F32)
    x_faces = [jax.ShapeDtypeStruct((n, g.cz), BF16) for n in g.face_rows(0)]
    y_faces = [jax.ShapeDtypeStruct((n, g.cz), BF16) for n in g.face_rows(1)]
    nx = len(x_faces)
    ends = jax.ShapeDtypeStruct((8, g.flat), F32)
    table = jax.ShapeDtypeStruct((g.dom_count, g.table), F32)
    entries = [
        pltpu.SMEM((g.ent,), jnp.int32),
        pltpu.SMEM((g.ent,), jnp.int32),
        pltpu.SMEM((g.dom_count + 2 * g.plane,), jnp.int32),
        pltpu.SemaphoreType.DMA((2,)),
    ]
    slots = g.slots() * g.table
    sums = [pltpu.VMEM((slots, g.cz), F32) for _ in range(4)]
    spread = pltpu.VMEM((slots, g.cz), F32)
    indices = range(g.dom_count)

    def swap(array, *strides):
        pairs = [(i, i + sum(s * (1 - 2 * (i // s % 2)) for s in strides)) for i in indices]
        return lax.ppermute(array, "dom", pairs)

    def reverse(array):
        pairs = [(i, i - i % g.third + g.third - 1 - i % g.third) for i in indices]
        return lax.ppermute(array, "dom", pairs)

    def local_and_ends(scale, which, values, prev, part):
        energy = (scale / HALF_WIDTH) * kb_energy
        energy = jnp.repeat(energy.reshape(g.dom_count, g.owned * g.nproj), g.no, axis=1)
        acc = call(
            functools.partial(inside_kernel, g, scale, len(prev) > 0),
            "inside_" + which,
            field,
            [],
            [values, pot, *prev],
            [VMEM] * (2 + len(prev)),
        )

        inputs = [values]
        outputs = [ends, ends]
        after = []
        if g.butterfly:
            inputs += [part, swap(part, g.plane), swap(part, g.third), swap(part, g.plane, g.third)]
            outputs.append(table)
            after.append(inputs[-2])
        faces = call(
            functools.partial(pack_faces_kernel, g, len(after)),
            "faces_" + which,
            [*x_faces, *y_faces],
            [],
            [values, *after],
            [VMEM] * (1 + len(after)),
        )
        from_x = swap_faces(g, faces[:nx], g.plane, g.first)
        from_y = swap_faces(g, faces[nx:], g.third, g.second)
        inputs += [energy]
        first, second, *sent = call(
            functools.partial(pack_kernel, g), "pack_" + which, outputs, [], inputs, [VMEM] * len(inputs)
        )
        first, second = swap(first, 1), reverse(second)
        tables = [sent[-1], swap(sent[-1], 2)] if g.butterfly else [lax.psum(part, "dom")]
        acc = call(
            functools.partial(nonlocal_kernel, g, scale),
            "nonlocal_" + which,
            field,
            [pltpu.VMEM(table.shape, F32), *entries, spread],
            [acc, projf, energy, blk, atom, first, second, *tables],
            [VMEM] * 3 + [HBM] * 2 + [VMEM] * (2 + len(tables)),
        )
        return acc, from_x + from_y

    v, projf, pot, part = call(
        functools.partial(first_kernel, g),
        "tables_first",
        [field, jax.ShapeDtypeStruct(proj.shape, F32), jax.ShapeDtypeStruct(pot.shape, F32), table],
        [
            pltpu.VMEM(orb.shape, F32),
            pltpu.VMEM(proj.shape, BF16),
            pltpu.SemaphoreType.DMA((3,)),
            *entries,
            *sums,
        ],
        [orb, proj, pot, blk, atom],
        [HBM] * 5,
    )
    acc, received = local_and_ends(1.0, "first", v, [], part)
    u, part = call(
        functools.partial(middle_kernel, g),
        "tables_second",
        [field, table],
        [*entries, *sums],
        [acc, projf, blk, atom, *received],
        [VMEM] * 2 + [HBM] * 2 + [VMEM] * len(received),
    )
    acc, received = local_and_ends(2.0, "second", u, [v], part)
    weights = call(
        functools.partial(panel_kernel, g),
        "panel",
        jax.ShapeDtypeStruct((16 * g.no, 32 * g.no), BF16),
        [],
        [panel],
        [VMEM],
    )
    rotated = None
    pieces = []
    parts = halves(g, 0)
    for number, (_, count) in enumerate(parts):
        inputs = [acc, *received[nx:]] if number < len(parts) - 1 else [acc, *received]
        filtered = call(
            functools.partial(last_kernel, g, number),
            "filtered_%d" % number,
            jax.ShapeDtypeStruct((count * g.slab, g.cz), BF16),
            [pltpu.VMEM((count * g.slab, g.cz), F32)],
            inputs,
            [VMEM] * len(inputs),
        )
        pieces.append((filtered, lax.ppermute(filtered, "band", [(0, 1), (1, 0)]), count))
    for number, (filtered, other, count) in enumerate(pieces):
        inputs = [filtered, other, weights] + ([] if rotated is None else [rotated])
        rotated = call(
            functools.partial(rotate_kernel, g, number),
            "rotate_%d" % number,
            jax.ShapeDtypeStruct((g.no, g.rows, g.cz), F32),
            [pltpu.VMEM((g.no, count * g.cy, g.cz), F32), pltpu.SemaphoreType.DMA((count * g.cy // 16,))],
            inputs,
            [VMEM] * 3 + [HBM] * (len(inputs) - 3),
            out_specs=HBM,
            input_output_aliases={} if rotated is None else {3: 0},
        )
    return rotated.reshape(orbitals.shape)


def solution(mesh):
    in_specs = (
        P("dom", "band", None, None, None),
        P("dom", None, None, None),
        P("dom", None, None),
        P("dom"),
        P("dom"),
        P(),
        P(),
    )
    out_specs = P("dom", "band", None, None, None)
    return jax.shard_map(shards, mesh=mesh, in_specs=in_specs, out_specs=out_specs, check_vma=False)
```

```python
import functools

import jax
import jax.numpy as jnp
from jax import lax
from jax.experimental import pallas as pl
from jax.experimental.pallas import tpu as pltpu
from jax.sharding import PartitionSpec as P

RADIUS = 6
COEFFS = (
    -5369.0 / 1800.0,
    12.0 / 7.0,
    -15.0 / 56.0,
    10.0 / 189.0,
    -1.0 / 112.0,
    2.0 / 1925.0,
    -1.0 / 16632.0,
)
KINETIC = -3.125
CENTER = 36.0
HALF_WIDTH = 34.0
WEIGHT = [KINETIC * c / HALF_WIDTH for c in COEFFS]
DIAGONAL = (3.0 * KINETIC * COEFFS[0] - CENTER) / HALF_WIDTH

F32 = jnp.float32
BF16 = jnp.bfloat16
VMEM = pl.BlockSpec(memory_space=pltpu.VMEM)
HBM = pl.BlockSpec(memory_space=pltpu.HBM)
NT = (((1,), (1,)), ((), ()))
TN = (((0,), (0,)), ((), ()))
NN = (((1,), (0,)), ((), ()))


def split2(x):
    high = x.astype(BF16)
    low = (x - high.astype(F32)).astype(BF16)
    return high, low


def iota(shape, dim):
    return lax.broadcasted_iota(jnp.int32, shape, dim)


def weight_at(distance, scale):
    out = jnp.zeros(distance.shape, F32)
    for k in range(1, RADIUS + 1):
        out = jnp.where(distance == k, scale * WEIGHT[k], out)
    return out


class Geometry:
    def __init__(self, orbitals, entries, nproj, atoms, dom_count):
        _, self.no, self.cx, self.cy, self.cz = orbitals
        self.rows = self.cx * self.cy
        self.flat = self.rows * self.no
        self.ent = entries
        self.nproj = nproj
        self.dom_count = dom_count
        self.owned = atoms // dom_count
        self.third = 4
        self.second = min(8, dom_count // 8)
        self.plane = self.second * self.third
        self.first = dom_count // self.plane
        self.table = self.owned * nproj * self.no
        self.slab = self.cy * self.no
        self.fold = self.flat // self.table
        self.butterfly = self.first == 2 and self.second == 2 and dom_count <= 2 * self.fold
        assert self.no == 8

    def faces(self, dom, dim):
        if dim == 0:
            extent, place = self.first, dom // self.plane
        else:
            extent, place = self.second, dom // self.third % self.second
        if extent == 2:
            return [(1 - place, None)]
        if extent > 2:
            return [(0, place > 0), (1, place < extent - 1)]
        return []

    def face_rows(self, dim):
        rows = RADIUS * self.slab if dim == 0 else self.cx * RADIUS * self.no
        return [rows] * len(self.faces(0, dim))

    def steps(self, dom):
        out = [0]
        for extent, stride in ((self.first, self.plane), (self.second, self.third), (self.third, 1)):
            if extent == 2:
                out.append((1 - 2 * (dom // stride % 2)) * stride)
            elif extent > 2:
                out.extend([stride, -stride])
        return out

    def slots(self):
        return len(self.steps(0))


def layer(side, length, j):
    if isinstance(side, int):
        return length - 1 - j if side else j
    return side * (length - 1 - j) + (1 - side) * j


def aligned(start, unit):
    return start if isinstance(start, int) else pl.multiple_of(start, unit)


def pack_x(g, dom, v_ref, refs):
    for (side, _), out in zip(g.faces(dom, 0), refs):
        for j in range(RADIUS):
            at = aligned(layer(side, g.cx, j) * g.slab, g.slab)
            out[j * g.slab : (j + 1) * g.slab, :] = v_ref[pl.ds(at, g.slab), :].astype(BF16)


def pack_y(g, dom, v_ref, refs):
    size = RADIUS * g.no
    for (side, _), out in zip(g.faces(dom, 1), refs):
        for x in range(g.cx):
            pieces = []
            for j in range(RADIUS):
                at = aligned(x * g.slab + layer(side, g.cy, j) * g.no, g.no)
                pieces.append(v_ref[pl.ds(at, g.no), :])
            out[x * size : (x + 1) * size, :] = jnp.concatenate(pieces, axis=0).astype(BF16)


def end_columns(g, dom):
    row, col = iota((16, g.cz), 0), iota((16, g.cz), 1)
    odd = dom % 2
    side = jnp.where(row < 8, 1 - odd, odd)
    return jnp.where(side == 1, g.cz - 1 - col, col), row


def pack_ends(g, dom, v_ref, first_ref, second_ref):
    inward, row = end_columns(g, dom)
    pick = jnp.where((inward == row % 8) & (row % 8 < RADIUS), 1.0, 0.0).astype(BF16)
    pick = jnp.concatenate([pick, pick], axis=1)
    for x in range(g.cx):
        rows = slice(x * g.slab, (x + 1) * g.slab)
        both = jnp.concatenate(split2(v_ref[rows, :]), axis=1)
        ends = lax.dot_general(pick, both, NT, preferred_element_type=F32)
        first_ref[:, rows] = ends[:8]
        second_ref[:, rows] = ends[8:]


def put_table(g, message, table):
    for n in range(g.dom_count):
        at = RADIUS + n // g.fold
        lanes = n % g.fold * g.table
        message[at : at + 1, lanes : lanes + g.table] = table[n : n + 1, :]


def get_table(g, message):
    rows = []
    for n in range(g.dom_count):
        at = RADIUS + n // g.fold
        lanes = n % g.fold * g.table
        rows.append(message[at : at + 1, lanes : lanes + g.table])
    return jnp.concatenate(rows, axis=0)


def fill_lut(g, dom, lut):
    for number, step in enumerate(g.steps(dom)):
        lut[g.plane + dom + step] = number * g.owned


def column_of(g, lut, atom):
    if g.owned & (g.owned - 1):
        owner = lax.div(atom, jnp.int32(g.owned))
        return lut[owner + g.plane] + (atom - owner * g.owned)
    owner = lax.shift_right_logical(atom, jnp.int32(g.owned.bit_length() - 1))
    return lut[owner + g.plane] + (atom & (g.owned - 1))


def inner_tables(g, dom, v_ref, projf, blk, atom, lut, sums, table):
    size = g.nproj * g.no

    unroll = 64

    def step(i, _):
        for u in range(unroll):
            part = sums[u % len(sums)]
            e = i * unroll + u
            col = column_of(g, lut, atom[e])
            v = v_ref[pl.ds(pl.multiple_of(blk[e] * g.no, g.no), g.no), :]
            for p in range(g.nproj):
                at = pl.ds(pl.multiple_of(col * size + p * g.no, g.no), g.no)
                coef = jnp.broadcast_to(projf[e, p : p + 1, :], v.shape)
                part[at, :] += v * coef
        return 0

    lax.fori_loop(0, g.ent // unroll, step, 0)
    total = sums[0][...]
    for part in sums[1:]:
        total = total + part[...]
    both = jnp.concatenate(split2(total), axis=1)
    ones = jnp.ones((8, both.shape[1]), BF16)
    summed = lax.dot_general(ones, both, NT, preferred_element_type=F32)
    table[...] = jnp.zeros(table.shape, F32)
    for number, step in enumerate(g.steps(dom)):
        owner = jnp.clip(dom + step, 0, g.dom_count - 1)
        table[pl.ds(owner, 1), :] += summed[0:1, number * g.table : (number + 1) * g.table]


def clear(sums):
    for part in sums:
        part[...] = jnp.zeros(part.shape, F32)


def entry_copies(blk_hbm, atom_hbm, blk, atom, sem):
    copies = [
        pltpu.make_async_copy(blk_hbm, blk, sem.at[0]),
        pltpu.make_async_copy(atom_hbm, atom, sem.at[1]),
    ]
    for copy in copies:
        copy.start()
    return copies


def first_kernel(g, orb_hbm, proj_hbm, pot_hbm, blk_hbm, atom_hbm, v_ref, projf, pot, table, *scratch):
    orb, proj, sem, blk, atom, lut, entry_sem = scratch[:7]
    sums = scratch[7:]
    copies = [
        pltpu.make_async_copy(orb_hbm, orb, sem.at[0]),
        pltpu.make_async_copy(proj_hbm, proj, sem.at[1]),
        pltpu.make_async_copy(pot_hbm, pot, sem.at[2]),
    ]
    for copy in copies:
        copy.start()
    copies += entry_copies(blk_hbm, atom_hbm, blk, atom, entry_sem)
    dom = lax.axis_index("dom")
    fill_lut(g, dom, lut)
    clear(sums)
    copies[1].wait()
    projf[...] = proj[...].astype(F32)
    copies[0].wait()
    for r in range(g.rows):
        v_ref[r * g.no : (r + 1) * g.no, :] = orb[pl.ds(r, g.no, stride=g.rows), :]
    for copy in copies[2:]:
        copy.wait()
    inner_tables(g, dom, v_ref, projf, blk, atom, lut, sums, table)


def pack_kernel(g, *refs):
    part, from_x, from_y, from_xy = refs[:4]
    ends, outs, group = refs[4:6], refs[-3:-1], refs[-1]
    group[...] = (part[...] + from_x[...]) + (from_y[...] + from_xy[...])
    for source, out in zip(ends, outs):
        out[...] = source[...]
        put_table(g, out, group)


def pack_faces_kernel(g, nafter, v_ref, *refs):
    nx = len(g.face_rows(0))
    dom = lax.axis_index("dom")
    refs = refs[nafter:]
    pack_x(g, dom, v_ref, refs[:nx])
    pack_y(g, dom, v_ref, refs[nx:-2])
    pack_ends(g, dom, v_ref, *refs[-2:])


def inside_kernel(g, scale, subtract, v_ref, pot, *refs):
    prev, out = refs if subtract else (None, refs[0])
    row, col = iota((g.cz, g.cz), 0), iota((g.cz, g.cz), 1)
    high, low = split2(weight_at(jnp.abs(row - col), scale))
    band = jnp.concatenate([high, low], axis=1)
    band = jnp.concatenate([band, band], axis=0)

    def cell(x, y):
        at = (x * g.cy + y) * g.no
        return v_ref[at : at + g.no, :]

    for x in range(g.cx):
        both = jnp.concatenate(split2(v_ref[x * g.slab : (x + 1) * g.slab, :]), axis=1)
        along = lax.dot_general(both, band, NN, preferred_element_type=F32)
        for y in range(g.cy):
            at = (x * g.cy + y) * g.no
            rows = slice(y * g.no, (y + 1) * g.no)
            here = cell(x, y)
            diag = jnp.broadcast_to(pot[x * g.cy + y : x * g.cy + y + 1, :], here.shape)
            total = along[rows, : g.cz] + along[rows, g.cz :]
            total = total + (scale * DIAGONAL + (scale / HALF_WIDTH) * diag) * here
            if subtract:
                total = total - prev[at : at + g.no, :]
            for k in range(1, RADIUS + 1):
                near = []
                for a, b in ((x - k, y), (x + k, y), (x, y - k), (x, y + k)):
                    if 0 <= a < g.cx and 0 <= b < g.cy:
                        near.append(cell(a, b))
                if near:
                    total = total + (scale * WEIGHT[k]) * sum(near[1:], near[0])
            out[at : at + g.no, :] = total


def flag(present):
    return 1.0 if present is None else jnp.where(present, 1.0, 0.0)


def add_ends(g, dom, scale, acc, low, high, out):
    inward, row = end_columns(g, dom)
    middle = (dom % g.third > 0) & (dom % g.third < g.third - 1)
    present = (row % 8 < RADIUS) & ((row < 8) | middle)
    coef = jnp.where(present, weight_at(inward + row % 8 + 1, scale), 0.0)
    c_high, c_low = split2(coef)
    coefs = jnp.concatenate([c_high, c_high, c_low, c_low], axis=0)
    for x in range(g.cx):
        rows = slice(x * g.slab, (x + 1) * g.slab)
        h_high, h_low = split2(jnp.concatenate([low[:, rows], high[:, rows]], axis=0))
        halo = jnp.concatenate([h_high, h_low, h_high, h_low], axis=0)
        out[rows, :] = acc[rows, :] + lax.dot_general(halo, coefs, TN, preferred_element_type=F32)


def add_x_faces(g, dom, scale, face_refs, out, count):
    unit = 2 * g.no
    for (side, present), face in zip(g.faces(dom, 0), face_refs):
        for y in range(0, g.cy, 2):
            starts = [j * g.slab + y * g.no for j in range(RADIUS)]
            part = [flag(present) * face[at : at + unit, :].astype(F32) for at in starts]
            for i in range(RADIUS):
                at = aligned(layer(side, count, i) * g.slab + y * g.no, unit)
                total = out[pl.ds(at, unit), :]
                for j in range(RADIUS - i):
                    total = total + (scale * WEIGHT[i + j + 1]) * part[j]
                out[pl.ds(at, unit), :] = total


def add_y_faces(g, dom, scale, face_refs, out, start, count):
    size = RADIUS * g.no
    for (side, present), face in zip(g.faces(dom, 1), face_refs):
        for x in range(count):
            part = face[pl.ds(aligned((start + x) * size, 16), size), :]
            part = flag(present) * part.astype(F32)
            for i in range(RADIUS):
                at = aligned(x * g.slab + layer(side, g.cy, i) * g.no, g.no)
                total = out[pl.ds(at, g.no), :]
                for j in range(RADIUS - i):
                    total = total + (scale * WEIGHT[i + j + 1]) * part[j * g.no : (j + 1) * g.no]
                out[pl.ds(at, g.no), :] = total


def add_nonlocal(g, dom, table, energy, projf, blk, atom, lut, spread, out):
    size = g.nproj * g.no
    lanes = g.table
    count = g.slots()
    rows = []
    for step in g.steps(dom):
        owner = pl.ds(jnp.clip(dom + step, 0, g.dom_count - 1), 1)
        rows.append(table[owner, :] * energy[owner, :])
    rows.append(jnp.zeros((8 - count, lanes), F32))
    scaled = jnp.concatenate(rows, axis=0)
    high = scaled.astype(BF16)
    rest = scaled - high.astype(F32)
    mid = rest.astype(BF16)
    low = (rest - mid.astype(F32)).astype(BF16)
    parts = jnp.concatenate([high, mid, low], axis=0)
    wide = count * g.cz
    row, col = iota((24, wide), 0), iota((24, wide), 1)
    ones = jnp.where(row % 8 == col // g.cz, 1.0, 0.0).astype(BF16)
    out_all = lax.dot_general(parts, ones, TN, preferred_element_type=F32)
    for number in range(count):
        spread[number * lanes : (number + 1) * lanes, :] = out_all[:, number * g.cz : (number + 1) * g.cz]
    unroll = 64

    def step(i, _):
        additions = []
        for u in range(unroll):
            e = i * unroll + u
            col = column_of(g, lut, atom[e])
            total = None
            for p in range(g.nproj):
                at = pl.ds(pl.multiple_of(col * size + p * g.no, g.no), g.no)
                coef = jnp.broadcast_to(projf[e, p : p + 1, :], (g.no, g.cz))
                term = spread[at, :] * coef
                total = term if total is None else total + term
            additions.append((pl.ds(pl.multiple_of(blk[e] * g.no, g.no), g.no), total))
        for at, total in additions:
            out[at, :] += total
        return 0

    lax.fori_loop(0, g.ent // unroll, step, 0)


def nonlocal_kernel(g, scale, far, acc, projf, energy, blk_hbm, atom_hbm, first, second, *refs):
    table, blk, atom, lut, sem, spread = refs[-6:]
    out = refs[-7]
    filtered = None
    if far:
        out, filtered = refs[-8:-6]
        y_refs = refs[-8 - len(g.face_rows(1)) : -8]
    copies = entry_copies(blk_hbm, atom_hbm, blk, atom, sem)
    dom = lax.axis_index("dom")
    fill_lut(g, dom, lut)
    if g.butterfly:
        group, opposite = refs[:2]
        table[...] = (group[...] + get_table(g, first)) + (get_table(g, second) + opposite[...])
    else:
        table[...] = refs[0][...]
    add_ends(g, dom, scale, acc, first, second, out)
    for copy in copies:
        copy.wait()
    add_nonlocal(g, dom, table, energy, projf, blk, atom, lut, spread, out)
    if far:
        start, count = halves(g, dom)[0]
        rows = pl.ds(aligned(start * g.slab, g.slab), count * g.slab)
        add_y_faces(g, dom, scale, y_refs, out.at[rows, :], start, count)
        filtered[...] = out[rows, :].astype(BF16)


def middle_kernel(g, acc, projf, blk_hbm, atom_hbm, *refs):
    nx, ny = len(g.face_rows(0)), len(g.face_rows(1))
    faces = refs[: nx + ny]
    u_ref, table, blk, atom, lut, sem = refs[nx + ny : nx + ny + 6]
    sums = refs[nx + ny + 6 :]
    copies = entry_copies(blk_hbm, atom_hbm, blk, atom, sem)
    dom = lax.axis_index("dom")
    fill_lut(g, dom, lut)
    clear(sums)
    u_ref[...] = acc[...]
    add_x_faces(g, dom, 1.0, faces[:nx], u_ref, g.cx)
    add_y_faces(g, dom, 1.0, faces[nx:], u_ref, 0, g.cx)
    for copy in copies:
        copy.wait()
    inner_tables(g, dom, u_ref, projf, blk, atom, lut, sums, table)


def halves(g, dom):
    if g.first != 2 or g.cx != 2 * RADIUS:
        return [(0, g.cx)]
    side = 1 - dom // g.plane
    return [((1 - side) * RADIUS, RADIUS), (side * RADIUS, RADIUS)]


def last_kernel(g, acc, *refs):
    nx = len(g.face_rows(0))
    filtered, work = refs[-2:]
    dom = lax.axis_index("dom")
    start, count = halves(g, dom)[-1]
    work[...] = acc[pl.ds(aligned(start * g.slab, g.slab), count * g.slab), :]
    add_x_faces(g, dom, 2.0, refs[:nx], work, count)
    add_y_faces(g, dom, 2.0, refs[nx:-2], work, start, count)
    filtered[...] = work[...].astype(BF16)


def panel_kernel(g, panel, weights):
    band = lax.axis_index("band")
    group = 16
    span = group * g.no
    norb = panel.shape[0]
    row, col = iota((span, norb), 0), iota((span, norb), 1)
    pick_out = jnp.where(col == band * g.no + row // group, 1.0, 0.0).astype(BF16)
    picked = lax.dot_general(pick_out, panel[...], NT, preferred_element_type=F32).astype(BF16)
    row, col = iota((norb, 2 * span), 0), iota((norb, 2 * span), 1)
    source = jnp.where(col < span, band, 1 - band) * g.no + col % g.no
    pick_in = jnp.where(row == source, 1.0, 0.0).astype(BF16)
    spread = lax.dot_general(picked, pick_in, NN, preferred_element_type=F32)
    row, col = iota((span, 2 * span), 0), iota((span, 2 * span), 1)
    same = row % group == (col % span) // g.no
    weights[...] = jnp.where(same, spread, 0.0).astype(BF16)


def rotate_kernel(g, number, own, other, weights, *refs):
    out_hbm, out, sem = refs[-3:]
    start, count = halves(g, lax.axis_index("dom"))[number]
    group = 16
    span = group * g.no
    copies = []
    size = count * g.cy
    for n in range(size // group):
        rows = slice(n * span, (n + 1) * span)
        both = jnp.concatenate([own[rows, :], other[rows, :]], axis=0)
        result = lax.dot_general(weights[...], both, NN, preferred_element_type=F32)
        for j in range(g.no):
            out[j, n * group : (n + 1) * group, :] = result[j * group : (j + 1) * group, :]
        to = pl.ds(aligned(start * g.cy + n * group, group), group)
        source = out.at[:, pl.ds(n * group, group), :]
        copies.append(pltpu.make_async_copy(source, out_hbm.at[:, to, :], sem.at[n]))
        copies[-1].start()
    for copy in copies:
        copy.wait()


def call(kernel, name, out_shape, scratch, args, specs, **options):
    return pl.pallas_call(
        kernel,
        name=name,
        out_shape=out_shape,
        in_specs=specs,
        out_specs=options.pop("out_specs", jax.tree.map(lambda _: VMEM, out_shape)),
        scratch_shapes=scratch,
        compiler_params=pltpu.CompilerParams(vmem_limit_bytes=48 * 1024 * 1024),
        cost_estimate=pl.CostEstimate(flops=1000, bytes_accessed=1000, transcendentals=0),
        **options,
    )(*args)


def shift(g, array, stride, extent, step):
    pairs = []
    for i in range(g.dom_count):
        place = i // stride % extent
        pairs.append((i, i + ((place + step) % extent - place) * stride))
    return lax.ppermute(array, "dom", pairs)


def swap_faces(g, faces, stride, extent):
    if extent == 2:
        return [shift(g, faces[0], stride, extent, 1)]
    if extent > 2:
        return [shift(g, faces[1], stride, extent, 1), shift(g, faces[0], stride, extent, -1)]
    return []


def shards(orbitals, potential, projectors, entry_atom, entry_block, kb_energy, panel):
    g = Geometry(
        orbitals.shape, projectors.shape[0], projectors.shape[1], kb_energy.shape[0], lax.axis_size("dom")
    )

    def in_hbm(array):
        return pltpu.with_memory_space_constraint(array, pltpu.HBM)

    orb = in_hbm(orbitals.reshape(g.flat, g.cz))
    pot = in_hbm(potential.reshape(g.rows, g.cz))
    proj = in_hbm(projectors)
    blk, atom = in_hbm(entry_block), in_hbm(entry_atom)
    field = jax.ShapeDtypeStruct((g.flat, g.cz), F32)
    x_faces = [jax.ShapeDtypeStruct((n, g.cz), BF16) for n in g.face_rows(0)]
    y_faces = [jax.ShapeDtypeStruct((n, g.cz), BF16) for n in g.face_rows(1)]
    nx = len(x_faces)
    ends = jax.ShapeDtypeStruct((8, g.flat), F32)
    table = jax.ShapeDtypeStruct((g.dom_count, g.table), F32)
    entries = [
        pltpu.SMEM((g.ent,), jnp.int32),
        pltpu.SMEM((g.ent,), jnp.int32),
        pltpu.SMEM((g.dom_count + 2 * g.plane,), jnp.int32),
        pltpu.SemaphoreType.DMA((2,)),
    ]
    slots = g.slots() * g.table
    sums = [pltpu.VMEM((slots, g.cz), F32) for _ in range(4)]
    spread = pltpu.VMEM((slots, g.cz), F32)
    indices = range(g.dom_count)

    def swap(array, *strides):
        pairs = [(i, i + sum(s * (1 - 2 * (i // s % 2)) for s in strides)) for i in indices]
        return lax.ppermute(array, "dom", pairs)

    def reverse(array):
        pairs = [(i, i - i % g.third + g.third - 1 - i % g.third) for i in indices]
        return lax.ppermute(array, "dom", pairs)

    def local_and_ends(scale, which, values, prev, part):
        energy = (scale / HALF_WIDTH) * kb_energy
        energy = jnp.repeat(energy.reshape(g.dom_count, g.owned * g.nproj), g.no, axis=1)
        acc = call(
            functools.partial(inside_kernel, g, scale, len(prev) > 0),
            "inside_" + which,
            field,
            [],
            [values, pot, *prev],
            [VMEM] * (2 + len(prev)),
        )

        after = []
        if g.butterfly:
            tables = [part, swap(part, g.plane), swap(part, g.third), swap(part, g.plane, g.third)]
            after.append(tables[2])
        *faces, first, second = call(
            functools.partial(pack_faces_kernel, g, len(after)),
            "faces_" + which,
            [*x_faces, *y_faces, ends, ends],
            [],
            [values, *after],
            [VMEM] * (1 + len(after)),
        )
        from_x = swap_faces(g, faces[:nx], g.plane, g.first)
        from_y = swap_faces(g, faces[nx:], g.third, g.second)
        if g.butterfly:
            first, second, group = call(
                functools.partial(pack_kernel, g),
                "pack_" + which,
                [ends, ends, table],
                [],
                [*tables, first, second, energy],
                [VMEM] * 7,
            )
        first, second = swap(first, 1), reverse(second)
        tables = [group, swap(group, 2)] if g.butterfly else [lax.psum(part, "dom")]
        far = []
        if prev and len(halves(g, 0)) == 2:
            far = [jax.ShapeDtypeStruct((halves(g, 0)[0][1] * g.slab, g.cz), BF16)]
            tables += from_y
        out = call(
            functools.partial(nonlocal_kernel, g, scale, len(far) > 0),
            "nonlocal_" + which,
            [field, *far],
            [pltpu.VMEM(table.shape, F32), *entries, spread],
            [acc, projf, energy, blk, atom, first, second, *tables],
            [VMEM] * 3 + [HBM] * 2 + [VMEM] * (2 + len(tables)),
        )
        return out, from_x + from_y

    v, projf, pot, part = call(
        functools.partial(first_kernel, g),
        "tables_first",
        [field, jax.ShapeDtypeStruct(proj.shape, F32), jax.ShapeDtypeStruct(pot.shape, F32), table],
        [
            pltpu.VMEM(orb.shape, F32),
            pltpu.VMEM(proj.shape, BF16),
            pltpu.SemaphoreType.DMA((3,)),
            *entries,
            *sums,
        ],
        [orb, proj, pot, blk, atom],
        [HBM] * 5,
    )
    (acc,), received = local_and_ends(1.0, "first", v, [], part)
    u, part = call(
        functools.partial(middle_kernel, g),
        "tables_second",
        [field, table],
        [*entries, *sums],
        [acc, projf, blk, atom, *received],
        [VMEM] * 2 + [HBM] * 2 + [VMEM] * len(received),
    )
    (acc, *far), received = local_and_ends(2.0, "second", u, [v], part)
    weights = call(
        functools.partial(panel_kernel, g),
        "panel",
        jax.ShapeDtypeStruct((16 * g.no, 32 * g.no), BF16),
        [],
        [panel],
        [VMEM],
    )
    rotated = None
    pieces = []
    parts = halves(g, 0)
    for number, (_, count) in enumerate(parts):
        if number < len(far):
            filtered = far[number]
        else:
            inputs = [acc, *received]
            filtered = call(
                functools.partial(last_kernel, g),
                "filtered",
                jax.ShapeDtypeStruct((count * g.slab, g.cz), BF16),
                [pltpu.VMEM((count * g.slab, g.cz), F32)],
                inputs,
                [VMEM] * len(inputs),
            )
        pieces.append((filtered, lax.ppermute(filtered, "band", [(0, 1), (1, 0)]), count))
    for number, (filtered, other, count) in enumerate(pieces):
        inputs = [filtered, other, weights] + ([] if rotated is None else [rotated])
        rotated = call(
            functools.partial(rotate_kernel, g, number),
            "rotate_%d" % number,
            jax.ShapeDtypeStruct((g.no, g.rows, g.cz), F32),
            [pltpu.VMEM((g.no, count * g.cy, g.cz), F32), pltpu.SemaphoreType.DMA((count * g.cy // 16,))],
            inputs,
            [VMEM] * 3 + [HBM] * (len(inputs) - 3),
            out_specs=HBM,
            input_output_aliases={} if rotated is None else {3: 0},
        )
    return rotated.reshape(orbitals.shape)


def solution(mesh):
    in_specs = (
        P("dom", "band", None, None, None),
        P("dom", None, None, None),
        P("dom", None, None),
        P("dom"),
        P("dom"),
        P(),
        P(),
    )
    out_specs = P("dom", "band", None, None, None)
    return jax.shard_map(shards, mesh=mesh, in_specs=in_specs, out_specs=out_specs, check_vma=False)
```

```python
import functools

import jax
import jax.numpy as jnp
from jax import lax
from jax.experimental import pallas as pl
from jax.experimental.pallas import tpu as pltpu
from jax.sharding import PartitionSpec as P

RADIUS = 6
PIECES = 3
COEFFS = (
    -5369.0 / 1800.0,
    12.0 / 7.0,
    -15.0 / 56.0,
    10.0 / 189.0,
    -1.0 / 112.0,
    2.0 / 1925.0,
    -1.0 / 16632.0,
)
KINETIC = -3.125
CENTER = 36.0
HALF_WIDTH = 34.0
WEIGHT = [KINETIC * c / HALF_WIDTH for c in COEFFS]
DIAGONAL = (3.0 * KINETIC * COEFFS[0] - CENTER) / HALF_WIDTH

F32 = jnp.float32
BF16 = jnp.bfloat16
VMEM = pl.BlockSpec(memory_space=pltpu.VMEM)
HBM = pl.BlockSpec(memory_space=pltpu.HBM)
NT = (((1,), (1,)), ((), ()))
TN = (((0,), (0,)), ((), ()))
NN = (((1,), (0,)), ((), ()))


def split2(x):
    high = x.astype(BF16)
    low = (x - high.astype(F32)).astype(BF16)
    return high, low


def iota(shape, dim):
    return lax.broadcasted_iota(jnp.int32, shape, dim)


def weight_at(distance, scale):
    out = jnp.zeros(distance.shape, F32)
    for k in range(1, RADIUS + 1):
        out = jnp.where(distance == k, scale * WEIGHT[k], out)
    return out


class Geometry:
    def __init__(self, orbitals, entries, nproj, atoms, dom_count):
        _, self.no, self.cx, self.cy, self.cz = orbitals
        self.rows = self.cx * self.cy
        self.flat = self.rows * self.no
        self.ent = entries
        self.nproj = nproj
        self.dom_count = dom_count
        self.owned = atoms // dom_count
        self.third = 4
        self.second = min(8, dom_count // 8)
        self.plane = self.second * self.third
        self.first = dom_count // self.plane
        self.table = self.owned * nproj * self.no
        self.slab = self.cy * self.no
        self.fold = self.flat // self.table
        self.butterfly = self.first == 2 and self.second == 2 and dom_count <= 2 * self.fold
        assert self.no == 8

    def faces(self, dom, dim):
        if dim == 0:
            extent, place = self.first, dom // self.plane
        else:
            extent, place = self.second, dom // self.third % self.second
        if extent == 2:
            return [(1 - place, None)]
        if extent > 2:
            return [(0, place > 0), (1, place < extent - 1)]
        return []

    def face_rows(self, dim):
        rows = RADIUS * self.slab if dim == 0 else self.cx * RADIUS * self.no
        return [rows] * len(self.faces(0, dim))

    def steps(self, dom):
        out = [0]
        for extent, stride in ((self.first, self.plane), (self.second, self.third), (self.third, 1)):
            if extent == 2:
                out.append((1 - 2 * (dom // stride % 2)) * stride)
            elif extent > 2:
                out.extend([stride, -stride])
        return out

    def slots(self):
        return len(self.steps(0))


def layer(side, length, j):
    if isinstance(side, int):
        return length - 1 - j if side else j
    return side * (length - 1 - j) + (1 - side) * j


def aligned(start, unit):
    return start if isinstance(start, int) else pl.multiple_of(start, unit)


def pack_x(g, dom, v_ref, refs):
    for (side, _), out in zip(g.faces(dom, 0), refs):
        for j in range(RADIUS):
            at = aligned(layer(side, g.cx, j) * g.slab, g.slab)
            out[j * g.slab : (j + 1) * g.slab, :] = v_ref[pl.ds(at, g.slab), :].astype(BF16)


def pack_y(g, dom, v_ref, refs):
    size = RADIUS * g.no
    for (side, _), out in zip(g.faces(dom, 1), refs):
        for x in range(g.cx):
            pieces = []
            for j in range(RADIUS):
                at = aligned(x * g.slab + layer(side, g.cy, j) * g.no, g.no)
                pieces.append(v_ref[pl.ds(at, g.no), :])
            out[x * size : (x + 1) * size, :] = jnp.concatenate(pieces, axis=0).astype(BF16)


def end_columns(g, dom):
    row, col = iota((16, g.cz), 0), iota((16, g.cz), 1)
    odd = dom % 2
    side = jnp.where(row < 8, 1 - odd, odd)
    return jnp.where(side == 1, g.cz - 1 - col, col), row


def pack_ends(g, dom, v_ref, first_ref, second_ref):
    inward, row = end_columns(g, dom)
    pick = jnp.where((inward == row % 8) & (row % 8 < RADIUS), 1.0, 0.0).astype(BF16)
    pick = jnp.concatenate([pick, pick], axis=1)
    for x in range(g.cx):
        rows = slice(x * g.slab, (x + 1) * g.slab)
        both = jnp.concatenate(split2(v_ref[rows, :]), axis=1)
        ends = lax.dot_general(pick, both, NT, preferred_element_type=F32)
        first_ref[:, rows] = ends[:8]
        second_ref[:, rows] = ends[8:]


def put_table(g, message, table):
    for n in range(g.dom_count):
        at = RADIUS + n // g.fold
        lanes = n % g.fold * g.table
        message[at : at + 1, lanes : lanes + g.table] = table[n : n + 1, :]


def get_table(g, message):
    rows = []
    for n in range(g.dom_count):
        at = RADIUS + n // g.fold
        lanes = n % g.fold * g.table
        rows.append(message[at : at + 1, lanes : lanes + g.table])
    return jnp.concatenate(rows, axis=0)


def fill_lut(g, dom, lut):
    for number, step in enumerate(g.steps(dom)):
        lut[g.plane + dom + step] = number * g.owned


def column_of(g, lut, atom):
    if g.owned & (g.owned - 1):
        owner = lax.div(atom, jnp.int32(g.owned))
        return lut[owner + g.plane] + (atom - owner * g.owned)
    owner = lax.shift_right_logical(atom, jnp.int32(g.owned.bit_length() - 1))
    return lut[owner + g.plane] + (atom & (g.owned - 1))


def inner_tables(g, dom, v_ref, projf, blk, atom, lut, sums, table):
    size = g.nproj * g.no

    unroll = 32

    def step(i, _):
        for u in range(unroll):
            part = sums[u % len(sums)]
            e = i * unroll + u
            col = column_of(g, lut, atom[e])
            v = v_ref[pl.ds(pl.multiple_of(blk[e] * g.no, g.no), g.no), :]
            for p in range(g.nproj):
                at = pl.ds(pl.multiple_of(col * size + p * g.no, g.no), g.no)
                coef = jnp.broadcast_to(projf[e, p : p + 1, :], v.shape)
                part[at, :] += v * coef
        return 0

    lax.fori_loop(0, g.ent // unroll, step, 0)
    total = sums[0][...]
    for part in sums[1:]:
        total = total + part[...]
    both = jnp.concatenate(split2(total), axis=1)
    ones = jnp.ones((8, both.shape[1]), BF16)
    summed = lax.dot_general(ones, both, NT, preferred_element_type=F32)
    table[...] = jnp.zeros(table.shape, F32)
    for number, step in enumerate(g.steps(dom)):
        owner = jnp.clip(dom + step, 0, g.dom_count - 1)
        table[pl.ds(owner, 1), :] += summed[0:1, number * g.table : (number + 1) * g.table]


def clear(sums):
    for part in sums:
        part[...] = jnp.zeros(part.shape, F32)


def entry_copies(blk_hbm, atom_hbm, blk, atom, sem):
    copies = [
        pltpu.make_async_copy(blk_hbm, blk, sem.at[0]),
        pltpu.make_async_copy(atom_hbm, atom, sem.at[1]),
    ]
    for copy in copies:
        copy.start()
    return copies


def first_kernel(g, orb_hbm, proj_hbm, pot_hbm, blk_hbm, atom_hbm, v_ref, projf, pot, table, *scratch):
    orb, proj, sem, blk, atom, lut, entry_sem = scratch[:7]
    sums = scratch[7:]
    copies = [
        pltpu.make_async_copy(proj_hbm, proj, sem.at[0]),
        pltpu.make_async_copy(pot_hbm, pot, sem.at[1]),
    ]
    for copy in copies:
        copy.start()
    size = g.rows // PIECES
    pieces = []
    for n in range(PIECES):
        for o in range(g.no):
            at = pl.ds(o * g.rows + n * size, size)
            pieces.append(pltpu.make_async_copy(orb_hbm.at[at, :], orb.at[at, :], sem.at[2 + len(pieces)]))
            pieces[-1].start()
    copies += entry_copies(blk_hbm, atom_hbm, blk, atom, entry_sem)
    dom = lax.axis_index("dom")
    fill_lut(g, dom, lut)
    clear(sums)
    copies[0].wait()
    projf[...] = proj[...].astype(F32)
    for r in range(g.rows):
        if r % size == 0:
            for piece in pieces[r // size * g.no : (r // size + 1) * g.no]:
                piece.wait()
        v_ref[r * g.no : (r + 1) * g.no, :] = orb[pl.ds(r, g.no, stride=g.rows), :]
    for copy in copies[1:]:
        copy.wait()
    inner_tables(g, dom, v_ref, projf, blk, atom, lut, sums, table)


def pack_kernel(g, v_ref, energy, *refs):
    if g.butterfly:
        part, from_x, from_y, from_xy = refs[:4]
        group = refs[-1]
        group[...] = (part[...] + from_x[...]) + (from_y[...] + from_xy[...])
        refs = refs[:-1]
    first, second = refs[-2:]
    pack_ends(g, lax.axis_index("dom"), v_ref, first, second)
    if g.butterfly:
        put_table(g, first, group)
        put_table(g, second, group)


def pack_faces_kernel(g, nafter, v_ref, *refs):
    nx = len(g.face_rows(0))
    dom = lax.axis_index("dom")
    refs = refs[nafter:]
    pack_x(g, dom, v_ref, refs[:nx])
    pack_y(g, dom, v_ref, refs[nx:])


def inside_kernel(g, scale, subtract, v_ref, pot, *refs):
    prev, out = refs if subtract else (None, refs[0])
    row, col = iota((g.cz, g.cz), 0), iota((g.cz, g.cz), 1)
    high, low = split2(weight_at(jnp.abs(row - col), scale))
    band = jnp.concatenate([high, low], axis=1)
    band = jnp.concatenate([band, band], axis=0)

    def cell(x, y):
        at = (x * g.cy + y) * g.no
        return v_ref[at : at + g.no, :]

    for x in range(g.cx):
        both = jnp.concatenate(split2(v_ref[x * g.slab : (x + 1) * g.slab, :]), axis=1)
        along = lax.dot_general(both, band, NN, preferred_element_type=F32)
        for y in range(g.cy):
            at = (x * g.cy + y) * g.no
            rows = slice(y * g.no, (y + 1) * g.no)
            here = cell(x, y)
            diag = jnp.broadcast_to(pot[x * g.cy + y : x * g.cy + y + 1, :], here.shape)
            total = along[rows, : g.cz] + along[rows, g.cz :]
            total = total + (scale * DIAGONAL + (scale / HALF_WIDTH) * diag) * here
            if subtract:
                total = total - prev[at : at + g.no, :]
            for k in range(1, RADIUS + 1):
                near = []
                for a, b in ((x - k, y), (x + k, y), (x, y - k), (x, y + k)):
                    if 0 <= a < g.cx and 0 <= b < g.cy:
                        near.append(cell(a, b))
                if near:
                    total = total + (scale * WEIGHT[k]) * sum(near[1:], near[0])
            out[at : at + g.no, :] = total


def flag(present):
    return 1.0 if present is None else jnp.where(present, 1.0, 0.0)


def add_ends(g, dom, scale, acc, low, high, others, out):
    inward, row = end_columns(g, dom)
    middle = (dom % g.third > 0) & (dom % g.third < g.third - 1)
    present = (row % 8 < RADIUS) & ((row < 8) | middle)
    coef = jnp.where(present, weight_at(inward + row % 8 + 1, scale), 0.0)
    c_high, c_low = split2(coef)
    coefs = jnp.concatenate([c_high, c_high, c_low, c_low], axis=0)
    for x in range(g.cx):
        rows = slice(x * g.slab, (x + 1) * g.slab)
        h_high, h_low = split2(jnp.concatenate([low[:, rows], high[:, rows]], axis=0))
        halo = jnp.concatenate([h_high, h_low, h_high, h_low], axis=0)
        total = acc[rows, :]
        for other in others:
            total = total + other[rows, :]
        out[rows, :] = total + lax.dot_general(halo, coefs, TN, preferred_element_type=F32)


def add_x_faces(g, dom, scale, face_refs, out, count):
    unit = 2 * g.no
    for (side, present), face in zip(g.faces(dom, 0), face_refs):
        for y in range(0, g.cy, 2):
            starts = [j * g.slab + y * g.no for j in range(RADIUS)]
            part = [flag(present) * face[at : at + unit, :].astype(F32) for at in starts]
            for i in range(RADIUS):
                at = aligned(layer(side, count, i) * g.slab + y * g.no, unit)
                total = out[pl.ds(at, unit), :]
                for j in range(RADIUS - i):
                    total = total + (scale * WEIGHT[i + j + 1]) * part[j]
                out[pl.ds(at, unit), :] = total


def add_y_faces(g, dom, scale, face_refs, out, start, count):
    size = RADIUS * g.no
    for (side, present), face in zip(g.faces(dom, 1), face_refs):
        for x in range(count):
            part = face[pl.ds(aligned((start + x) * size, 16), size), :]
            part = flag(present) * part.astype(F32)
            for i in range(RADIUS):
                at = aligned(x * g.slab + layer(side, g.cy, i) * g.no, g.no)
                total = out[pl.ds(at, g.no), :]
                for j in range(RADIUS - i):
                    total = total + (scale * WEIGHT[i + j + 1]) * part[j * g.no : (j + 1) * g.no]
                out[pl.ds(at, g.no), :] = total


def spread_rows(g, dom, table, energy, spread):
    lanes = g.table
    count = g.slots()
    rows = []
    for step in g.steps(dom):
        owner = pl.ds(jnp.clip(dom + step, 0, g.dom_count - 1), 1)
        rows.append(table[owner, :] * energy[owner, :])
    rows.append(jnp.zeros((8 - count, lanes), F32))
    scaled = jnp.concatenate(rows, axis=0)
    high = scaled.astype(BF16)
    rest = scaled - high.astype(F32)
    mid = rest.astype(BF16)
    low = (rest - mid.astype(F32)).astype(BF16)
    parts = jnp.concatenate([high, mid, low], axis=0)
    wide = count * g.cz
    row, col = iota((24, wide), 0), iota((24, wide), 1)
    ones = jnp.where(row % 8 == col // g.cz, 1.0, 0.0).astype(BF16)
    out_all = lax.dot_general(parts, ones, TN, preferred_element_type=F32)
    for number in range(count):
        spread[number * lanes : (number + 1) * lanes, :] = out_all[:, number * g.cz : (number + 1) * g.cz]

def add_nonlocal(g, projf, blk, atom, lut, spread, outs):
    size = g.nproj * g.no
    unroll = 32

    def step(i, _):
        for u in range(unroll):
            e = i * unroll + u
            col = column_of(g, lut, atom[e])
            total = None
            for p in range(g.nproj):
                at = pl.ds(pl.multiple_of(col * size + p * g.no, g.no), g.no)
                coef = jnp.broadcast_to(projf[e, p : p + 1, :], (g.no, g.cz))
                term = spread[at, :] * coef
                total = term if total is None else total + term
            at = pl.ds(pl.multiple_of(blk[e] * g.no, g.no), g.no)
            outs[u % len(outs)][at, :] += total
        return 0

    lax.fori_loop(0, g.ent // unroll, step, 0)


def nonlocal_kernel(g, scale, far, acc, projf, energy, blk_hbm, atom_hbm, first, second, *refs):
    table, blk, atom, lut, sem, spread, *sums = refs[-8:]
    out = refs[-9]
    if far:
        out, filtered = refs[-10:-8]
        y_refs = refs[-10 - len(g.face_rows(1)) : -10]
    copies = entry_copies(blk_hbm, atom_hbm, blk, atom, sem)
    dom = lax.axis_index("dom")
    fill_lut(g, dom, lut)
    if g.butterfly:
        group, opposite = refs[:2]
        table[...] = (group[...] + get_table(g, first)) + (get_table(g, second) + opposite[...])
    else:
        table[...] = refs[0][...]
    spread_rows(g, dom, table, energy, spread)
    clear(sums)
    for copy in copies:
        copy.wait()
    add_nonlocal(g, projf, blk, atom, lut, spread, sums)
    add_ends(g, dom, scale, acc, first, second, sums, out)
    if far:
        start, count = halves(g, dom)[0]
        rows = pl.ds(aligned(start * g.slab, g.slab), count * g.slab)
        add_y_faces(g, dom, scale, y_refs, out.at[rows, :], start, count)
        filtered[...] = out[rows, :].astype(BF16)


def middle_kernel(g, acc, projf, blk_hbm, atom_hbm, *refs):
    nx, ny = len(g.face_rows(0)), len(g.face_rows(1))
    faces = refs[: nx + ny]
    u_ref, table, blk, atom, lut, sem = refs[nx + ny : nx + ny + 6]
    sums = refs[nx + ny + 6 :]
    copies = entry_copies(blk_hbm, atom_hbm, blk, atom, sem)
    dom = lax.axis_index("dom")
    fill_lut(g, dom, lut)
    clear(sums)
    u_ref[...] = acc[...]
    add_x_faces(g, dom, 1.0, faces[:nx], u_ref, g.cx)
    add_y_faces(g, dom, 1.0, faces[nx:], u_ref, 0, g.cx)
    for copy in copies:
        copy.wait()
    inner_tables(g, dom, u_ref, projf, blk, atom, lut, sums, table)


def halves(g, dom):
    if g.first != 2 or g.cx != 2 * RADIUS:
        return [(0, g.cx)]
    side = 1 - dom // g.plane
    return [((1 - side) * RADIUS, RADIUS), (side * RADIUS, RADIUS)]


def last_kernel(g, acc, *refs):
    nx = len(g.face_rows(0))
    filtered, work = refs[-2:]
    dom = lax.axis_index("dom")
    start, count = halves(g, dom)[-1]
    work[...] = acc[pl.ds(aligned(start * g.slab, g.slab), count * g.slab), :]
    add_x_faces(g, dom, 2.0, refs[:nx], work, count)
    add_y_faces(g, dom, 2.0, refs[nx:-2], work, start, count)
    filtered[...] = work[...].astype(BF16)


def panel_kernel(g, panel, weights):
    band = lax.axis_index("band")
    group = 16
    span = group * g.no
    norb = panel.shape[0]
    row, col = iota((span, norb), 0), iota((span, norb), 1)
    pick_out = jnp.where(col == band * g.no + row // group, 1.0, 0.0).astype(BF16)
    picked = lax.dot_general(pick_out, panel[...], NT, preferred_element_type=F32).astype(BF16)
    row, col = iota((norb, 2 * span), 0), iota((norb, 2 * span), 1)
    source = jnp.where(col < span, band, 1 - band) * g.no + col % g.no
    pick_in = jnp.where(row == source, 1.0, 0.0).astype(BF16)
    spread = lax.dot_general(picked, pick_in, NN, preferred_element_type=F32)
    row, col = iota((span, 2 * span), 0), iota((span, 2 * span), 1)
    same = row % group == (col % span) // g.no
    weights[...] = jnp.where(same, spread, 0.0).astype(BF16)


def rotate_kernel(g, number, own, other, weights, *refs):
    out_hbm, out, sem = refs[-3:]
    start, count = halves(g, lax.axis_index("dom"))[number]
    group = 16
    span = group * g.no
    copies = []
    size = count * g.cy
    for n in range(size // group):
        rows = slice(n * span, (n + 1) * span)
        both = jnp.concatenate([own[rows, :], other[rows, :]], axis=0)
        result = lax.dot_general(weights[...], both, NN, preferred_element_type=F32)
        for j in range(g.no):
            out[j, n * group : (n + 1) * group, :] = result[j * group : (j + 1) * group, :]
        to = pl.ds(aligned(start * g.cy + n * group, group), group)
        source = out.at[:, pl.ds(n * group, group), :]
        copies.append(pltpu.make_async_copy(source, out_hbm.at[:, to, :], sem.at[n]))
        copies[-1].start()
    for copy in copies:
        copy.wait()


def call(kernel, name, out_shape, scratch, args, specs, **options):
    return pl.pallas_call(
        kernel,
        name=name,
        out_shape=out_shape,
        in_specs=specs,
        out_specs=options.pop("out_specs", jax.tree.map(lambda _: VMEM, out_shape)),
        scratch_shapes=scratch,
        compiler_params=pltpu.CompilerParams(vmem_limit_bytes=48 * 1024 * 1024),
        cost_estimate=pl.CostEstimate(flops=1000, bytes_accessed=1000, transcendentals=0),
        **options,
    )(*args)


def shift(g, array, stride, extent, step):
    pairs = []
    for i in range(g.dom_count):
        place = i // stride % extent
        pairs.append((i, i + ((place + step) % extent - place) * stride))
    return lax.ppermute(array, "dom", pairs)


def swap_faces(g, faces, stride, extent):
    if extent == 2:
        return [shift(g, faces[0], stride, extent, 1)]
    if extent > 2:
        return [shift(g, faces[1], stride, extent, 1), shift(g, faces[0], stride, extent, -1)]
    return []


def shards(orbitals, potential, projectors, entry_atom, entry_block, kb_energy, panel):
    g = Geometry(
        orbitals.shape, projectors.shape[0], projectors.shape[1], kb_energy.shape[0], lax.axis_size("dom")
    )

    def in_hbm(array):
        return pltpu.with_memory_space_constraint(array, pltpu.HBM)

    orb = in_hbm(orbitals.reshape(g.flat, g.cz))
    pot = in_hbm(potential.reshape(g.rows, g.cz))
    proj = in_hbm(projectors)
    blk, atom = in_hbm(entry_block), in_hbm(entry_atom)
    field = jax.ShapeDtypeStruct((g.flat, g.cz), F32)
    x_faces = [jax.ShapeDtypeStruct((n, g.cz), BF16) for n in g.face_rows(0)]
    y_faces = [jax.ShapeDtypeStruct((n, g.cz), BF16) for n in g.face_rows(1)]
    nx = len(x_faces)
    ends = jax.ShapeDtypeStruct((8, g.flat), F32)
    table = jax.ShapeDtypeStruct((g.dom_count, g.table), F32)
    entries = [
        pltpu.SMEM((g.ent,), jnp.int32),
        pltpu.SMEM((g.ent,), jnp.int32),
        pltpu.SMEM((g.dom_count + 2 * g.plane,), jnp.int32),
        pltpu.SemaphoreType.DMA((2,)),
    ]
    slots = g.slots() * g.table
    sums = [pltpu.VMEM((slots, g.cz), F32) for _ in range(4)]
    spread = pltpu.VMEM((slots, g.cz), F32)
    indices = range(g.dom_count)

    def swap(array, *strides):
        pairs = [(i, i + sum(s * (1 - 2 * (i // s % 2)) for s in strides)) for i in indices]
        return lax.ppermute(array, "dom", pairs)

    def reverse(array):
        pairs = [(i, i - i % g.third + g.third - 1 - i % g.third) for i in indices]
        return lax.ppermute(array, "dom", pairs)

    def local_and_ends(scale, which, values, prev, part):
        energy = (scale / HALF_WIDTH) * kb_energy
        energy = jnp.repeat(energy.reshape(g.dom_count, g.owned * g.nproj), g.no, axis=1)
        acc = call(
            functools.partial(inside_kernel, g, scale, len(prev) > 0),
            "inside_" + which,
            field,
            [],
            [values, pot, *prev],
            [VMEM] * (2 + len(prev)),
        )

        after = []
        tables = []
        if g.butterfly:
            tables = [part, swap(part, g.plane), swap(part, g.third), swap(part, g.plane, g.third)]
            after.append(tables[2])
        faces = call(
            functools.partial(pack_faces_kernel, g, len(after)),
            "faces_" + which,
            [*x_faces, *y_faces],
            [],
            [values, *after],
            [VMEM] * (1 + len(after)),
        )
        from_x = swap_faces(g, faces[:nx], g.plane, g.first)
        from_y = swap_faces(g, faces[nx:], g.third, g.second)
        first, second, *group = call(
            functools.partial(pack_kernel, g),
            "pack_" + which,
            [ends, ends, table] if g.butterfly else [ends, ends],
            [],
            [values, energy, *tables],
            [VMEM] * (2 + len(tables)),
        )
        first, second = swap(first, 1), reverse(second)
        tables = [*group, swap(group[0], 2)] if g.butterfly else [lax.psum(part, "dom")]
        far = []
        if prev and len(halves(g, 0)) == 2:
            far = [jax.ShapeDtypeStruct((halves(g, 0)[0][1] * g.slab, g.cz), BF16)]
            tables += from_y
        out = call(
            functools.partial(nonlocal_kernel, g, scale, len(far) > 0),
            "nonlocal_" + which,
            [field, *far],
            [pltpu.VMEM(table.shape, F32), *entries, spread] + [pltpu.VMEM(field.shape, F32)] * 2,
            [acc, projf, energy, blk, atom, first, second, *tables],
            [VMEM] * 3 + [HBM] * 2 + [VMEM] * (2 + len(tables)),
        )
        return out, from_x + from_y

    v, projf, pot, part = call(
        functools.partial(first_kernel, g),
        "tables_first",
        [field, jax.ShapeDtypeStruct(proj.shape, F32), jax.ShapeDtypeStruct(pot.shape, F32), table],
        [
            pltpu.VMEM(orb.shape, F32),
            pltpu.VMEM(proj.shape, BF16),
            pltpu.SemaphoreType.DMA((2 + PIECES * g.no,)),
            *entries,
            *sums,
        ],
        [orb, proj, pot, blk, atom],
        [HBM] * 5,
    )
    (acc,), received = local_and_ends(1.0, "first", v, [], part)
    u, part = call(
        functools.partial(middle_kernel, g),
        "tables_second",
        [field, table],
        [*entries, *sums],
        [acc, projf, blk, atom, *received],
        [VMEM] * 2 + [HBM] * 2 + [VMEM] * len(received),
    )
    (acc, *far), received = local_and_ends(2.0, "second", u, [v], part)
    weights = call(
        functools.partial(panel_kernel, g),
        "panel",
        jax.ShapeDtypeStruct((16 * g.no, 32 * g.no), BF16),
        [],
        [panel],
        [VMEM],
    )
    rotated = None
    pieces = []
    parts = halves(g, 0)
    for number, (_, count) in enumerate(parts):
        if number < len(far):
            filtered = far[number]
        else:
            inputs = [acc, *received]
            filtered = call(
                functools.partial(last_kernel, g),
                "filtered",
                jax.ShapeDtypeStruct((count * g.slab, g.cz), BF16),
                [pltpu.VMEM((count * g.slab, g.cz), F32)],
                inputs,
                [VMEM] * len(inputs),
            )
        pieces.append((filtered, lax.ppermute(filtered, "band", [(0, 1), (1, 0)]), count))
    for number, (filtered, other, count) in enumerate(pieces):
        inputs = [filtered, other, weights] + ([] if rotated is None else [rotated])
        rotated = call(
            functools.partial(rotate_kernel, g, number),
            "rotate_%d" % number,
            jax.ShapeDtypeStruct((g.no, g.rows, g.cz), F32),
            [pltpu.VMEM((g.no, count * g.cy, g.cz), F32), pltpu.SemaphoreType.DMA((count * g.cy // 16,))],
            inputs,
            [VMEM] * 3 + [HBM] * (len(inputs) - 3),
            out_specs=HBM,
            input_output_aliases={} if rotated is None else {3: 0},
        )
    return rotated.reshape(orbitals.shape)


def solution(mesh):
    in_specs = (
        P("dom", "band", None, None, None),
        P("dom", None, None, None),
        P("dom", None, None),
        P("dom"),
        P("dom"),
        P(),
        P(),
    )
    out_specs = P("dom", "band", None, None, None)
    return jax.shard_map(shards, mesh=mesh, in_specs=in_specs, out_specs=out_specs, check_vma=False)
```

```python
import functools

import jax
import jax.numpy as jnp
from jax import lax
from jax.experimental import pallas as pl
from jax.experimental.pallas import tpu as pltpu
from jax.sharding import PartitionSpec as P

RADIUS = 6
PIECES = 3
COEFFS = (
    -5369.0 / 1800.0,
    12.0 / 7.0,
    -15.0 / 56.0,
    10.0 / 189.0,
    -1.0 / 112.0,
    2.0 / 1925.0,
    -1.0 / 16632.0,
)
KINETIC = -3.125
CENTER = 36.0
HALF_WIDTH = 34.0
WEIGHT = [KINETIC * c / HALF_WIDTH for c in COEFFS]
DIAGONAL = (3.0 * KINETIC * COEFFS[0] - CENTER) / HALF_WIDTH

F32 = jnp.float32
BF16 = jnp.bfloat16
VMEM = pl.BlockSpec(memory_space=pltpu.VMEM)
HBM = pl.BlockSpec(memory_space=pltpu.HBM)
NT = (((1,), (1,)), ((), ()))
TN = (((0,), (0,)), ((), ()))
NN = (((1,), (0,)), ((), ()))


def split2(x):
    high = x.astype(BF16)
    low = (x - high.astype(F32)).astype(BF16)
    return high, low


def iota(shape, dim):
    return lax.broadcasted_iota(jnp.int32, shape, dim)


def weight_at(distance, scale):
    out = jnp.zeros(distance.shape, F32)
    for k in range(1, RADIUS + 1):
        out = jnp.where(distance == k, scale * WEIGHT[k], out)
    return out


class Geometry:
    def __init__(self, orbitals, entries, nproj, atoms, dom_count):
        _, self.no, self.cx, self.cy, self.cz = orbitals
        self.rows = self.cx * self.cy
        self.flat = self.rows * self.no
        self.ent = entries
        self.nproj = nproj
        self.dom_count = dom_count
        self.owned = atoms // dom_count
        self.third = 4
        self.second = min(8, dom_count // 8)
        self.plane = self.second * self.third
        self.first = dom_count // self.plane
        self.table = self.owned * nproj * self.no
        self.slab = self.cy * self.no
        self.fold = self.flat // self.table
        self.butterfly = self.first == 2 and self.second == 2 and dom_count <= 2 * self.fold
        assert self.no == 8

    def faces(self, dom, dim):
        if dim == 0:
            extent, place = self.first, dom // self.plane
        else:
            extent, place = self.second, dom // self.third % self.second
        if extent == 2:
            return [(1 - place, None)]
        if extent > 2:
            return [(0, place > 0), (1, place < extent - 1)]
        return []

    def face_rows(self, dim):
        rows = RADIUS * self.slab if dim == 0 else self.cx * RADIUS * self.no
        return [rows] * len(self.faces(0, dim))

    def steps(self, dom):
        out = [0]
        for extent, stride in ((self.first, self.plane), (self.second, self.third), (self.third, 1)):
            if extent == 2:
                out.append((1 - 2 * (dom // stride % 2)) * stride)
            elif extent > 2:
                out.extend([stride, -stride])
        return out

    def slots(self):
        return len(self.steps(0))


def layer(side, length, j):
    if isinstance(side, int):
        return length - 1 - j if side else j
    return side * (length - 1 - j) + (1 - side) * j


def aligned(start, unit):
    return start if isinstance(start, int) else pl.multiple_of(start, unit)


def pack_x(g, dom, v_ref, refs):
    for (side, _), out in zip(g.faces(dom, 0), refs):
        for j in range(RADIUS):
            at = aligned(layer(side, g.cx, j) * g.slab, g.slab)
            out[j * g.slab : (j + 1) * g.slab, :] = v_ref[pl.ds(at, g.slab), :].astype(BF16)


def pack_y(g, dom, v_ref, refs):
    size = RADIUS * g.no
    for (side, _), out in zip(g.faces(dom, 1), refs):
        for x in range(g.cx):
            pieces = []
            for j in range(RADIUS):
                at = aligned(x * g.slab + layer(side, g.cy, j) * g.no, g.no)
                pieces.append(v_ref[pl.ds(at, g.no), :])
            out[x * size : (x + 1) * size, :] = jnp.concatenate(pieces, axis=0).astype(BF16)


def end_columns(g, dom):
    row, col = iota((16, g.cz), 0), iota((16, g.cz), 1)
    odd = dom % 2
    side = jnp.where(row < 8, 1 - odd, odd)
    return jnp.where(side == 1, g.cz - 1 - col, col), row


def pack_ends(g, dom, v_ref, first_ref, second_ref):
    inward, row = end_columns(g, dom)
    pick = jnp.where((inward == row % 8) & (row % 8 < RADIUS), 1.0, 0.0).astype(BF16)
    pick = jnp.concatenate([pick, pick], axis=1)
    for x in range(g.cx):
        rows = slice(x * g.slab, (x + 1) * g.slab)
        both = jnp.concatenate(split2(v_ref[rows, :]), axis=1)
        ends = lax.dot_general(pick, both, NT, preferred_element_type=F32)
        first_ref[:, rows] = ends[:8]
        second_ref[:, rows] = ends[8:]


def put_table(g, message, table):
    for n in range(g.dom_count):
        at = RADIUS + n // g.fold
        lanes = n % g.fold * g.table
        message[at : at + 1, lanes : lanes + g.table] = table[n : n + 1, :]


def get_table(g, message):
    rows = []
    for n in range(g.dom_count):
        at = RADIUS + n // g.fold
        lanes = n % g.fold * g.table
        rows.append(message[at : at + 1, lanes : lanes + g.table])
    return jnp.concatenate(rows, axis=0)


def fill_lut(g, dom, lut):
    for number, step in enumerate(g.steps(dom)):
        lut[g.plane + dom + step] = number * g.owned


def column_of(g, lut, atom):
    if g.owned & (g.owned - 1):
        owner = lax.div(atom, jnp.int32(g.owned))
        return lut[owner + g.plane] + (atom - owner * g.owned)
    owner = lax.shift_right_logical(atom, jnp.int32(g.owned.bit_length() - 1))
    return lut[owner + g.plane] + (atom & (g.owned - 1))


def inner_tables(g, dom, v_ref, projf, blk, atom, lut, sums, table):
    size = g.nproj * g.no

    unroll = 32

    def step(i, _):
        for u in range(unroll):
            part = sums[u % len(sums)]
            e = i * unroll + u
            col = column_of(g, lut, atom[e])
            v = v_ref[pl.ds(pl.multiple_of(blk[e] * g.no, g.no), g.no), :]
            for p in range(g.nproj):
                at = pl.ds(pl.multiple_of(col * size + p * g.no, g.no), g.no)
                coef = jnp.broadcast_to(projf[e, p : p + 1, :], v.shape)
                part[at, :] += v * coef
        return 0

    lax.fori_loop(0, g.ent // unroll, step, 0)
    total = sums[0][...]
    for part in sums[1:]:
        total = total + part[...]
    both = jnp.concatenate(split2(total), axis=1)
    ones = jnp.ones((8, both.shape[1]), BF16)
    summed = lax.dot_general(ones, both, NT, preferred_element_type=F32)
    table[...] = jnp.zeros(table.shape, F32)
    for number, step in enumerate(g.steps(dom)):
        owner = jnp.clip(dom + step, 0, g.dom_count - 1)
        table[pl.ds(owner, 1), :] += summed[0:1, number * g.table : (number + 1) * g.table]


def clear(sums):
    for part in sums:
        part[...] = jnp.zeros(part.shape, F32)


def entry_copies(blk_hbm, atom_hbm, blk, atom, sem):
    copies = [
        pltpu.make_async_copy(blk_hbm, blk, sem.at[0]),
        pltpu.make_async_copy(atom_hbm, atom, sem.at[1]),
    ]
    for copy in copies:
        copy.start()
    return copies


def first_kernel(g, orb_hbm, proj_hbm, pot_hbm, blk_hbm, atom_hbm, v_ref, projf, pot, table, *scratch):
    orb, proj, sem, blk, atom, lut, entry_sem = scratch[:7]
    sums = scratch[7:]
    copies = [
        pltpu.make_async_copy(proj_hbm, proj, sem.at[0]),
        pltpu.make_async_copy(pot_hbm, pot, sem.at[1]),
    ]
    for copy in copies:
        copy.start()
    size = g.rows // PIECES
    pieces = []
    for n in range(PIECES):
        for o in range(g.no):
            at = pl.ds(o * g.rows + n * size, size)
            pieces.append(pltpu.make_async_copy(orb_hbm.at[at, :], orb.at[at, :], sem.at[2 + len(pieces)]))
            pieces[-1].start()
    copies += entry_copies(blk_hbm, atom_hbm, blk, atom, entry_sem)
    dom = lax.axis_index("dom")
    fill_lut(g, dom, lut)
    clear(sums)
    copies[0].wait()
    projf[...] = proj[...].astype(F32)
    for r in range(g.rows):
        if r % size == 0:
            for piece in pieces[r // size * g.no : (r // size + 1) * g.no]:
                piece.wait()
        v_ref[r * g.no : (r + 1) * g.no, :] = orb[pl.ds(r, g.no, stride=g.rows), :]
    for copy in copies[1:]:
        copy.wait()
    inner_tables(g, dom, v_ref, projf, blk, atom, lut, sums, table)


def pack_kernel(g, v_ref, energy, *refs):
    if g.butterfly:
        part, from_x, from_y, from_xy = refs[:4]
        group = refs[-1]
        group[...] = (part[...] + from_x[...]) + (from_y[...] + from_xy[...])
        refs = refs[:-1]
    first, second = refs[-2:]
    pack_ends(g, lax.axis_index("dom"), v_ref, first, second)
    if g.butterfly:
        put_table(g, first, group)
        put_table(g, second, group)


def pack_faces_kernel(g, nafter, v_ref, *refs):
    nx = len(g.face_rows(0))
    dom = lax.axis_index("dom")
    refs = refs[nafter:]
    pack_x(g, dom, v_ref, refs[:nx])
    pack_y(g, dom, v_ref, refs[nx:])


def inside_kernel(g, scale, subtract, v_ref, pot, *refs):
    prev, out = refs if subtract else (None, refs[0])
    row, col = iota((g.cz, g.cz), 0), iota((g.cz, g.cz), 1)
    high, low = split2(weight_at(jnp.abs(row - col), scale))
    band = jnp.concatenate([high, low], axis=1)
    band = jnp.concatenate([band, band], axis=0)

    def cell(x, y):
        at = (x * g.cy + y) * g.no
        return v_ref[at : at + g.no, :]

    for x in range(g.cx):
        both = jnp.concatenate(split2(v_ref[x * g.slab : (x + 1) * g.slab, :]), axis=1)
        along = lax.dot_general(both, band, NN, preferred_element_type=F32)
        for y in range(g.cy):
            at = (x * g.cy + y) * g.no
            rows = slice(y * g.no, (y + 1) * g.no)
            here = cell(x, y)
            diag = jnp.broadcast_to(pot[x * g.cy + y : x * g.cy + y + 1, :], here.shape)
            total = along[rows, : g.cz] + along[rows, g.cz :]
            total = total + (scale * DIAGONAL + (scale / HALF_WIDTH) * diag) * here
            if subtract:
                total = total - prev[at : at + g.no, :]
            for k in range(1, RADIUS + 1):
                near = []
                for a, b in ((x - k, y), (x + k, y), (x, y - k), (x, y + k)):
                    if 0 <= a < g.cx and 0 <= b < g.cy:
                        near.append(cell(a, b))
                if near:
                    total = total + (scale * WEIGHT[k]) * sum(near[1:], near[0])
            out[at : at + g.no, :] = total


def flag(present):
    return 1.0 if present is None else jnp.where(present, 1.0, 0.0)


def add_ends(g, dom, scale, acc, low, high, others, out, start, count):
    inward, row = end_columns(g, dom)
    middle = (dom % g.third > 0) & (dom % g.third < g.third - 1)
    present = (row % 8 < RADIUS) & ((row < 8) | middle)
    coef = jnp.where(present, weight_at(inward + row % 8 + 1, scale), 0.0)
    c_high, c_low = split2(coef)
    coefs = jnp.concatenate([c_high, c_high, c_low, c_low], axis=0)
    for x in range(count):
        rows = pl.ds(aligned((start + x) * g.slab, g.slab), g.slab)
        h_high, h_low = split2(jnp.concatenate([low[:, rows], high[:, rows]], axis=0))
        halo = jnp.concatenate([h_high, h_low, h_high, h_low], axis=0)
        total = acc[rows, :]
        for other in others:
            total = total + other[rows, :]
        total = total + lax.dot_general(halo, coefs, TN, preferred_element_type=F32)
        out[x * g.slab : (x + 1) * g.slab, :] = total


def add_x_faces(g, dom, scale, face_refs, out, count):
    unit = 2 * g.no
    for (side, present), face in zip(g.faces(dom, 0), face_refs):
        for y in range(0, g.cy, 2):
            starts = [j * g.slab + y * g.no for j in range(RADIUS)]
            part = [flag(present) * face[at : at + unit, :].astype(F32) for at in starts]
            for i in range(RADIUS):
                at = aligned(layer(side, count, i) * g.slab + y * g.no, unit)
                total = out[pl.ds(at, unit), :]
                for j in range(RADIUS - i):
                    total = total + (scale * WEIGHT[i + j + 1]) * part[j]
                out[pl.ds(at, unit), :] = total


def add_y_faces(g, dom, scale, face_refs, out, start, count):
    size = RADIUS * g.no
    for (side, present), face in zip(g.faces(dom, 1), face_refs):
        for x in range(count):
            part = face[pl.ds(aligned((start + x) * size, 16), size), :]
            part = flag(present) * part.astype(F32)
            for i in range(RADIUS):
                at = aligned(x * g.slab + layer(side, g.cy, i) * g.no, g.no)
                total = out[pl.ds(at, g.no), :]
                for j in range(RADIUS - i):
                    total = total + (scale * WEIGHT[i + j + 1]) * part[j * g.no : (j + 1) * g.no]
                out[pl.ds(at, g.no), :] = total


def spread_rows(g, dom, table, energy, spread):
    lanes = g.table
    count = g.slots()
    rows = []
    for step in g.steps(dom):
        owner = pl.ds(jnp.clip(dom + step, 0, g.dom_count - 1), 1)
        rows.append(table[owner, :] * energy[owner, :])
    rows.append(jnp.zeros((8 - count, lanes), F32))
    scaled = jnp.concatenate(rows, axis=0)
    high = scaled.astype(BF16)
    rest = scaled - high.astype(F32)
    mid = rest.astype(BF16)
    low = (rest - mid.astype(F32)).astype(BF16)
    parts = jnp.concatenate([high, mid, low], axis=0)
    wide = count * g.cz
    row, col = iota((24, wide), 0), iota((24, wide), 1)
    ones = jnp.where(row % 8 == col // g.cz, 1.0, 0.0).astype(BF16)
    out_all = lax.dot_general(parts, ones, TN, preferred_element_type=F32)
    for number in range(count):
        spread[number * lanes : (number + 1) * lanes, :] = out_all[:, number * g.cz : (number + 1) * g.cz]

def add_nonlocal(g, projf, blk, atom, lut, spread, outs):
    size = g.nproj * g.no
    unroll = 32

    def step(i, _):
        for u in range(unroll):
            e = i * unroll + u
            col = column_of(g, lut, atom[e])
            total = None
            for p in range(g.nproj):
                at = pl.ds(pl.multiple_of(col * size + p * g.no, g.no), g.no)
                coef = jnp.broadcast_to(projf[e, p : p + 1, :], (g.no, g.cz))
                term = spread[at, :] * coef
                total = term if total is None else total + term
            at = pl.ds(pl.multiple_of(blk[e] * g.no, g.no), g.no)
            outs[u % len(outs)][at, :] += total
        return 0

    lax.fori_loop(0, g.ent // unroll, step, 0)


def nonlocal_kernel(g, scale, far, acc, projf, energy, blk_hbm, atom_hbm, first, second, *refs):
    if far:
        filtered, *sums, table, blk, atom, lut, sem, spread, out = refs[-10:]
        y_refs = refs[-10 - len(g.face_rows(1)) : -10]
    else:
        out, table, blk, atom, lut, sem, spread, *sums = refs[-9:]
    copies = entry_copies(blk_hbm, atom_hbm, blk, atom, sem)
    dom = lax.axis_index("dom")
    fill_lut(g, dom, lut)
    if g.butterfly:
        group, opposite = refs[:2]
        table[...] = (group[...] + get_table(g, first)) + (get_table(g, second) + opposite[...])
    else:
        table[...] = refs[0][...]
    spread_rows(g, dom, table, energy, spread)
    clear(sums)
    for copy in copies:
        copy.wait()
    add_nonlocal(g, projf, blk, atom, lut, spread, sums)
    start, count = halves(g, dom)[0] if far else (0, g.cx)
    add_ends(g, dom, scale, acc, first, second, sums, out, start, count)
    if far:
        add_y_faces(g, dom, scale, y_refs, out, start, count)
        filtered[...] = out[...].astype(BF16)


def middle_kernel(g, acc, projf, blk_hbm, atom_hbm, *refs):
    nx, ny = len(g.face_rows(0)), len(g.face_rows(1))
    faces = refs[: nx + ny]
    u_ref, table, blk, atom, lut, sem = refs[nx + ny : nx + ny + 6]
    sums = refs[nx + ny + 6 :]
    copies = entry_copies(blk_hbm, atom_hbm, blk, atom, sem)
    dom = lax.axis_index("dom")
    fill_lut(g, dom, lut)
    clear(sums)
    u_ref[...] = acc[...]
    add_x_faces(g, dom, 1.0, faces[:nx], u_ref, g.cx)
    add_y_faces(g, dom, 1.0, faces[nx:], u_ref, 0, g.cx)
    for copy in copies:
        copy.wait()
    inner_tables(g, dom, u_ref, projf, blk, atom, lut, sums, table)


def halves(g, dom):
    if g.first != 2 or g.cx != 2 * RADIUS:
        return [(0, g.cx)]
    side = 1 - dom // g.plane
    return [((1 - side) * RADIUS, RADIUS), (side * RADIUS, RADIUS)]


def last_kernel(g, rest, acc, *refs):
    nx = len(g.face_rows(0))
    filtered, work = refs[-2:]
    dom = lax.axis_index("dom")
    start, count = halves(g, dom)[-1]
    if rest:
        first, second, *sums = refs[:4]
        add_ends(g, dom, 2.0, acc, first, second, sums, work, start, count)
        refs = refs[4:]
    else:
        work[...] = acc[pl.ds(aligned(start * g.slab, g.slab), count * g.slab), :]
    add_x_faces(g, dom, 2.0, refs[:nx], work, count)
    add_y_faces(g, dom, 2.0, refs[nx:-2], work, start, count)
    filtered[...] = work[...].astype(BF16)


def panel_kernel(g, panel, weights):
    band = lax.axis_index("band")
    group = 16
    span = group * g.no
    norb = panel.shape[0]
    row, col = iota((span, norb), 0), iota((span, norb), 1)
    pick_out = jnp.where(col == band * g.no + row // group, 1.0, 0.0).astype(BF16)
    picked = lax.dot_general(pick_out, panel[...], NT, preferred_element_type=F32).astype(BF16)
    row, col = iota((norb, 2 * span), 0), iota((norb, 2 * span), 1)
    source = jnp.where(col < span, band, 1 - band) * g.no + col % g.no
    pick_in = jnp.where(row == source, 1.0, 0.0).astype(BF16)
    spread = lax.dot_general(picked, pick_in, NN, preferred_element_type=F32)
    row, col = iota((span, 2 * span), 0), iota((span, 2 * span), 1)
    same = row % group == (col % span) // g.no
    weights[...] = jnp.where(same, spread, 0.0).astype(BF16)


def rotate_kernel(g, number, own, other, weights, *refs):
    out_hbm, out, sem = refs[-3:]
    start, count = halves(g, lax.axis_index("dom"))[number]
    group = 16
    span = group * g.no
    copies = []
    size = count * g.cy
    for n in range(size // group):
        rows = slice(n * span, (n + 1) * span)
        both = jnp.concatenate([own[rows, :], other[rows, :]], axis=0)
        result = lax.dot_general(weights[...], both, NN, preferred_element_type=F32)
        for j in range(g.no):
            out[j, n * group : (n + 1) * group, :] = result[j * group : (j + 1) * group, :]
        to = pl.ds(aligned(start * g.cy + n * group, group), group)
        source = out.at[:, pl.ds(n * group, group), :]
        copies.append(pltpu.make_async_copy(source, out_hbm.at[:, to, :], sem.at[n]))
        copies[-1].start()
    for copy in copies:
        copy.wait()


def call(kernel, name, out_shape, scratch, args, specs, **options):
    return pl.pallas_call(
        kernel,
        name=name,
        out_shape=out_shape,
        in_specs=specs,
        out_specs=options.pop("out_specs", jax.tree.map(lambda _: VMEM, out_shape)),
        scratch_shapes=scratch,
        compiler_params=pltpu.CompilerParams(vmem_limit_bytes=48 * 1024 * 1024),
        cost_estimate=pl.CostEstimate(flops=1000, bytes_accessed=1000, transcendentals=0),
        **options,
    )(*args)


def shift(g, array, stride, extent, step):
    pairs = []
    for i in range(g.dom_count):
        place = i // stride % extent
        pairs.append((i, i + ((place + step) % extent - place) * stride))
    return lax.ppermute(array, "dom", pairs)


def swap_faces(g, faces, stride, extent):
    if extent == 2:
        return [shift(g, faces[0], stride, extent, 1)]
    if extent > 2:
        return [shift(g, faces[1], stride, extent, 1), shift(g, faces[0], stride, extent, -1)]
    return []


def shards(orbitals, potential, projectors, entry_atom, entry_block, kb_energy, panel):
    g = Geometry(
        orbitals.shape, projectors.shape[0], projectors.shape[1], kb_energy.shape[0], lax.axis_size("dom")
    )

    def in_hbm(array):
        return pltpu.with_memory_space_constraint(array, pltpu.HBM)

    orb = in_hbm(orbitals.reshape(g.flat, g.cz))
    pot = in_hbm(potential.reshape(g.rows, g.cz))
    proj = in_hbm(projectors)
    blk, atom = in_hbm(entry_block), in_hbm(entry_atom)
    field = jax.ShapeDtypeStruct((g.flat, g.cz), F32)
    x_faces = [jax.ShapeDtypeStruct((n, g.cz), BF16) for n in g.face_rows(0)]
    y_faces = [jax.ShapeDtypeStruct((n, g.cz), BF16) for n in g.face_rows(1)]
    nx = len(x_faces)
    ends = jax.ShapeDtypeStruct((8, g.flat), F32)
    table = jax.ShapeDtypeStruct((g.dom_count, g.table), F32)
    entries = [
        pltpu.SMEM((g.ent,), jnp.int32),
        pltpu.SMEM((g.ent,), jnp.int32),
        pltpu.SMEM((g.dom_count + 2 * g.plane,), jnp.int32),
        pltpu.SemaphoreType.DMA((2,)),
    ]
    slots = g.slots() * g.table
    sums = [pltpu.VMEM((slots, g.cz), F32) for _ in range(4)]
    spread = pltpu.VMEM((slots, g.cz), F32)
    indices = range(g.dom_count)

    def swap(array, *strides):
        pairs = [(i, i + sum(s * (1 - 2 * (i // s % 2)) for s in strides)) for i in indices]
        return lax.ppermute(array, "dom", pairs)

    def reverse(array):
        pairs = [(i, i - i % g.third + g.third - 1 - i % g.third) for i in indices]
        return lax.ppermute(array, "dom", pairs)

    def local_and_ends(scale, which, values, prev, part):
        energy = (scale / HALF_WIDTH) * kb_energy
        energy = jnp.repeat(energy.reshape(g.dom_count, g.owned * g.nproj), g.no, axis=1)
        acc = call(
            functools.partial(inside_kernel, g, scale, len(prev) > 0),
            "inside_" + which,
            field,
            [],
            [values, pot, *prev],
            [VMEM] * (2 + len(prev)),
        )

        after = []
        tables = []
        if g.butterfly:
            tables = [part, swap(part, g.third), swap(part, g.plane), swap(part, g.plane, g.third)]
            after.append(tables[1])
        faces = call(
            functools.partial(pack_faces_kernel, g, len(after)),
            "faces_" + which,
            [*x_faces, *y_faces],
            [],
            [values, *after],
            [VMEM] * (1 + len(after)),
        )
        from_x = swap_faces(g, faces[:nx], g.plane, g.first)
        from_y = swap_faces(g, faces[nx:], g.third, g.second)
        first, second, *group = call(
            functools.partial(pack_kernel, g),
            "pack_" + which,
            [ends, ends, table] if g.butterfly else [ends, ends],
            [],
            [values, energy, *tables, *faces],
            [VMEM] * (2 + len(tables) + len(faces)),
        )
        first, second = swap(first, 1), reverse(second)
        tables = [*group, swap(group[0], 2)] if g.butterfly else [lax.psum(part, "dom")]
        far = prev and len(halves(g, 0)) == 2
        scratch = [pltpu.VMEM(table.shape, F32), *entries, spread]
        outputs = [field]
        if far:
            half = halves(g, 0)[0][1] * g.slab
            outputs = [jax.ShapeDtypeStruct((half, g.cz), BF16), field, field]
            scratch.append(pltpu.VMEM((half, g.cz), F32))
            tables += from_y
        else:
            scratch += [pltpu.VMEM(field.shape, F32)] * 2
        out = call(
            functools.partial(nonlocal_kernel, g, scale, far),
            "nonlocal_" + which,
            outputs,
            scratch,
            [acc, projf, energy, blk, atom, first, second, *tables],
            [VMEM] * 3 + [HBM] * 2 + [VMEM] * (2 + len(tables)),
        )
        if far:
            out = [acc, first, second, *out[1:], out[0]]
        return out, from_x + from_y

    v, projf, pot, part = call(
        functools.partial(first_kernel, g),
        "tables_first",
        [field, jax.ShapeDtypeStruct(proj.shape, F32), jax.ShapeDtypeStruct(pot.shape, F32), table],
        [
            pltpu.VMEM(orb.shape, F32),
            pltpu.VMEM(proj.shape, BF16),
            pltpu.SemaphoreType.DMA((2 + PIECES * g.no,)),
            *entries,
            *sums,
        ],
        [orb, proj, pot, blk, atom],
        [HBM] * 5,
    )
    (acc,), received = local_and_ends(1.0, "first", v, [], part)
    u, part = call(
        functools.partial(middle_kernel, g),
        "tables_second",
        [field, table],
        [*entries, *sums],
        [acc, projf, blk, atom, *received],
        [VMEM] * 2 + [HBM] * 2 + [VMEM] * len(received),
    )
    out, received = local_and_ends(2.0, "second", u, [v], part)
    far = out[5:]
    weights = call(
        functools.partial(panel_kernel, g),
        "panel",
        jax.ShapeDtypeStruct((16 * g.no, 32 * g.no), BF16),
        [],
        [panel],
        [VMEM],
    )
    rotated = None
    pieces = []
    parts = halves(g, 0)
    for number, (_, count) in enumerate(parts):
        if number < len(far):
            filtered = far[number]
        else:
            inputs = [*out[:5], *received]
            filtered = call(
                functools.partial(last_kernel, g, len(far) > 0),
                "filtered",
                jax.ShapeDtypeStruct((count * g.slab, g.cz), BF16),
                [pltpu.VMEM((count * g.slab, g.cz), F32)],
                inputs,
                [VMEM] * len(inputs),
            )
        pieces.append((filtered, lax.ppermute(filtered, "band", [(0, 1), (1, 0)]), count))
    for number, (filtered, other, count) in enumerate(pieces):
        inputs = [filtered, other, weights] + ([] if rotated is None else [rotated])
        rotated = call(
            functools.partial(rotate_kernel, g, number),
            "rotate_%d" % number,
            jax.ShapeDtypeStruct((g.no, g.rows, g.cz), F32),
            [pltpu.VMEM((g.no, count * g.cy, g.cz), F32), pltpu.SemaphoreType.DMA((count * g.cy // 16,))],
            inputs,
            [VMEM] * 3 + [HBM] * (len(inputs) - 3),
            out_specs=HBM,
            input_output_aliases={} if rotated is None else {3: 0},
        )
    return rotated.reshape(orbitals.shape)


def solution(mesh):
    in_specs = (
        P("dom", "band", None, None, None),
        P("dom", None, None, None),
        P("dom", None, None),
        P("dom"),
        P("dom"),
        P(),
        P(),
    )
    out_specs = P("dom", "band", None, None, None)
    return jax.shard_map(shards, mesh=mesh, in_specs=in_specs, out_specs=out_specs, check_vma=False)
```

```python
import functools

import jax
import jax.numpy as jnp
from jax import lax
from jax.experimental import pallas as pl
from jax.experimental.pallas import tpu as pltpu
from jax.sharding import PartitionSpec as P

RADIUS = 6
PIECES = 3
COEFFS = (
    -5369.0 / 1800.0,
    12.0 / 7.0,
    -15.0 / 56.0,
    10.0 / 189.0,
    -1.0 / 112.0,
    2.0 / 1925.0,
    -1.0 / 16632.0,
)
KINETIC = -3.125
CENTER = 36.0
HALF_WIDTH = 34.0
WEIGHT = [KINETIC * c / HALF_WIDTH for c in COEFFS]
DIAGONAL = (3.0 * KINETIC * COEFFS[0] - CENTER) / HALF_WIDTH

F32 = jnp.float32
BF16 = jnp.bfloat16
VMEM = pl.BlockSpec(memory_space=pltpu.VMEM)
HBM = pl.BlockSpec(memory_space=pltpu.HBM)
NT = (((1,), (1,)), ((), ()))
TN = (((0,), (0,)), ((), ()))
NN = (((1,), (0,)), ((), ()))


def split2(x):
    high = x.astype(BF16)
    low = (x - high.astype(F32)).astype(BF16)
    return high, low


def iota(shape, dim):
    return lax.broadcasted_iota(jnp.int32, shape, dim)


def weight_at(distance, scale):
    out = jnp.zeros(distance.shape, F32)
    for k in range(1, RADIUS + 1):
        out = jnp.where(distance == k, scale * WEIGHT[k], out)
    return out


class Geometry:
    def __init__(self, orbitals, entries, nproj, atoms, dom_count):
        _, self.no, self.cx, self.cy, self.cz = orbitals
        self.rows = self.cx * self.cy
        self.flat = self.rows * self.no
        self.ent = entries
        self.nproj = nproj
        self.dom_count = dom_count
        self.owned = atoms // dom_count
        self.third = 4
        self.second = min(8, dom_count // 8)
        self.plane = self.second * self.third
        self.first = dom_count // self.plane
        self.table = self.owned * nproj * self.no
        self.slab = self.cy * self.no
        self.fold = self.flat // self.table
        self.butterfly = self.first == 2 and self.second == 2 and dom_count <= 2 * self.fold
        assert self.no == 8

    def faces(self, dom, dim):
        if dim == 0:
            extent, place = self.first, dom // self.plane
        else:
            extent, place = self.second, dom // self.third % self.second
        if extent == 2:
            return [(1 - place, None)]
        if extent > 2:
            return [(0, place > 0), (1, place < extent - 1)]
        return []

    def face_rows(self, dim):
        rows = RADIUS * self.slab if dim == 0 else self.cx * RADIUS * self.no
        return [rows] * len(self.faces(0, dim))

    def steps(self, dom):
        out = [0]
        for extent, stride in ((self.first, self.plane), (self.second, self.third), (self.third, 1)):
            if extent == 2:
                out.append((1 - 2 * (dom // stride % 2)) * stride)
            elif extent > 2:
                out.extend([stride, -stride])
        return out

    def slots(self):
        return len(self.steps(0))


def layer(side, length, j):
    if isinstance(side, int):
        return length - 1 - j if side else j
    return side * (length - 1 - j) + (1 - side) * j


def aligned(start, unit):
    return start if isinstance(start, int) else pl.multiple_of(start, unit)


def pack_x(g, dom, v_ref, refs):
    for (side, _), out in zip(g.faces(dom, 0), refs):
        for j in range(RADIUS):
            at = aligned(layer(side, g.cx, j) * g.slab, g.slab)
            out[j * g.slab : (j + 1) * g.slab, :] = v_ref[pl.ds(at, g.slab), :].astype(BF16)


def pack_y(g, dom, v_ref, refs):
    size = RADIUS * g.no
    for (side, _), out in zip(g.faces(dom, 1), refs):
        for x in range(g.cx):
            pieces = []
            for j in range(RADIUS):
                at = aligned(x * g.slab + layer(side, g.cy, j) * g.no, g.no)
                pieces.append(v_ref[pl.ds(at, g.no), :])
            out[x * size : (x + 1) * size, :] = jnp.concatenate(pieces, axis=0).astype(BF16)


def end_columns(g, dom):
    row, col = iota((16, g.cz), 0), iota((16, g.cz), 1)
    odd = dom % 2
    side = jnp.where(row < 8, 1 - odd, odd)
    return jnp.where(side == 1, g.cz - 1 - col, col), row


def pack_ends(g, dom, v_ref, first_ref, second_ref):
    inward, row = end_columns(g, dom)
    pick = jnp.where((inward == row % 8) & (row % 8 < RADIUS), 1.0, 0.0).astype(BF16)
    pick = jnp.concatenate([pick, pick], axis=1)
    for x in range(g.cx):
        rows = slice(x * g.slab, (x + 1) * g.slab)
        both = jnp.concatenate(split2(v_ref[rows, :]), axis=1)
        ends = lax.dot_general(pick, both, NT, preferred_element_type=F32)
        first_ref[:, rows] = ends[:8]
        second_ref[:, rows] = ends[8:]


def put_table(g, message, table):
    for n in range(g.dom_count):
        at = RADIUS + n // g.fold
        lanes = n % g.fold * g.table
        message[at : at + 1, lanes : lanes + g.table] = table[n : n + 1, :]


def get_table(g, message):
    rows = []
    for n in range(g.dom_count):
        at = RADIUS + n // g.fold
        lanes = n % g.fold * g.table
        rows.append(message[at : at + 1, lanes : lanes + g.table])
    return jnp.concatenate(rows, axis=0)


def fill_lut(g, dom, lut):
    for number, step in enumerate(g.steps(dom)):
        lut[g.plane + dom + step] = number * g.owned


def column_of(g, lut, atom):
    if g.owned & (g.owned - 1):
        owner = lax.div(atom, jnp.int32(g.owned))
        return lut[owner + g.plane] + (atom - owner * g.owned)
    owner = lax.shift_right_logical(atom, jnp.int32(g.owned.bit_length() - 1))
    return lut[owner + g.plane] + (atom & (g.owned - 1))


def inner_tables(g, dom, v_ref, projf, blk, atom, lut, sums, table):
    size = g.nproj * g.no

    unroll = 32

    def step(i, _):
        for u in range(unroll):
            part = sums[u % len(sums)]
            e = i * unroll + u
            col = column_of(g, lut, atom[e])
            v = v_ref[pl.ds(pl.multiple_of(blk[e] * g.no, g.no), g.no), :]
            for p in range(g.nproj):
                at = pl.ds(pl.multiple_of(col * size + p * g.no, g.no), g.no)
                coef = jnp.broadcast_to(projf[e, p : p + 1, :], v.shape)
                part[at, :] += v * coef
        return 0

    lax.fori_loop(0, g.ent // unroll, step, 0)
    total = sums[0][...]
    for part in sums[1:]:
        total = total + part[...]
    both = jnp.concatenate(split2(total), axis=1)
    ones = jnp.ones((8, both.shape[1]), BF16)
    summed = lax.dot_general(ones, both, NT, preferred_element_type=F32)
    table[...] = jnp.zeros(table.shape, F32)
    for number, step in enumerate(g.steps(dom)):
        owner = jnp.clip(dom + step, 0, g.dom_count - 1)
        table[pl.ds(owner, 1), :] += summed[0:1, number * g.table : (number + 1) * g.table]


def clear(sums):
    for part in sums:
        part[...] = jnp.zeros(part.shape, F32)


def entry_copies(blk_hbm, atom_hbm, blk, atom, sem):
    copies = [
        pltpu.make_async_copy(blk_hbm, blk, sem.at[0]),
        pltpu.make_async_copy(atom_hbm, atom, sem.at[1]),
    ]
    for copy in copies:
        copy.start()
    return copies


def first_kernel(g, orb_hbm, proj_hbm, pot_hbm, blk_hbm, atom_hbm, v_ref, projf, pot, table, *scratch):
    orb, proj, sem, blk, atom, lut, entry_sem = scratch[:7]
    sums = scratch[7:]
    copies = [
        pltpu.make_async_copy(proj_hbm, proj, sem.at[0]),
        pltpu.make_async_copy(pot_hbm, pot, sem.at[1]),
    ]
    for copy in copies:
        copy.start()
    size = g.rows // PIECES
    pieces = []
    for n in range(PIECES):
        for o in range(g.no):
            at = pl.ds(o * g.rows + n * size, size)
            pieces.append(pltpu.make_async_copy(orb_hbm.at[at, :], orb.at[at, :], sem.at[2 + len(pieces)]))
            pieces[-1].start()
    copies += entry_copies(blk_hbm, atom_hbm, blk, atom, entry_sem)
    dom = lax.axis_index("dom")
    fill_lut(g, dom, lut)
    clear(sums)
    copies[0].wait()
    projf[...] = proj[...].astype(F32)
    for r in range(g.rows):
        if r % size == 0:
            for piece in pieces[r // size * g.no : (r // size + 1) * g.no]:
                piece.wait()
        v_ref[r * g.no : (r + 1) * g.no, :] = orb[pl.ds(r, g.no, stride=g.rows), :]
    for copy in copies[1:]:
        copy.wait()
    inner_tables(g, dom, v_ref, projf, blk, atom, lut, sums, table)


def pack_kernel(g, count, *refs):
    source, refs = refs[:count], refs[count:]
    part, from_x, from_y, from_xy = refs[:4]
    outs, group = refs[-3:-1], refs[-1]
    group[...] = (part[...] + from_x[...]) + (from_y[...] + from_xy[...])
    if len(source) == 1:
        pack_ends(g, lax.axis_index("dom"), *source, *outs)
    for n, out in enumerate(outs):
        if len(source) == 2:
            out[...] = source[n][...]
        put_table(g, out, group)


def pack_faces_kernel(g, nafter, v_ref, *refs):
    nx = len(g.face_rows(0))
    dom = lax.axis_index("dom")
    refs = refs[nafter:]
    pack_x(g, dom, v_ref, refs[:nx])
    ny = len(g.face_rows(1))
    pack_y(g, dom, v_ref, refs[nx : nx + ny])
    if len(refs) > nx + ny:
        pack_ends(g, dom, v_ref, *refs[nx + ny :])


def inside_kernel(g, scale, subtract, v_ref, pot, *refs):
    prev, out = refs if subtract else (None, refs[0])
    row, col = iota((g.cz, g.cz), 0), iota((g.cz, g.cz), 1)
    high, low = split2(weight_at(jnp.abs(row - col), scale))
    band = jnp.concatenate([high, low], axis=1)
    band = jnp.concatenate([band, band], axis=0)

    def cell(x, y):
        at = (x * g.cy + y) * g.no
        return v_ref[at : at + g.no, :]

    for x in range(g.cx):
        both = jnp.concatenate(split2(v_ref[x * g.slab : (x + 1) * g.slab, :]), axis=1)
        along = lax.dot_general(both, band, NN, preferred_element_type=F32)
        for y in range(g.cy):
            at = (x * g.cy + y) * g.no
            rows = slice(y * g.no, (y + 1) * g.no)
            here = cell(x, y)
            diag = jnp.broadcast_to(pot[x * g.cy + y : x * g.cy + y + 1, :], here.shape)
            total = along[rows, : g.cz] + along[rows, g.cz :]
            total = total + (scale * DIAGONAL + (scale / HALF_WIDTH) * diag) * here
            if subtract:
                total = total - prev[at : at + g.no, :]
            for k in range(1, RADIUS + 1):
                near = []
                for a, b in ((x - k, y), (x + k, y), (x, y - k), (x, y + k)):
                    if 0 <= a < g.cx and 0 <= b < g.cy:
                        near.append(cell(a, b))
                if near:
                    total = total + (scale * WEIGHT[k]) * sum(near[1:], near[0])
            out[at : at + g.no, :] = total


def flag(present):
    return 1.0 if present is None else jnp.where(present, 1.0, 0.0)


def add_ends(g, dom, scale, acc, low, high, others, out, start, count):
    inward, row = end_columns(g, dom)
    middle = (dom % g.third > 0) & (dom % g.third < g.third - 1)
    present = (row % 8 < RADIUS) & ((row < 8) | middle)
    coef = jnp.where(present, weight_at(inward + row % 8 + 1, scale), 0.0)
    c_high, c_low = split2(coef)
    coefs = jnp.concatenate([c_high, c_high, c_low, c_low], axis=0)
    for x in range(count):
        rows = pl.ds(aligned((start + x) * g.slab, g.slab), g.slab)
        h_high, h_low = split2(jnp.concatenate([low[:, rows], high[:, rows]], axis=0))
        halo = jnp.concatenate([h_high, h_low, h_high, h_low], axis=0)
        total = acc[rows, :]
        for other in others:
            total = total + other[rows, :]
        total = total + lax.dot_general(halo, coefs, TN, preferred_element_type=F32)
        out[x * g.slab : (x + 1) * g.slab, :] = total


def add_x_faces(g, dom, scale, face_refs, out, count):
    unit = 2 * g.no
    for (side, present), face in zip(g.faces(dom, 0), face_refs):
        for y in range(0, g.cy, 2):
            starts = [j * g.slab + y * g.no for j in range(RADIUS)]
            part = [flag(present) * face[at : at + unit, :].astype(F32) for at in starts]
            for i in range(RADIUS):
                at = aligned(layer(side, count, i) * g.slab + y * g.no, unit)
                total = out[pl.ds(at, unit), :]
                for j in range(RADIUS - i):
                    total = total + (scale * WEIGHT[i + j + 1]) * part[j]
                out[pl.ds(at, unit), :] = total


def add_y_faces(g, dom, scale, face_refs, out, start, count):
    size = RADIUS * g.no
    for (side, present), face in zip(g.faces(dom, 1), face_refs):
        for x in range(count):
            part = face[pl.ds(aligned((start + x) * size, 16), size), :]
            part = flag(present) * part.astype(F32)
            for i in range(RADIUS):
                at = aligned(x * g.slab + layer(side, g.cy, i) * g.no, g.no)
                total = out[pl.ds(at, g.no), :]
                for j in range(RADIUS - i):
                    total = total + (scale * WEIGHT[i + j + 1]) * part[j * g.no : (j + 1) * g.no]
                out[pl.ds(at, g.no), :] = total


def spread_rows(g, dom, table, energy, spread):
    lanes = g.table
    count = g.slots()
    rows = []
    for step in g.steps(dom):
        owner = pl.ds(jnp.clip(dom + step, 0, g.dom_count - 1), 1)
        rows.append(table[owner, :] * energy[owner, :])
    rows.append(jnp.zeros((8 - count, lanes), F32))
    scaled = jnp.concatenate(rows, axis=0)
    high = scaled.astype(BF16)
    rest = scaled - high.astype(F32)
    mid = rest.astype(BF16)
    low = (rest - mid.astype(F32)).astype(BF16)
    parts = jnp.concatenate([high, mid, low], axis=0)
    wide = count * g.cz
    row, col = iota((24, wide), 0), iota((24, wide), 1)
    ones = jnp.where(row % 8 == col // g.cz, 1.0, 0.0).astype(BF16)
    out_all = lax.dot_general(parts, ones, TN, preferred_element_type=F32)
    for number in range(count):
        spread[number * lanes : (number + 1) * lanes, :] = out_all[:, number * g.cz : (number + 1) * g.cz]

def add_nonlocal(g, projf, blk, atom, lut, spread, outs):
    size = g.nproj * g.no
    unroll = 32

    def step(i, _):
        for u in range(unroll):
            e = i * unroll + u
            col = column_of(g, lut, atom[e])
            total = None
            for p in range(g.nproj):
                at = pl.ds(pl.multiple_of(col * size + p * g.no, g.no), g.no)
                coef = jnp.broadcast_to(projf[e, p : p + 1, :], (g.no, g.cz))
                term = spread[at, :] * coef
                total = term if total is None else total + term
            at = pl.ds(pl.multiple_of(blk[e] * g.no, g.no), g.no)
            outs[u % len(outs)][at, :] += total
        return 0

    lax.fori_loop(0, g.ent // unroll, step, 0)


def nonlocal_kernel(g, scale, far, acc, projf, energy, blk_hbm, atom_hbm, first, second, *refs):
    if far:
        filtered, *sums, table, blk, atom, lut, sem, spread, out = refs[-10:]
        y_refs = refs[-10 - len(g.face_rows(1)) : -10]
    else:
        out, table, blk, atom, lut, sem, spread, *sums = refs[-9:]
    copies = entry_copies(blk_hbm, atom_hbm, blk, atom, sem)
    dom = lax.axis_index("dom")
    fill_lut(g, dom, lut)
    if g.butterfly:
        group, opposite = refs[:2]
        table[...] = (group[...] + get_table(g, first)) + (get_table(g, second) + opposite[...])
    else:
        table[...] = refs[0][...]
    spread_rows(g, dom, table, energy, spread)
    clear(sums)
    for copy in copies:
        copy.wait()
    add_nonlocal(g, projf, blk, atom, lut, spread, sums)
    start, count = halves(g, dom)[0] if far else (0, g.cx)
    add_ends(g, dom, scale, acc, first, second, sums, out, start, count)
    if far:
        add_y_faces(g, dom, scale, y_refs, out, start, count)
        filtered[...] = out[...].astype(BF16)


def middle_kernel(g, acc, projf, blk_hbm, atom_hbm, *refs):
    nx, ny = len(g.face_rows(0)), len(g.face_rows(1))
    faces = refs[: nx + ny]
    u_ref, table, blk, atom, lut, sem = refs[nx + ny : nx + ny + 6]
    sums = refs[nx + ny + 6 :]
    copies = entry_copies(blk_hbm, atom_hbm, blk, atom, sem)
    dom = lax.axis_index("dom")
    fill_lut(g, dom, lut)
    clear(sums)
    u_ref[...] = acc[...]
    add_x_faces(g, dom, 1.0, faces[:nx], u_ref, g.cx)
    add_y_faces(g, dom, 1.0, faces[nx:], u_ref, 0, g.cx)
    for copy in copies:
        copy.wait()
    inner_tables(g, dom, u_ref, projf, blk, atom, lut, sums, table)


def halves(g, dom):
    if g.first != 2 or g.cx != 2 * RADIUS:
        return [(0, g.cx)]
    side = 1 - dom // g.plane
    return [((1 - side) * RADIUS, RADIUS), (side * RADIUS, RADIUS)]


def last_kernel(g, rest, acc, *refs):
    nx = len(g.face_rows(0))
    filtered, work = refs[-2:]
    dom = lax.axis_index("dom")
    start, count = halves(g, dom)[-1]
    if rest:
        first, second, *sums = refs[:4]
        add_ends(g, dom, 2.0, acc, first, second, sums, work, start, count)
        refs = refs[4:]
    else:
        work[...] = acc[pl.ds(aligned(start * g.slab, g.slab), count * g.slab), :]
    add_x_faces(g, dom, 2.0, refs[:nx], work, count)
    add_y_faces(g, dom, 2.0, refs[nx:-2], work, start, count)
    filtered[...] = work[...].astype(BF16)


def panel_kernel(g, panel, weights):
    band = lax.axis_index("band")
    group = 16
    span = group * g.no
    norb = panel.shape[0]
    row, col = iota((span, norb), 0), iota((span, norb), 1)
    pick_out = jnp.where(col == band * g.no + row // group, 1.0, 0.0).astype(BF16)
    picked = lax.dot_general(pick_out, panel[...], NT, preferred_element_type=F32).astype(BF16)
    row, col = iota((norb, 2 * span), 0), iota((norb, 2 * span), 1)
    source = jnp.where(col < span, band, 1 - band) * g.no + col % g.no
    pick_in = jnp.where(row == source, 1.0, 0.0).astype(BF16)
    spread = lax.dot_general(picked, pick_in, NN, preferred_element_type=F32)
    row, col = iota((span, 2 * span), 0), iota((span, 2 * span), 1)
    same = row % group == (col % span) // g.no
    weights[...] = jnp.where(same, spread, 0.0).astype(BF16)


def rotate_kernel(g, number, own, other, weights, *refs):
    out_hbm, out, sem = refs[-3:]
    start, count = halves(g, lax.axis_index("dom"))[number]
    group = 16
    span = group * g.no
    copies = []
    size = count * g.cy
    for n in range(size // group):
        rows = slice(n * span, (n + 1) * span)
        both = jnp.concatenate([own[rows, :], other[rows, :]], axis=0)
        result = lax.dot_general(weights[...], both, NN, preferred_element_type=F32)
        for j in range(g.no):
            out[j, n * group : (n + 1) * group, :] = result[j * group : (j + 1) * group, :]
        to = pl.ds(aligned(start * g.cy + n * group, group), group)
        source = out.at[:, pl.ds(n * group, group), :]
        copies.append(pltpu.make_async_copy(source, out_hbm.at[:, to, :], sem.at[n]))
        copies[-1].start()
    for copy in copies:
        copy.wait()


def call(kernel, name, out_shape, scratch, args, specs, **options):
    return pl.pallas_call(
        kernel,
        name=name,
        out_shape=out_shape,
        in_specs=specs,
        out_specs=options.pop("out_specs", jax.tree.map(lambda _: VMEM, out_shape)),
        scratch_shapes=scratch,
        compiler_params=pltpu.CompilerParams(vmem_limit_bytes=48 * 1024 * 1024),
        cost_estimate=pl.CostEstimate(flops=1000, bytes_accessed=1000, transcendentals=0),
        **options,
    )(*args)


def shift(g, array, stride, extent, step):
    pairs = []
    for i in range(g.dom_count):
        place = i // stride % extent
        pairs.append((i, i + ((place + step) % extent - place) * stride))
    return lax.ppermute(array, "dom", pairs)


def swap_faces(g, faces, stride, extent):
    if extent == 2:
        return [shift(g, faces[0], stride, extent, 1)]
    if extent > 2:
        return [shift(g, faces[1], stride, extent, 1), shift(g, faces[0], stride, extent, -1)]
    return []


def shards(orbitals, potential, projectors, entry_atom, entry_block, kb_energy, panel):
    g = Geometry(
        orbitals.shape, projectors.shape[0], projectors.shape[1], kb_energy.shape[0], lax.axis_size("dom")
    )

    def in_hbm(array):
        return pltpu.with_memory_space_constraint(array, pltpu.HBM)

    orb = in_hbm(orbitals.reshape(g.flat, g.cz))
    pot = in_hbm(potential.reshape(g.rows, g.cz))
    proj = in_hbm(projectors)
    blk, atom = in_hbm(entry_block), in_hbm(entry_atom)
    field = jax.ShapeDtypeStruct((g.flat, g.cz), F32)
    x_faces = [jax.ShapeDtypeStruct((n, g.cz), BF16) for n in g.face_rows(0)]
    y_faces = [jax.ShapeDtypeStruct((n, g.cz), BF16) for n in g.face_rows(1)]
    nx = len(x_faces)
    ends = jax.ShapeDtypeStruct((8, g.flat), F32)
    table = jax.ShapeDtypeStruct((g.dom_count, g.table), F32)
    entries = [
        pltpu.SMEM((g.ent,), jnp.int32),
        pltpu.SMEM((g.ent,), jnp.int32),
        pltpu.SMEM((g.dom_count + 2 * g.plane,), jnp.int32),
        pltpu.SemaphoreType.DMA((2,)),
    ]
    slots = g.slots() * g.table
    sums = [pltpu.VMEM((slots, g.cz), F32) for _ in range(4)]
    spread = pltpu.VMEM((slots, g.cz), F32)
    indices = range(g.dom_count)

    def swap(array, *strides):
        pairs = [(i, i + sum(s * (1 - 2 * (i // s % 2)) for s in strides)) for i in indices]
        return lax.ppermute(array, "dom", pairs)

    def reverse(array):
        pairs = [(i, i - i % g.third + g.third - 1 - i % g.third) for i in indices]
        return lax.ppermute(array, "dom", pairs)

    def local_and_ends(scale, which, values, prev, part):
        energy = (scale / HALF_WIDTH) * kb_energy
        energy = jnp.repeat(energy.reshape(g.dom_count, g.owned * g.nproj), g.no, axis=1)
        acc = call(
            functools.partial(inside_kernel, g, scale, len(prev) > 0),
            "inside_" + which,
            field,
            [],
            [values, pot, *prev],
            [VMEM] * (2 + len(prev)),
        )

        after = []
        tables = []
        if g.butterfly:
            routes = [(g.third,), (g.plane, g.third), (g.plane,)]
            if not prev:
                routes = [(g.third,), (g.plane,), (g.plane, g.third)]
            tables = [part] + [swap(part, *route) for route in routes]
            after.append(tables[1])
        packed = [ends, ends] if prev or not g.butterfly else []
        faces = call(
            functools.partial(pack_faces_kernel, g, len(after)),
            "faces_" + which,
            [*x_faces, *y_faces, *packed],
            [],
            [values, *after],
            [VMEM] * (1 + len(after)),
        )
        both = nx + len(y_faces)
        from_x = swap_faces(g, faces[:nx], g.plane, g.first)
        from_y = swap_faces(g, faces[nx:both], g.third, g.second)
        source = faces[both:] or [values]
        if g.butterfly:
            first, second, group = call(
                functools.partial(pack_kernel, g, len(source)),
                "pack_" + which,
                [ends, ends, table],
                [],
                [*source, *tables, energy],
                [VMEM] * (len(source) + 5),
            )
        else:
            first, second = source
        first, second = swap(first, 1), reverse(second)
        tables = [group, swap(group, 2)] if g.butterfly else [lax.psum(part, "dom")]
        far = prev and len(halves(g, 0)) == 2
        scratch = [pltpu.VMEM(table.shape, F32), *entries, spread]
        outputs = [field]
        if far:
            half = halves(g, 0)[0][1] * g.slab
            outputs = [jax.ShapeDtypeStruct((half, g.cz), BF16), field, field]
            scratch.append(pltpu.VMEM((half, g.cz), F32))
            tables += from_y
        else:
            scratch += [pltpu.VMEM(field.shape, F32)] * 2
        out = call(
            functools.partial(nonlocal_kernel, g, scale, far),
            "nonlocal_" + which,
            outputs,
            scratch,
            [acc, projf, energy, blk, atom, first, second, *tables],
            [VMEM] * 3 + [HBM] * 2 + [VMEM] * (2 + len(tables)),
        )
        if far:
            out = [acc, first, second, *out[1:], out[0]]
        return out, from_x + from_y

    v, projf, pot, part = call(
        functools.partial(first_kernel, g),
        "tables_first",
        [field, jax.ShapeDtypeStruct(proj.shape, F32), jax.ShapeDtypeStruct(pot.shape, F32), table],
        [
            pltpu.VMEM(orb.shape, F32),
            pltpu.VMEM(proj.shape, BF16),
            pltpu.SemaphoreType.DMA((2 + PIECES * g.no,)),
            *entries,
            *sums,
        ],
        [orb, proj, pot, blk, atom],
        [HBM] * 5,
    )
    (acc,), received = local_and_ends(1.0, "first", v, [], part)
    u, part = call(
        functools.partial(middle_kernel, g),
        "tables_second",
        [field, table],
        [*entries, *sums],
        [acc, projf, blk, atom, *received],
        [VMEM] * 2 + [HBM] * 2 + [VMEM] * len(received),
    )
    out, received = local_and_ends(2.0, "second", u, [v], part)
    far = out[5:]
    weights = call(
        functools.partial(panel_kernel, g),
        "panel",
        jax.ShapeDtypeStruct((16 * g.no, 32 * g.no), BF16),
        [],
        [panel],
        [VMEM],
    )
    rotated = None
    pieces = []
    parts = halves(g, 0)
    for number, (_, count) in enumerate(parts):
        if number < len(far):
            filtered = far[number]
        else:
            inputs = [*out[:5], *received]
            filtered = call(
                functools.partial(last_kernel, g, len(far) > 0),
                "filtered",
                jax.ShapeDtypeStruct((count * g.slab, g.cz), BF16),
                [pltpu.VMEM((count * g.slab, g.cz), F32)],
                inputs,
                [VMEM] * len(inputs),
            )
        pieces.append((filtered, lax.ppermute(filtered, "band", [(0, 1), (1, 0)]), count))
    for number, (filtered, other, count) in enumerate(pieces):
        inputs = [filtered, other, weights] + ([] if rotated is None else [rotated])
        rotated = call(
            functools.partial(rotate_kernel, g, number),
            "rotate_%d" % number,
            jax.ShapeDtypeStruct((g.no, g.rows, g.cz), F32),
            [pltpu.VMEM((g.no, count * g.cy, g.cz), F32), pltpu.SemaphoreType.DMA((count * g.cy // 16,))],
            inputs,
            [VMEM] * 3 + [HBM] * (len(inputs) - 3),
            out_specs=HBM,
            input_output_aliases={} if rotated is None else {3: 0},
        )
    return rotated.reshape(orbitals.shape)


def solution(mesh):
    in_specs = (
        P("dom", "band", None, None, None),
        P("dom", None, None, None),
        P("dom", None, None),
        P("dom"),
        P("dom"),
        P(),
        P(),
    )
    out_specs = P("dom", "band", None, None, None)
    return jax.shard_map(shards, mesh=mesh, in_specs=in_specs, out_specs=out_specs, check_vma=False)
```

```python
import functools

import jax
import jax.numpy as jnp
from jax import lax
from jax.experimental import pallas as pl
from jax.experimental.pallas import tpu as pltpu
from jax.sharding import PartitionSpec as P

RADIUS = 6
PIECES = 3
COEFFS = (
    -5369.0 / 1800.0,
    12.0 / 7.0,
    -15.0 / 56.0,
    10.0 / 189.0,
    -1.0 / 112.0,
    2.0 / 1925.0,
    -1.0 / 16632.0,
)
KINETIC = -3.125
CENTER = 36.0
HALF_WIDTH = 34.0
WEIGHT = [KINETIC * c / HALF_WIDTH for c in COEFFS]
DIAGONAL = (3.0 * KINETIC * COEFFS[0] - CENTER) / HALF_WIDTH

F32 = jnp.float32
BF16 = jnp.bfloat16
VMEM = pl.BlockSpec(memory_space=pltpu.VMEM)
HBM = pl.BlockSpec(memory_space=pltpu.HBM)
NT = (((1,), (1,)), ((), ()))
TN = (((0,), (0,)), ((), ()))
NN = (((1,), (0,)), ((), ()))


def split2(x):
    high = x.astype(BF16)
    low = (x - high.astype(F32)).astype(BF16)
    return high, low


def iota(shape, dim):
    return lax.broadcasted_iota(jnp.int32, shape, dim)


def weight_at(distance, scale):
    out = jnp.zeros(distance.shape, F32)
    for k in range(1, RADIUS + 1):
        out = jnp.where(distance == k, scale * WEIGHT[k], out)
    return out


class Geometry:
    def __init__(self, orbitals, entries, nproj, atoms, dom_count):
        _, self.no, self.cx, self.cy, self.cz = orbitals
        self.rows = self.cx * self.cy
        self.flat = self.rows * self.no
        self.ent = entries
        self.nproj = nproj
        self.dom_count = dom_count
        self.owned = atoms // dom_count
        self.third = 4
        self.second = min(8, dom_count // 8)
        self.plane = self.second * self.third
        self.first = dom_count // self.plane
        self.table = self.owned * nproj * self.no
        self.slab = self.cy * self.no
        self.fold = self.flat // self.table
        self.butterfly = self.first == 2 and self.second == 2 and dom_count <= 2 * self.fold
        assert self.no == 8

    def faces(self, dom, dim):
        if dim == 0:
            extent, place = self.first, dom // self.plane
        else:
            extent, place = self.second, dom // self.third % self.second
        if extent == 2:
            return [(1 - place, None)]
        if extent > 2:
            return [(0, place > 0), (1, place < extent - 1)]
        return []

    def face_rows(self, dim):
        rows = RADIUS * self.slab if dim == 0 else self.cx * RADIUS * self.no
        return [rows] * len(self.faces(0, dim))

    def steps(self, dom):
        out = [0]
        for extent, stride in ((self.first, self.plane), (self.second, self.third), (self.third, 1)):
            if extent == 2:
                out.append((1 - 2 * (dom // stride % 2)) * stride)
            elif extent > 2:
                out.extend([stride, -stride])
        return out

    def slots(self):
        return len(self.steps(0))


def layer(side, length, j):
    if isinstance(side, int):
        return length - 1 - j if side else j
    return side * (length - 1 - j) + (1 - side) * j


def aligned(start, unit):
    return start if isinstance(start, int) else pl.multiple_of(start, unit)


def pack_x(g, dom, v_ref, refs):
    for (side, _), out in zip(g.faces(dom, 0), refs):
        for j in range(RADIUS):
            at = aligned(layer(side, g.cx, j) * g.slab, g.slab)
            out[j * g.slab : (j + 1) * g.slab, :] = v_ref[pl.ds(at, g.slab), :].astype(BF16)


def pack_y(g, dom, v_ref, refs):
    size = RADIUS * g.no
    for (side, _), out in zip(g.faces(dom, 1), refs):
        for x in range(g.cx):
            pieces = []
            for j in range(RADIUS):
                at = aligned(x * g.slab + layer(side, g.cy, j) * g.no, g.no)
                pieces.append(v_ref[pl.ds(at, g.no), :])
            out[x * size : (x + 1) * size, :] = jnp.concatenate(pieces, axis=0).astype(BF16)


def end_columns(g, dom):
    row, col = iota((16, g.cz), 0), iota((16, g.cz), 1)
    odd = dom % 2
    side = jnp.where(row < 8, 1 - odd, odd)
    return jnp.where(side == 1, g.cz - 1 - col, col), row


def pack_ends(g, dom, v_ref, first_ref, second_ref):
    inward, row = end_columns(g, dom)
    pick = jnp.where((inward == row % 8) & (row % 8 < RADIUS), 1.0, 0.0).astype(BF16)
    pick = jnp.concatenate([pick, pick], axis=1)
    for x in range(g.cx):
        rows = slice(x * g.slab, (x + 1) * g.slab)
        both = jnp.concatenate(split2(v_ref[rows, :]), axis=1)
        ends = lax.dot_general(pick, both, NT, preferred_element_type=F32)
        first_ref[:, rows] = ends[:8]
        second_ref[:, rows] = ends[8:]


def put_table(g, message, table):
    for n in range(g.dom_count):
        at = RADIUS + n // g.fold
        lanes = n % g.fold * g.table
        message[at : at + 1, lanes : lanes + g.table] = table[n : n + 1, :]


def get_table(g, message):
    rows = []
    for n in range(g.dom_count):
        at = RADIUS + n // g.fold
        lanes = n % g.fold * g.table
        rows.append(message[at : at + 1, lanes : lanes + g.table])
    return jnp.concatenate(rows, axis=0)


def fill_lut(g, dom, lut):
    for number, step in enumerate(g.steps(dom)):
        lut[g.plane + dom + step] = number * g.owned


def column_of(g, lut, atom):
    if g.owned & (g.owned - 1):
        owner = lax.div(atom, jnp.int32(g.owned))
        return lut[owner + g.plane] + (atom - owner * g.owned)
    owner = lax.shift_right_logical(atom, jnp.int32(g.owned.bit_length() - 1))
    return lut[owner + g.plane] + (atom & (g.owned - 1))


def inner_tables(g, dom, v_ref, projf, blk, atom, lut, sums, table):
    size = g.nproj * g.no

    unroll = 32

    def step(i, _):
        for u in range(unroll):
            part = sums[u % len(sums)]
            e = i * unroll + u
            col = column_of(g, lut, atom[e])
            v = v_ref[pl.ds(pl.multiple_of(blk[e] * g.no, g.no), g.no), :]
            for p in range(g.nproj):
                at = pl.ds(pl.multiple_of(col * size + p * g.no, g.no), g.no)
                coef = jnp.broadcast_to(projf[e, p : p + 1, :], v.shape)
                part[at, :] += v * coef
        return 0

    lax.fori_loop(0, g.ent // unroll, step, 0)
    total = sums[0][...]
    for part in sums[1:]:
        total = total + part[...]
    both = jnp.concatenate(split2(total), axis=1)
    ones = jnp.ones((8, both.shape[1]), BF16)
    summed = lax.dot_general(ones, both, NT, preferred_element_type=F32)
    table[...] = jnp.zeros(table.shape, F32)
    for number, step in enumerate(g.steps(dom)):
        owner = jnp.clip(dom + step, 0, g.dom_count - 1)
        table[pl.ds(owner, 1), :] += summed[0:1, number * g.table : (number + 1) * g.table]


def clear(sums):
    for part in sums:
        part[...] = jnp.zeros(part.shape, F32)


def entry_copies(blk_hbm, atom_hbm, blk, atom, sem):
    copies = [
        pltpu.make_async_copy(blk_hbm, blk, sem.at[0]),
        pltpu.make_async_copy(atom_hbm, atom, sem.at[1]),
    ]
    for copy in copies:
        copy.start()
    return copies


def first_kernel(g, orb_hbm, proj_hbm, pot_hbm, blk_hbm, atom_hbm, v_ref, projf, pot, table, *scratch):
    orb, proj, sem, blk, atom, lut, entry_sem = scratch[:7]
    sums = scratch[7:]
    copies = [
        pltpu.make_async_copy(proj_hbm, proj, sem.at[0]),
        pltpu.make_async_copy(pot_hbm, pot, sem.at[1]),
    ]
    for copy in copies:
        copy.start()
    size = g.rows // PIECES
    pieces = []
    for n in range(PIECES):
        for o in range(g.no):
            at = pl.ds(o * g.rows + n * size, size)
            pieces.append(pltpu.make_async_copy(orb_hbm.at[at, :], orb.at[at, :], sem.at[2 + len(pieces)]))
            pieces[-1].start()
    copies += entry_copies(blk_hbm, atom_hbm, blk, atom, entry_sem)
    dom = lax.axis_index("dom")
    fill_lut(g, dom, lut)
    clear(sums)
    copies[0].wait()
    projf[...] = proj[...].astype(F32)
    for r in range(g.rows):
        if r % size == 0:
            for piece in pieces[r // size * g.no : (r // size + 1) * g.no]:
                piece.wait()
        v_ref[r * g.no : (r + 1) * g.no, :] = orb[pl.ds(r, g.no, stride=g.rows), :]
    for copy in copies[1:]:
        copy.wait()
    inner_tables(g, dom, v_ref, projf, blk, atom, lut, sums, table)


def pack_kernel(g, count, *refs):
    source, refs = refs[:count], refs[count:]
    part, from_x, from_y, from_xy = refs[:4]
    outs, group = refs[-3:-1], refs[-1]
    group[...] = (part[...] + from_x[...]) + (from_y[...] + from_xy[...])
    if len(source) == 1:
        pack_ends(g, lax.axis_index("dom"), *source, *outs)
    for n, out in enumerate(outs):
        if len(source) == 2:
            out[...] = source[n][...]
        put_table(g, out, group)


def pack_faces_kernel(g, nafter, v_ref, *refs):
    nx = len(g.face_rows(0))
    dom = lax.axis_index("dom")
    refs = refs[nafter:]
    pack_x(g, dom, v_ref, refs[:nx])
    ny = len(g.face_rows(1))
    pack_y(g, dom, v_ref, refs[nx : nx + ny])
    if len(refs) > nx + ny:
        pack_ends(g, dom, v_ref, *refs[nx + ny :])


def inside_kernel(g, scale, subtract, v_ref, pot, *refs):
    prev, out = refs if subtract else (None, refs[0])
    row, col = iota((g.cz, g.cz), 0), iota((g.cz, g.cz), 1)
    high, low = split2(weight_at(jnp.abs(row - col), scale))
    band = jnp.concatenate([high, low], axis=1)
    band = jnp.concatenate([band, band], axis=0)

    def cell(x, y):
        at = (x * g.cy + y) * g.no
        return v_ref[at : at + g.no, :]

    for x in range(g.cx):
        both = jnp.concatenate(split2(v_ref[x * g.slab : (x + 1) * g.slab, :]), axis=1)
        along = lax.dot_general(both, band, NN, preferred_element_type=F32)
        for y in range(g.cy):
            at = (x * g.cy + y) * g.no
            rows = slice(y * g.no, (y + 1) * g.no)
            here = cell(x, y)
            diag = jnp.broadcast_to(pot[x * g.cy + y : x * g.cy + y + 1, :], here.shape)
            total = along[rows, : g.cz] + along[rows, g.cz :]
            total = total + (scale * DIAGONAL + (scale / HALF_WIDTH) * diag) * here
            if subtract:
                total = total - prev[at : at + g.no, :]
            for k in range(1, RADIUS + 1):
                near = []
                for a, b in ((x - k, y), (x + k, y), (x, y - k), (x, y + k)):
                    if 0 <= a < g.cx and 0 <= b < g.cy:
                        near.append(cell(a, b))
                if near:
                    total = total + (scale * WEIGHT[k]) * sum(near[1:], near[0])
            out[at : at + g.no, :] = total


def flag(present):
    return 1.0 if present is None else jnp.where(present, 1.0, 0.0)


def add_ends(g, dom, scale, acc, low, high, others, out, start, count):
    inward, row = end_columns(g, dom)
    middle = (dom % g.third > 0) & (dom % g.third < g.third - 1)
    present = (row % 8 < RADIUS) & ((row < 8) | middle)
    coef = jnp.where(present, weight_at(inward + row % 8 + 1, scale), 0.0)
    c_high, c_low = split2(coef)
    coefs = jnp.concatenate([c_high, c_high, c_low, c_low], axis=0)
    for x in range(count):
        rows = pl.ds(aligned((start + x) * g.slab, g.slab), g.slab)
        h_high, h_low = split2(jnp.concatenate([low[:, rows], high[:, rows]], axis=0))
        halo = jnp.concatenate([h_high, h_low, h_high, h_low], axis=0)
        total = acc[rows, :]
        for other in others:
            total = total + other[rows, :]
        total = total + lax.dot_general(halo, coefs, TN, preferred_element_type=F32)
        out[x * g.slab : (x + 1) * g.slab, :] = total


def add_x_faces(g, dom, scale, face_refs, out, count):
    unit = 2 * g.no
    for (side, present), face in zip(g.faces(dom, 0), face_refs):
        for y in range(0, g.cy, 2):
            starts = [j * g.slab + y * g.no for j in range(RADIUS)]
            part = [flag(present) * face[at : at + unit, :].astype(F32) for at in starts]
            for i in range(RADIUS):
                at = aligned(layer(side, count, i) * g.slab + y * g.no, unit)
                total = out[pl.ds(at, unit), :]
                for j in range(RADIUS - i):
                    total = total + (scale * WEIGHT[i + j + 1]) * part[j]
                out[pl.ds(at, unit), :] = total


def add_y_faces(g, dom, scale, face_refs, out, start, count):
    size = RADIUS * g.no
    for (side, present), face in zip(g.faces(dom, 1), face_refs):
        for x in range(count):
            part = face[pl.ds(aligned((start + x) * size, 16), size), :]
            part = flag(present) * part.astype(F32)
            for i in range(RADIUS):
                at = aligned(x * g.slab + layer(side, g.cy, i) * g.no, g.no)
                total = out[pl.ds(at, g.no), :]
                for j in range(RADIUS - i):
                    total = total + (scale * WEIGHT[i + j + 1]) * part[j * g.no : (j + 1) * g.no]
                out[pl.ds(at, g.no), :] = total


def spread_rows(g, dom, table, energy, spread):
    lanes = g.table
    count = g.slots()
    rows = []
    for step in g.steps(dom):
        owner = pl.ds(jnp.clip(dom + step, 0, g.dom_count - 1), 1)
        rows.append(table[owner, :] * energy[owner, :])
    rows.append(jnp.zeros((8 - count, lanes), F32))
    scaled = jnp.concatenate(rows, axis=0)
    high = scaled.astype(BF16)
    rest = scaled - high.astype(F32)
    mid = rest.astype(BF16)
    low = (rest - mid.astype(F32)).astype(BF16)
    parts = jnp.concatenate([high, mid, low], axis=0)
    wide = count * g.cz
    row, col = iota((24, wide), 0), iota((24, wide), 1)
    ones = jnp.where(row % 8 == col // g.cz, 1.0, 0.0).astype(BF16)
    out_all = lax.dot_general(parts, ones, TN, preferred_element_type=F32)
    for number in range(count):
        spread[number * lanes : (number + 1) * lanes, :] = out_all[:, number * g.cz : (number + 1) * g.cz]

def add_nonlocal(g, projf, blk, atom, lut, spread, outs):
    size = g.nproj * g.no
    unroll = 32

    def step(i, _):
        for u in range(unroll):
            e = i * unroll + u
            col = column_of(g, lut, atom[e])
            total = None
            for p in range(g.nproj):
                at = pl.ds(pl.multiple_of(col * size + p * g.no, g.no), g.no)
                coef = jnp.broadcast_to(projf[e, p : p + 1, :], (g.no, g.cz))
                term = spread[at, :] * coef
                total = term if total is None else total + term
            at = pl.ds(pl.multiple_of(blk[e] * g.no, g.no), g.no)
            outs[u % len(outs)][at, :] += total
        return 0

    lax.fori_loop(0, g.ent // unroll, step, 0)


def nonlocal_kernel(g, scale, far, with_y, acc, projf, energy, blk_hbm, atom_hbm, first, second, *refs):
    if far:
        filtered, *sums, table, blk, atom, lut, sem, spread, out = refs[-10:]
        rest = refs[:-10]
    else:
        out, table, blk, atom, lut, sem, spread, *sums = refs[-9:]
        rest = refs[:-9]
    y_refs = rest[len(rest) - len(g.face_rows(1)) :]
    copies = entry_copies(blk_hbm, atom_hbm, blk, atom, sem)
    dom = lax.axis_index("dom")
    fill_lut(g, dom, lut)
    if g.butterfly:
        group, opposite = refs[:2]
        table[...] = (group[...] + get_table(g, first)) + (get_table(g, second) + opposite[...])
    else:
        table[...] = refs[0][...]
    spread_rows(g, dom, table, energy, spread)
    clear(sums)
    for copy in copies:
        copy.wait()
    add_nonlocal(g, projf, blk, atom, lut, spread, sums)
    start, count = halves(g, dom)[0] if far else (0, g.cx)
    add_ends(g, dom, scale, acc, first, second, sums, out, start, count)
    if with_y:
        add_y_faces(g, dom, scale, y_refs, out, start, count)
    if far:
        filtered[...] = out[...].astype(BF16)


def middle_kernel(g, acc, projf, blk_hbm, atom_hbm, *refs):
    nx, ny = len(g.face_rows(0)), len(g.face_rows(1))
    faces = refs[: nx + ny]
    u_ref, table, blk, atom, lut, sem = refs[nx + ny : nx + ny + 6]
    sums = refs[nx + ny + 6 :]
    copies = entry_copies(blk_hbm, atom_hbm, blk, atom, sem)
    dom = lax.axis_index("dom")
    fill_lut(g, dom, lut)
    clear(sums)
    u_ref[...] = acc[...]
    add_x_faces(g, dom, 1.0, faces[:nx], u_ref, g.cx)
    add_y_faces(g, dom, 1.0, faces[nx:], u_ref, 0, g.cx)
    for copy in copies:
        copy.wait()
    inner_tables(g, dom, u_ref, projf, blk, atom, lut, sums, table)


def halves(g, dom):
    if g.first != 2 or g.cx != 2 * RADIUS:
        return [(0, g.cx)]
    side = 1 - dom // g.plane
    return [((1 - side) * RADIUS, RADIUS), (side * RADIUS, RADIUS)]


def strips(g, dom):
    parts = halves(g, dom)
    if len(parts) == 1:
        return parts
    start, count = parts[1]
    return [parts[0], (start, count - 2), (start + count - 2, 2)]


def last_kernel(g, rest, acc, *refs):
    nx = len(g.face_rows(0))
    work = refs[-1]
    dom = lax.axis_index("dom")
    start, count = halves(g, dom)[-1]
    if rest:
        first, second, *sums = refs[:4]
        refs = refs[4:]
        add_ends(g, dom, 2.0, acc, first, second, sums, work, start, count)
        add_y_faces(g, dom, 2.0, refs[nx : nx + len(g.face_rows(1))], work, start, count)
        parts = strips(g, 0)[1:]
    else:
        work[...] = acc[...]
        parts = strips(g, 0)
    add_x_faces(g, dom, 2.0, refs[:nx], work, count)
    at = 0
    for out, (_, layers) in zip(refs[-1 - len(parts) : -1], parts):
        size = layers * g.slab
        out[...] = work[at : at + size, :].astype(BF16)
        at += size


def panel_kernel(g, panel, weights):
    band = lax.axis_index("band")
    group = 16
    span = group * g.no
    norb = panel.shape[0]
    row, col = iota((span, norb), 0), iota((span, norb), 1)
    pick_out = jnp.where(col == band * g.no + row // group, 1.0, 0.0).astype(BF16)
    picked = lax.dot_general(pick_out, panel[...], NT, preferred_element_type=F32).astype(BF16)
    row, col = iota((norb, 2 * span), 0), iota((norb, 2 * span), 1)
    source = jnp.where(col < span, band, 1 - band) * g.no + col % g.no
    pick_in = jnp.where(row == source, 1.0, 0.0).astype(BF16)
    spread = lax.dot_general(picked, pick_in, NN, preferred_element_type=F32)
    row, col = iota((span, 2 * span), 0), iota((span, 2 * span), 1)
    same = row % group == (col % span) // g.no
    weights[...] = jnp.where(same, spread, 0.0).astype(BF16)


def rotate_kernel(g, number, own, other, weights, *refs):
    out_hbm, out, sem = refs[-3:]
    start, count = strips(g, lax.axis_index("dom"))[number]
    group = 16
    span = group * g.no
    copies = []
    size = count * g.cy
    for n in range(size // group):
        rows = slice(n * span, (n + 1) * span)
        both = jnp.concatenate([own[rows, :], other[rows, :]], axis=0)
        result = lax.dot_general(weights[...], both, NN, preferred_element_type=F32)
        for j in range(g.no):
            out[j, n * group : (n + 1) * group, :] = result[j * group : (j + 1) * group, :]
        to = pl.ds(aligned(start * g.cy + n * group, group), group)
        source = out.at[:, pl.ds(n * group, group), :]
        copies.append(pltpu.make_async_copy(source, out_hbm.at[:, to, :], sem.at[n]))
        copies[-1].start()
    for copy in copies:
        copy.wait()


def call(kernel, name, out_shape, scratch, args, specs, **options):
    return pl.pallas_call(
        kernel,
        name=name,
        out_shape=out_shape,
        in_specs=specs,
        out_specs=options.pop("out_specs", jax.tree.map(lambda _: VMEM, out_shape)),
        scratch_shapes=scratch,
        compiler_params=pltpu.CompilerParams(vmem_limit_bytes=48 * 1024 * 1024),
        cost_estimate=pl.CostEstimate(flops=1000, bytes_accessed=1000, transcendentals=0),
        **options,
    )(*args)


def shift(g, array, stride, extent, step):
    pairs = []
    for i in range(g.dom_count):
        place = i // stride % extent
        pairs.append((i, i + ((place + step) % extent - place) * stride))
    return lax.ppermute(array, "dom", pairs)


def swap_faces(g, faces, stride, extent):
    if extent == 2:
        return [shift(g, faces[0], stride, extent, 1)]
    if extent > 2:
        return [shift(g, faces[1], stride, extent, 1), shift(g, faces[0], stride, extent, -1)]
    return []


def shards(orbitals, potential, projectors, entry_atom, entry_block, kb_energy, panel):
    g = Geometry(
        orbitals.shape, projectors.shape[0], projectors.shape[1], kb_energy.shape[0], lax.axis_size("dom")
    )

    def in_hbm(array):
        return pltpu.with_memory_space_constraint(array, pltpu.HBM)

    orb = in_hbm(orbitals.reshape(g.flat, g.cz))
    pot = in_hbm(potential.reshape(g.rows, g.cz))
    proj = in_hbm(projectors)
    blk, atom = in_hbm(entry_block), in_hbm(entry_atom)
    field = jax.ShapeDtypeStruct((g.flat, g.cz), F32)
    x_faces = [jax.ShapeDtypeStruct((n, g.cz), BF16) for n in g.face_rows(0)]
    y_faces = [jax.ShapeDtypeStruct((n, g.cz), BF16) for n in g.face_rows(1)]
    nx = len(x_faces)
    ends = jax.ShapeDtypeStruct((8, g.flat), F32)
    table = jax.ShapeDtypeStruct((g.dom_count, g.table), F32)
    entries = [
        pltpu.SMEM((g.ent,), jnp.int32),
        pltpu.SMEM((g.ent,), jnp.int32),
        pltpu.SMEM((g.dom_count + 2 * g.plane,), jnp.int32),
        pltpu.SemaphoreType.DMA((2,)),
    ]
    slots = g.slots() * g.table
    sums = [pltpu.VMEM((slots, g.cz), F32) for _ in range(4)]
    spread = pltpu.VMEM((slots, g.cz), F32)
    indices = range(g.dom_count)

    def swap(array, *strides):
        pairs = [(i, i + sum(s * (1 - 2 * (i // s % 2)) for s in strides)) for i in indices]
        return lax.ppermute(array, "dom", pairs)

    def reverse(array):
        pairs = [(i, i - i % g.third + g.third - 1 - i % g.third) for i in indices]
        return lax.ppermute(array, "dom", pairs)

    def local_and_ends(scale, which, values, prev, part):
        energy = (scale / HALF_WIDTH) * kb_energy
        energy = jnp.repeat(energy.reshape(g.dom_count, g.owned * g.nproj), g.no, axis=1)
        acc = call(
            functools.partial(inside_kernel, g, scale, len(prev) > 0),
            "inside_" + which,
            field,
            [],
            [values, pot, *prev],
            [VMEM] * (2 + len(prev)),
        )

        after = []
        tables = []
        if g.butterfly:
            routes = [(g.third,), (g.plane, g.third), (g.plane,)]
            if not prev:
                routes = [(g.third,), (g.plane,), (g.plane, g.third)]
            tables = [part] + [swap(part, *route) for route in routes]
            after.append(tables[1])
        packed = [ends, ends] if prev or not g.butterfly else []
        faces = call(
            functools.partial(pack_faces_kernel, g, len(after)),
            "faces_" + which,
            [*x_faces, *y_faces, *packed],
            [],
            [values, *after],
            [VMEM] * (1 + len(after)),
        )
        both = nx + len(y_faces)
        from_x = swap_faces(g, faces[:nx], g.plane, g.first)
        from_y = swap_faces(g, faces[nx:both], g.third, g.second)
        source = faces[both:] or [values]
        if g.butterfly:
            first, second, group = call(
                functools.partial(pack_kernel, g, len(source)),
                "pack_" + which,
                [ends, ends, table],
                [],
                [*source, *tables, energy],
                [VMEM] * (len(source) + 5),
            )
        else:
            first, second = source
        first, second = swap(first, 1), reverse(second)
        tables = [group, swap(group, 2)] if g.butterfly else [lax.psum(part, "dom")]
        far = prev and len(halves(g, 0)) == 2
        scratch = [pltpu.VMEM(table.shape, F32), *entries, spread]
        outputs = [field]
        if far:
            half = halves(g, 0)[0][1] * g.slab
            outputs = [jax.ShapeDtypeStruct((half, g.cz), BF16), field, field]
            scratch.append(pltpu.VMEM((half, g.cz), F32))
        else:
            scratch += [pltpu.VMEM(field.shape, F32)] * 2
        tables += from_y if prev else []
        out = call(
            functools.partial(nonlocal_kernel, g, scale, far, len(prev) > 0),
            "nonlocal_" + which,
            outputs,
            scratch,
            [acc, projf, energy, blk, atom, first, second, *tables],
            [VMEM] * 3 + [HBM] * 2 + [VMEM] * (2 + len(tables)),
        )
        if far:
            out = [acc, first, second, *out[1:], out[0]]
        return out, from_x, from_y

    v, projf, pot, part = call(
        functools.partial(first_kernel, g),
        "tables_first",
        [field, jax.ShapeDtypeStruct(proj.shape, F32), jax.ShapeDtypeStruct(pot.shape, F32), table],
        [
            pltpu.VMEM(orb.shape, F32),
            pltpu.VMEM(proj.shape, BF16),
            pltpu.SemaphoreType.DMA((2 + PIECES * g.no,)),
            *entries,
            *sums,
        ],
        [orb, proj, pot, blk, atom],
        [HBM] * 5,
    )
    (acc,), from_x, from_y = local_and_ends(1.0, "first", v, [], part)
    received = [*from_x, *from_y]
    u, part = call(
        functools.partial(middle_kernel, g),
        "tables_second",
        [field, table],
        [*entries, *sums],
        [acc, projf, blk, atom, *received],
        [VMEM] * 2 + [HBM] * 2 + [VMEM] * len(received),
    )
    out, from_x, from_y = local_and_ends(2.0, "second", u, [v], part)
    far = out[5:]
    weights = call(
        functools.partial(panel_kernel, g),
        "panel",
        jax.ShapeDtypeStruct((16 * g.no, 32 * g.no), BF16),
        [],
        [panel],
        [VMEM],
    )
    rotated = None
    parts = strips(g, 0)
    inputs = [*out[:5], *from_x, *from_y] if far else [*out, *from_x]
    near = call(
        functools.partial(last_kernel, g, len(far) > 0),
        "filtered",
        [jax.ShapeDtypeStruct((count * g.slab, g.cz), BF16) for _, count in parts[len(far) :]],
        [pltpu.VMEM((halves(g, 0)[-1][1] * g.slab, g.cz), F32)],
        inputs,
        [VMEM] * len(inputs),
    )
    pieces = []
    for filtered, (_, count) in zip([*far, *near], parts):
        pieces.append((filtered, lax.ppermute(filtered, "band", [(0, 1), (1, 0)]), count))
    for number, (filtered, other, count) in enumerate(pieces):
        inputs = [filtered, other, weights] + ([] if rotated is None else [rotated])
        rotated = call(
            functools.partial(rotate_kernel, g, number),
            "rotate_%d" % number,
            jax.ShapeDtypeStruct((g.no, g.rows, g.cz), F32),
            [pltpu.VMEM((g.no, count * g.cy, g.cz), F32), pltpu.SemaphoreType.DMA((count * g.cy // 16,))],
            inputs,
            [VMEM] * 3 + [HBM] * (len(inputs) - 3),
            out_specs=HBM,
            input_output_aliases={} if rotated is None else {3: 0},
        )
    return rotated.reshape(orbitals.shape)


def solution(mesh):
    in_specs = (
        P("dom", "band", None, None, None),
        P("dom", None, None, None),
        P("dom", None, None),
        P("dom"),
        P("dom"),
        P(),
        P(),
    )
    out_specs = P("dom", "band", None, None, None)
    return jax.shard_map(shards, mesh=mesh, in_specs=in_specs, out_specs=out_specs, check_vma=False)
```

```python
import functools

import jax
import jax.numpy as jnp
from jax import lax
from jax.experimental import pallas as pl
from jax.experimental.pallas import tpu as pltpu
from jax.sharding import PartitionSpec as P

RADIUS = 6
PIECES = 3
COEFFS = (
    -5369.0 / 1800.0,
    12.0 / 7.0,
    -15.0 / 56.0,
    10.0 / 189.0,
    -1.0 / 112.0,
    2.0 / 1925.0,
    -1.0 / 16632.0,
)
KINETIC = -3.125
CENTER = 36.0
HALF_WIDTH = 34.0
WEIGHT = [KINETIC * c / HALF_WIDTH for c in COEFFS]
DIAGONAL = (3.0 * KINETIC * COEFFS[0] - CENTER) / HALF_WIDTH

F32 = jnp.float32
BF16 = jnp.bfloat16
VMEM = pl.BlockSpec(memory_space=pltpu.VMEM)
HBM = pl.BlockSpec(memory_space=pltpu.HBM)
NT = (((1,), (1,)), ((), ()))
TN = (((0,), (0,)), ((), ()))
NN = (((1,), (0,)), ((), ()))


def split2(x):
    high = x.astype(BF16)
    low = (x - high.astype(F32)).astype(BF16)
    return high, low


def iota(shape, dim):
    return lax.broadcasted_iota(jnp.int32, shape, dim)


def weight_at(distance, scale):
    out = jnp.zeros(distance.shape, F32)
    for k in range(1, RADIUS + 1):
        out = jnp.where(distance == k, scale * WEIGHT[k], out)
    return out


class Geometry:
    def __init__(self, orbitals, entries, nproj, atoms, dom_count):
        _, self.no, self.cx, self.cy, self.cz = orbitals
        self.rows = self.cx * self.cy
        self.flat = self.rows * self.no
        self.ent = entries
        self.nproj = nproj
        self.dom_count = dom_count
        self.owned = atoms // dom_count
        self.third = 4
        self.second = min(8, dom_count // 8)
        self.plane = self.second * self.third
        self.first = dom_count // self.plane
        self.table = self.owned * nproj * self.no
        self.slab = self.cy * self.no
        self.fold = self.flat // self.table
        self.butterfly = self.first == 2 and self.second == 2 and dom_count <= 2 * self.fold
        assert self.no == 8

    def faces(self, dom, dim):
        if dim == 0:
            extent, place = self.first, dom // self.plane
        else:
            extent, place = self.second, dom // self.third % self.second
        if extent == 2:
            return [(1 - place, None)]
        if extent > 2:
            return [(0, place > 0), (1, place < extent - 1)]
        return []

    def face_rows(self, dim):
        rows = RADIUS * self.slab if dim == 0 else self.cx * RADIUS * self.no
        return [rows] * len(self.faces(0, dim))

    def steps(self, dom):
        out = [0]
        for extent, stride in ((self.first, self.plane), (self.second, self.third), (self.third, 1)):
            if extent == 2:
                out.append((1 - 2 * (dom // stride % 2)) * stride)
            elif extent > 2:
                out.extend([stride, -stride])
        return out

    def slots(self):
        return len(self.steps(0))


def layer(side, length, j):
    if isinstance(side, int):
        return length - 1 - j if side else j
    return side * (length - 1 - j) + (1 - side) * j


def aligned(start, unit):
    return start if isinstance(start, int) else pl.multiple_of(start, unit)


def pack_x(g, dom, v_ref, refs):
    for (side, _), out in zip(g.faces(dom, 0), refs):
        for j in range(RADIUS):
            at = aligned(layer(side, g.cx, j) * g.slab, g.slab)
            out[j * g.slab : (j + 1) * g.slab, :] = v_ref[pl.ds(at, g.slab), :].astype(BF16)


def pack_y(g, dom, v_ref, refs):
    size = RADIUS * g.no
    for (side, _), out in zip(g.faces(dom, 1), refs):
        for x in range(g.cx):
            pieces = []
            for j in range(RADIUS):
                at = aligned(x * g.slab + layer(side, g.cy, j) * g.no, g.no)
                pieces.append(v_ref[pl.ds(at, g.no), :])
            out[x * size : (x + 1) * size, :] = jnp.concatenate(pieces, axis=0).astype(BF16)


def end_columns(g, dom):
    row, col = iota((16, g.cz), 0), iota((16, g.cz), 1)
    odd = dom % 2
    side = jnp.where(row < 8, 1 - odd, odd)
    return jnp.where(side == 1, g.cz - 1 - col, col), row


def pack_ends(g, dom, v_ref, first_ref, second_ref):
    inward, row = end_columns(g, dom)
    pick = jnp.where((inward == row % 8) & (row % 8 < RADIUS), 1.0, 0.0).astype(BF16)
    pick = jnp.concatenate([pick, pick], axis=1)
    for x in range(g.cx):
        rows = slice(x * g.slab, (x + 1) * g.slab)
        both = jnp.concatenate(split2(v_ref[rows, :]), axis=1)
        ends = lax.dot_general(pick, both, NT, preferred_element_type=F32)
        first_ref[:, rows] = ends[:8]
        second_ref[:, rows] = ends[8:]


def put_table(g, message, table):
    for n in range(g.dom_count):
        at = RADIUS + n // g.fold
        lanes = n % g.fold * g.table
        message[at : at + 1, lanes : lanes + g.table] = table[n : n + 1, :]


def get_table(g, message):
    rows = []
    for n in range(g.dom_count):
        at = RADIUS + n // g.fold
        lanes = n % g.fold * g.table
        rows.append(message[at : at + 1, lanes : lanes + g.table])
    return jnp.concatenate(rows, axis=0)


def fill_lut(g, dom, lut):
    for number, step in enumerate(g.steps(dom)):
        lut[g.plane + dom + step] = number * g.owned


def column_of(g, lut, atom):
    if g.owned & (g.owned - 1):
        owner = lax.div(atom, jnp.int32(g.owned))
        return lut[owner + g.plane] + (atom - owner * g.owned)
    owner = lax.shift_right_logical(atom, jnp.int32(g.owned.bit_length() - 1))
    return lut[owner + g.plane] + (atom & (g.owned - 1))


def inner_tables(g, dom, v_ref, projf, blk, atom, lut, sums, table):
    size = g.nproj * g.no

    unroll = 32

    def step(i, _):
        for u in range(unroll):
            part = sums[u % len(sums)]
            e = i * unroll + u
            col = column_of(g, lut, atom[e])
            v = v_ref[pl.ds(pl.multiple_of(blk[e] * g.no, g.no), g.no), :]
            for p in range(g.nproj):
                at = pl.ds(pl.multiple_of(col * size + p * g.no, g.no), g.no)
                coef = jnp.broadcast_to(projf[e, p : p + 1, :], v.shape)
                part[at, :] += v * coef
        return 0

    lax.fori_loop(0, g.ent // unroll, step, 0)
    total = sums[0][...]
    for part in sums[1:]:
        total = total + part[...]
    both = jnp.concatenate(split2(total), axis=1)
    ones = jnp.ones((8, both.shape[1]), BF16)
    summed = lax.dot_general(ones, both, NT, preferred_element_type=F32)
    table[...] = jnp.zeros(table.shape, F32)
    for number, step in enumerate(g.steps(dom)):
        owner = jnp.clip(dom + step, 0, g.dom_count - 1)
        table[pl.ds(owner, 1), :] += summed[0:1, number * g.table : (number + 1) * g.table]


def clear(sums):
    for part in sums:
        part[...] = jnp.zeros(part.shape, F32)


def entry_copies(blk_hbm, atom_hbm, blk, atom, sem):
    copies = [
        pltpu.make_async_copy(blk_hbm, blk, sem.at[0]),
        pltpu.make_async_copy(atom_hbm, atom, sem.at[1]),
    ]
    for copy in copies:
        copy.start()
    return copies


def first_kernel(g, orb_hbm, proj_hbm, pot_hbm, blk_hbm, atom_hbm, v_ref, projf, pot, table, *scratch):
    orb, proj, sem, blk, atom, lut, entry_sem = scratch[:7]
    sums = scratch[7:]
    copies = [
        pltpu.make_async_copy(proj_hbm, proj, sem.at[0]),
        pltpu.make_async_copy(pot_hbm, pot, sem.at[1]),
    ]
    for copy in copies:
        copy.start()
    size = g.rows // PIECES
    pieces = []
    for n in range(PIECES):
        for o in range(g.no):
            at = pl.ds(o * g.rows + n * size, size)
            pieces.append(pltpu.make_async_copy(orb_hbm.at[at, :], orb.at[at, :], sem.at[2 + len(pieces)]))
            pieces[-1].start()
    copies += entry_copies(blk_hbm, atom_hbm, blk, atom, entry_sem)
    dom = lax.axis_index("dom")
    fill_lut(g, dom, lut)
    clear(sums)
    copies[0].wait()
    projf[...] = proj[...].astype(F32)
    for r in range(g.rows):
        if r % size == 0:
            for piece in pieces[r // size * g.no : (r // size + 1) * g.no]:
                piece.wait()
        v_ref[r * g.no : (r + 1) * g.no, :] = orb[pl.ds(r, g.no, stride=g.rows), :]
    for copy in copies[1:]:
        copy.wait()
    inner_tables(g, dom, v_ref, projf, blk, atom, lut, sums, table)


def pack_kernel(g, count, *refs):
    source, refs = refs[:count], refs[count:]
    part, from_x, from_y, from_xy = refs[:4]
    outs, group = refs[-3:-1], refs[-1]
    group[...] = (part[...] + from_x[...]) + (from_y[...] + from_xy[...])
    if len(source) == 1:
        pack_ends(g, lax.axis_index("dom"), *source, *outs)
    for n, out in enumerate(outs):
        if len(source) == 2:
            out[...] = source[n][...]
        put_table(g, out, group)


def pack_faces_kernel(g, nafter, v_ref, *refs):
    nx = len(g.face_rows(0))
    dom = lax.axis_index("dom")
    refs = refs[nafter:]
    pack_x(g, dom, v_ref, refs[:nx])
    ny = len(g.face_rows(1))
    pack_y(g, dom, v_ref, refs[nx : nx + ny])
    if len(refs) > nx + ny:
        pack_ends(g, dom, v_ref, *refs[nx + ny :])


def inside_kernel(g, scale, subtract, v_ref, pot, *refs):
    prev, out = refs if subtract else (None, refs[0])
    row, col = iota((g.cz, g.cz), 0), iota((g.cz, g.cz), 1)
    high, low = split2(weight_at(jnp.abs(row - col), scale))
    band = jnp.concatenate([high, low], axis=1)
    band = jnp.concatenate([band, band], axis=0)

    def cell(x, y):
        at = (x * g.cy + y) * g.no
        return v_ref[at : at + g.no, :]

    for x in range(g.cx):
        both = jnp.concatenate(split2(v_ref[x * g.slab : (x + 1) * g.slab, :]), axis=1)
        along = lax.dot_general(both, band, NN, preferred_element_type=F32)
        for y in range(g.cy):
            at = (x * g.cy + y) * g.no
            rows = slice(y * g.no, (y + 1) * g.no)
            here = cell(x, y)
            diag = jnp.broadcast_to(pot[x * g.cy + y : x * g.cy + y + 1, :], here.shape)
            total = along[rows, : g.cz] + along[rows, g.cz :]
            total = total + (scale * DIAGONAL + (scale / HALF_WIDTH) * diag) * here
            if subtract:
                total = total - prev[at : at + g.no, :]
            for k in range(1, RADIUS + 1):
                near = []
                for a, b in ((x - k, y), (x + k, y), (x, y - k), (x, y + k)):
                    if 0 <= a < g.cx and 0 <= b < g.cy:
                        near.append(cell(a, b))
                if near:
                    total = total + (scale * WEIGHT[k]) * sum(near[1:], near[0])
            out[at : at + g.no, :] = total


def flag(present):
    return 1.0 if present is None else jnp.where(present, 1.0, 0.0)


def add_ends(g, dom, scale, acc, low, high, others, out, start, count):
    inward, row = end_columns(g, dom)
    middle = (dom % g.third > 0) & (dom % g.third < g.third - 1)
    present = (row % 8 < RADIUS) & ((row < 8) | middle)
    coef = jnp.where(present, weight_at(inward + row % 8 + 1, scale), 0.0)
    c_high, c_low = split2(coef)
    coefs = jnp.concatenate([c_high, c_high, c_low, c_low], axis=0)
    for x in range(count):
        rows = pl.ds(aligned((start + x) * g.slab, g.slab), g.slab)
        h_high, h_low = split2(jnp.concatenate([low[:, rows], high[:, rows]], axis=0))
        halo = jnp.concatenate([h_high, h_low, h_high, h_low], axis=0)
        total = acc[rows, :]
        for other in others:
            total = total + other[rows, :]
        total = total + lax.dot_general(halo, coefs, TN, preferred_element_type=F32)
        out[x * g.slab : (x + 1) * g.slab, :] = total


def add_x_faces(g, dom, scale, face_refs, out, count):
    unit = 2 * g.no
    for (side, present), face in zip(g.faces(dom, 0), face_refs):
        for y in range(0, g.cy, 2):
            starts = [j * g.slab + y * g.no for j in range(RADIUS)]
            part = [flag(present) * face[at : at + unit, :].astype(F32) for at in starts]
            for i in range(RADIUS):
                at = aligned(layer(side, count, i) * g.slab + y * g.no, unit)
                total = out[pl.ds(at, unit), :]
                for j in range(RADIUS - i):
                    total = total + (scale * WEIGHT[i + j + 1]) * part[j]
                out[pl.ds(at, unit), :] = total


def add_y_faces(g, dom, scale, face_refs, out, start, count):
    size = RADIUS * g.no
    for (side, present), face in zip(g.faces(dom, 1), face_refs):
        for x in range(count):
            part = face[pl.ds(aligned((start + x) * size, 16), size), :]
            part = flag(present) * part.astype(F32)
            for i in range(RADIUS):
                at = aligned(x * g.slab + layer(side, g.cy, i) * g.no, g.no)
                total = out[pl.ds(at, g.no), :]
                for j in range(RADIUS - i):
                    total = total + (scale * WEIGHT[i + j + 1]) * part[j * g.no : (j + 1) * g.no]
                out[pl.ds(at, g.no), :] = total


def spread_rows(g, dom, table, energy, wide, spread):
    lanes = g.table
    count = g.slots()
    row, col = iota((g.nproj, lanes), 0), iota((g.nproj, lanes), 1)
    pick = jnp.where(row == col // g.no % g.nproj, 1.0, 0.0)
    if energy.shape[0] == g.nproj:
        wide[...] = lax.dot_general(
            energy[...], pick, TN, precision=lax.Precision.HIGHEST, preferred_element_type=F32
        )
    place = iota((1, lanes), 1) // (g.nproj * g.no)
    rows = []
    for step in g.steps(dom):
        owner = jnp.clip(dom + step, 0, g.dom_count - 1)
        if energy.shape[0] == g.nproj:
            factor = jnp.zeros((1, lanes), F32)
            for a in range(g.owned):
                factor = jnp.where(place == a, wide[pl.ds(owner * g.owned + a, 1), :], factor)
        else:
            factor = energy[pl.ds(owner, 1), :]
        rows.append(table[pl.ds(owner, 1), :] * factor)
    rows.append(jnp.zeros((8 - count, lanes), F32))
    scaled = jnp.concatenate(rows, axis=0)
    high = scaled.astype(BF16)
    rest = scaled - high.astype(F32)
    mid = rest.astype(BF16)
    low = (rest - mid.astype(F32)).astype(BF16)
    parts = jnp.concatenate([high, mid, low], axis=0)
    row, col = iota((24, count * g.cz), 0), iota((24, count * g.cz), 1)
    ones = jnp.where(row % 8 == col // g.cz, 1.0, 0.0).astype(BF16)
    out_all = lax.dot_general(parts, ones, TN, preferred_element_type=F32)
    for number in range(count):
        spread[number * lanes : (number + 1) * lanes, :] = out_all[:, number * g.cz : (number + 1) * g.cz]

def add_nonlocal(g, projf, blk, atom, lut, spread, outs):
    size = g.nproj * g.no
    unroll = 32

    def step(i, _):
        for u in range(unroll):
            e = i * unroll + u
            col = column_of(g, lut, atom[e])
            total = None
            for p in range(g.nproj):
                at = pl.ds(pl.multiple_of(col * size + p * g.no, g.no), g.no)
                coef = jnp.broadcast_to(projf[e, p : p + 1, :], (g.no, g.cz))
                term = spread[at, :] * coef
                total = term if total is None else total + term
            at = pl.ds(pl.multiple_of(blk[e] * g.no, g.no), g.no)
            outs[u % len(outs)][at, :] += total
        return 0

    lax.fori_loop(0, g.ent // unroll, step, 0)


def nonlocal_kernel(g, scale, far, with_y, acc, projf, energy, blk_hbm, atom_hbm, first, second, *refs):
    if far:
        filtered, *sums, table, wide, blk, atom, lut, sem, spread, out = refs[-11:]
        rest = refs[:-11]
    else:
        out, table, wide, blk, atom, lut, sem, spread, *sums = refs[-10:]
        rest = refs[:-10]
    y_refs = rest[len(rest) - len(g.face_rows(1)) :]
    copies = entry_copies(blk_hbm, atom_hbm, blk, atom, sem)
    dom = lax.axis_index("dom")
    fill_lut(g, dom, lut)
    if g.butterfly:
        group, opposite = refs[:2]
        table[...] = (group[...] + get_table(g, first)) + (get_table(g, second) + opposite[...])
    else:
        table[...] = refs[0][...]
    spread_rows(g, dom, table, energy, wide, spread)
    clear(sums)
    for copy in copies:
        copy.wait()
    add_nonlocal(g, projf, blk, atom, lut, spread, sums)
    start, count = halves(g, dom)[0] if far else (0, g.cx)
    add_ends(g, dom, scale, acc, first, second, sums, out, start, count)
    if with_y:
        add_y_faces(g, dom, scale, y_refs, out, start, count)
    if far:
        filtered[...] = out[...].astype(BF16)


def middle_kernel(g, acc, projf, blk_hbm, atom_hbm, *refs):
    nx, ny = len(g.face_rows(0)), len(g.face_rows(1))
    faces = refs[: nx + ny]
    u_ref, table, blk, atom, lut, sem = refs[nx + ny : nx + ny + 6]
    sums = refs[nx + ny + 6 :]
    copies = entry_copies(blk_hbm, atom_hbm, blk, atom, sem)
    dom = lax.axis_index("dom")
    fill_lut(g, dom, lut)
    clear(sums)
    u_ref[...] = acc[...]
    add_x_faces(g, dom, 1.0, faces[:nx], u_ref, g.cx)
    add_y_faces(g, dom, 1.0, faces[nx:], u_ref, 0, g.cx)
    for copy in copies:
        copy.wait()
    inner_tables(g, dom, u_ref, projf, blk, atom, lut, sums, table)


def halves(g, dom):
    if g.first != 2 or g.cx != 2 * RADIUS:
        return [(0, g.cx)]
    side = 1 - dom // g.plane
    return [((1 - side) * RADIUS, RADIUS), (side * RADIUS, RADIUS)]


def strips(g, dom):
    parts = halves(g, dom)
    if len(parts) == 1:
        return parts
    start, count = parts[1]
    return [parts[0], (start, count - 2), (start + count - 2, 2)]


def last_kernel(g, rest, acc, *refs):
    nx = len(g.face_rows(0))
    work = refs[-1]
    dom = lax.axis_index("dom")
    start, count = halves(g, dom)[-1]
    if rest:
        first, second, *sums = refs[:4]
        refs = refs[4:]
        add_ends(g, dom, 2.0, acc, first, second, sums, work, start, count)
        add_y_faces(g, dom, 2.0, refs[nx : nx + len(g.face_rows(1))], work, start, count)
        parts = strips(g, 0)[1:]
    else:
        work[...] = acc[...]
        parts = strips(g, 0)
    add_x_faces(g, dom, 2.0, refs[:nx], work, count)
    at = 0
    for out, (_, layers) in zip(refs[-1 - len(parts) : -1], parts):
        size = layers * g.slab
        out[...] = work[at : at + size, :].astype(BF16)
        at += size


def panel_kernel(g, panel, weights):
    band = lax.axis_index("band")
    group = 16
    span = group * g.no
    norb = panel.shape[0]
    row, col = iota((span, norb), 0), iota((span, norb), 1)
    pick_out = jnp.where(col == band * g.no + row // group, 1.0, 0.0).astype(BF16)
    picked = lax.dot_general(pick_out, panel[...], NT, preferred_element_type=F32).astype(BF16)
    row, col = iota((norb, 2 * span), 0), iota((norb, 2 * span), 1)
    source = jnp.where(col < span, band, 1 - band) * g.no + col % g.no
    pick_in = jnp.where(row == source, 1.0, 0.0).astype(BF16)
    spread = lax.dot_general(picked, pick_in, NN, preferred_element_type=F32)
    row, col = iota((span, 2 * span), 0), iota((span, 2 * span), 1)
    same = row % group == (col % span) // g.no
    weights[...] = jnp.where(same, spread, 0.0).astype(BF16)


def rotate_kernel(g, number, own, other, weights, *refs):
    out_hbm, out, sem = refs[-3:]
    start, count = strips(g, lax.axis_index("dom"))[number]
    group = 16
    span = group * g.no
    copies = []
    size = count * g.cy
    for n in range(size // group):
        rows = slice(n * span, (n + 1) * span)
        both = jnp.concatenate([own[rows, :], other[rows, :]], axis=0)
        result = lax.dot_general(weights[...], both, NN, preferred_element_type=F32)
        for j in range(g.no):
            out[j, n * group : (n + 1) * group, :] = result[j * group : (j + 1) * group, :]
        to = pl.ds(aligned(start * g.cy + n * group, group), group)
        source = out.at[:, pl.ds(n * group, group), :]
        copies.append(pltpu.make_async_copy(source, out_hbm.at[:, to, :], sem.at[n]))
        copies[-1].start()
    for copy in copies:
        copy.wait()


def call(kernel, name, out_shape, scratch, args, specs, **options):
    return pl.pallas_call(
        kernel,
        name=name,
        out_shape=out_shape,
        in_specs=specs,
        out_specs=options.pop("out_specs", jax.tree.map(lambda _: VMEM, out_shape)),
        scratch_shapes=scratch,
        compiler_params=pltpu.CompilerParams(vmem_limit_bytes=48 * 1024 * 1024),
        cost_estimate=pl.CostEstimate(flops=1000, bytes_accessed=1000, transcendentals=0),
        **options,
    )(*args)


def shift(g, array, stride, extent, step):
    pairs = []
    for i in range(g.dom_count):
        place = i // stride % extent
        pairs.append((i, i + ((place + step) % extent - place) * stride))
    return lax.ppermute(array, "dom", pairs)


def swap_faces(g, faces, stride, extent):
    if extent == 2:
        return [shift(g, faces[0], stride, extent, 1)]
    if extent > 2:
        return [shift(g, faces[1], stride, extent, 1), shift(g, faces[0], stride, extent, -1)]
    return []


def shards(orbitals, potential, projectors, entry_atom, entry_block, kb_energy, panel):
    g = Geometry(
        orbitals.shape, projectors.shape[0], projectors.shape[1], kb_energy.shape[0], lax.axis_size("dom")
    )

    def in_hbm(array):
        return pltpu.with_memory_space_constraint(array, pltpu.HBM)

    orb = in_hbm(orbitals.reshape(g.flat, g.cz))
    pot = in_hbm(potential.reshape(g.rows, g.cz))
    proj = in_hbm(projectors)
    blk, atom = in_hbm(entry_block), in_hbm(entry_atom)
    field = jax.ShapeDtypeStruct((g.flat, g.cz), F32)
    x_faces = [jax.ShapeDtypeStruct((n, g.cz), BF16) for n in g.face_rows(0)]
    y_faces = [jax.ShapeDtypeStruct((n, g.cz), BF16) for n in g.face_rows(1)]
    nx = len(x_faces)
    ends = jax.ShapeDtypeStruct((8, g.flat), F32)
    table = jax.ShapeDtypeStruct((g.dom_count, g.table), F32)
    entries = [
        pltpu.SMEM((g.ent,), jnp.int32),
        pltpu.SMEM((g.ent,), jnp.int32),
        pltpu.SMEM((g.dom_count + 2 * g.plane,), jnp.int32),
        pltpu.SemaphoreType.DMA((2,)),
    ]
    slots = g.slots() * g.table
    sums = [pltpu.VMEM((slots, g.cz), F32) for _ in range(4)]
    spread = pltpu.VMEM((slots, g.cz), F32)
    indices = range(g.dom_count)

    def swap(array, *strides):
        pairs = [(i, i + sum(s * (1 - 2 * (i // s % 2)) for s in strides)) for i in indices]
        return lax.ppermute(array, "dom", pairs)

    def reverse(array):
        pairs = [(i, i - i % g.third + g.third - 1 - i % g.third) for i in indices]
        return lax.ppermute(array, "dom", pairs)

    def local_and_ends(scale, which, values, prev, part):
        energy = (scale / HALF_WIDTH) * kb_energy
        if prev:
            energy = jnp.repeat(energy.reshape(g.dom_count, g.owned * g.nproj), g.no, axis=1)
        else:
            energy = energy.T
        acc = call(
            functools.partial(inside_kernel, g, scale, len(prev) > 0),
            "inside_" + which,
            field,
            [],
            [values, pot, *prev],
            [VMEM] * (2 + len(prev)),
        )

        after = []
        tables = []
        if g.butterfly:
            routes = [(g.third,), (g.plane, g.third), (g.plane,)]
            if not prev:
                routes = [(g.third,), (g.plane,), (g.plane, g.third)]
            tables = [part] + [swap(part, *route) for route in routes]
            after.append(tables[1])
        packed = [ends, ends] if prev or not g.butterfly else []
        faces = call(
            functools.partial(pack_faces_kernel, g, len(after)),
            "faces_" + which,
            [*x_faces, *y_faces, *packed],
            [],
            [values, *after],
            [VMEM] * (1 + len(after)),
        )
        both = nx + len(y_faces)
        from_x = swap_faces(g, faces[:nx], g.plane, g.first)
        from_y = swap_faces(g, faces[nx:both], g.third, g.second)
        source = faces[both:] or [values]
        if g.butterfly:
            first, second, group = call(
                functools.partial(pack_kernel, g, len(source)),
                "pack_" + which,
                [ends, ends, table],
                [],
                [*source, *tables, energy],
                [VMEM] * (len(source) + 5),
            )
        else:
            first, second = source
        first, second = swap(first, 1), reverse(second)
        tables = [group, swap(group, 2)] if g.butterfly else [lax.psum(part, "dom")]
        far = prev and len(halves(g, 0)) == 2
        wide = pltpu.VMEM((kb_energy.shape[0], g.table), F32)
        scratch = [pltpu.VMEM(table.shape, F32), wide, *entries, spread]
        outputs = [field]
        if far:
            half = halves(g, 0)[0][1] * g.slab
            outputs = [jax.ShapeDtypeStruct((half, g.cz), BF16), field, field]
            scratch.append(pltpu.VMEM((half, g.cz), F32))
        else:
            scratch += [pltpu.VMEM(field.shape, F32)] * 2
        tables += from_y if prev else []
        out = call(
            functools.partial(nonlocal_kernel, g, scale, far, len(prev) > 0),
            "nonlocal_" + which,
            outputs,
            scratch,
            [acc, projf, energy, blk, atom, first, second, *tables],
            [VMEM] * 3 + [HBM] * 2 + [VMEM] * (2 + len(tables)),
        )
        if far:
            out = [acc, first, second, *out[1:], out[0]]
        return out, from_x, from_y

    v, projf, pot, part = call(
        functools.partial(first_kernel, g),
        "tables_first",
        [field, jax.ShapeDtypeStruct(proj.shape, F32), jax.ShapeDtypeStruct(pot.shape, F32), table],
        [
            pltpu.VMEM(orb.shape, F32),
            pltpu.VMEM(proj.shape, BF16),
            pltpu.SemaphoreType.DMA((2 + PIECES * g.no,)),
            *entries,
            *sums,
        ],
        [orb, proj, pot, blk, atom],
        [HBM] * 5,
    )
    (acc,), from_x, from_y = local_and_ends(1.0, "first", v, [], part)
    received = [*from_x, *from_y]
    u, part = call(
        functools.partial(middle_kernel, g),
        "tables_second",
        [field, table],
        [*entries, *sums],
        [acc, projf, blk, atom, *received],
        [VMEM] * 2 + [HBM] * 2 + [VMEM] * len(received),
    )
    out, from_x, from_y = local_and_ends(2.0, "second", u, [v], part)
    far = out[5:]
    weights = call(
        functools.partial(panel_kernel, g),
        "panel",
        jax.ShapeDtypeStruct((16 * g.no, 32 * g.no), BF16),
        [],
        [panel],
        [VMEM],
    )
    rotated = None
    parts = strips(g, 0)
    inputs = [*out[:5], *from_x, *from_y] if far else [*out, *from_x]
    near = call(
        functools.partial(last_kernel, g, len(far) > 0),
        "filtered",
        [jax.ShapeDtypeStruct((count * g.slab, g.cz), BF16) for _, count in parts[len(far) :]],
        [pltpu.VMEM((halves(g, 0)[-1][1] * g.slab, g.cz), F32)],
        inputs,
        [VMEM] * len(inputs),
    )
    pieces = []
    for filtered, (_, count) in zip([*far, *near], parts):
        pieces.append((filtered, lax.ppermute(filtered, "band", [(0, 1), (1, 0)]), count))
    for number, (filtered, other, count) in enumerate(pieces):
        inputs = [filtered, other, weights] + ([] if rotated is None else [rotated])
        rotated = call(
            functools.partial(rotate_kernel, g, number),
            "rotate_%d" % number,
            jax.ShapeDtypeStruct((g.no, g.rows, g.cz), F32),
            [pltpu.VMEM((g.no, count * g.cy, g.cz), F32), pltpu.SemaphoreType.DMA((count * g.cy // 16,))],
            inputs,
            [VMEM] * 3 + [HBM] * (len(inputs) - 3),
            out_specs=HBM,
            input_output_aliases={} if rotated is None else {3: 0},
        )
    return rotated.reshape(orbitals.shape)


def solution(mesh):
    in_specs = (
        P("dom", "band", None, None, None),
        P("dom", None, None, None),
        P("dom", None, None),
        P("dom"),
        P("dom"),
        P(),
        P(),
    )
    out_specs = P("dom", "band", None, None, None)
    return jax.shard_map(shards, mesh=mesh, in_specs=in_specs, out_specs=out_specs, check_vma=False)
```
